128 devices in a mesh: dp: 8 (over z, core), wide: 16 (over x, y).
Axes of the slice: x: 4, y: 4, z: 4, core: 2. Of those that a mesh axis runs over, the one named last changes fastest.
Arguments:
- weights_flat: float32 [344064], P(('dp', 'wide')), as said below
- moment_one: float32 [344064], P(('dp', 'wide')), as said below
- moment_two: float32 [344064], P(('dp', 'wide')), as said below
- codes: float32 [32768, 256], P(('dp', 'wide')), may hold values from -1.8 to 1.8
- code_first: float32 [32768, 256], P(('dp', 'wide'))
- code_second: float32 [32768, 256], P(('dp', 'wide')), as said below
- coords: float32 [3, 131072], P(None, ('dp', 'wide')), may hold values from -1 to 1
- distances: float32 [131072], P(('dp', 'wide')), may hold values from -0.5 to 0.5
- shape_index: int32 [131072], P(('dp', 'wide')), may hold values from 0 to 32767, as said below
Outputs:
- loss_value: float32 [], replicated
- grad_norm: float32 [], replicated
- new_weights: float32 [344064], P(('dp', 'wide'))
- new_moment_one: float32 [344064], P(('dp', 'wide'))
- new_moment_two: float32 [344064], P(('dp', 'wide'))
- weights_copy: bfloat16 [344064], P(('dp', 'wide'))
- new_codes: float32 [32768, 256], P(('dp', 'wide'))
- new_code_first: float32 [32768, 256], P(('dp', 'wide'))
- new_code_second: float32 [32768, 256], P(('dp', 'wide'))
- codes_copy: bfloat16 [32768, 256], P(('dp', 'wide'))
The draws below stay inside these ranges and needn't reach their ends.
Inputs may be any that keep to these rules, and one draw needn't show every extreme that they name: `shape_index`: of the points of one device, at most 16 have shapes among one device's 256 rows of the table; this is reached on every device, and one device's rows are named by 16 points of every device. `weights_flat`: entries after the first 329714 are zero. `moment_one`: entries after the first 329714 are zero. `moment_two`: Positive, and zero after the first 329714 entries. `code_second`: Positive.
All inputs are finite; a program needn't handle non-finite values.
Results may differ from the reference program's by a relative error of at most 0.001.
Values sent between devices are 32-bit elements; how exact they have to be, the bound alone decides.
No kernel may reach another device: no remote copies, remote signals or barrier semaphores. Data moves between devices by JAX's collectives and lax.ppermute only.
A program may use at most 128 MiB of HBM per device.

```python
import math
import jax
import jax.numpy as jnp
from jax import lax

LATENT = 256
HID = 512
PTS_DEV = 1024
CODE_DEV = 256
STEP = 10
NPARAM = 329714
FLAT = 344064
POINTS = 131072
CODES = 32768
CAP = 16
N_DP = 8
N_WIDE = 16


CLIP = 0.001


def grad_scale():
    return CLIP / math.sqrt(NPARAM + POINTS * LATENT)


def code_scale():
    return CLIP * math.sqrt(PTS_DEV / CODE_DEV) * 0.4 / POINTS


def layout_mask():
    return (jnp.arange(FLAT) < NPARAM).astype(jnp.float32)


def draw_weights_flat(key, part):
    key = jax.random.fold_in(key, 1)
    subkeys = jax.random.split(key, 8)
    middle = HID - LATENT - 3
    width_in = LATENT + 3
    first_dir = jax.random.normal(subkeys[0], (middle, width_in), jnp.float32) * width_in ** (-0.5)
    first_gain = jax.random.uniform(subkeys[1], (middle, 1), jnp.float32, 1.0, 3.0)
    first_bias = jax.random.normal(subkeys[2], (middle, 1), jnp.float32) * 0.2
    second_dir = jax.random.normal(subkeys[3], (HID, HID), jnp.float32) * HID ** (-0.5)
    second_gain = jax.random.uniform(subkeys[4], (HID, 1), jnp.float32, 1.0, 3.0)
    second_bias = jax.random.normal(subkeys[5], (HID, 1), jnp.float32) * 0.2
    head_weight = jax.random.normal(subkeys[6], (HID, 1), jnp.float32) * (0.3 * HID ** (-0.5))
    head_bias = jax.random.normal(subkeys[7], (1,), jnp.float32) * 0.05
    first_block = jnp.concatenate([first_dir, first_gain, first_bias], axis=1).reshape(-1)
    second_block = jnp.concatenate([second_dir, second_gain, second_bias, head_weight], axis=1).reshape(-1)
    zeros = jnp.zeros((FLAT - NPARAM,), jnp.float32)
    return jnp.concatenate([first_block, second_block, head_bias, zeros])


def draw_moment_one(key, part):
    key = jax.random.fold_in(key, 2)
    return jax.random.normal(key, (FLAT,), jnp.float32) * (0.11 * grad_scale()) * layout_mask()


def draw_moment_two(key, part):
    key = jax.random.fold_in(key, 3)
    factor = jax.random.uniform(key, (FLAT,), jnp.float32, 1.0, 4.0)
    return factor * (0.001 * grad_scale() ** 2) * layout_mask()


def draw_code_first(key, part):
    key = jax.random.fold_in(key, 4)
    return jax.random.normal(key, (CODES, LATENT), jnp.float32) * (0.11 * code_scale())


def draw_code_second(key, part):
    key = jax.random.fold_in(key, 5)
    factor = jax.random.uniform(key, (CODES, LATENT), jnp.float32, 1.0, 4.0)
    return factor * (0.001 * code_scale() ** 2)


def draw_shape_index(key, part):
    key = jax.random.fold_in(key, 6)
    subkeys = jax.random.split(key, 6)
    devices = N_DP * N_WIDE
    every_slot = devices * CAP
    preferred_device = jax.random.randint(subkeys[0], (), 0, devices)
    preferred_slots = jax.random.randint(subkeys[1], (devices, 4), 0, devices)
    slot_ratings = jax.random.randint(subkeys[2], (devices, every_slot), 0, 1024)
    owning_device = jnp.arange(every_slot, dtype=jnp.int32) // CAP
    extra_reward = jnp.where(owning_device[None, :] == preferred_device, 16384, 0)
    extra_reward = extra_reward + 2048 * jnp.sum((owning_device[None, None, :] == preferred_slots[:, :, None]).astype(jnp.int32), axis=1)
    device_ordering = (slot_ratings + extra_reward) * every_slot + jnp.arange(every_slot, dtype=jnp.int32)[None, :]
    chosen = jax.lax.top_k(device_ordering, PTS_DEV)[1].astype(jnp.int32)
    chosen = jax.random.permutation(subkeys[3], chosen, axis=1, independent=True)
    owners = chosen // CAP
    row_index = jax.random.randint(subkeys[4], (devices, PTS_DEV), 0, CODE_DEV)
    return (owners * CODE_DEV + row_index).reshape(POINTS).astype(jnp.int32)


def level_of(key, shape, cuts, smallest, top_value):
    level = 1.0
    for position, parts in cuts:
        draws = jax.random.uniform(jax.random.fold_in(jax.random.fold_in(key, 6), position), (parts,), jnp.float32, smallest / len(cuts), top_value / len(cuts))
        level = level * jnp.repeat(jnp.exp(draws), shape[position] // parts).reshape((-1,) + (1,) * (len(shape) - 1 - position))
    return level


def noise(key, extent, spread, reach, cuts=(), held_as=jnp.bfloat16):
    entries = spread * jax.random.normal(key, extent, jnp.float32)
    if cuts:
        entries = entries * level_of(key, extent, cuts, -0.22, 0.18)
    return jnp.clip(entries, -reach, reach).astype(held_as)


def setup_inputs(seed: int = 0) -> dict:
    keys = jax.random.split(jax.random.key(seed), 10)
    return {
        "weights_flat": draw_weights_flat(jax.random.fold_in(keys[9], 71), 0),
        "moment_one": draw_moment_one(jax.random.fold_in(keys[9], 71), 0),
        "moment_two": draw_moment_two(jax.random.fold_in(keys[9], 71), 0),
        "codes": noise(keys[3], (CODES, LATENT), 0.3, 1.8, ((0, 128),), jnp.float32),
        "code_first": draw_code_first(jax.random.fold_in(keys[9], 71), 0),
        "code_second": draw_code_second(jax.random.fold_in(keys[9], 71), 0),
        "coords": jnp.clip(jax.random.uniform(keys[6], (3, POINTS), jnp.float32, -1.0, 1.0) * level_of(keys[6], (3, POINTS), ((1, 128),), -0.4, 0.0), -1.0, 1.0),
        "distances": noise(keys[7], (POINTS,), 0.1, 0.5, ((0, 128),), jnp.float32),
        "shape_index": draw_shape_index(jax.random.fold_in(keys[9], 71), 0),
    }


@jax.custom_vjp
def low(v):
    return lax.optimization_barrier(v.astype(jnp.bfloat16)).astype(jnp.float32)

@jax.custom_vjp
def low_back(v):
    return v

def low_keep(v):
    return (low(v), None)

def low_pass(kept, grad):
    return (grad,)

def back_keep(v):
    return (v, None)

def back_low(kept, grad):
    return (low(grad),)
low.defvjp(low_keep, low_pass)
low_back.defvjp(back_keep, back_low)
DELTA = 0.1
SMOOTH = 0.01
CODE_WEIGHT = 0.001
EIK_WEIGHT = 0.1
CLIP = 0.001
WEIGHT_RATE = 0.02
CODE_RATE = 0.15
BETA_ONE = 0.9
BETA_TWO = 0.999
ADAM_EPS = 1e-08
DECAY = 0.01
HIGH = lax.Precision.HIGHEST

def unpack(flat):
    middle = HID - LATENT - 3
    width_in = LATENT + 3
    first_size = middle * (width_in + 2)
    second_size = HID * (HID + 3)
    first_block = flat[:first_size].reshape(middle, width_in + 2)
    second_block = flat[first_size:first_size + second_size].reshape(HID, HID + 3)
    head_bias = flat[first_size + second_size:first_size + second_size + 1]
    return [first_block[:, :width_in].T, first_block[:, width_in], first_block[:, width_in + 1], second_block[:, :HID].T, second_block[:, HID], second_block[:, HID + 1], second_block[:, HID + 2], head_bias]

def normed(direction, gain):
    return direction * (gain * lax.rsqrt(lax.optimization_barrier(jnp.sum(direction * direction, axis=0)) + 1e-12))

def forward_points(pieces, latent, spots):
    first_dir, first_gain, first_bias, second_dir, second_gain, second_bias, head_weight, head_bias = pieces
    joined = jnp.concatenate([latent, spots], axis=1)
    hidden_one = jax.nn.silu(jnp.dot(joined, normed(first_dir, first_gain), precision=HIGH) + first_bias)
    widened = jnp.concatenate([hidden_one, joined], axis=1)
    hidden_two = jax.nn.silu(jnp.dot(widened, normed(second_dir, second_gain), precision=HIGH) + second_bias)
    return jnp.tanh(jnp.dot(hidden_two, head_weight, precision=HIGH) + head_bias[0])

def point_losses(pieces, latent, spots, targets):
    predicted, pullback = jax.vjp(lambda places: forward_points(pieces, latent, places), spots)
    slope, = pullback(jnp.ones_like(predicted))
    eikonal = (lax.optimization_barrier(jnp.sum(slope * slope, axis=1)) - 1.0) ** 2
    misfit = DELTA * jnp.tanh(predicted / DELTA) - DELTA * jnp.tanh(targets / DELTA)
    fitting = jnp.sqrt(misfit * misfit + SMOOTH * SMOOTH)
    return fitting + CODE_WEIGHT * lax.optimization_barrier(jnp.sum(latent * latent, axis=1)) + EIK_WEIGHT * eikonal

def adam_update(value, first, second, grad, rate):
    first_new = BETA_ONE * first + (1.0 - BETA_ONE) * grad
    second_new = BETA_TWO * second + (1.0 - BETA_TWO) * grad * grad
    first_hat = first_new / (1.0 - BETA_ONE ** STEP)
    second_hat = second_new / (1.0 - BETA_TWO ** STEP)
    value_new = value - rate * (first_hat / (jnp.sqrt(second_hat) + ADAM_EPS) + DECAY * value)
    return (value_new, first_new, second_new)

def reference(weights_flat, moment_one, moment_two, codes, code_first, code_second, coords, distances, shape_index):
    width = min(4096, POINTS)
    offsets = jnp.arange(POINTS // width, dtype=jnp.int32) * width

    def whole_loss(flat, table):
        pieces = unpack(flat)

        def block_fn(offset):
            spots = lax.dynamic_slice_in_dim(coords, offset, width, 1).T
            wanted = lax.dynamic_slice_in_dim(shape_index, offset, width, 0)
            targets = lax.dynamic_slice_in_dim(distances, offset, width, 0)
            latent = jnp.take(table, wanted, axis=0)
            return jnp.sum(point_losses(pieces, latent, spots, targets))
        return jnp.sum(lax.map(jax.checkpoint(block_fn), offsets)) / POINTS
    loss_value, pullback = jax.vjp(whole_loss, weights_flat, codes)
    weight_grad, code_grad = pullback(jnp.ones_like(loss_value))
    grad_norm = jnp.sqrt(jnp.sum(weight_grad * weight_grad) + jnp.sum(code_grad * code_grad))
    factor = jnp.minimum(1.0, CLIP / (grad_norm + 1e-06))
    new_weights, first_new, second_new = adam_update(weights_flat, moment_one, moment_two, factor * weight_grad, WEIGHT_RATE)
    new_codes, code_first_new, code_second_new = adam_update(codes, code_first, code_second, factor * code_grad, CODE_RATE)
    return (loss_value, grad_norm, new_weights, first_new, second_new, new_weights.astype(jnp.bfloat16), new_codes, code_first_new, code_second_new, new_codes.astype(jnp.bfloat16))
```

```python
import jax
import jax.numpy as jnp
from jax import lax
from jax.sharding import PartitionSpec as P

LATENT = 256
HID = 512
STEP = 10


DELTA = 0.1
SMOOTH = 0.01
CODE_WEIGHT = 0.001
EIK_WEIGHT = 0.1
CLIP = 0.001
WEIGHT_RATE = 0.02
CODE_RATE = 0.15
BETA_ONE = 0.9
BETA_TWO = 0.999
ADAM_EPS = 1e-08
DECAY = 0.01
HIGH = lax.Precision.HIGHEST


def unpack(flat):
    middle = HID - LATENT - 3
    width_in = LATENT + 3
    first_size = middle * (width_in + 2)
    second_size = HID * (HID + 3)
    first_block = flat[:first_size].reshape(middle, width_in + 2)
    second_block = flat[first_size : first_size + second_size].reshape(HID, HID + 3)
    head_bias = flat[first_size + second_size : first_size + second_size + 1]
    return [
        first_block[:, :width_in].T,
        first_block[:, width_in],
        first_block[:, width_in + 1],
        second_block[:, :HID].T,
        second_block[:, HID],
        second_block[:, HID + 1],
        second_block[:, HID + 2],
        head_bias,
    ]


def normed(direction, gain):
    return direction * (gain * lax.rsqrt(jnp.sum(direction * direction, axis=0) + 1e-12))


def forward_points(pieces, latent, spots):
    (
        first_dir,
        first_gain,
        first_bias,
        second_dir,
        second_gain,
        second_bias,
        head_weight,
        head_bias,
    ) = pieces
    joined = jnp.concatenate([latent, spots], axis=1)
    hidden_one = jax.nn.silu(
        jnp.dot(joined, normed(first_dir, first_gain), precision=HIGH) + first_bias
    )
    widened = jnp.concatenate([hidden_one, joined], axis=1)
    hidden_two = jax.nn.silu(
        jnp.dot(widened, normed(second_dir, second_gain), precision=HIGH) + second_bias
    )
    return jnp.tanh(jnp.dot(hidden_two, head_weight, precision=HIGH) + head_bias[0])


def point_losses(pieces, latent, spots, targets):
    predicted, pullback = jax.vjp(lambda places: forward_points(pieces, latent, places), spots)
    (slope,) = pullback(jnp.ones_like(predicted))
    eikonal = (jnp.sum(slope * slope, axis=1) - 1.0) ** 2
    misfit = DELTA * jnp.tanh(predicted / DELTA) - DELTA * jnp.tanh(targets / DELTA)
    fitting = jnp.sqrt(misfit * misfit + SMOOTH * SMOOTH)
    return fitting + CODE_WEIGHT * jnp.sum(latent * latent, axis=1) + EIK_WEIGHT * eikonal


def adam_update(value, first, second, grad, rate):
    first_new = BETA_ONE * first + (1.0 - BETA_ONE) * grad
    second_new = BETA_TWO * second + (1.0 - BETA_TWO) * grad * grad
    first_hat = first_new / (1.0 - BETA_ONE**STEP)
    second_hat = second_new / (1.0 - BETA_TWO**STEP)
    value_new = value - rate * (first_hat / (jnp.sqrt(second_hat) + ADAM_EPS) + DECAY * value)
    return (value_new, first_new, second_new)


def body(
    weights_flat,
    moment_one,
    moment_two,
    codes,
    code_first,
    code_second,
    coords,
    distances,
    shape_index,
):
    count = coords.shape[1]
    devices = lax.axis_size(("dp", "wide"))
    table_rows = codes.shape[0]
    capacity = max(2, 2 * count // devices)
    every_slot = devices * capacity
    all_points = count * devices
    row = lax.all_gather(weights_flat, "wide", axis=0, tiled=True)
    whole = lax.all_gather(row, "dp", axis=0, tiled=True)
    owners = shape_index // table_rows
    row_index = shape_index % table_rows
    order = jnp.arange(count, dtype=jnp.int32)
    before = (owners[:, None] == owners[None, :]) & (order[None, :] < order[:, None])
    placed = jnp.sum(before.astype(jnp.int32), axis=1)
    slot_index = owners * capacity + placed
    packed = jnp.concatenate(
        [coords, distances[None, :], row_index[None, :].astype(jnp.float32)], axis=0
    )
    outgoing = jnp.zeros((5, every_slot), jnp.float32).at[4].set(-1.0).at[:, slot_index].set(packed)
    n_dp, n_wide = lax.axis_size("dp"), lax.axis_size("wide")
    boxes = outgoing.reshape(5, n_dp, n_wide, capacity).transpose(2, 1, 0, 3)
    boxes = lax.all_to_all(boxes, "wide", split_axis=0, concat_axis=0)
    boxes = lax.all_to_all(boxes.transpose(1, 0, 2, 3), "dp", split_axis=0, concat_axis=0)
    arrived = boxes.transpose(2, 0, 1, 3).reshape(5, every_slot)
    rows_in = arrived[4].astype(jnp.int32)
    filled = (rows_in >= 0).astype(jnp.float32)
    safe_rows = jnp.maximum(rows_in, 0)

    def local_loss(flat, table):
        latent = jnp.take(table, safe_rows, axis=0)
        losses = point_losses(unpack(flat), latent, arrived[0:3].T, arrived[3])
        return jnp.sum(filled * losses) / all_points

    loss_part, pullback = jax.vjp(local_loss, whole, codes)
    weight_full, code_grad = pullback(jnp.ones_like(loss_part))
    pieces = weight_full.reshape(n_dp, n_wide, weights_flat.shape[0]).transpose(1, 0, 2)
    pieces = jnp.sum(lax.all_to_all(pieces, "wide", split_axis=0, concat_axis=0), axis=0)
    weight_grad = jnp.sum(lax.all_to_all(pieces, "dp", split_axis=0, concat_axis=0), axis=0)
    squares_part = jnp.sum(weight_grad * weight_grad) + jnp.sum(code_grad * code_grad)
    totals = lax.psum(jnp.stack([loss_part, squares_part]), "wide")
    totals = lax.psum(totals, "dp")
    loss_value, squares = totals[0], totals[1]
    grad_norm = jnp.sqrt(squares)
    factor = jnp.minimum(1.0, CLIP / (grad_norm + 1e-06))
    new_weights, first_new, second_new = adam_update(
        weights_flat, moment_one, moment_two, factor * weight_grad, WEIGHT_RATE
    )
    new_codes, code_first_new, code_second_new = adam_update(
        codes, code_first, code_second, factor * code_grad, CODE_RATE
    )
    return (
        loss_value,
        grad_norm,
        new_weights,
        first_new,
        second_new,
        new_weights.astype(jnp.bfloat16),
        new_codes,
        code_first_new,
        code_second_new,
        new_codes.astype(jnp.bfloat16),
    )


def solution(mesh):
    return jax.shard_map(
        body,
        mesh=mesh,
        in_specs=(
            P(("dp", "wide")),
            P(("dp", "wide")),
            P(("dp", "wide")),
            P(("dp", "wide"), None),
            P(("dp", "wide"), None),
            P(("dp", "wide"), None),
            P(None, ("dp", "wide")),
            P(("dp", "wide")),
            P(("dp", "wide")),
        ),
        out_specs=(
            P(),
            P(),
            P(("dp", "wide")),
            P(("dp", "wide")),
            P(("dp", "wide")),
            P(("dp", "wide")),
            P(("dp", "wide"), None),
            P(("dp", "wide"), None),
            P(("dp", "wide"), None),
            P(("dp", "wide"), None),
        ),
        check_vma=False,
    )
```

```python
import jax
import jax.numpy as jnp
from jax import lax
from jax.experimental import pallas as pl
from jax.experimental.pallas import tpu as pltpu
from jax.sharding import Mesh
from jax.sharding import PartitionSpec as P

LATENT = 256
HID = 512
MIDDLE = HID - LATENT - 3
STEP = 10

DELTA = 0.1
SMOOTH = 0.01
CODE_WEIGHT = 0.001
EIK_WEIGHT = 0.1
CLIP = 0.001
WEIGHT_RATE = 0.02
CODE_RATE = 0.15
BETA_ONE = 0.9
BETA_TWO = 0.999
ADAM_EPS = 1e-08
DECAY = 0.01

LANES = 128
DEVICES = 128
PEERS = 64
SHARD_ROWS = 21
BOX_ROWS = 24
SLOTS = 16
POINTS_DEV = 1024
CODE_ROWS = 256
FLAT_ROWS = DEVICES * SHARD_ROWS
BLOCK = 256
ALL_POINTS = POINTS_DEV * DEVICES

F32 = jnp.float32
BF16 = jnp.bfloat16
ALL = ("z", "core", "wide")


def rows_of_lanes(lead, shape):
    return lax.broadcasted_iota(jnp.int32, shape, lead)


def halves(v):
    high = v.astype(BF16)
    return high, (v - high.astype(F32)).astype(BF16)


def thirds(v):
    high = v.astype(BF16).astype(F32)
    rest = v - high
    mid = rest.astype(BF16).astype(F32)
    return high, mid, rest - mid


def mm(a, b):
    return lax.dot_general(a, b, (((1,), (0,)), ((), ())), preferred_element_type=F32)


def mm_nt(a, b):
    return lax.dot_general(a, b, (((1,), (1,)), ((), ())), preferred_element_type=F32)


def beside(*parts):
    return jnp.concatenate(parts, axis=1)


def total_of(v):
    return jnp.sum(jnp.sum(v, axis=0, keepdims=True), axis=1, keepdims=True)


def stacked(*parts):
    return jnp.concatenate(parts, axis=0)


def pack_kernel(weights_ref, coords_ref, distances_ref, index_ref, out_ref):
    shard = stacked(weights_ref[...], jnp.zeros((BOX_ROWS - SHARD_ROWS, LANES), F32))
    for peer in range(PEERS):
        out_ref[peer * BOX_ROWS : (peer + 1) * BOX_ROWS, :] = shard
    index = index_ref[...]
    owner = lax.shift_right_logical(index, 8)
    row = lax.bitwise_and(index, CODE_ROWS - 1)
    sent = (rows_of_lanes(0, (DEVICES, POINTS_DEV)) == owner).astype(F32)
    sent_low = sent.astype(BF16)
    width = 256
    earlier = rows_of_lanes(0, (width, width)) < rows_of_lanes(1, (width, width))
    earlier = earlier.astype(F32).astype(BF16)
    ones = jnp.ones((width, width), BF16)
    ranks = [
        mm(sent_low[:, : (part + 1) * width], stacked(*([ones] * part + [earlier])))
        for part in range(POINTS_DEV // width)
    ]
    placed = jnp.sum(sent * beside(*ranks), axis=0, keepdims=True).astype(jnp.int32)
    at_slot = rows_of_lanes(0, (SLOTS, POINTS_DEV)) == placed
    values = [coords_ref[i : i + 1, :] for i in range(3)]
    values += [distances_ref[...], (row + 1).astype(F32)]
    pieces = [[], [], []]
    for value in values:
        for k, third in enumerate(thirds(value)):
            pieces[k].append(jnp.where(at_slot, third, 0.0))
    spare = jnp.zeros((LANES - SLOTS * len(values), POINTS_DEV), F32)
    boxes = mm_nt(
        beside(sent_low, sent_low, sent_low),
        beside(*[stacked(*piece, spare).astype(BF16) for piece in pieces]),
    )
    for z in range(4):
        for core in range(2):
            first = z * 32 + core * 16
            out_ref[pl.ds(z * 16 * BOX_ROWS + SHARD_ROWS + core, 16, stride=BOX_ROWS), :] = boxes[
                first : first + 16, :
            ]


def unit_groups(count, stride_rows, extra, first_entry):
    for group in range(count):
        entry = first_entry + group * 8 * (stride_rows * LANES + extra)
        yield group, entry // LANES, entry % LANES


def unpack_units(flat_ref, out_ref, count, stride_rows, extra, first_entry):
    lane = rows_of_lanes(1, (8, LANES))
    slope = rows_of_lanes(0, (8, LANES)) * extra
    for group, first, shift in unit_groups(count, stride_rows, extra, first_entry):
        start = slope + shift
        wraps = shift + 7 * extra >= LANES
        turn = lax.bitwise_and(lane + start, LANES - 1)
        tiles = []
        for a in range(stride_rows + 2 + wraps):
            tile = flat_ref[pl.ds(first + a, 8, stride=stride_rows), :]
            tiles.append(jnp.take_along_axis(tile, turn, axis=1, mode="promise_in_bounds"))
        for c in range(stride_rows + 1):
            value = jnp.where(lane + start < LANES, tiles[c], tiles[c + 1])
            if wraps:
                value = jnp.where(lane + start < 2 * LANES, value, tiles[c + 2])
            out_ref[group * 8 : group * 8 + 8, c * LANES : (c + 1) * LANES] = value


def pack_units(value_ref, flat_ref, count, stride_rows, extra, first_entry, adding):
    lane = rows_of_lanes(1, (8, LANES))
    slope = rows_of_lanes(0, (8, LANES)) * extra
    zero = jnp.zeros((8, LANES), F32)
    for group, first, shift in unit_groups(count, stride_rows, extra, first_entry):
        start = slope + shift
        wraps = shift + 7 * extra >= LANES
        wanted = range(stride_rows, stride_rows + 1 + wraps + 1) if adding else range(stride_rows)
        rolled = {}

        turn = lax.bitwise_and(lane - start, LANES - 1)

        def tile(c, rolled=rolled, group=group, turn=turn):
            if c < 0 or c > stride_rows:
                return zero
            if c not in rolled:
                value = value_ref[group * 8 : group * 8 + 8, c * LANES : (c + 1) * LANES]
                rolled[c] = jnp.take_along_axis(value, turn, axis=1, mode="promise_in_bounds")
            return rolled[c]

        for a in wanted:
            value = jnp.where(lane >= start, tile(a), tile(a - 1))
            if wraps:
                value = jnp.where(lane >= start - LANES, value, tile(a - 2))
            rows = pl.ds(first + a, 8, stride=stride_rows)
            if adding:
                flat_ref[rows, :] = flat_ref[rows, :] + value
            else:
                flat_ref[rows, :] = value


FIRST_UNITS = (32, 2, 5, 0)
SECOND_UNITS = (64, 4, 3, MIDDLE * (LATENT + 5))
HEAD_ENTRY = MIDDLE * (LATENT + 5) + HID * (HID + 3)


def silu_parts(v):
    gate = 0.5 * jnp.tanh(0.5 * v) + 0.5
    rest = 1.0 - gate
    value = v * gate
    slope = gate + value * rest
    curve = rest * (gate + gate + value * (rest - gate))
    return value, slope, curve


def main_kernel(
    core_ref,
    mine_ref,
    other_ref,
    codes_ref,
    out_ref,
    code_grad_ref,
    flat,
    first_w,
    second_w,
    lhs_one,
    lhs_two,
    lhs_back,
    latent_w,
    coord_w,
    head_w,
    spots,
    sum_two,
    sum_codes,
    sum_coord,
    sum_head,
    sum_count,
    sum_loss,
    act_one,
    slope_one,
    curve_one,
    back_one,
    hid_hi,
    hid_lo,
    hot,
    act_two,
    slope_two,
    curve_two,
    gate_hi,
    gate_lo,
    tang_hi,
    tang_lo,
    near_hi,
    near_lo,
    bar_hi,
    bar_lo,
    low_hi,
    low_lo,
):
    core = core_ref[0]

    for which in range(2):

        @pl.when(core == which)
        def _(which=which):
            for d in range(DEVICES):
                z, c, w = d // 32, d // 16 % 2, d % 16
                box = (z * 16 + w) * BOX_ROWS
                source = mine_ref if c == which else other_ref
                flat[d * SHARD_ROWS : d * SHARD_ROWS + BOX_ROWS, :] = source[box : box + BOX_ROWS, :]
            rows = pl.ds(SHARD_ROWS + which, PEERS, stride=BOX_ROWS)
            spots[...] = stacked(mine_ref[rows, :], other_ref[rows, :]).T

    unpack_units(flat, first_w, *FIRST_UNITS)
    unpack_units(flat, second_w, *SECOND_UNITS)
    head_bias = flat[HEAD_ENTRY // LANES : HEAD_ENTRY // LANES + 1, :][
        :, HEAD_ENTRY % LANES : HEAD_ENTRY % LANES + 1
    ]

    lane = rows_of_lanes(1, (256, LANES))
    unit = rows_of_lanes(0, (256, LANES))
    real = unit < MIDDLE

    first_low = jnp.where(beside(real, real), first_w[:, : 2 * LANES], 0.0)
    first_end = jnp.where(real, first_w[:, 2 * LANES :], 0.0)
    first_near = jnp.where(lane < 3, first_end, 0.0)
    first_gain = first_end[:, 3:4]
    first_bias = first_end[:, 4:5]
    first_w[:, : 2 * LANES] = first_low
    first_w[:, 2 * LANES :] = first_end
    first_root = lax.rsqrt(
        jnp.sum(first_low * first_low, axis=1, keepdims=True)
        + jnp.sum(first_near * first_near, axis=1, keepdims=True)
        + 1e-12
    )
    first_scale = first_gain * first_root
    first_low = first_low * first_scale
    first_near = first_near * first_scale
    latent_w[0:256, :] = first_low
    for i in range(3):
        coord_w[:, i * LANES : (i + 1) * LANES] = jnp.broadcast_to(
            first_near[:, i : i + 1], (256, LANES)
        )

    second_a = second_w[:, 0:256]
    second_b = second_w[:, 256:512]
    second_gain = second_w[:, 512:513]
    second_bias = second_w[:, 513:514]
    head_w[...] = jnp.broadcast_to(second_w[:, 514:515], (HID, LANES))
    second_root = lax.rsqrt(
        jnp.sum(second_a * second_a + second_b * second_b, axis=1, keepdims=True) + 1e-12
    )
    second_scale = second_gain * second_root
    second_a = second_a * second_scale
    second_b = second_b * second_scale
    is_hidden = rows_of_lanes(1, (HID, 256)) < MIDDLE
    hidden_cols = jnp.where(is_hidden, second_a, second_b)
    latent_cols = pltpu.roll(jnp.where(is_hidden, second_b, second_a), 3, 1)
    latent_w[256:768, :] = latent_cols

    hidden_hi, hidden_lo = halves(hidden_cols)
    lhs_two[:, 0:256] = hidden_hi
    lhs_two[:, 256:512] = hidden_hi
    lhs_two[:, 512:768] = hidden_lo
    back_hi, back_lo = halves(hidden_cols.T)
    lhs_back[:, 0:512] = back_hi
    lhs_back[:, 512:1024] = back_hi
    lhs_back[:, 1024:1536] = back_lo

    code_hi, code_lo = halves(codes_ref[...])
    weight_hi, weight_lo = halves(latent_w[...])
    by_code = mm_nt(
        beside(weight_hi, weight_hi, weight_lo), beside(code_hi, code_lo, code_hi)
    )
    one_hi, one_lo = halves(by_code[0:256, :] + first_bias)
    lhs_one[:, 0:256] = one_hi
    lhs_one[:, 256:512] = one_lo
    two_hi, two_lo = halves(by_code[256:768, :] + second_bias)
    lhs_two[:, 768:1024] = two_hi
    lhs_two[:, 1024:1280] = two_lo
    spread = jnp.where((unit - MIDDLE == lane) & (lane < 3), 1.0, first_near)
    near_parts = thirds(spread)
    near_lhs = near_parts[0]
    for place, k in enumerate((0, 0, 1, 1, 2)):
        near_lhs = near_lhs + pltpu.roll(near_parts[k], 8 * (place + 1), 1)
    lhs_one[:, 512:640] = near_lhs.astype(BF16)

    for ref in (sum_two, sum_codes, sum_coord, sum_head, sum_count, sum_loss):
        ref[...] = jnp.zeros(ref.shape, F32)

    def feature(which, step, sub):
        first = which * SLOTS + step * 4 + sub * 2
        return beside(spots[pl.ds(first, 1), :], spots[pl.ds(first + 1, 1), :])

    blank5 = jnp.zeros((5, BLOCK), F32)
    subs = range(2)
    chunk = 32

    def step_body(step, carry):
        place = [[feature(i, step, s) for i in range(3)] for s in subs]
        target = [feature(3, step, s) for s in subs]
        code_row = [feature(4, step, s) for s in subs]
        valid = [(code_row[s] > 0.5).astype(F32) for s in subs]
        near8 = [stacked(*place[s], blank5) for s in subs]
        near_pieces = [thirds(near8[s]) for s in subs]

        for s in subs:
            wanted = code_row[s] - 1.0
            for r in range(0, CODE_ROWS, chunk):
                mark = jnp.where(
                    (rows_of_lanes(0, (chunk, BLOCK)) + r).astype(F32) == wanted, 1.0, 0.0
                )
                hot[s, r : r + chunk, :] = mark.astype(BF16)
                sum_count[r : r + chunk, :] += mark[:, :LANES] + mark[:, LANES:]

        for s in subs:
            high, mid, low = near_pieces[s]
            near_rhs = stacked(
                high, mid, low, high, mid, high, jnp.zeros((80, BLOCK), F32)
            ).astype(BF16)
            act_one[s] = mm(lhs_one[...], stacked(hot[s], hot[s], near_rhs))
        for s in subs:
            for r in range(0, 256, chunk):
                pre = act_one[s, r : r + chunk, :]
                value, slope, curve = silu_parts(pre)
                if r + chunk == 256:
                    inside = rows_of_lanes(0, (chunk, BLOCK)) + r < MIDDLE
                    value = jnp.where(inside, value, pre)
                    slope = jnp.where(inside, slope, 0.0)
                    curve = jnp.where(inside, curve, 0.0)
                high, low = halves(value)
                hid_hi[s, r : r + chunk, :] = high
                hid_lo[s, r : r + chunk, :] = low
                slope_one[s, r : r + chunk, :] = slope
                curve_one[s, r : r + chunk, :] = curve

        for s in subs:
            act_two[s] = mm(
                lhs_two[...], stacked(hid_hi[s], hid_lo[s], hid_hi[s], hot[s], hot[s])
            )
        summed = []
        for s in subs:
            total = jnp.zeros((8, BLOCK), F32)
            for r in range(0, HID, chunk):
                value, slope, curve = silu_parts(act_two[s, r : r + chunk, :])
                head = beside(head_w[r : r + chunk, :], head_w[r : r + chunk, :])
                weighed = head * value
                for k in range(0, chunk, 8):
                    total = total + weighed[k : k + 8, :]
                high, low = halves(head * slope)
                gate_hi[s, r : r + chunk, :] = high
                gate_lo[s, r : r + chunk, :] = low
                act_two[s, r : r + chunk, :] = value
                slope_two[s, r : r + chunk, :] = slope
                curve_two[s, r : r + chunk, :] = curve
            summed.append(jnp.sum(total, axis=0, keepdims=True))

        for s in subs:
            back_one[s] = mm(lhs_back[...], stacked(gate_hi[s], gate_lo[s], gate_hi[s]))
        leads = []
        for s in subs:
            totals = [jnp.zeros((8, BLOCK), F32) for _ in range(3)]
            for r in range(0, 256, chunk):
                grad = back_one[s, r : r + chunk, :] * slope_one[s, r : r + chunk, :]
                high, low = halves(grad)
                near_hi[s, r : r + chunk, :] = high
                near_lo[s, r : r + chunk, :] = low
                for i in range(3):
                    col = coord_w[r : r + chunk, i * LANES : (i + 1) * LANES]
                    weighed = beside(col, col) * grad
                    for k in range(0, chunk, 8):
                        totals[i] = totals[i] + weighed[k : k + 8, :]
            leads.append(
                [
                    jnp.sum(totals[i], axis=0, keepdims=True)
                    + back_one[s, MIDDLE + i : MIDDLE + i + 1, :]
                    for i in range(3)
                ]
            )

        bars, pulls = [], []
        for s in subs:
            predicted = jnp.tanh(summed[s] + head_bias)
            flank = 1.0 - predicted * predicted
            slope = [flank * q for q in leads[s]]
            excess = slope[0] * slope[0] + slope[1] * slope[1] + slope[2] * slope[2] - 1.0
            capped = jnp.tanh(predicted / DELTA)
            misfit = DELTA * capped - DELTA * jnp.tanh(target[s] / DELTA)
            fitting = jnp.sqrt(misfit * misfit + SMOOTH * SMOOTH)
            loss = fitting + EIK_WEIGHT * excess * excess
            sum_loss[0:1, :] += valid[s] * loss
            share = valid[s] * (1.0 / ALL_POINTS)
            pull = [(4.0 * EIK_WEIGHT) * excess * v for v in slope]
            by_flank = sum(p * q for p, q in zip(pull, leads[s]))
            by_predicted = misfit / fitting * (1.0 - capped * capped) - 2.0 * predicted * by_flank
            bars.append(share * by_predicted * flank)
            sum_loss[1:2, :] += bars[s]
            pulls.append([share * flank * p for p in pull])

        for s in subs:
            last = stacked(blank5, *pulls[s])
            for r in range(0, 256, chunk):
                grad = 0.0
                for i in range(3):
                    col = coord_w[r : r + chunk, i * LANES : (i + 1) * LANES]
                    grad = grad + beside(col, col) * pulls[s][i]
                through = grad * slope_one[s, r : r + chunk, :]
                if r + chunk == 256:
                    inside = rows_of_lanes(0, (8, BLOCK)) < MIDDLE - 248
                    through = stacked(
                        through[: chunk - 8], jnp.where(inside, through[chunk - 8 :], last)
                    )
                high, low = halves(through)
                tang_hi[s, r : r + chunk, :] = high
                tang_lo[s, r : r + chunk, :] = low
                curve_one[s, r : r + chunk, :] = (
                    grad * back_one[s, r : r + chunk, :] * curve_one[s, r : r + chunk, :]
                )
        tangents = []
        for s in subs:
            tangents.append(
                mm(lhs_two[:, 0:768], stacked(tang_hi[s], tang_lo[s], tang_hi[s]))
            )
        for s in subs:
            for r in range(0, HID, chunk):
                tangent = tangents[s][r : r + chunk, :]
                slope = slope_two[s, r : r + chunk, :]
                head = beside(head_w[r : r + chunk, :], head_w[r : r + chunk, :])
                bar = head * (bars[s] * slope + tangent * curve_two[s, r : r + chunk, :])
                by_head = act_two[s, r : r + chunk, :] * bars[s] + slope * tangent
                sum_head[r : r + chunk, :] += by_head[:, :LANES] + by_head[:, LANES:]
                high, low = halves(bar)
                bar_hi[s, r : r + chunk, :] = high
                bar_lo[s, r : r + chunk, :] = low

        for s in subs:
            back_one[s] = mm(lhs_back[...], stacked(bar_hi[s], bar_lo[s], bar_hi[s]))
        left, right = [], []
        for s in subs:
            left += [bar_hi[s], bar_hi[s], bar_lo[s], gate_hi[s], gate_hi[s], gate_lo[s]]
            right += [hid_hi[s], hid_lo[s], hid_hi[s], tang_hi[s], tang_lo[s], tang_hi[s]]
        sum_two[...] += mm_nt(beside(*left), beside(*right))
        hots = beside(hot[0], hot[0], hot[1], hot[1])
        sum_codes[256:768, :] += mm_nt(beside(bar_hi[0], bar_lo[0], bar_hi[1], bar_lo[1]), hots)

        for s in subs:
            for r in range(0, 256, chunk):
                bar = (
                    back_one[s, r : r + chunk, :] * slope_one[s, r : r + chunk, :]
                    + curve_one[s, r : r + chunk, :]
                )
                high, low = halves(bar)
                low_hi[s, r : r + chunk, :] = high
                low_lo[s, r : r + chunk, :] = low
        sum_codes[0:256, :] += mm_nt(beside(low_hi[0], low_lo[0], low_hi[1], low_lo[1]), hots)
        left, right = [], []
        for s in subs:
            seen = stacked(near_pieces[s][0], near_pieces[s][1]).astype(BF16)
            pulled = stacked(*pulls[s], blank5)
            high = pulled.astype(BF16).astype(F32)
            pulled = stacked(high, pulled - high).astype(BF16)
            left += [seen, seen, pulled, pulled]
            right += [low_hi[s], low_lo[s], near_hi[s], near_lo[s]]
        sum_coord[...] += mm_nt(beside(*left), beside(*right))
        return carry

    lax.fori_loop(0, SLOTS * DEVICES // (2 * BLOCK), step_body, 0)

    codes = codes_ref[...]
    count = jnp.sum(sum_count[...], axis=1, keepdims=True)
    by_code = sum_codes[...]
    turned_hi, turned_lo = halves(by_code.T)
    weight_hi, weight_lo = halves(latent_w[...])
    code_grad = mm(
        beside(turned_hi, turned_hi, turned_lo), stacked(weight_hi, weight_lo, weight_hi)
    )
    code_grad = code_grad + (2.0 * CODE_WEIGHT / ALL_POINTS) * count * codes
    code_grad_ref[...] = code_grad
    code_squares = total_of(code_grad * code_grad)
    loss = jnp.sum(sum_loss[0:1, :], axis=1, keepdims=True)
    loss = loss + CODE_WEIGHT * total_of(count * codes * codes)
    loss = loss / ALL_POINTS

    code_hi, code_lo = halves(codes)
    by_hi, by_lo = halves(by_code)
    latent_grad = mm(beside(by_hi, by_hi, by_lo), stacked(code_hi, code_lo, code_hi))
    bias_grad = jnp.sum(by_code, axis=1, keepdims=True)

    near_grad = sum_coord[0:8, :] + sum_coord[8:16, :]
    near_grad = stacked(near_grad, jnp.zeros((LANES - 8, 256), F32)).T
    near_grad = jnp.where(lane < 3, near_grad, 0.0)
    low_grad = latent_grad[0:256, :]
    first_low = first_w[:, : 2 * LANES]
    first_near = jnp.where(lane < 3, first_w[:, 2 * LANES :], 0.0)
    along = jnp.sum(first_low * low_grad, axis=1, keepdims=True)
    along = along + jnp.sum(first_near * near_grad, axis=1, keepdims=True)
    inward = first_scale * first_root * first_root * along
    end = first_scale * near_grad - first_near * inward
    end = jnp.where(lane == 3, first_root * along, end)
    end = jnp.where(lane == 4, bias_grad[0:256, :], end)
    low_grad = first_scale * low_grad - first_low * inward
    first_w[:, : 2 * LANES] = jnp.where(beside(real, real), low_grad, 0.0)
    first_w[:, 2 * LANES :] = jnp.where(real, end, 0.0)

    hidden_grad = sum_two[...]
    moved = pltpu.roll(latent_grad[256:768, :], 256 - 3, 1)
    grad_a = jnp.where(is_hidden, hidden_grad, moved)
    grad_b = jnp.where(is_hidden, moved, hidden_grad)
    second_a = second_w[:, 0:256]
    second_b = second_w[:, 256:512]
    along = jnp.sum(second_a * grad_a + second_b * grad_b, axis=1, keepdims=True)
    inward = second_scale * second_root * second_root * along
    second_w[:, 0:256] = second_scale * grad_a - second_a * inward
    second_w[:, 256:512] = second_scale * grad_b - second_b * inward
    head_grad = jnp.sum(sum_head[...], axis=1, keepdims=True)
    lane = rows_of_lanes(1, (HID, LANES))
    end = jnp.where(lane == 0, second_root * along, 0.0)
    end = jnp.where(lane == 1, bias_grad[256:768, :], end)
    second_w[:, 512:640] = jnp.where(lane == 2, head_grad, end)

    flat[...] = jnp.zeros(flat.shape, F32)
    for adding in (False, True):
        pack_units(first_w, flat, *FIRST_UNITS, adding)
        pack_units(second_w, flat, *SECOND_UNITS, adding)
    row = HEAD_ENTRY // LANES
    lane = rows_of_lanes(1, (1, LANES))
    bias_total = jnp.sum(sum_loss[1:2, :], axis=1, keepdims=True)
    flat[row : row + 1, :] = flat[row : row + 1, :] + jnp.where(
        lane == HEAD_ENTRY % LANES, bias_total, 0.0
    )
    sub = rows_of_lanes(0, (8, LANES))
    wide = rows_of_lanes(1, (8, LANES))
    info = jnp.where((sub == 5) & (wide == 0), loss, 0.0)
    info = jnp.where((sub == 5) & (wide == 1), code_squares, info)
    for d in range(DEVICES):
        z, c, w = d // 32, d // 16 % 2, d % 16
        half = jnp.where(core == c, 0, PEERS * BOX_ROWS)
        base = pl.multiple_of(half + (z * 16 + w) * BOX_ROWS, 8)
        first = d * SHARD_ROWS
        out_ref[pl.ds(base, 16), :] = flat[first : first + 16, :]
        out_ref[pl.ds(base + 16, 8), :] = jnp.where(sub < 5, flat[first + 16 : first + 24, :], info)


def vmem(count):
    return [pl.BlockSpec(memory_space=pltpu.VMEM)] * count


PARAMS = pltpu.CompilerParams(vmem_limit_bytes=48 * 1024 * 1024)


def pack_boxes(weights, coords, distances, index):
    return pl.pallas_call(
        pack_kernel,
        out_shape=jax.ShapeDtypeStruct((PEERS * BOX_ROWS, LANES), F32),
        in_specs=vmem(4),
        out_specs=vmem(1)[0],
        compiler_params=PARAMS,
    )(weights, coords, distances, index)


def main_call(core, mine, other, codes):
    pair = (2, 256, BLOCK)
    pair_two = (2, HID, BLOCK)
    scratch = [
        ((FLAT_ROWS + 8, LANES), F32),
        ((256, 3 * LANES), F32),
        ((HID, 5 * LANES), F32),
        ((256, 640), BF16),
        ((HID, 1280), BF16),
        ((256, 1536), BF16),
        ((768, 256), F32),
        ((256, 3 * LANES), F32),
        ((HID, LANES), F32),
        ((LANES, LANES), F32),
        ((HID, 256), F32),
        ((768, 256), F32),
        ((16, 256), F32),
        ((HID, LANES), F32),
        ((CODE_ROWS, LANES), F32),
        ((2, BLOCK), F32),
        (pair, F32),
        (pair, F32),
        (pair, F32),
        (pair, F32),
        (pair, BF16),
        (pair, BF16),
        (pair, BF16),
        (pair_two, F32),
        (pair_two, F32),
        (pair_two, F32),
        (pair_two, BF16),
        (pair_two, BF16),
        (pair, BF16),
        (pair, BF16),
        (pair, BF16),
        (pair, BF16),
        (pair_two, BF16),
        (pair_two, BF16),
        (pair, BF16),
        (pair, BF16),
    ]
    return pl.pallas_call(
        main_kernel,
        out_shape=(
            jax.ShapeDtypeStruct((2 * PEERS * BOX_ROWS, LANES), F32),
            jax.ShapeDtypeStruct((CODE_ROWS, LATENT), F32),
        ),
        in_specs=[pl.BlockSpec(memory_space=pltpu.SMEM)] + vmem(3),
        out_specs=tuple(vmem(2)),
        scratch_shapes=[pltpu.VMEM(shape, dtype) for shape, dtype in scratch],
        compiler_params=PARAMS,
    )(core, mine, other, codes)


def adam_update(value, first, second, grad, rate):
    first_new = BETA_ONE * first + (1.0 - BETA_ONE) * grad
    second_new = BETA_TWO * second + (1.0 - BETA_TWO) * grad * grad
    first_hat = first_new / (1.0 - BETA_ONE**STEP)
    second_hat = second_new / (1.0 - BETA_TWO**STEP)
    value_new = value - rate * (first_hat / (jnp.sqrt(second_hat) + ADAM_EPS) + DECAY * value)
    return (value_new, first_new, second_new)


def swap_cores(v):
    return lax.ppermute(v, "core", [(0, 1), (1, 0)])


def exchange(v):
    return lax.all_to_all(v, ("z", "wide"), split_axis=0, concat_axis=0)


def body(
    weights_flat,
    moment_one,
    moment_two,
    codes,
    code_first,
    code_second,
    coords,
    distances,
    shape_index,
):
    boxes = pack_boxes(
        weights_flat.reshape(SHARD_ROWS, LANES),
        coords,
        distances.reshape(1, POINTS_DEV),
        shape_index.reshape(1, POINTS_DEV),
    )
    mine = exchange(boxes.reshape(PEERS, BOX_ROWS, LANES))
    other = swap_cores(mine)
    core = lax.axis_index("core").astype(jnp.int32).reshape(1)
    grads, code_grad = main_call(
        core,
        mine.reshape(PEERS * BOX_ROWS, LANES),
        other.reshape(PEERS * BOX_ROWS, LANES),
        codes,
    )
    grads = grads.reshape(2, PEERS, BOX_ROWS, LANES)
    pair_sum = grads[0] + swap_cores(grads[1])
    shard = jnp.sum(exchange(pair_sum), axis=0)
    weight_grad = shard[:SHARD_ROWS]
    loss_value = shard[SHARD_ROWS, 0]
    code_squares = shard[SHARD_ROWS, 1]
    squares = jnp.sum(weight_grad * weight_grad)
    seen = exchange(jnp.broadcast_to(squares, (PEERS, 1, LANES)))
    squares = jnp.sum(seen[:, 0, 0]).reshape(1, 1)
    squares = (squares + swap_cores(squares)).reshape(())
    grad_norm = jnp.sqrt(squares + code_squares)
    factor = jnp.minimum(1.0, CLIP / (grad_norm + 1e-06))
    new_weights, first_new, second_new = adam_update(
        weights_flat, moment_one, moment_two, factor * weight_grad.reshape(-1), WEIGHT_RATE
    )
    new_codes, code_first_new, code_second_new = adam_update(
        codes, code_first, code_second, factor * code_grad, CODE_RATE
    )
    return (
        loss_value,
        grad_norm,
        new_weights,
        first_new,
        second_new,
        new_weights.astype(BF16),
        new_codes,
        code_first_new,
        code_second_new,
        new_codes.astype(BF16),
    )


def solution(mesh):
    parts = Mesh(mesh.devices.reshape(4, 2, 16), ALL)
    return jax.shard_map(
        body,
        mesh=parts,
        in_specs=(
            P(ALL),
            P(ALL),
            P(ALL),
            P(ALL, None),
            P(ALL, None),
            P(ALL, None),
            P(None, ALL),
            P(ALL),
            P(ALL),
        ),
        out_specs=(
            P(),
            P(),
            P(ALL),
            P(ALL),
            P(ALL),
            P(ALL),
            P(ALL, None),
            P(ALL, None),
            P(ALL, None),
            P(ALL, None),
        ),
        check_vma=False,
    )
```

```python
import jax
import jax.numpy as jnp
from jax import lax
from jax.experimental import pallas as pl
from jax.experimental.pallas import tpu as pltpu
from jax.sharding import PartitionSpec as P

LATENT = 256
HID = 512
MIDDLE = HID - LATENT - 3
STEP = 10

DELTA = 0.1
SMOOTH = 0.01
CODE_WEIGHT = 0.001
EIK_WEIGHT = 0.1
CLIP = 0.001
WEIGHT_RATE = 0.02
CODE_RATE = 0.15
BETA_ONE = 0.9
BETA_TWO = 0.999
ADAM_EPS = 1e-08
DECAY = 0.01

LANES = 128
DEVICES = 128
CHIPS = 64
SHARD_ROWS = 21
BOX_ROWS = 24
RING = 4
LINE_ROWS = RING * BOX_ROWS
PLANE_ROWS = RING * LINE_ROWS
CORE_ROWS = RING * PLANE_ROWS
SLOTS = 16
POINTS_DEV = 1024
CODE_ROWS = 256
FLAT_ROWS = DEVICES * SHARD_ROWS
BLOCK = 256
ALL_POINTS = POINTS_DEV * DEVICES

F32 = jnp.float32
BF16 = jnp.bfloat16
ALL = ("dp", "wide")


def coordinates(device):
    return device // 4 % 4, device % 4, device // 32, device // 16 % 2


def device_at(x, y, z, core):
    return z * 32 + core * 16 + x * 4 + y


def neighbour(device, ring, hops):
    x, y, z, core = coordinates(device)
    axis = (ring + core) % 3
    place = [x, y, z]
    place[axis] = (place[axis] + hops) % RING
    return device_at(*place, core)


def shifted(v, ring, hops):
    return lax.ppermute(v, ALL, [(d, neighbour(d, ring, hops)) for d in range(DEVICES)])


def swap_cores(v):
    return lax.ppermute(v, ALL, [(d, d ^ 16) for d in range(DEVICES)])


def relative_devices(device, shape):
    row = lax.broadcasted_iota(jnp.int32, shape, 0)
    ra, rb, rc = row >> 5, (row >> 3) & 3, (row >> 1) & 3
    x, y = (device >> 2) & 3, device & 3
    z, core = device >> 5, (device >> 4) & 1
    first = core == 0
    dx, dy, dz = (
        jnp.where(first, ra, rc),
        jnp.where(first, rb, ra),
        jnp.where(first, rc, rb),
    )
    return ((z + dz) & 3) * 32 + (core ^ (row & 1)) * 16 + ((x + dx) & 3) * 4 + ((y + dy) & 3)


def relative_place(device, core, ra, rb, rc, sign):
    x, y, z = (device >> 2) & 3, device & 3, device >> 5
    dx, dy, dz = (ra, rb, rc) if core == 0 else (rc, ra, rb)
    return (
        ((z + sign * dz) & 3) * 32 + core * 16 + ((x + sign * dx) & 3) * 4 + ((y + sign * dy) & 3)
    )


def rows_of_lanes(lead, shape):
    return lax.broadcasted_iota(jnp.int32, shape, lead)


def halves(v):
    high = v.astype(BF16)
    return high, (v - high.astype(F32)).astype(BF16)


def thirds(v):
    high = v.astype(BF16).astype(F32)
    rest = v - high
    mid = rest.astype(BF16).astype(F32)
    return high, mid, rest - mid


def mm(a, b):
    return lax.dot_general(a, b, (((1,), (0,)), ((), ())), preferred_element_type=F32)


def mm_nt(a, b):
    return lax.dot_general(a, b, (((1,), (1,)), ((), ())), preferred_element_type=F32)


def beside(*parts):
    return jnp.concatenate(parts, axis=1)


def total_of(v):
    return jnp.sum(jnp.sum(v, axis=0, keepdims=True), axis=1, keepdims=True)


def stacked(*parts):
    return jnp.concatenate(parts, axis=0)


def pack_kernel(
    device_ref, weights_hbm, coords_hbm, distances_hbm, index_hbm, *refs
):
    outs, (weights_ref, coords_ref, distances_ref, index_ref, sems) = refs[:RING], refs[RING:]
    copies = [
        pltpu.make_async_copy(source, target, sems.at[i])
        for i, (source, target) in enumerate(
            [
                (index_hbm, index_ref),
                (weights_hbm, weights_ref),
                (coords_hbm, coords_ref),
                (distances_hbm, distances_ref),
            ]
        )
    ]
    for copy in copies:
        copy.start()
    for copy in copies:
        copy.wait()
    shard = stacked(weights_ref[...], jnp.zeros((BOX_ROWS - SHARD_ROWS, LANES), F32))
    index = index_ref[...]
    owner = lax.shift_right_logical(index, 8)
    row = lax.bitwise_and(index, CODE_ROWS - 1)
    sent = (relative_devices(device_ref[0], (DEVICES, POINTS_DEV)) == owner).astype(F32)
    sent_low = sent.astype(BF16)
    width = 256
    earlier = rows_of_lanes(0, (width, width)) < rows_of_lanes(1, (width, width))
    earlier = earlier.astype(F32).astype(BF16)
    ones = jnp.ones((width, width), BF16)
    ranks = [
        mm(sent_low[:, : (part + 1) * width], stacked(*([ones] * part + [earlier])))
        for part in range(POINTS_DEV // width)
    ]
    placed = jnp.sum(sent * beside(*ranks), axis=0, keepdims=True).astype(jnp.int32)
    at_slot = rows_of_lanes(0, (SLOTS, POINTS_DEV)) == placed
    values = [coords_ref[i : i + 1, :] for i in range(3)]
    values += [distances_ref[...], (row + 1).astype(F32)]
    pieces = [[], [], []]
    for value in values:
        for k, third in enumerate(thirds(value)):
            pieces[k].append(jnp.where(at_slot, third, 0.0))
    spare = jnp.zeros((LANES - SLOTS * len(values), POINTS_DEV), F32)
    boxes = mm_nt(
        beside(sent_low, sent_low, sent_low),
        beside(*[stacked(*piece, spare).astype(BF16) for piece in pieces]),
    )
    for r in range(RING):
        outs[r][0:BOX_ROWS, :] = shard
        outs[r][BOX_ROWS:, :] = boxes[r * 32 : r * 32 + 32, :]


def unit_groups(count, stride_rows, extra, first_entry):
    for group in range(count):
        entry = first_entry + group * 8 * (stride_rows * LANES + extra)
        yield group, entry // LANES, entry % LANES


def unpack_units(flat_ref, out_ref, count, stride_rows, extra, first_entry):
    lane = rows_of_lanes(1, (8, LANES))
    slope = rows_of_lanes(0, (8, LANES)) * extra
    for group, first, shift in unit_groups(count, stride_rows, extra, first_entry):
        start = slope + shift
        wraps = shift + 7 * extra >= LANES
        turn = lax.bitwise_and(lane + start, LANES - 1)
        tiles = []
        for a in range(stride_rows + 2 + wraps):
            tile = flat_ref[pl.ds(first + a, 8, stride=stride_rows), :]
            tiles.append(jnp.take_along_axis(tile, turn, axis=1, mode="promise_in_bounds"))
        for c in range(stride_rows + 1):
            value = jnp.where(lane + start < LANES, tiles[c], tiles[c + 1])
            if wraps:
                value = jnp.where(lane + start < 2 * LANES, value, tiles[c + 2])
            out_ref[group * 8 : group * 8 + 8, c * LANES : (c + 1) * LANES] = value


def pack_units(value_ref, flat_ref, count, stride_rows, extra, first_entry, adding):
    lane = rows_of_lanes(1, (8, LANES))
    slope = rows_of_lanes(0, (8, LANES)) * extra
    zero = jnp.zeros((8, LANES), F32)
    for group, first, shift in unit_groups(count, stride_rows, extra, first_entry):
        start = slope + shift
        wraps = shift + 7 * extra >= LANES
        wanted = range(stride_rows, stride_rows + 1 + wraps + 1) if adding else range(stride_rows)
        rolled = {}

        turn = lax.bitwise_and(lane - start, LANES - 1)

        def tile(c, rolled=rolled, group=group, turn=turn):
            if c < 0 or c > stride_rows:
                return zero
            if c not in rolled:
                value = value_ref[group * 8 : group * 8 + 8, c * LANES : (c + 1) * LANES]
                rolled[c] = jnp.take_along_axis(value, turn, axis=1, mode="promise_in_bounds")
            return rolled[c]

        for a in wanted:
            value = jnp.where(lane >= start, tile(a), tile(a - 1))
            if wraps:
                value = jnp.where(lane >= start - LANES, value, tile(a - 2))
            rows = pl.ds(first + a, 8, stride=stride_rows)
            if adding:
                flat_ref[rows, :] = flat_ref[rows, :] + value
            else:
                flat_ref[rows, :] = value


FIRST_UNITS = (32, 2, 5, 0)
SECOND_UNITS = (64, 4, 3, MIDDLE * (LATENT + 5))
HEAD_ENTRY = MIDDLE * (LATENT + 5) + HID * (HID + 3)


def silu_parts(v):
    gate = 0.5 * jnp.tanh(0.5 * v) + 0.5
    rest = 1.0 - gate
    value = v * gate
    slope = gate + value * rest
    curve = rest * (gate + gate + value * (rest - gate))
    return value, slope, curve


def main_kernel(
    device_ref,
    mine_ref,
    other_ref,
    codes_ref,
    keep_ref,
    give_ref,
    code_grad_ref,
    flat,
    first_w,
    second_w,
    lhs_one,
    lhs_two,
    lhs_back,
    latent_w,
    coord_w,
    head_w,
    spots,
    sum_two,
    sum_codes,
    sum_coord,
    sum_head,
    sum_count,
    sum_loss,
    act_one,
    slope_one,
    curve_one,
    back_one,
    hid_hi,
    hid_lo,
    hot,
    act_two,
    slope_two,
    curve_two,
    gate_hi,
    gate_lo,
    tang_hi,
    tang_lo,
    near_hi,
    near_lo,
    bar_hi,
    bar_lo,
    low_hi,
    low_lo,
):
    device = device_ref[0]
    core = (device >> 4) & 1

    for which in range(2):

        @pl.when(core == which)
        def _(which=which):
            for c in range(2):
                source = mine_ref if c == which else other_ref
                for place in range(CHIPS):
                    rc, rb, ra = place // 16, place // 4 % 4, place % 4
                    first = relative_place(device, c, ra, rb, rc, -1) * SHARD_ROWS
                    box = place * BOX_ROWS
                    flat[pl.ds(first, SHARD_ROWS), :] = source[box : box + SHARD_ROWS, :]

    spots[...] = stacked(
        mine_ref[pl.ds(CORE_ROWS, CHIPS, stride=2), :],
        other_ref[pl.ds(CORE_ROWS + 1, CHIPS, stride=2), :],
    ).T

    unpack_units(flat, first_w, *FIRST_UNITS)
    unpack_units(flat, second_w, *SECOND_UNITS)
    head_bias = flat[HEAD_ENTRY // LANES : HEAD_ENTRY // LANES + 1, :][
        :, HEAD_ENTRY % LANES : HEAD_ENTRY % LANES + 1
    ]

    lane = rows_of_lanes(1, (256, LANES))
    unit = rows_of_lanes(0, (256, LANES))
    real = unit < MIDDLE

    first_low = jnp.where(beside(real, real), first_w[:, : 2 * LANES], 0.0)
    first_end = jnp.where(real, first_w[:, 2 * LANES :], 0.0)
    first_near = jnp.where(lane < 3, first_end, 0.0)
    first_gain = first_end[:, 3:4]
    first_bias = first_end[:, 4:5]
    first_w[:, : 2 * LANES] = first_low
    first_w[:, 2 * LANES :] = first_end
    first_root = lax.rsqrt(
        jnp.sum(first_low * first_low, axis=1, keepdims=True)
        + jnp.sum(first_near * first_near, axis=1, keepdims=True)
        + 1e-12
    )
    first_scale = first_gain * first_root
    first_low = first_low * first_scale
    first_near = first_near * first_scale
    latent_w[0:256, :] = first_low
    for i in range(3):
        coord_w[:, i * LANES : (i + 1) * LANES] = jnp.broadcast_to(
            first_near[:, i : i + 1], (256, LANES)
        )

    second_a = second_w[:, 0:256]
    second_b = second_w[:, 256:512]
    second_gain = second_w[:, 512:513]
    second_bias = second_w[:, 513:514]
    head_w[...] = jnp.broadcast_to(second_w[:, 514:515], (HID, LANES))
    second_root = lax.rsqrt(
        jnp.sum(second_a * second_a + second_b * second_b, axis=1, keepdims=True) + 1e-12
    )
    second_scale = second_gain * second_root
    second_a = second_a * second_scale
    second_b = second_b * second_scale
    is_hidden = rows_of_lanes(1, (HID, 256)) < MIDDLE
    hidden_cols = jnp.where(is_hidden, second_a, second_b)
    latent_cols = pltpu.roll(jnp.where(is_hidden, second_b, second_a), 3, 1)
    latent_w[256:768, :] = latent_cols

    hidden_hi, hidden_lo = halves(hidden_cols)
    lhs_two[:, 0:256] = hidden_hi
    lhs_two[:, 256:512] = hidden_hi
    lhs_two[:, 512:768] = hidden_lo
    back_hi, back_lo = halves(hidden_cols.T)
    lhs_back[:, 0:512] = back_hi
    lhs_back[:, 512:1024] = back_hi
    lhs_back[:, 1024:1536] = back_lo

    code_hi, code_lo = halves(codes_ref[...])
    weight_hi, weight_lo = halves(latent_w[...])
    by_code = mm_nt(
        beside(weight_hi, weight_hi, weight_lo), beside(code_hi, code_lo, code_hi)
    )
    one_hi, one_lo = halves(by_code[0:256, :] + first_bias)
    lhs_one[:, 0:256] = one_hi
    lhs_one[:, 256:512] = one_lo
    two_hi, two_lo = halves(by_code[256:768, :] + second_bias)
    lhs_two[:, 768:1024] = two_hi
    lhs_two[:, 1024:1280] = two_lo
    spread = jnp.where((unit - MIDDLE == lane) & (lane < 3), 1.0, first_near)
    near_parts = thirds(spread)
    near_lhs = near_parts[0]
    for place, k in enumerate((0, 0, 1, 1, 2)):
        near_lhs = near_lhs + pltpu.roll(near_parts[k], 8 * (place + 1), 1)
    lhs_one[:, 512:640] = near_lhs.astype(BF16)

    for ref in (sum_two, sum_codes, sum_coord, sum_head, sum_count, sum_loss):
        ref[...] = jnp.zeros(ref.shape, F32)

    def feature(which, step, sub):
        first = which * SLOTS + step * 4 + sub * 2
        return beside(spots[pl.ds(first, 1), :], spots[pl.ds(first + 1, 1), :])

    blank5 = jnp.zeros((5, BLOCK), F32)
    subs = range(2)
    chunk = 32

    def step_body(step, carry):
        place = [[feature(i, step, s) for i in range(3)] for s in subs]
        target = [feature(3, step, s) for s in subs]
        code_row = [feature(4, step, s) for s in subs]
        valid = [(code_row[s] > 0.5).astype(F32) for s in subs]
        near8 = [stacked(*place[s], blank5) for s in subs]
        near_pieces = [thirds(near8[s]) for s in subs]

        for s in subs:
            wanted = code_row[s] - 1.0
            for r in range(0, CODE_ROWS, chunk):
                mark = jnp.where(
                    (rows_of_lanes(0, (chunk, BLOCK)) + r).astype(F32) == wanted, 1.0, 0.0
                )
                hot[s, r : r + chunk, :] = mark.astype(BF16)
                sum_count[r : r + chunk, :] += mark[:, :LANES] + mark[:, LANES:]

        for s in subs:
            high, mid, low = near_pieces[s]
            near_rhs = stacked(
                high, mid, low, high, mid, high, jnp.zeros((80, BLOCK), F32)
            ).astype(BF16)
            act_one[s] = mm(lhs_one[...], stacked(hot[s], hot[s], near_rhs))
        for s in subs:
            for r in range(0, 256, chunk):
                pre = act_one[s, r : r + chunk, :]
                value, slope, curve = silu_parts(pre)
                if r + chunk == 256:
                    inside = rows_of_lanes(0, (chunk, BLOCK)) + r < MIDDLE
                    value = jnp.where(inside, value, pre)
                    slope = jnp.where(inside, slope, 0.0)
                    curve = jnp.where(inside, curve, 0.0)
                high, low = halves(value)
                hid_hi[s, r : r + chunk, :] = high
                hid_lo[s, r : r + chunk, :] = low
                slope_one[s, r : r + chunk, :] = slope
                curve_one[s, r : r + chunk, :] = curve

        for s in subs:
            act_two[s] = mm(
                lhs_two[...], stacked(hid_hi[s], hid_lo[s], hid_hi[s], hot[s], hot[s])
            )
        summed = []
        for s in subs:
            total = jnp.zeros((8, BLOCK), F32)
            for r in range(0, HID, chunk):
                value, slope, curve = silu_parts(act_two[s, r : r + chunk, :])
                head = beside(head_w[r : r + chunk, :], head_w[r : r + chunk, :])
                weighed = head * value
                for k in range(0, chunk, 8):
                    total = total + weighed[k : k + 8, :]
                high, low = halves(head * slope)
                gate_hi[s, r : r + chunk, :] = high
                gate_lo[s, r : r + chunk, :] = low
                act_two[s, r : r + chunk, :] = value
                slope_two[s, r : r + chunk, :] = slope
                curve_two[s, r : r + chunk, :] = curve
            summed.append(jnp.sum(total, axis=0, keepdims=True))

        for s in subs:
            back_one[s] = mm(lhs_back[...], stacked(gate_hi[s], gate_lo[s], gate_hi[s]))
        leads = []
        for s in subs:
            totals = [jnp.zeros((8, BLOCK), F32) for _ in range(3)]
            for r in range(0, 256, chunk):
                grad = back_one[s, r : r + chunk, :] * slope_one[s, r : r + chunk, :]
                high, low = halves(grad)
                near_hi[s, r : r + chunk, :] = high
                near_lo[s, r : r + chunk, :] = low
                for i in range(3):
                    col = coord_w[r : r + chunk, i * LANES : (i + 1) * LANES]
                    weighed = beside(col, col) * grad
                    for k in range(0, chunk, 8):
                        totals[i] = totals[i] + weighed[k : k + 8, :]
            leads.append(
                [
                    jnp.sum(totals[i], axis=0, keepdims=True)
                    + back_one[s, MIDDLE + i : MIDDLE + i + 1, :]
                    for i in range(3)
                ]
            )

        bars, pulls = [], []
        for s in subs:
            predicted = jnp.tanh(summed[s] + head_bias)
            flank = 1.0 - predicted * predicted
            slope = [flank * q for q in leads[s]]
            excess = slope[0] * slope[0] + slope[1] * slope[1] + slope[2] * slope[2] - 1.0
            capped = jnp.tanh(predicted / DELTA)
            misfit = DELTA * capped - DELTA * jnp.tanh(target[s] / DELTA)
            fitting = jnp.sqrt(misfit * misfit + SMOOTH * SMOOTH)
            loss = fitting + EIK_WEIGHT * excess * excess
            sum_loss[0:1, :] += valid[s] * loss
            share = valid[s] * (1.0 / ALL_POINTS)
            pull = [(4.0 * EIK_WEIGHT) * excess * v for v in slope]
            by_flank = sum(p * q for p, q in zip(pull, leads[s]))
            by_predicted = misfit / fitting * (1.0 - capped * capped) - 2.0 * predicted * by_flank
            bars.append(share * by_predicted * flank)
            sum_loss[1:2, :] += bars[s]
            pulls.append([share * flank * p for p in pull])

        for s in subs:
            last = stacked(blank5, *pulls[s])
            for r in range(0, 256, chunk):
                grad = 0.0
                for i in range(3):
                    col = coord_w[r : r + chunk, i * LANES : (i + 1) * LANES]
                    grad = grad + beside(col, col) * pulls[s][i]
                through = grad * slope_one[s, r : r + chunk, :]
                if r + chunk == 256:
                    inside = rows_of_lanes(0, (8, BLOCK)) < MIDDLE - 248
                    through = stacked(
                        through[: chunk - 8], jnp.where(inside, through[chunk - 8 :], last)
                    )
                high, low = halves(through)
                tang_hi[s, r : r + chunk, :] = high
                tang_lo[s, r : r + chunk, :] = low
                curve_one[s, r : r + chunk, :] = (
                    grad * back_one[s, r : r + chunk, :] * curve_one[s, r : r + chunk, :]
                )
        tangents = []
        for s in subs:
            tangents.append(
                mm(lhs_two[:, 0:768], stacked(tang_hi[s], tang_lo[s], tang_hi[s]))
            )
        for s in subs:
            for r in range(0, HID, chunk):
                tangent = tangents[s][r : r + chunk, :]
                slope = slope_two[s, r : r + chunk, :]
                head = beside(head_w[r : r + chunk, :], head_w[r : r + chunk, :])
                bar = head * (bars[s] * slope + tangent * curve_two[s, r : r + chunk, :])
                by_head = act_two[s, r : r + chunk, :] * bars[s] + slope * tangent
                sum_head[r : r + chunk, :] += by_head[:, :LANES] + by_head[:, LANES:]
                high, low = halves(bar)
                bar_hi[s, r : r + chunk, :] = high
                bar_lo[s, r : r + chunk, :] = low

        for s in subs:
            back_one[s] = mm(lhs_back[...], stacked(bar_hi[s], bar_lo[s], bar_hi[s]))
        left, right = [], []
        for s in subs:
            left += [bar_hi[s], bar_hi[s], bar_lo[s], gate_hi[s], gate_hi[s], gate_lo[s]]
            right += [hid_hi[s], hid_lo[s], hid_hi[s], tang_hi[s], tang_lo[s], tang_hi[s]]
        sum_two[...] += mm_nt(beside(*left), beside(*right))
        hots = beside(hot[0], hot[0], hot[1], hot[1])
        sum_codes[256:768, :] += mm_nt(beside(bar_hi[0], bar_lo[0], bar_hi[1], bar_lo[1]), hots)

        for s in subs:
            for r in range(0, 256, chunk):
                bar = (
                    back_one[s, r : r + chunk, :] * slope_one[s, r : r + chunk, :]
                    + curve_one[s, r : r + chunk, :]
                )
                high, low = halves(bar)
                low_hi[s, r : r + chunk, :] = high
                low_lo[s, r : r + chunk, :] = low
        sum_codes[0:256, :] += mm_nt(beside(low_hi[0], low_lo[0], low_hi[1], low_lo[1]), hots)
        left, right = [], []
        for s in subs:
            seen = stacked(near_pieces[s][0], near_pieces[s][1]).astype(BF16)
            pulled = stacked(*pulls[s], blank5)
            high = pulled.astype(BF16).astype(F32)
            pulled = stacked(high, pulled - high).astype(BF16)
            left += [seen, seen, pulled, pulled]
            right += [low_hi[s], low_lo[s], near_hi[s], near_lo[s]]
        sum_coord[...] += mm_nt(beside(*left), beside(*right))
        return carry

    lax.fori_loop(0, SLOTS * DEVICES // (2 * BLOCK), step_body, 0)

    codes = codes_ref[...]
    count = jnp.sum(sum_count[...], axis=1, keepdims=True)
    by_code = sum_codes[...]
    turned_hi, turned_lo = halves(by_code.T)
    weight_hi, weight_lo = halves(latent_w[...])
    code_grad = mm(
        beside(turned_hi, turned_hi, turned_lo), stacked(weight_hi, weight_lo, weight_hi)
    )
    code_grad = code_grad + (2.0 * CODE_WEIGHT / ALL_POINTS) * count * codes
    code_grad_ref[...] = code_grad
    code_squares = total_of(code_grad * code_grad)
    loss = jnp.sum(sum_loss[0:1, :], axis=1, keepdims=True)
    loss = loss + CODE_WEIGHT * total_of(count * codes * codes)
    loss = loss / ALL_POINTS

    code_hi, code_lo = halves(codes)
    by_hi, by_lo = halves(by_code)
    latent_grad = mm(beside(by_hi, by_hi, by_lo), stacked(code_hi, code_lo, code_hi))
    bias_grad = jnp.sum(by_code, axis=1, keepdims=True)

    near_grad = sum_coord[0:8, :] + sum_coord[8:16, :]
    near_grad = stacked(near_grad, jnp.zeros((LANES - 8, 256), F32)).T
    near_grad = jnp.where(lane < 3, near_grad, 0.0)
    low_grad = latent_grad[0:256, :]
    first_low = first_w[:, : 2 * LANES]
    first_near = jnp.where(lane < 3, first_w[:, 2 * LANES :], 0.0)
    along = jnp.sum(first_low * low_grad, axis=1, keepdims=True)
    along = along + jnp.sum(first_near * near_grad, axis=1, keepdims=True)
    inward = first_scale * first_root * first_root * along
    end = first_scale * near_grad - first_near * inward
    end = jnp.where(lane == 3, first_root * along, end)
    end = jnp.where(lane == 4, bias_grad[0:256, :], end)
    low_grad = first_scale * low_grad - first_low * inward
    first_w[:, : 2 * LANES] = jnp.where(beside(real, real), low_grad, 0.0)
    first_w[:, 2 * LANES :] = jnp.where(real, end, 0.0)

    hidden_grad = sum_two[...]
    moved = pltpu.roll(latent_grad[256:768, :], 256 - 3, 1)
    grad_a = jnp.where(is_hidden, hidden_grad, moved)
    grad_b = jnp.where(is_hidden, moved, hidden_grad)
    second_a = second_w[:, 0:256]
    second_b = second_w[:, 256:512]
    along = jnp.sum(second_a * grad_a + second_b * grad_b, axis=1, keepdims=True)
    inward = second_scale * second_root * second_root * along
    second_w[:, 0:256] = second_scale * grad_a - second_a * inward
    second_w[:, 256:512] = second_scale * grad_b - second_b * inward
    head_grad = jnp.sum(sum_head[...], axis=1, keepdims=True)
    lane = rows_of_lanes(1, (HID, LANES))
    end = jnp.where(lane == 0, second_root * along, 0.0)
    end = jnp.where(lane == 1, bias_grad[256:768, :], end)
    second_w[:, 512:640] = jnp.where(lane == 2, head_grad, end)

    flat[...] = jnp.zeros(flat.shape, F32)
    for adding in (False, True):
        pack_units(first_w, flat, *FIRST_UNITS, adding)
        pack_units(second_w, flat, *SECOND_UNITS, adding)
    row = HEAD_ENTRY // LANES
    lane = rows_of_lanes(1, (1, LANES))
    bias_total = jnp.sum(sum_loss[1:2, :], axis=1, keepdims=True)
    flat[row : row + 1, :] = flat[row : row + 1, :] + jnp.where(
        lane == HEAD_ENTRY % LANES, bias_total, 0.0
    )
    sub = rows_of_lanes(0, (8, LANES))
    wide = rows_of_lanes(1, (8, LANES))
    info = jnp.where((sub == 5) & (wide == 0), loss, 0.0)
    info = jnp.where((sub == 5) & (wide == 1), code_squares, info)
    for which in range(2):

        @pl.when(core == which)
        def _(which=which):
            for c in range(2):
                target = keep_ref if c == which else give_ref
                for place in range(CHIPS):
                    rc, rb, ra = place // 16, place // 4 % 4, place % 4
                    first = relative_place(device, c, ra, rb, rc, 1) * SHARD_ROWS
                    box = place * BOX_ROWS
                    target[box : box + 16, :] = flat[pl.ds(first, 16), :]
                    target[box + 16 : box + 24, :] = jnp.where(
                        sub < 5, flat[pl.ds(first + 16, 8), :], info
                    )


def vmem(count):
    return [pl.BlockSpec(memory_space=pltpu.VMEM)] * count


PARAMS = pltpu.CompilerParams(vmem_limit_bytes=48 * 1024 * 1024)


ANY = pl.BlockSpec(memory_space=pl.ANY)
SMEM = pl.BlockSpec(memory_space=pltpu.SMEM)


def pack_boxes(device, weights, coords, distances, index):
    box = jax.ShapeDtypeStruct((BOX_ROWS + 32, LANES), F32)
    return pl.pallas_call(
        pack_kernel,
        out_shape=(box,) * RING,
        in_specs=[SMEM] + [ANY] * 4,
        out_specs=tuple(vmem(RING)),
        scratch_shapes=[
            pltpu.VMEM(weights.shape, F32),
            pltpu.VMEM(coords.shape, F32),
            pltpu.VMEM(distances.shape, F32),
            pltpu.VMEM(index.shape, jnp.int32),
            pltpu.SemaphoreType.DMA((4,)),
        ],
        compiler_params=PARAMS,
    )(device, weights, coords, distances, index)


def main_call(device, mine, other, codes):
    pair = (2, 256, BLOCK)
    pair_two = (2, HID, BLOCK)
    scratch = [
        ((FLAT_ROWS + 8, LANES), F32),
        ((256, 3 * LANES), F32),
        ((HID, 5 * LANES), F32),
        ((256, 640), BF16),
        ((HID, 1280), BF16),
        ((256, 1536), BF16),
        ((768, 256), F32),
        ((256, 3 * LANES), F32),
        ((HID, LANES), F32),
        ((LANES, LANES), F32),
        ((HID, 256), F32),
        ((768, 256), F32),
        ((16, 256), F32),
        ((HID, LANES), F32),
        ((CODE_ROWS, LANES), F32),
        ((2, BLOCK), F32),
        (pair, F32),
        (pair, F32),
        (pair, F32),
        (pair, F32),
        (pair, BF16),
        (pair, BF16),
        (pair, BF16),
        (pair_two, F32),
        (pair_two, F32),
        (pair_two, F32),
        (pair_two, BF16),
        (pair_two, BF16),
        (pair, BF16),
        (pair, BF16),
        (pair, BF16),
        (pair, BF16),
        (pair_two, BF16),
        (pair_two, BF16),
        (pair, BF16),
        (pair, BF16),
    ]
    return pl.pallas_call(
        main_kernel,
        out_shape=(
            jax.ShapeDtypeStruct((CORE_ROWS, LANES), F32),
            jax.ShapeDtypeStruct((CORE_ROWS, LANES), F32),
            jax.ShapeDtypeStruct((CODE_ROWS, LATENT), F32),
        ),
        in_specs=[SMEM] + vmem(3),
        out_specs=tuple(vmem(3)),
        scratch_shapes=[pltpu.VMEM(shape, dtype) for shape, dtype in scratch],
        compiler_params=PARAMS,
    )(device, mine, other, codes)


def adam_update(value, first, second, grad, rate):
    first_new = BETA_ONE * first + (1.0 - BETA_ONE) * grad
    second_new = BETA_TWO * second + (1.0 - BETA_TWO) * grad * grad
    first_hat = first_new / (1.0 - BETA_ONE**STEP)
    second_hat = second_new / (1.0 - BETA_TWO**STEP)
    value_new = value - rate * (first_hat / (jnp.sqrt(second_hat) + ADAM_EPS) + DECAY * value)
    return (value_new, first_new, second_new)


def gather_rings(boxes):
    got = [boxes[0]] + [shifted(boxes[r], 0, r) for r in range(1, RING)]
    line = jnp.concatenate([v[:BOX_ROWS] for v in got])
    message = [
        jnp.concatenate([line] + [v[BOX_ROWS + 8 * r : BOX_ROWS + 8 * r + 8] for v in got])
        for r in range(RING)
    ]
    got = [message[0]] + [shifted(message[r], 1, r) for r in range(1, RING)]
    plane = jnp.concatenate([v[:LINE_ROWS] for v in got])
    points = jnp.concatenate([v[LINE_ROWS:] for v in got]).reshape(16, RING, 2, LANES)
    points = [points[:, r].reshape(32, LANES) for r in range(RING)]
    across = shifted(points[2], 2, 2)
    behind = shifted(jnp.concatenate([plane, points[1]]), 2, 1)
    ahead = shifted(jnp.concatenate([plane, points[3]]), 2, 3)
    half = PLANE_ROWS // 2
    far_low = shifted(behind[:half], 2, 1)
    far_high = shifted(ahead[half:PLANE_ROWS], 2, 3)
    return jnp.concatenate(
        [
            plane,
            behind[:PLANE_ROWS],
            far_low,
            far_high,
            ahead[:PLANE_ROWS],
            points[0],
            behind[PLANE_ROWS:],
            across,
            ahead[PLANE_ROWS:],
        ]
    )


def reduce_rings(total):
    part = [total[r * PLANE_ROWS : (r + 1) * PLANE_ROWS] for r in range(RING)]
    half = PLANE_ROWS // 2
    low = shifted(part[2][:half], 2, 1)
    high = shifted(part[2][half:], 2, 3)
    onward = jnp.concatenate([part[1][:half] + low, part[1][half:]])
    back = jnp.concatenate([part[3][:half], part[3][half:] + high])
    total = part[0] + shifted(onward, 2, 1) + shifted(back, 2, 3)
    for ring, rows in ((1, LINE_ROWS), (0, BOX_ROWS)):
        part = [total[r * rows : (r + 1) * rows] for r in range(RING)]
        total = part[0] + sum(shifted(part[r], ring, r) for r in range(1, RING))
    return total


def sum_everywhere(v):
    v = v + swap_cores(v)
    for ring in range(3):
        v = v + sum(shifted(v, ring, r) for r in range(1, RING))
    return v


def body(
    weights_flat,
    moment_one,
    moment_two,
    codes,
    code_first,
    code_second,
    coords,
    distances,
    shape_index,
):
    device = (lax.axis_index("dp") * 16 + lax.axis_index("wide")).astype(jnp.int32).reshape(1)
    boxes = pack_boxes(
        device,
        weights_flat.reshape(SHARD_ROWS, LANES),
        coords,
        distances.reshape(1, POINTS_DEV),
        shape_index.reshape(1, POINTS_DEV),
    )
    mine = gather_rings(boxes)
    other = swap_cores(mine)
    keep, give, code_grad = main_call(device, mine, other, codes)
    shard = reduce_rings(keep + swap_cores(give))
    weight_grad = shard[:SHARD_ROWS]
    loss_value = shard[SHARD_ROWS, 0]
    code_squares = shard[SHARD_ROWS, 1]
    squares = sum_everywhere(jnp.sum(weight_grad * weight_grad).reshape(1, 1)).reshape(())
    grad_norm = jnp.sqrt(squares + code_squares)
    factor = jnp.minimum(1.0, CLIP / (grad_norm + 1e-06))
    new_weights, first_new, second_new = adam_update(
        weights_flat, moment_one, moment_two, factor * weight_grad.reshape(-1), WEIGHT_RATE
    )
    new_codes, code_first_new, code_second_new = adam_update(
        codes, code_first, code_second, factor * code_grad, CODE_RATE
    )
    return (
        loss_value,
        grad_norm,
        new_weights,
        first_new,
        second_new,
        new_weights.astype(BF16),
        new_codes,
        code_first_new,
        code_second_new,
        new_codes.astype(BF16),
    )


def solution(mesh):
    flat, rows = P(ALL), P(ALL, None)
    return jax.shard_map(
        body,
        mesh=mesh,
        in_specs=(flat, flat, flat, rows, rows, rows, P(None, ALL), flat, flat),
        out_specs=(P(), P(), flat, flat, flat, flat, rows, rows, rows, rows),
        check_vma=False,
    )
```

```python
import jax
import jax.numpy as jnp
from jax import lax
from jax.experimental import pallas as pl
from jax.experimental.pallas import tpu as pltpu
from jax.sharding import Mesh
from jax.sharding import PartitionSpec as P

LATENT = 256
HID = 512
MIDDLE = HID - LATENT - 3
STEP = 10

DELTA = 0.1
SMOOTH = 0.01
CODE_WEIGHT = 0.001
EIK_WEIGHT = 0.1
CLIP = 0.001
WEIGHT_RATE = 0.02
CODE_RATE = 0.15
BETA_ONE = 0.9
BETA_TWO = 0.999
ADAM_EPS = 1e-08
DECAY = 0.01

LANES = 128
DEVICES = 128
PEERS = 64
SHARD_ROWS = 21
BOX_ROWS = 24
SLOTS = 16
POINTS_DEV = 1024
CODE_ROWS = 256
FLAT_ROWS = DEVICES * SHARD_ROWS
BLOCK = 256
SUBS = 4
ALL_POINTS = POINTS_DEV * DEVICES

F32 = jnp.float32
BF16 = jnp.bfloat16
ALL = ("z", "core", "wide")


def rows_of_lanes(lead, shape):
    return lax.broadcasted_iota(jnp.int32, shape, lead)


def halves(v):
    high = v.astype(BF16)
    return high, (v - high.astype(F32)).astype(BF16)


def thirds(v):
    high = v.astype(BF16).astype(F32)
    rest = v - high
    mid = rest.astype(BF16).astype(F32)
    return high, mid, rest - mid


def mm(a, b):
    return lax.dot_general(a, b, (((1,), (0,)), ((), ())), preferred_element_type=F32)


def mm_nt(a, b):
    return lax.dot_general(a, b, (((1,), (1,)), ((), ())), preferred_element_type=F32)


def beside(*parts):
    return jnp.concatenate(parts, axis=1)


def total_of(v):
    return jnp.sum(jnp.sum(v, axis=0, keepdims=True), axis=1, keepdims=True)


def stacked(*parts):
    return jnp.concatenate(parts, axis=0)


def pack_kernel(
    weights_hbm,
    coords_hbm,
    distances_hbm,
    index_hbm,
    out_ref,
    weights_ref,
    coords_ref,
    distances_ref,
    index_ref,
    sems,
):
    pairs = [
        (index_hbm, index_ref),
        (weights_hbm, weights_ref),
        (coords_hbm, coords_ref),
        (distances_hbm, distances_ref),
    ]
    copies = [
        pltpu.make_async_copy(source, target, sems.at[i])
        for i, (source, target) in enumerate(pairs)
    ]
    for copy in copies:
        copy.start()
    for copy in copies:
        copy.wait()
    shard = stacked(weights_ref[...], jnp.zeros((BOX_ROWS - SHARD_ROWS, LANES), F32))
    for peer in range(PEERS):
        out_ref[peer * BOX_ROWS : (peer + 1) * BOX_ROWS, :] = shard
    index = index_ref[...]
    owner = lax.shift_right_logical(index, 8)
    row = lax.bitwise_and(index, CODE_ROWS - 1)
    sent = (rows_of_lanes(0, (DEVICES, POINTS_DEV)) == owner).astype(F32)
    sent_low = sent.astype(BF16)
    width = 256
    earlier = rows_of_lanes(0, (width, width)) < rows_of_lanes(1, (width, width))
    earlier = earlier.astype(F32).astype(BF16)
    ones = jnp.ones((width, width), BF16)
    ranks = [
        mm(sent_low[:, : (part + 1) * width], stacked(*([ones] * part + [earlier])))
        for part in range(POINTS_DEV // width)
    ]
    placed = jnp.sum(sent * beside(*ranks), axis=0, keepdims=True).astype(jnp.int32)
    at_slot = rows_of_lanes(0, (SLOTS, POINTS_DEV)) == placed
    values = [coords_ref[i : i + 1, :] for i in range(3)]
    values += [distances_ref[...], (row + 1).astype(F32)]
    pieces = [[], [], []]
    for value in values:
        for k, third in enumerate(thirds(value)):
            pieces[k].append(jnp.where(at_slot, third, 0.0))
    spare = jnp.zeros((LANES - SLOTS * len(values), POINTS_DEV), F32)
    boxes = mm_nt(
        beside(sent_low, sent_low, sent_low),
        beside(*[stacked(*piece, spare).astype(BF16) for piece in pieces]),
    )
    for z in range(4):
        for core in range(2):
            first = z * 32 + core * 16
            out_ref[pl.ds(z * 16 * BOX_ROWS + SHARD_ROWS + core, 16, stride=BOX_ROWS), :] = boxes[
                first : first + 16, :
            ]


def unit_groups(count, stride_rows, extra, first_entry):
    for group in range(count):
        entry = first_entry + group * 8 * (stride_rows * LANES + extra)
        yield group, entry // LANES, entry % LANES


def unpack_units(flat_ref, out_ref, count, stride_rows, extra, first_entry):
    lane = rows_of_lanes(1, (8, LANES))
    slope = rows_of_lanes(0, (8, LANES)) * extra
    for group, first, shift in unit_groups(count, stride_rows, extra, first_entry):
        start = slope + shift
        wraps = shift + 7 * extra >= LANES
        turn = lax.bitwise_and(lane + start, LANES - 1)
        tiles = []
        for a in range(stride_rows + 2 + wraps):
            tile = flat_ref[pl.ds(first + a, 8, stride=stride_rows), :]
            tiles.append(jnp.take_along_axis(tile, turn, axis=1, mode="promise_in_bounds"))
        for c in range(stride_rows + 1):
            value = jnp.where(lane + start < LANES, tiles[c], tiles[c + 1])
            if wraps:
                value = jnp.where(lane + start < 2 * LANES, value, tiles[c + 2])
            out_ref[group * 8 : group * 8 + 8, c * LANES : (c + 1) * LANES] = value


def pack_units(value_ref, flat_ref, count, stride_rows, extra, first_entry, adding):
    lane = rows_of_lanes(1, (8, LANES))
    slope = rows_of_lanes(0, (8, LANES)) * extra
    zero = jnp.zeros((8, LANES), F32)
    for group, first, shift in unit_groups(count, stride_rows, extra, first_entry):
        start = slope + shift
        wraps = shift + 7 * extra >= LANES
        wanted = range(stride_rows, stride_rows + 1 + wraps + 1) if adding else range(stride_rows)
        rolled = {}

        turn = lax.bitwise_and(lane - start, LANES - 1)

        def tile(c, rolled=rolled, group=group, turn=turn):
            if c < 0 or c > stride_rows:
                return zero
            if c not in rolled:
                value = value_ref[group * 8 : group * 8 + 8, c * LANES : (c + 1) * LANES]
                rolled[c] = jnp.take_along_axis(value, turn, axis=1, mode="promise_in_bounds")
            return rolled[c]

        for a in wanted:
            value = jnp.where(lane >= start, tile(a), tile(a - 1))
            if wraps:
                value = jnp.where(lane >= start - LANES, value, tile(a - 2))
            rows = pl.ds(first + a, 8, stride=stride_rows)
            if adding:
                flat_ref[rows, :] = flat_ref[rows, :] + value
            else:
                flat_ref[rows, :] = value


FIRST_UNITS = (32, 2, 5, 0)
SECOND_UNITS = (64, 4, 3, MIDDLE * (LATENT + 5))
HEAD_ENTRY = MIDDLE * (LATENT + 5) + HID * (HID + 3)


def silu_parts(v):
    gate = 0.5 * jnp.tanh(0.5 * v) + 0.5
    rest = 1.0 - gate
    value = v * gate
    slope = gate + value * rest
    curve = rest * (gate + gate + value * (rest - gate))
    return value, slope, curve


def main_kernel(
    core_ref,
    mine_ref,
    other_ref,
    codes_ref,
    keep_ref,
    give_ref,
    code_grad_ref,
    flat,
    first_w,
    second_w,
    lhs_one,
    lhs_two,
    lhs_back,
    latent_w,
    coord_w,
    head_w,
    spots,
    sum_two,
    sum_codes,
    sum_coord,
    sum_head,
    sum_count,
    sum_loss,
    act_one,
    slope_one,
    curve_one,
    back_one,
    hid_hi,
    hid_lo,
    hot,
    act_two,
    slope_two,
    curve_two,
    gate_hi,
    gate_lo,
    tang_hi,
    tang_lo,
    near_hi,
    near_lo,
    bar_hi,
    bar_lo,
    low_hi,
    low_lo,
):
    core = core_ref[0]

    for which in range(2):

        @pl.when(core == which)
        def _(which=which):
            for d in range(DEVICES):
                z, c, w = d // 32, d // 16 % 2, d % 16
                box = (z * 16 + w) * BOX_ROWS
                source = mine_ref if c == which else other_ref
                flat[d * SHARD_ROWS : d * SHARD_ROWS + BOX_ROWS, :] = source[box : box + BOX_ROWS, :]
            rows = pl.ds(SHARD_ROWS + which, PEERS, stride=BOX_ROWS)
            spots[...] = stacked(mine_ref[rows, :], other_ref[rows, :]).T

    unpack_units(flat, first_w, *FIRST_UNITS)
    unpack_units(flat, second_w, *SECOND_UNITS)
    head_bias = flat[HEAD_ENTRY // LANES : HEAD_ENTRY // LANES + 1, :][
        :, HEAD_ENTRY % LANES : HEAD_ENTRY % LANES + 1
    ]

    lane = rows_of_lanes(1, (256, LANES))
    unit = rows_of_lanes(0, (256, LANES))
    real = unit < MIDDLE

    first_low = jnp.where(beside(real, real), first_w[:, : 2 * LANES], 0.0)
    first_end = jnp.where(real, first_w[:, 2 * LANES :], 0.0)
    first_near = jnp.where(lane < 3, first_end, 0.0)
    first_gain = first_end[:, 3:4]
    first_bias = first_end[:, 4:5]
    first_w[:, : 2 * LANES] = first_low
    first_w[:, 2 * LANES :] = first_end
    first_root = lax.rsqrt(
        jnp.sum(first_low * first_low, axis=1, keepdims=True)
        + jnp.sum(first_near * first_near, axis=1, keepdims=True)
        + 1e-12
    )
    first_scale = first_gain * first_root
    first_low = first_low * first_scale
    first_near = first_near * first_scale
    latent_w[0:256, :] = first_low
    for i in range(3):
        coord_w[:, i * LANES : (i + 1) * LANES] = jnp.broadcast_to(
            first_near[:, i : i + 1], (256, LANES)
        )

    second_a = second_w[:, 0:256]
    second_b = second_w[:, 256:512]
    second_gain = second_w[:, 512:513]
    second_bias = second_w[:, 513:514]
    head_w[...] = jnp.broadcast_to(second_w[:, 514:515], (HID, LANES))
    second_root = lax.rsqrt(
        jnp.sum(second_a * second_a + second_b * second_b, axis=1, keepdims=True) + 1e-12
    )
    second_scale = second_gain * second_root
    second_a = second_a * second_scale
    second_b = second_b * second_scale
    is_hidden = rows_of_lanes(1, (HID, 256)) < MIDDLE
    hidden_cols = jnp.where(is_hidden, second_a, second_b)
    latent_cols = pltpu.roll(jnp.where(is_hidden, second_b, second_a), 3, 1)
    latent_w[256:768, :] = latent_cols

    hidden_hi, hidden_lo = halves(hidden_cols)
    lhs_two[:, 0:256] = hidden_hi
    lhs_two[:, 256:512] = hidden_hi
    lhs_two[:, 512:768] = hidden_lo
    back_hi, back_lo = halves(hidden_cols.T)
    lhs_back[:, 0:512] = back_hi
    lhs_back[:, 512:1024] = back_hi
    lhs_back[:, 1024:1536] = back_lo

    code_hi, code_lo = halves(codes_ref[...])
    weight_hi, weight_lo = halves(latent_w[...])
    by_code = mm_nt(
        beside(weight_hi, weight_hi, weight_lo), beside(code_hi, code_lo, code_hi)
    )
    one_hi, one_lo = halves(by_code[0:256, :] + first_bias)
    lhs_one[:, 0:256] = one_hi
    lhs_one[:, 256:512] = one_lo
    two_hi, two_lo = halves(by_code[256:768, :] + second_bias)
    lhs_two[:, 768:1024] = two_hi
    lhs_two[:, 1024:1280] = two_lo
    spread = jnp.where((unit - MIDDLE == lane) & (lane < 3), 1.0, first_near)
    near_parts = thirds(spread)
    near_lhs = near_parts[0]
    for place, k in enumerate((0, 0, 1, 1, 2)):
        near_lhs = near_lhs + pltpu.roll(near_parts[k], 8 * (place + 1), 1)
    lhs_one[:, 512:640] = near_lhs.astype(BF16)

    for ref in (sum_two, sum_codes, sum_coord, sum_head, sum_count, sum_loss):
        ref[...] = jnp.zeros(ref.shape, F32)

    def feature(which, step, sub):
        first = which * SLOTS + (step * SUBS + sub) * 2
        return beside(spots[pl.ds(first, 1), :], spots[pl.ds(first + 1, 1), :])

    blank5 = jnp.zeros((5, BLOCK), F32)
    subs = range(SUBS)
    chunk = 32

    def step_body(step, carry):
        place = [[feature(i, step, s) for i in range(3)] for s in subs]
        target = [feature(3, step, s) for s in subs]
        code_row = [feature(4, step, s) for s in subs]
        valid = [(code_row[s] > 0.5).astype(F32) for s in subs]
        near8 = [stacked(*place[s], blank5) for s in subs]
        near_pieces = [thirds(near8[s]) for s in subs]

        for s in subs:
            wanted = code_row[s] - 1.0
            for r in range(0, CODE_ROWS, chunk):
                mark = jnp.where(
                    (rows_of_lanes(0, (chunk, BLOCK)) + r).astype(F32) == wanted, 1.0, 0.0
                )
                hot[s, r : r + chunk, :] = mark.astype(BF16)
                sum_count[r : r + chunk, :] += mark[:, :LANES] + mark[:, LANES:]

        for s in subs:
            high, mid, low = near_pieces[s]
            near_rhs = stacked(
                high, mid, low, high, mid, high, jnp.zeros((80, BLOCK), F32)
            ).astype(BF16)
            act_one[s] = mm(lhs_one[...], stacked(hot[s], hot[s], near_rhs))
        for s in subs:
            for r in range(0, 256, chunk):
                pre = act_one[s, r : r + chunk, :]
                value, slope, curve = silu_parts(pre)
                if r + chunk == 256:
                    inside = rows_of_lanes(0, (chunk, BLOCK)) + r < MIDDLE
                    value = jnp.where(inside, value, pre)
                    slope = jnp.where(inside, slope, 0.0)
                    curve = jnp.where(inside, curve, 0.0)
                high, low = halves(value)
                hid_hi[s, r : r + chunk, :] = high
                hid_lo[s, r : r + chunk, :] = low
                slope_one[s, r : r + chunk, :] = slope
                curve_one[s, r : r + chunk, :] = curve

        for s in subs:
            act_two[s] = mm(
                lhs_two[...], stacked(hid_hi[s], hid_lo[s], hid_hi[s], hot[s], hot[s])
            )
        summed = []
        for s in subs:
            total = jnp.zeros((8, BLOCK), F32)
            for r in range(0, HID, chunk):
                value, slope, curve = silu_parts(act_two[s, r : r + chunk, :])
                head = beside(head_w[r : r + chunk, :], head_w[r : r + chunk, :])
                weighed = head * value
                for k in range(0, chunk, 8):
                    total = total + weighed[k : k + 8, :]
                high, low = halves(head * slope)
                gate_hi[s, r : r + chunk, :] = high
                gate_lo[s, r : r + chunk, :] = low
                act_two[s, r : r + chunk, :] = value
                slope_two[s, r : r + chunk, :] = slope
                curve_two[s, r : r + chunk, :] = curve
            summed.append(jnp.sum(total, axis=0, keepdims=True))

        for s in subs:
            back_one[s] = mm(lhs_back[...], stacked(gate_hi[s], gate_lo[s], gate_hi[s]))
        leads = []
        for s in subs:
            totals = [jnp.zeros((8, BLOCK), F32) for _ in range(3)]
            for r in range(0, 256, chunk):
                grad = back_one[s, r : r + chunk, :] * slope_one[s, r : r + chunk, :]
                high, low = halves(grad)
                near_hi[s, r : r + chunk, :] = high
                near_lo[s, r : r + chunk, :] = low
                for i in range(3):
                    col = coord_w[r : r + chunk, i * LANES : (i + 1) * LANES]
                    weighed = beside(col, col) * grad
                    for k in range(0, chunk, 8):
                        totals[i] = totals[i] + weighed[k : k + 8, :]
            leads.append(
                [
                    jnp.sum(totals[i], axis=0, keepdims=True)
                    + back_one[s, MIDDLE + i : MIDDLE + i + 1, :]
                    for i in range(3)
                ]
            )

        bars, pulls = [], []
        for s in subs:
            predicted = jnp.tanh(summed[s] + head_bias)
            flank = 1.0 - predicted * predicted
            slope = [flank * q for q in leads[s]]
            excess = slope[0] * slope[0] + slope[1] * slope[1] + slope[2] * slope[2] - 1.0
            capped = jnp.tanh(predicted / DELTA)
            misfit = DELTA * capped - DELTA * jnp.tanh(target[s] / DELTA)
            fitting = jnp.sqrt(misfit * misfit + SMOOTH * SMOOTH)
            loss = fitting + EIK_WEIGHT * excess * excess
            sum_loss[0:1, :] += valid[s] * loss
            share = valid[s] * (1.0 / ALL_POINTS)
            pull = [(4.0 * EIK_WEIGHT) * excess * v for v in slope]
            by_flank = sum(p * q for p, q in zip(pull, leads[s]))
            by_predicted = misfit / fitting * (1.0 - capped * capped) - 2.0 * predicted * by_flank
            bars.append(share * by_predicted * flank)
            sum_loss[1:2, :] += bars[s]
            pulls.append([share * flank * p for p in pull])

        for s in subs:
            last = stacked(blank5, *pulls[s])
            for r in range(0, 256, chunk):
                grad = 0.0
                for i in range(3):
                    col = coord_w[r : r + chunk, i * LANES : (i + 1) * LANES]
                    grad = grad + beside(col, col) * pulls[s][i]
                through = grad * slope_one[s, r : r + chunk, :]
                if r + chunk == 256:
                    inside = rows_of_lanes(0, (8, BLOCK)) < MIDDLE - 248
                    through = stacked(
                        through[: chunk - 8], jnp.where(inside, through[chunk - 8 :], last)
                    )
                high, low = halves(through)
                tang_hi[s, r : r + chunk, :] = high
                tang_lo[s, r : r + chunk, :] = low
                curve_one[s, r : r + chunk, :] = (
                    grad * back_one[s, r : r + chunk, :] * curve_one[s, r : r + chunk, :]
                )
        tangents = []
        for s in subs:
            tangents.append(
                mm(lhs_two[:, 0:768], stacked(tang_hi[s], tang_lo[s], tang_hi[s]))
            )
        for s in subs:
            for r in range(0, HID, chunk):
                tangent = tangents[s][r : r + chunk, :]
                slope = slope_two[s, r : r + chunk, :]
                head = beside(head_w[r : r + chunk, :], head_w[r : r + chunk, :])
                bar = head * (bars[s] * slope + tangent * curve_two[s, r : r + chunk, :])
                by_head = act_two[s, r : r + chunk, :] * bars[s] + slope * tangent
                sum_head[r : r + chunk, :] += by_head[:, :LANES] + by_head[:, LANES:]
                high, low = halves(bar)
                bar_hi[s, r : r + chunk, :] = high
                bar_lo[s, r : r + chunk, :] = low

        for s in subs:
            back_one[s] = mm(lhs_back[...], stacked(bar_hi[s], bar_lo[s], bar_hi[s]))
        left, right = [], []
        for s in subs:
            left += [bar_hi[s], bar_hi[s], bar_lo[s], gate_hi[s], gate_hi[s], gate_lo[s]]
            right += [hid_hi[s], hid_lo[s], hid_hi[s], tang_hi[s], tang_lo[s], tang_hi[s]]
        sum_two[...] += mm_nt(beside(*left), beside(*right))
        hots = beside(*[hot[s // 2] for s in range(2 * SUBS)])
        bars = beside(*[(bar_hi, bar_lo)[s % 2][s // 2] for s in range(2 * SUBS)])
        sum_codes[256:768, :] += mm_nt(bars, hots)

        for s in subs:
            for r in range(0, 256, chunk):
                bar = (
                    back_one[s, r : r + chunk, :] * slope_one[s, r : r + chunk, :]
                    + curve_one[s, r : r + chunk, :]
                )
                high, low = halves(bar)
                low_hi[s, r : r + chunk, :] = high
                low_lo[s, r : r + chunk, :] = low
        bars = beside(*[(low_hi, low_lo)[s % 2][s // 2] for s in range(2 * SUBS)])
        sum_codes[0:256, :] += mm_nt(bars, hots)
        left, right = [], []
        for s in subs:
            seen = stacked(near_pieces[s][0], near_pieces[s][1]).astype(BF16)
            pulled = stacked(*pulls[s], blank5)
            high = pulled.astype(BF16).astype(F32)
            pulled = stacked(high, pulled - high).astype(BF16)
            left += [seen, seen, pulled, pulled]
            right += [low_hi[s], low_lo[s], near_hi[s], near_lo[s]]
        sum_coord[...] += mm_nt(beside(*left), beside(*right))
        return carry

    lax.fori_loop(0, SLOTS * DEVICES // (SUBS * BLOCK), step_body, 0)

    codes = codes_ref[...]
    count = jnp.sum(sum_count[...], axis=1, keepdims=True)
    by_code = sum_codes[...]
    turned_hi, turned_lo = halves(by_code.T)
    weight_hi, weight_lo = halves(latent_w[...])
    code_grad = mm(
        beside(turned_hi, turned_hi, turned_lo), stacked(weight_hi, weight_lo, weight_hi)
    )
    code_grad = code_grad + (2.0 * CODE_WEIGHT / ALL_POINTS) * count * codes
    code_grad_ref[...] = code_grad
    code_squares = total_of(code_grad * code_grad)
    loss = jnp.sum(sum_loss[0:1, :], axis=1, keepdims=True)
    loss = loss + CODE_WEIGHT * total_of(count * codes * codes)
    loss = loss / ALL_POINTS

    code_hi, code_lo = halves(codes)
    by_hi, by_lo = halves(by_code)
    latent_grad = mm(beside(by_hi, by_hi, by_lo), stacked(code_hi, code_lo, code_hi))
    bias_grad = jnp.sum(by_code, axis=1, keepdims=True)

    near_grad = sum_coord[0:8, :] + sum_coord[8:16, :]
    near_grad = stacked(near_grad, jnp.zeros((LANES - 8, 256), F32)).T
    near_grad = jnp.where(lane < 3, near_grad, 0.0)
    low_grad = latent_grad[0:256, :]
    first_low = first_w[:, : 2 * LANES]
    first_near = jnp.where(lane < 3, first_w[:, 2 * LANES :], 0.0)
    along = jnp.sum(first_low * low_grad, axis=1, keepdims=True)
    along = along + jnp.sum(first_near * near_grad, axis=1, keepdims=True)
    inward = first_scale * first_root * first_root * along
    end = first_scale * near_grad - first_near * inward
    end = jnp.where(lane == 3, first_root * along, end)
    end = jnp.where(lane == 4, bias_grad[0:256, :], end)
    low_grad = first_scale * low_grad - first_low * inward
    first_w[:, : 2 * LANES] = jnp.where(beside(real, real), low_grad, 0.0)
    first_w[:, 2 * LANES :] = jnp.where(real, end, 0.0)

    hidden_grad = sum_two[...]
    moved = pltpu.roll(latent_grad[256:768, :], 256 - 3, 1)
    grad_a = jnp.where(is_hidden, hidden_grad, moved)
    grad_b = jnp.where(is_hidden, moved, hidden_grad)
    second_a = second_w[:, 0:256]
    second_b = second_w[:, 256:512]
    along = jnp.sum(second_a * grad_a + second_b * grad_b, axis=1, keepdims=True)
    inward = second_scale * second_root * second_root * along
    second_w[:, 0:256] = second_scale * grad_a - second_a * inward
    second_w[:, 256:512] = second_scale * grad_b - second_b * inward
    head_grad = jnp.sum(sum_head[...], axis=1, keepdims=True)
    lane = rows_of_lanes(1, (HID, LANES))
    end = jnp.where(lane == 0, second_root * along, 0.0)
    end = jnp.where(lane == 1, bias_grad[256:768, :], end)
    second_w[:, 512:640] = jnp.where(lane == 2, head_grad, end)

    flat[...] = jnp.zeros(flat.shape, F32)
    for adding in (False, True):
        pack_units(first_w, flat, *FIRST_UNITS, adding)
        pack_units(second_w, flat, *SECOND_UNITS, adding)
    row = HEAD_ENTRY // LANES
    lane = rows_of_lanes(1, (1, LANES))
    bias_total = jnp.sum(sum_loss[1:2, :], axis=1, keepdims=True)
    flat[row : row + 1, :] = flat[row : row + 1, :] + jnp.where(
        lane == HEAD_ENTRY % LANES, bias_total, 0.0
    )
    sub = rows_of_lanes(0, (8, LANES))
    wide = rows_of_lanes(1, (8, LANES))
    info = jnp.where((sub == 5) & (wide == 0), loss, 0.0)
    info = jnp.where((sub == 5) & (wide == 1), code_squares, info)
    for which in range(2):

        @pl.when(core == which)
        def _(which=which):
            for d in range(DEVICES):
                z, c, w = d // 32, d // 16 % 2, d % 16
                target = keep_ref if c == which else give_ref
                box = (z * 16 + w) * BOX_ROWS
                first = d * SHARD_ROWS
                target[box : box + 16, :] = flat[first : first + 16, :]
                target[box + 16 : box + 24, :] = jnp.where(
                    sub < 5, flat[first + 16 : first + 24, :], info
                )


def vmem(count):
    return [pl.BlockSpec(memory_space=pltpu.VMEM)] * count


PARAMS = pltpu.CompilerParams(vmem_limit_bytes=48 * 1024 * 1024)


HBM = pl.BlockSpec(memory_space=pltpu.HBM)


def pack_boxes(weights, coords, distances, index):
    return pl.pallas_call(
        pack_kernel,
        out_shape=jax.ShapeDtypeStruct((PEERS * BOX_ROWS, LANES), F32),
        in_specs=[HBM] * 4,
        out_specs=vmem(1)[0],
        scratch_shapes=[
            pltpu.VMEM(weights.shape, F32),
            pltpu.VMEM(coords.shape, F32),
            pltpu.VMEM(distances.shape, F32),
            pltpu.VMEM(index.shape, jnp.int32),
            pltpu.SemaphoreType.DMA((4,)),
        ],
        compiler_params=PARAMS,
    )(weights, coords, distances, index)


def main_call(core, mine, other, codes):
    pair = (SUBS, 256, BLOCK)
    pair_two = (SUBS, HID, BLOCK)
    scratch = [
        ((FLAT_ROWS + 8, LANES), F32),
        ((256, 3 * LANES), F32),
        ((HID, 5 * LANES), F32),
        ((256, 640), BF16),
        ((HID, 1280), BF16),
        ((256, 1536), BF16),
        ((768, 256), F32),
        ((256, 3 * LANES), F32),
        ((HID, LANES), F32),
        ((LANES, LANES), F32),
        ((HID, 256), F32),
        ((768, 256), F32),
        ((16, 256), F32),
        ((HID, LANES), F32),
        ((CODE_ROWS, LANES), F32),
        ((2, BLOCK), F32),
        (pair, F32),
        (pair, F32),
        (pair, F32),
        (pair, F32),
        (pair, BF16),
        (pair, BF16),
        (pair, BF16),
        (pair_two, F32),
        (pair_two, F32),
        (pair_two, F32),
        (pair_two, BF16),
        (pair_two, BF16),
        (pair, BF16),
        (pair, BF16),
        (pair, BF16),
        (pair, BF16),
        (pair_two, BF16),
        (pair_two, BF16),
        (pair, BF16),
        (pair, BF16),
    ]
    return pl.pallas_call(
        main_kernel,
        out_shape=(
            jax.ShapeDtypeStruct((PEERS * BOX_ROWS, LANES), F32),
            jax.ShapeDtypeStruct((PEERS * BOX_ROWS, LANES), F32),
            jax.ShapeDtypeStruct((CODE_ROWS, LATENT), F32),
        ),
        in_specs=[pl.BlockSpec(memory_space=pltpu.SMEM)] + vmem(3),
        out_specs=tuple(vmem(3)),
        scratch_shapes=[pltpu.VMEM(shape, dtype) for shape, dtype in scratch],
        compiler_params=PARAMS,
    )(core, mine, other, codes)


def adam_update(value, first, second, grad, rate):
    first_new = BETA_ONE * first + (1.0 - BETA_ONE) * grad
    second_new = BETA_TWO * second + (1.0 - BETA_TWO) * grad * grad
    first_hat = first_new / (1.0 - BETA_ONE**STEP)
    second_hat = second_new / (1.0 - BETA_TWO**STEP)
    value_new = value - rate * (first_hat / (jnp.sqrt(second_hat) + ADAM_EPS) + DECAY * value)
    return (value_new, first_new, second_new)


def shard_kernel(parts_ref, shard_ref, squares_ref):
    total = parts_ref[0:BOX_ROWS, :]
    for peer in range(1, PEERS):
        total = total + parts_ref[peer * BOX_ROWS : (peer + 1) * BOX_ROWS, :]
    shard_ref[...] = total
    grad = total[:SHARD_ROWS, :]
    squares_ref[...] = jnp.broadcast_to(total_of(grad * grad), squares_ref.shape)


def sum_shards(parts):
    return pl.pallas_call(
        shard_kernel,
        out_shape=(
            jax.ShapeDtypeStruct((BOX_ROWS, LANES), F32),
            jax.ShapeDtypeStruct((8, LANES), F32),
        ),
        in_specs=vmem(1),
        out_specs=tuple(vmem(2)),
        compiler_params=PARAMS,
    )(parts)


def update_kernel(
    seen_ref,
    shard_ref,
    weights_ref,
    moment_one_ref,
    moment_two_ref,
    codes_ref,
    code_first_ref,
    code_second_ref,
    code_grad_ref,
    loss_out,
    norm_out,
    weights_out,
    moment_one_out,
    moment_two_out,
    weights_copy_out,
    codes_out,
    code_first_out,
    code_second_out,
    codes_copy_out,
):
    total = seen_ref[0:8, :]
    for peer in range(1, PEERS):
        total = total + seen_ref[peer * 8 : peer * 8 + 8, :]
    loss_out[...] = shard_ref[SHARD_ROWS : SHARD_ROWS + 1, 0:1]
    norm = jnp.sqrt(total[0:1, 0:1] + shard_ref[SHARD_ROWS : SHARD_ROWS + 1, 1:2])
    norm_out[...] = norm
    factor = jnp.minimum(1.0, CLIP / (norm + 1e-06))
    value, first, second = adam_update(
        weights_ref[...],
        moment_one_ref[...],
        moment_two_ref[...],
        factor * shard_ref[0:SHARD_ROWS, :],
        WEIGHT_RATE,
    )
    weights_out[...] = value
    moment_one_out[...] = first
    moment_two_out[...] = second
    weights_copy_out[...] = value.astype(BF16)
    for r in range(0, CODE_ROWS, 32):
        rows = slice(r, r + 32)
        value, first, second = adam_update(
            codes_ref[rows, :],
            code_first_ref[rows, :],
            code_second_ref[rows, :],
            factor * code_grad_ref[rows, :],
            CODE_RATE,
        )
        codes_out[rows, :] = value
        code_first_out[rows, :] = first
        code_second_out[rows, :] = second
        codes_copy_out[rows, :] = value.astype(BF16)


def update_all(*args):
    scalar = jax.ShapeDtypeStruct((1, 1), F32)
    shard = [jax.ShapeDtypeStruct((SHARD_ROWS, LANES), t) for t in (F32, F32, F32, BF16)]
    table = [jax.ShapeDtypeStruct((CODE_ROWS, LATENT), t) for t in (F32, F32, F32, BF16)]
    return pl.pallas_call(
        update_kernel,
        out_shape=(scalar, scalar, *shard, *table),
        in_specs=vmem(9),
        out_specs=tuple(vmem(10)),
        compiler_params=PARAMS,
    )(*args)


def swap_cores(v):
    return lax.ppermute(v, "core", [(0, 1), (1, 0)])


def exchange(v):
    return lax.all_to_all(v, ("z", "wide"), split_axis=0, concat_axis=0)


def body(
    weights_flat,
    moment_one,
    moment_two,
    codes,
    code_first,
    code_second,
    coords,
    distances,
    shape_index,
):
    boxes = pack_boxes(
        weights_flat.reshape(SHARD_ROWS, LANES),
        coords,
        distances.reshape(1, POINTS_DEV),
        shape_index.reshape(1, POINTS_DEV),
    )
    mine = exchange(boxes.reshape(PEERS, BOX_ROWS, LANES))
    other = swap_cores(mine)
    core = lax.axis_index("core").astype(jnp.int32).reshape(1)
    keep, give, code_grad = main_call(
        core,
        mine.reshape(PEERS * BOX_ROWS, LANES),
        other.reshape(PEERS * BOX_ROWS, LANES),
        codes,
    )
    pair_sum = (keep + swap_cores(give)).reshape(PEERS, BOX_ROWS, LANES)
    shard, squares = sum_shards(exchange(pair_sum).reshape(PEERS * BOX_ROWS, LANES))
    squares = squares + swap_cores(squares)
    seen = exchange(jnp.broadcast_to(squares, (PEERS, 8, LANES)))
    flat = lambda v: v.reshape(SHARD_ROWS, LANES)
    out = update_all(
        seen.reshape(PEERS * 8, LANES),
        shard,
        flat(weights_flat),
        flat(moment_one),
        flat(moment_two),
        codes,
        code_first,
        code_second,
        code_grad,
    )
    return (
        out[0].reshape(()),
        out[1].reshape(()),
        *[v.reshape(weights_flat.shape) for v in out[2:6]],
        *out[6:],
    )


def solution(mesh):
    parts = Mesh(mesh.devices.reshape(4, 2, 16), ALL)
    return jax.shard_map(
        body,
        mesh=parts,
        in_specs=(
            P(ALL),
            P(ALL),
            P(ALL),
            P(ALL, None),
            P(ALL, None),
            P(ALL, None),
            P(None, ALL),
            P(ALL),
            P(ALL),
        ),
        out_specs=(
            P(),
            P(),
            P(ALL),
            P(ALL),
            P(ALL),
            P(ALL),
            P(ALL, None),
            P(ALL, None),
            P(ALL, None),
            P(ALL, None),
        ),
        check_vma=False,
    )
```

```python
import jax
import jax.numpy as jnp
from jax import lax
from jax.experimental import pallas as pl
from jax.experimental.pallas import tpu as pltpu
from jax.sharding import Mesh
from jax.sharding import PartitionSpec as P

LATENT = 256
HID = 512
MIDDLE = HID - LATENT - 3
STEP = 10

DELTA = 0.1
SMOOTH = 0.01
CODE_WEIGHT = 0.001
EIK_WEIGHT = 0.1
CLIP = 0.001
WEIGHT_RATE = 0.02
CODE_RATE = 0.15
BETA_ONE = 0.9
BETA_TWO = 0.999
ADAM_EPS = 1e-08
DECAY = 0.01

LANES = 128
DEVICES = 128
PEERS = 64
SHARD_ROWS = 21
BOX_ROWS = 24
SLOTS = 16
POINTS_DEV = 1024
CODE_ROWS = 256
FLAT_ROWS = DEVICES * SHARD_ROWS
BLOCK = 512
SUBS = 2
TILES = BLOCK // LANES
ALL_POINTS = POINTS_DEV * DEVICES

F32 = jnp.float32
BF16 = jnp.bfloat16
ALL = ("z", "core", "wide")


def rows_of_lanes(lead, shape):
    return lax.broadcasted_iota(jnp.int32, shape, lead)


def halves(v):
    high = v.astype(BF16)
    return high, (v - high.astype(F32)).astype(BF16)


def thirds(v):
    high = v.astype(BF16).astype(F32)
    rest = v - high
    mid = rest.astype(BF16).astype(F32)
    return high, mid, rest - mid


def mm(a, b):
    return lax.dot_general(a, b, (((1,), (0,)), ((), ())), preferred_element_type=F32)


def mm_nt(a, b):
    return lax.dot_general(a, b, (((1,), (1,)), ((), ())), preferred_element_type=F32)


def beside(*parts):
    return jnp.concatenate(parts, axis=1)


def total_of(v):
    return jnp.sum(jnp.sum(v, axis=0, keepdims=True), axis=1, keepdims=True)


def stacked(*parts):
    return jnp.concatenate(parts, axis=0)


def pack_kernel(
    weights_hbm,
    coords_hbm,
    distances_hbm,
    index_hbm,
    out_ref,
    weights_ref,
    coords_ref,
    distances_ref,
    index_ref,
    sems,
):
    pairs = [
        (index_hbm, index_ref),
        (weights_hbm, weights_ref),
        (coords_hbm, coords_ref),
        (distances_hbm, distances_ref),
    ]
    copies = [
        pltpu.make_async_copy(source, target, sems.at[i])
        for i, (source, target) in enumerate(pairs)
    ]
    for copy in copies:
        copy.start()
    for copy in copies:
        copy.wait()
    shard = stacked(weights_ref[...], jnp.zeros((BOX_ROWS - SHARD_ROWS, LANES), F32))
    for peer in range(PEERS):
        out_ref[peer * BOX_ROWS : (peer + 1) * BOX_ROWS, :] = shard
    index = index_ref[...]
    owner = lax.shift_right_logical(index, 8)
    row = lax.bitwise_and(index, CODE_ROWS - 1)
    sent = (rows_of_lanes(0, (DEVICES, POINTS_DEV)) == owner).astype(F32)
    sent_low = sent.astype(BF16)
    width = 256
    earlier = rows_of_lanes(0, (width, width)) < rows_of_lanes(1, (width, width))
    earlier = earlier.astype(F32).astype(BF16)
    ones = jnp.ones((width, width), BF16)
    ranks = [
        mm(sent_low[:, : (part + 1) * width], stacked(*([ones] * part + [earlier])))
        for part in range(POINTS_DEV // width)
    ]
    placed = jnp.sum(sent * beside(*ranks), axis=0, keepdims=True).astype(jnp.int32)
    at_slot = rows_of_lanes(0, (SLOTS, POINTS_DEV)) == placed
    values = [coords_ref[i : i + 1, :] for i in range(3)]
    values += [distances_ref[...], (row + 1).astype(F32)]
    pieces = [[], [], []]
    for value in values:
        for k, third in enumerate(thirds(value)):
            pieces[k].append(jnp.where(at_slot, third, 0.0))
    spare = jnp.zeros((LANES - SLOTS * len(values), POINTS_DEV), F32)
    boxes = mm_nt(
        beside(sent_low, sent_low, sent_low),
        beside(*[stacked(*piece, spare).astype(BF16) for piece in pieces]),
    )
    for z in range(4):
        for core in range(2):
            first = z * 32 + core * 16
            out_ref[pl.ds(z * 16 * BOX_ROWS + SHARD_ROWS + core, 16, stride=BOX_ROWS), :] = boxes[
                first : first + 16, :
            ]


def unit_groups(count, stride_rows, extra, first_entry):
    for group in range(count):
        entry = first_entry + group * 8 * (stride_rows * LANES + extra)
        yield group, entry // LANES, entry % LANES


def unpack_units(flat_ref, out_ref, count, stride_rows, extra, first_entry):
    lane = rows_of_lanes(1, (8, LANES))
    slope = rows_of_lanes(0, (8, LANES)) * extra
    for group, first, shift in unit_groups(count, stride_rows, extra, first_entry):
        start = slope + shift
        wraps = shift + 7 * extra >= LANES
        turn = lax.bitwise_and(lane + start, LANES - 1)
        tiles = []
        for a in range(stride_rows + 2 + wraps):
            tile = flat_ref[pl.ds(first + a, 8, stride=stride_rows), :]
            tiles.append(jnp.take_along_axis(tile, turn, axis=1, mode="promise_in_bounds"))
        for c in range(stride_rows + 1):
            value = jnp.where(lane + start < LANES, tiles[c], tiles[c + 1])
            if wraps:
                value = jnp.where(lane + start < 2 * LANES, value, tiles[c + 2])
            out_ref[group * 8 : group * 8 + 8, c * LANES : (c + 1) * LANES] = value


def pack_units(value_ref, flat_ref, count, stride_rows, extra, first_entry, adding):
    lane = rows_of_lanes(1, (8, LANES))
    slope = rows_of_lanes(0, (8, LANES)) * extra
    zero = jnp.zeros((8, LANES), F32)
    for group, first, shift in unit_groups(count, stride_rows, extra, first_entry):
        start = slope + shift
        wraps = shift + 7 * extra >= LANES
        wanted = range(stride_rows, stride_rows + 1 + wraps + 1) if adding else range(stride_rows)
        rolled = {}

        turn = lax.bitwise_and(lane - start, LANES - 1)

        def tile(c, rolled=rolled, group=group, turn=turn):
            if c < 0 or c > stride_rows:
                return zero
            if c not in rolled:
                value = value_ref[group * 8 : group * 8 + 8, c * LANES : (c + 1) * LANES]
                rolled[c] = jnp.take_along_axis(value, turn, axis=1, mode="promise_in_bounds")
            return rolled[c]

        for a in wanted:
            value = jnp.where(lane >= start, tile(a), tile(a - 1))
            if wraps:
                value = jnp.where(lane >= start - LANES, value, tile(a - 2))
            rows = pl.ds(first + a, 8, stride=stride_rows)
            if adding:
                flat_ref[rows, :] = flat_ref[rows, :] + value
            else:
                flat_ref[rows, :] = value


FIRST_UNITS = (32, 2, 5, 0)
SECOND_UNITS = (64, 4, 3, MIDDLE * (LATENT + 5))
HEAD_ENTRY = MIDDLE * (LATENT + 5) + HID * (HID + 3)


def across(column):
    return beside(*[column] * TILES)


def folded(v):
    return sum(v[:, i * LANES : (i + 1) * LANES] for i in range(TILES))


def silu_parts(half):
    gate = jnp.tanh(half)
    low = 0.5 * gate
    bend = 0.5 - gate * low
    bent = half * gate
    return half + bent, (0.5 + low) + half * bend, bend * (1.0 - bent)


def silu_parts_twice(half):
    gate = jnp.tanh(half)
    bend = 1.0 - gate * gate
    bent = half * gate
    return half + bent, (1.0 + gate) + half * bend, bend * (1.0 - bent)


def main_kernel(
    core_ref,
    mine_ref,
    other_ref,
    codes_ref,
    keep_ref,
    give_ref,
    code_grad_ref,
    flat,
    first_w,
    second_w,
    lhs_one,
    lhs_two,
    lhs_back,
    latent_w,
    coord_w,
    head_w,
    spots,
    sum_two,
    sum_codes,
    sum_coord,
    sum_head,
    sum_count,
    sum_loss,
    act_one,
    slope_one,
    curve_one,
    back_one,
    hid_hi,
    hid_lo,
    hot,
    act_two,
    slope_two,
    curve_two,
    gate_hi,
    gate_lo,
    tang_hi,
    tang_lo,
    near_hi,
    near_lo,
    bar_hi,
    bar_lo,
    low_hi,
    low_lo,
):
    core = core_ref[0]

    for which in range(2):

        @pl.when(core == which)
        def _(which=which):
            for d in range(DEVICES):
                z, c, w = d // 32, d // 16 % 2, d % 16
                box = (z * 16 + w) * BOX_ROWS
                source = mine_ref if c == which else other_ref
                flat[d * SHARD_ROWS : d * SHARD_ROWS + BOX_ROWS, :] = source[box : box + BOX_ROWS, :]
            rows = pl.ds(SHARD_ROWS + which, PEERS, stride=BOX_ROWS)
            spots[...] = stacked(mine_ref[rows, :], other_ref[rows, :]).T

    unpack_units(flat, first_w, *FIRST_UNITS)
    unpack_units(flat, second_w, *SECOND_UNITS)
    head_bias = flat[HEAD_ENTRY // LANES : HEAD_ENTRY // LANES + 1, :][
        :, HEAD_ENTRY % LANES : HEAD_ENTRY % LANES + 1
    ]

    lane = rows_of_lanes(1, (256, LANES))
    unit = rows_of_lanes(0, (256, LANES))
    real = unit < MIDDLE

    first_low = jnp.where(beside(real, real), first_w[:, : 2 * LANES], 0.0)
    first_end = jnp.where(real, first_w[:, 2 * LANES :], 0.0)
    first_near = jnp.where(lane < 3, first_end, 0.0)
    first_gain = first_end[:, 3:4]
    first_bias = first_end[:, 4:5]
    first_w[:, : 2 * LANES] = first_low
    first_w[:, 2 * LANES :] = first_end
    first_root = lax.rsqrt(
        jnp.sum(first_low * first_low, axis=1, keepdims=True)
        + jnp.sum(first_near * first_near, axis=1, keepdims=True)
        + 1e-12
    )
    first_scale = first_gain * first_root
    first_low = first_low * first_scale
    first_near = first_near * first_scale
    latent_w[0:256, :] = first_low
    for i in range(3):
        coord_w[:, i * LANES : (i + 1) * LANES] = jnp.broadcast_to(
            first_near[:, i : i + 1], (256, LANES)
        )

    second_a = second_w[:, 0:256]
    second_b = second_w[:, 256:512]
    second_gain = second_w[:, 512:513]
    second_bias = second_w[:, 513:514]
    head = jnp.broadcast_to(second_w[:, 514:515], (HID, LANES))
    head_w[:, :LANES] = 0.5 * head
    head_w[:, LANES:] = head
    second_root = lax.rsqrt(
        jnp.sum(second_a * second_a + second_b * second_b, axis=1, keepdims=True) + 1e-12
    )
    second_scale = second_gain * second_root
    second_a = second_a * second_scale
    second_b = second_b * second_scale
    is_hidden = rows_of_lanes(1, (HID, 256)) < MIDDLE
    hidden_cols = jnp.where(is_hidden, second_a, second_b)
    latent_cols = pltpu.roll(jnp.where(is_hidden, second_b, second_a), 3, 1)
    latent_w[256:768, :] = latent_cols

    hidden_hi, hidden_lo = halves(0.5 * hidden_cols)
    lhs_two[:, 0:256] = hidden_hi
    lhs_two[:, 256:512] = hidden_hi
    lhs_two[:, 512:768] = hidden_lo
    back_hi, back_lo = halves(hidden_cols.T)
    lhs_back[:, 0:512] = back_hi
    lhs_back[:, 512:1024] = back_hi
    lhs_back[:, 1024:1536] = back_lo

    code_hi, code_lo = halves(codes_ref[...])
    weight_hi, weight_lo = halves(latent_w[...])
    by_code = mm_nt(
        beside(weight_hi, weight_hi, weight_lo), beside(code_hi, code_lo, code_hi)
    )
    one_hi, one_lo = halves(0.5 * (by_code[0:256, :] + first_bias))
    lhs_one[:, 0:256] = one_hi
    lhs_one[:, 256:512] = one_lo
    two_hi, two_lo = halves(0.5 * (by_code[256:768, :] + second_bias))
    lhs_two[:, 768:1024] = two_hi
    lhs_two[:, 1024:1280] = two_lo
    spread = jnp.where((unit - MIDDLE == lane) & (lane < 3), 1.0, first_near)
    near_parts = thirds(0.5 * spread)
    near_lhs = near_parts[0]
    for place, k in enumerate((0, 0, 1, 1, 2)):
        near_lhs = near_lhs + pltpu.roll(near_parts[k], 8 * (place + 1), 1)
    lhs_one[:, 512:640] = near_lhs.astype(BF16)

    for ref in (sum_two, sum_codes, sum_coord, sum_head, sum_count, sum_loss):
        ref[...] = jnp.zeros(ref.shape, F32)

    def feature(which, step, sub):
        first = which * SLOTS + (step * SUBS + sub) * TILES
        return beside(*[spots[pl.ds(first + i, 1), :] for i in range(TILES)])

    blank5 = jnp.zeros((5, BLOCK), F32)
    subs = range(SUBS)
    chunk = 8192 // BLOCK

    def step_body(step, carry):
        place = [[feature(i, step, s) for i in range(3)] for s in subs]
        target = [feature(3, step, s) for s in subs]
        code_row = [feature(4, step, s) for s in subs]
        valid = [(code_row[s] > 0.5).astype(F32) for s in subs]
        near8 = [stacked(*place[s], blank5) for s in subs]
        near_pieces = [thirds(near8[s]) for s in subs]

        for s in subs:
            wanted = code_row[s] - 1.0
            for r in range(0, CODE_ROWS, chunk):
                mark = jnp.where(
                    (rows_of_lanes(0, (chunk, BLOCK)) + r).astype(F32) == wanted, 1.0, 0.0
                )
                hot[s, r : r + chunk, :] = mark.astype(BF16)
                sum_count[r : r + chunk, :] += folded(mark)

        for s in subs:
            high, mid, low = near_pieces[s]
            near_rhs = stacked(
                high, mid, low, high, mid, high, jnp.zeros((80, BLOCK), F32)
            ).astype(BF16)
            act_one[s] = mm(lhs_one[...], stacked(hot[s], hot[s], near_rhs))
        for s in subs:
            for r in range(0, 256, chunk):
                pre = act_one[s, r : r + chunk, :]
                value, slope, curve = silu_parts(pre)
                if r + chunk == 256:
                    inside = rows_of_lanes(0, (chunk, BLOCK)) + r < MIDDLE
                    value = jnp.where(inside, value, pre + pre)
                    slope = jnp.where(inside, slope, 0.0)
                    curve = jnp.where(inside, curve, 0.0)
                high, low = halves(value)
                hid_hi[s, r : r + chunk, :] = high
                hid_lo[s, r : r + chunk, :] = low
                slope_one[s, r : r + chunk, :] = slope
                curve_one[s, r : r + chunk, :] = curve

        for s in subs:
            act_two[s] = mm(
                lhs_two[...], stacked(hid_hi[s], hid_lo[s], hid_hi[s], hot[s], hot[s])
            )
        summed = []
        for s in subs:
            total = jnp.zeros((8, BLOCK), F32)
            for r in range(0, HID, chunk):
                value, slope, curve = silu_parts_twice(act_two[s, r : r + chunk, :])
                head = across(head_w[r : r + chunk, :LANES])
                weighed = head * value
                for k in range(0, chunk, 8):
                    total = total + weighed[k : k + 8, :]
                high, low = halves(head * slope)
                gate_hi[s, r : r + chunk, :] = high
                gate_lo[s, r : r + chunk, :] = low
                act_two[s, r : r + chunk, :] = value
                slope_two[s, r : r + chunk, :] = slope
                curve_two[s, r : r + chunk, :] = curve
            summed.append(jnp.sum(total, axis=0, keepdims=True))

        for s in subs:
            back_one[s] = mm(lhs_back[...], stacked(gate_hi[s], gate_lo[s], gate_hi[s]))
        leads = []
        for s in subs:
            totals = [jnp.zeros((8, BLOCK), F32) for _ in range(3)]
            for r in range(0, 256, chunk):
                grad = back_one[s, r : r + chunk, :] * slope_one[s, r : r + chunk, :]
                high, low = halves(grad)
                near_hi[s, r : r + chunk, :] = high
                near_lo[s, r : r + chunk, :] = low
                for i in range(3):
                    col = coord_w[r : r + chunk, i * LANES : (i + 1) * LANES]
                    weighed = across(col) * grad
                    for k in range(0, chunk, 8):
                        totals[i] = totals[i] + weighed[k : k + 8, :]
            leads.append(
                [
                    jnp.sum(totals[i], axis=0, keepdims=True)
                    + back_one[s, MIDDLE + i : MIDDLE + i + 1, :]
                    for i in range(3)
                ]
            )

        bars, pulls = [], []
        for s in subs:
            predicted = jnp.tanh(2.0 * summed[s] + head_bias)
            flank = 1.0 - predicted * predicted
            slope = [flank * q for q in leads[s]]
            excess = slope[0] * slope[0] + slope[1] * slope[1] + slope[2] * slope[2] - 1.0
            capped = jnp.tanh(predicted / DELTA)
            misfit = DELTA * capped - DELTA * jnp.tanh(target[s] / DELTA)
            fitting = jnp.sqrt(misfit * misfit + SMOOTH * SMOOTH)
            loss = fitting + EIK_WEIGHT * excess * excess
            sum_loss[0:1, :] += valid[s] * loss
            share = valid[s] * (1.0 / ALL_POINTS)
            pull = [(4.0 * EIK_WEIGHT) * excess * v for v in slope]
            by_flank = sum(p * q for p, q in zip(pull, leads[s]))
            by_predicted = misfit / fitting * (1.0 - capped * capped) - 2.0 * predicted * by_flank
            bars.append(share * by_predicted * flank)
            sum_loss[1:2, :] += bars[s]
            pulls.append([share * flank * p for p in pull])

        half_bars = [0.5 * bar for bar in bars]

        for s in subs:
            last = stacked(blank5, *pulls[s])
            for r in range(0, 256, chunk):
                grad = 0.0
                for i in range(3):
                    col = coord_w[r : r + chunk, i * LANES : (i + 1) * LANES]
                    grad = grad + across(col) * pulls[s][i]
                through = grad * slope_one[s, r : r + chunk, :]
                if r + chunk == 256:
                    inside = rows_of_lanes(0, (8, BLOCK)) < MIDDLE - 248
                    through = stacked(
                        through[: chunk - 8], jnp.where(inside, through[chunk - 8 :], last)
                    )
                high, low = halves(through)
                tang_hi[s, r : r + chunk, :] = high
                tang_lo[s, r : r + chunk, :] = low
                curve_one[s, r : r + chunk, :] = (
                    grad * back_one[s, r : r + chunk, :] * curve_one[s, r : r + chunk, :]
                )
        tangents = []
        for s in subs:
            tangents.append(
                mm(lhs_two[:, 0:768], stacked(tang_hi[s], tang_lo[s], tang_hi[s]))
            )
        for s in subs:
            for r in range(0, HID, chunk):
                tangent = tangents[s][r : r + chunk, :]
                slope = slope_two[s, r : r + chunk, :]
                head = across(head_w[r : r + chunk, LANES:])
                bar = head * (half_bars[s] * slope + tangent * curve_two[s, r : r + chunk, :])
                by_head = act_two[s, r : r + chunk, :] * bars[s] + slope * tangent
                sum_head[r : r + chunk, :] += folded(by_head)
                high, low = halves(bar)
                bar_hi[s, r : r + chunk, :] = high
                bar_lo[s, r : r + chunk, :] = low

        for s in subs:
            back_one[s] = mm(lhs_back[...], stacked(bar_hi[s], bar_lo[s], bar_hi[s]))
        left, right = [], []
        for s in subs:
            left += [bar_hi[s], bar_hi[s], bar_lo[s], gate_hi[s], gate_hi[s], gate_lo[s]]
            right += [hid_hi[s], hid_lo[s], hid_hi[s], tang_hi[s], tang_lo[s], tang_hi[s]]
        sum_two[...] += mm_nt(beside(*left), beside(*right))
        hots = beside(*[hot[s // 2] for s in range(2 * SUBS)])
        bars = beside(*[(bar_hi, bar_lo)[s % 2][s // 2] for s in range(2 * SUBS)])
        sum_codes[256:768, :] += mm_nt(bars, hots)

        for s in subs:
            for r in range(0, 256, chunk):
                bar = (
                    back_one[s, r : r + chunk, :] * slope_one[s, r : r + chunk, :]
                    + curve_one[s, r : r + chunk, :]
                )
                high, low = halves(bar)
                low_hi[s, r : r + chunk, :] = high
                low_lo[s, r : r + chunk, :] = low
        bars = beside(*[(low_hi, low_lo)[s % 2][s // 2] for s in range(2 * SUBS)])
        sum_codes[0:256, :] += mm_nt(bars, hots)
        left, right = [], []
        for s in subs:
            seen = stacked(near_pieces[s][0], near_pieces[s][1]).astype(BF16)
            pulled = stacked(*pulls[s], blank5)
            high = pulled.astype(BF16).astype(F32)
            pulled = stacked(high, pulled - high).astype(BF16)
            left += [seen, seen, pulled, pulled]
            right += [low_hi[s], low_lo[s], near_hi[s], near_lo[s]]
        sum_coord[...] += mm_nt(beside(*left), beside(*right))
        return carry

    lax.fori_loop(0, SLOTS * DEVICES // (SUBS * BLOCK), step_body, 0)

    codes = codes_ref[...]
    count = jnp.sum(sum_count[...], axis=1, keepdims=True)
    by_code = sum_codes[...]
    turned_hi, turned_lo = halves(by_code.T)
    weight_hi, weight_lo = halves(latent_w[...])
    code_grad = mm(
        beside(turned_hi, turned_hi, turned_lo), stacked(weight_hi, weight_lo, weight_hi)
    )
    code_grad = code_grad + (2.0 * CODE_WEIGHT / ALL_POINTS) * count * codes
    code_grad_ref[...] = code_grad
    code_squares = total_of(code_grad * code_grad)
    loss = jnp.sum(sum_loss[0:1, :], axis=1, keepdims=True)
    loss = loss + CODE_WEIGHT * total_of(count * codes * codes)
    loss = loss / ALL_POINTS

    code_hi, code_lo = halves(codes)
    by_hi, by_lo = halves(by_code)
    latent_grad = mm(beside(by_hi, by_hi, by_lo), stacked(code_hi, code_lo, code_hi))
    bias_grad = jnp.sum(by_code, axis=1, keepdims=True)

    near_grad = sum_coord[0:8, :] + sum_coord[8:16, :]
    near_grad = stacked(near_grad, jnp.zeros((LANES - 8, 256), F32)).T
    near_grad = jnp.where(lane < 3, near_grad, 0.0)
    low_grad = latent_grad[0:256, :]
    first_low = first_w[:, : 2 * LANES]
    first_near = jnp.where(lane < 3, first_w[:, 2 * LANES :], 0.0)
    along = jnp.sum(first_low * low_grad, axis=1, keepdims=True)
    along = along + jnp.sum(first_near * near_grad, axis=1, keepdims=True)
    inward = first_scale * first_root * first_root * along
    end = first_scale * near_grad - first_near * inward
    end = jnp.where(lane == 3, first_root * along, end)
    end = jnp.where(lane == 4, bias_grad[0:256, :], end)
    low_grad = first_scale * low_grad - first_low * inward
    first_w[:, : 2 * LANES] = jnp.where(beside(real, real), low_grad, 0.0)
    first_w[:, 2 * LANES :] = jnp.where(real, end, 0.0)

    hidden_grad = sum_two[...]
    moved = pltpu.roll(latent_grad[256:768, :], 256 - 3, 1)
    grad_a = jnp.where(is_hidden, hidden_grad, moved)
    grad_b = jnp.where(is_hidden, moved, hidden_grad)
    second_a = second_w[:, 0:256]
    second_b = second_w[:, 256:512]
    along = jnp.sum(second_a * grad_a + second_b * grad_b, axis=1, keepdims=True)
    inward = second_scale * second_root * second_root * along
    second_w[:, 0:256] = second_scale * grad_a - second_a * inward
    second_w[:, 256:512] = second_scale * grad_b - second_b * inward
    head_grad = jnp.sum(sum_head[...], axis=1, keepdims=True)
    lane = rows_of_lanes(1, (HID, LANES))
    end = jnp.where(lane == 0, second_root * along, 0.0)
    end = jnp.where(lane == 1, bias_grad[256:768, :], end)
    second_w[:, 512:640] = jnp.where(lane == 2, head_grad, end)

    flat[...] = jnp.zeros(flat.shape, F32)
    for adding in (False, True):
        pack_units(first_w, flat, *FIRST_UNITS, adding)
        pack_units(second_w, flat, *SECOND_UNITS, adding)
    row = HEAD_ENTRY // LANES
    lane = rows_of_lanes(1, (1, LANES))
    bias_total = jnp.sum(sum_loss[1:2, :], axis=1, keepdims=True)
    flat[row : row + 1, :] = flat[row : row + 1, :] + jnp.where(
        lane == HEAD_ENTRY % LANES, bias_total, 0.0
    )
    sub = rows_of_lanes(0, (8, LANES))
    wide = rows_of_lanes(1, (8, LANES))
    info = jnp.where((sub == 5) & (wide == 0), loss, 0.0)
    info = jnp.where((sub == 5) & (wide == 1), code_squares, info)
    for which in range(2):

        @pl.when(core == which)
        def _(which=which):
            for d in range(DEVICES):
                z, c, w = d // 32, d // 16 % 2, d % 16
                target = keep_ref if c == which else give_ref
                box = (z * 16 + w) * BOX_ROWS
                first = d * SHARD_ROWS
                target[box : box + 16, :] = flat[first : first + 16, :]
                target[box + 16 : box + 24, :] = jnp.where(
                    sub < 5, flat[first + 16 : first + 24, :], info
                )


def vmem(count):
    return [pl.BlockSpec(memory_space=pltpu.VMEM)] * count


PARAMS = pltpu.CompilerParams(vmem_limit_bytes=48 * 1024 * 1024)


HBM = pl.BlockSpec(memory_space=pltpu.HBM)


def pack_boxes(weights, coords, distances, index):
    return pl.pallas_call(
        pack_kernel,
        out_shape=jax.ShapeDtypeStruct((PEERS * BOX_ROWS, LANES), F32),
        in_specs=[HBM] * 4,
        out_specs=vmem(1)[0],
        scratch_shapes=[
            pltpu.VMEM(weights.shape, F32),
            pltpu.VMEM(coords.shape, F32),
            pltpu.VMEM(distances.shape, F32),
            pltpu.VMEM(index.shape, jnp.int32),
            pltpu.SemaphoreType.DMA((4,)),
        ],
        compiler_params=pltpu.CompilerParams(vmem_limit_bytes=60 * 1024 * 1024),
    )(weights, coords, distances, index)


def main_call(core, mine, other, codes):
    pair = (SUBS, 256, BLOCK)
    pair_two = (SUBS, HID, BLOCK)
    scratch = [
        ((FLAT_ROWS + 8, LANES), F32),
        ((256, 3 * LANES), F32),
        ((HID, 5 * LANES), F32),
        ((256, 640), BF16),
        ((HID, 1280), BF16),
        ((256, 1536), BF16),
        ((768, 256), F32),
        ((256, 3 * LANES), F32),
        ((HID, 2 * LANES), F32),
        ((LANES, LANES), F32),
        ((HID, 256), F32),
        ((768, 256), F32),
        ((16, 256), F32),
        ((HID, LANES), F32),
        ((CODE_ROWS, LANES), F32),
        ((2, BLOCK), F32),
        (pair, F32),
        (pair, F32),
        (pair, F32),
        (pair, F32),
        (pair, BF16),
        (pair, BF16),
        (pair, BF16),
        (pair_two, F32),
        (pair_two, F32),
        (pair_two, F32),
        (pair_two, BF16),
        (pair_two, BF16),
        (pair, BF16),
        (pair, BF16),
        (pair, BF16),
        (pair, BF16),
        (pair_two, BF16),
        (pair_two, BF16),
        (pair, BF16),
        (pair, BF16),
    ]
    return pl.pallas_call(
        main_kernel,
        out_shape=(
            jax.ShapeDtypeStruct((PEERS * BOX_ROWS, LANES), F32),
            jax.ShapeDtypeStruct((PEERS * BOX_ROWS, LANES), F32),
            jax.ShapeDtypeStruct((CODE_ROWS, LATENT), F32),
        ),
        in_specs=[pl.BlockSpec(memory_space=pltpu.SMEM)] + vmem(3),
        out_specs=tuple(vmem(3)),
        scratch_shapes=[pltpu.VMEM(shape, dtype) for shape, dtype in scratch],
        compiler_params=PARAMS,
    )(core, mine, other, codes)


def adam_update(value, first, second, grad, rate):
    first_new = BETA_ONE * first + (1.0 - BETA_ONE) * grad
    second_new = BETA_TWO * second + (1.0 - BETA_TWO) * grad * grad
    first_hat = first_new / (1.0 - BETA_ONE**STEP)
    second_hat = second_new / (1.0 - BETA_TWO**STEP)
    value_new = value - rate * (first_hat / (jnp.sqrt(second_hat) + ADAM_EPS) + DECAY * value)
    return (value_new, first_new, second_new)


def shard_kernel(parts_ref, shard_ref, squares_ref):
    total = parts_ref[0:BOX_ROWS, :]
    for peer in range(1, PEERS):
        total = total + parts_ref[peer * BOX_ROWS : (peer + 1) * BOX_ROWS, :]
    shard_ref[...] = total
    grad = total[:SHARD_ROWS, :]
    squares_ref[...] = jnp.broadcast_to(total_of(grad * grad), squares_ref.shape)


def sum_shards(parts):
    return pl.pallas_call(
        shard_kernel,
        out_shape=(
            jax.ShapeDtypeStruct((BOX_ROWS, LANES), F32),
            jax.ShapeDtypeStruct((8, LANES), F32),
        ),
        in_specs=vmem(1),
        out_specs=tuple(vmem(2)),
        compiler_params=PARAMS,
    )(parts)


def update_kernel(
    seen_ref,
    shard_ref,
    weights_ref,
    moment_one_ref,
    moment_two_ref,
    codes_ref,
    code_first_ref,
    code_second_ref,
    code_grad_ref,
    loss_out,
    norm_out,
    weights_out,
    moment_one_out,
    moment_two_out,
    weights_copy_out,
    codes_out,
    code_first_out,
    code_second_out,
    codes_copy_out,
):
    total = seen_ref[0:8, :]
    for peer in range(1, PEERS):
        total = total + seen_ref[peer * 8 : peer * 8 + 8, :]
    loss_out[...] = shard_ref[SHARD_ROWS : SHARD_ROWS + 1, 0:1]
    norm = jnp.sqrt(total[0:1, 0:1] + shard_ref[SHARD_ROWS : SHARD_ROWS + 1, 1:2])
    norm_out[...] = norm
    factor = jnp.minimum(1.0, CLIP / (norm + 1e-06))
    value, first, second = adam_update(
        weights_ref[...],
        moment_one_ref[...],
        moment_two_ref[...],
        factor * shard_ref[0:SHARD_ROWS, :],
        WEIGHT_RATE,
    )
    weights_out[...] = value
    moment_one_out[...] = first
    moment_two_out[...] = second
    weights_copy_out[...] = value.astype(BF16)
    for r in range(0, CODE_ROWS, 32):
        rows = slice(r, r + 32)
        value, first, second = adam_update(
            codes_ref[rows, :],
            code_first_ref[rows, :],
            code_second_ref[rows, :],
            factor * code_grad_ref[rows, :],
            CODE_RATE,
        )
        codes_out[rows, :] = value
        code_first_out[rows, :] = first
        code_second_out[rows, :] = second
        codes_copy_out[rows, :] = value.astype(BF16)


def update_all(*args):
    scalar = jax.ShapeDtypeStruct((1, 1), F32)
    shard = [jax.ShapeDtypeStruct((SHARD_ROWS, LANES), t) for t in (F32, F32, F32, BF16)]
    table = [jax.ShapeDtypeStruct((CODE_ROWS, LATENT), t) for t in (F32, F32, F32, BF16)]
    return pl.pallas_call(
        update_kernel,
        out_shape=(scalar, scalar, *shard, *table),
        in_specs=vmem(9),
        out_specs=tuple(vmem(10)),
        compiler_params=PARAMS,
    )(*args)


def swap_cores(v):
    return lax.ppermute(v, "core", [(0, 1), (1, 0)])


def exchange(v):
    return lax.all_to_all(v, ("z", "wide"), split_axis=0, concat_axis=0)


def body(
    weights_flat,
    moment_one,
    moment_two,
    codes,
    code_first,
    code_second,
    coords,
    distances,
    shape_index,
):
    boxes = pack_boxes(
        weights_flat.reshape(SHARD_ROWS, LANES),
        coords,
        distances.reshape(1, POINTS_DEV),
        shape_index.reshape(1, POINTS_DEV),
    )
    mine = exchange(boxes.reshape(PEERS, BOX_ROWS, LANES))
    other = swap_cores(mine)
    core = lax.axis_index("core").astype(jnp.int32).reshape(1)
    keep, give, code_grad = main_call(
        core,
        mine.reshape(PEERS * BOX_ROWS, LANES),
        other.reshape(PEERS * BOX_ROWS, LANES),
        codes,
    )
    pair_sum = (keep + swap_cores(give)).reshape(PEERS, BOX_ROWS, LANES)
    shard, squares = sum_shards(exchange(pair_sum).reshape(PEERS * BOX_ROWS, LANES))
    squares = squares + swap_cores(squares)
    seen = exchange(jnp.broadcast_to(squares, (PEERS, 8, LANES)))
    flat = lambda v: v.reshape(SHARD_ROWS, LANES)
    out = update_all(
        seen.reshape(PEERS * 8, LANES),
        shard,
        flat(weights_flat),
        flat(moment_one),
        flat(moment_two),
        codes,
        code_first,
        code_second,
        code_grad,
    )
    return (
        out[0].reshape(()),
        out[1].reshape(()),
        *[v.reshape(weights_flat.shape) for v in out[2:6]],
        *out[6:],
    )


def solution(mesh):
    parts = Mesh(mesh.devices.reshape(4, 2, 16), ALL)
    return jax.shard_map(
        body,
        mesh=parts,
        in_specs=(
            P(ALL),
            P(ALL),
            P(ALL),
            P(ALL, None),
            P(ALL, None),
            P(ALL, None),
            P(None, ALL),
            P(ALL),
            P(ALL),
        ),
        out_specs=(
            P(),
            P(),
            P(ALL),
            P(ALL),
            P(ALL),
            P(ALL),
            P(ALL, None),
            P(ALL, None),
            P(ALL, None),
            P(ALL, None),
        ),
        check_vma=False,
    )
```

```python
import jax
import jax.numpy as jnp
from jax import lax
from jax.experimental import pallas as pl
from jax.experimental.pallas import tpu as pltpu
from jax.sharding import Mesh
from jax.sharding import PartitionSpec as P

LATENT = 256
HID = 512
MIDDLE = HID - LATENT - 3
STEP = 10

DELTA = 0.1
SMOOTH = 0.01
CODE_WEIGHT = 0.001
EIK_WEIGHT = 0.1
CLIP = 0.001
WEIGHT_RATE = 0.02
CODE_RATE = 0.15
BETA_ONE = 0.9
BETA_TWO = 0.999
ADAM_EPS = 1e-08
DECAY = 0.01

LANES = 128
DEVICES = 128
PEERS = 64
SHARD_ROWS = 21
BOX_ROWS = 24
SLOTS = 16
POINTS_DEV = 1024
CODE_ROWS = 256
FLAT_ROWS = DEVICES * SHARD_ROWS
BLOCK = 256
SUBS = 4
TILES = BLOCK // LANES
ALL_POINTS = POINTS_DEV * DEVICES

F32 = jnp.float32
BF16 = jnp.bfloat16
ALL = ("z", "core", "wide")


def rows_of_lanes(lead, shape):
    return lax.broadcasted_iota(jnp.int32, shape, lead)


def halves(v):
    high = v.astype(BF16)
    return high, (v - high.astype(F32)).astype(BF16)


def thirds(v):
    high = v.astype(BF16).astype(F32)
    rest = v - high
    mid = rest.astype(BF16).astype(F32)
    return high, mid, rest - mid


def mm(a, b):
    return lax.dot_general(a, b, (((1,), (0,)), ((), ())), preferred_element_type=F32)


def mm_nt(a, b):
    return lax.dot_general(a, b, (((1,), (1,)), ((), ())), preferred_element_type=F32)


def beside(*parts):
    return jnp.concatenate(parts, axis=1)


def total_of(v):
    return jnp.sum(jnp.sum(v, axis=0, keepdims=True), axis=1, keepdims=True)


def stacked(*parts):
    return jnp.concatenate(parts, axis=0)


def pack_kernel(
    weights_hbm,
    coords_hbm,
    distances_hbm,
    index_hbm,
    out_ref,
    weights_ref,
    coords_ref,
    distances_ref,
    index_ref,
    sems,
):
    pairs = [
        (index_hbm, index_ref),
        (weights_hbm, weights_ref),
        (coords_hbm, coords_ref),
        (distances_hbm, distances_ref),
    ]
    copies = [
        pltpu.make_async_copy(source, target, sems.at[i])
        for i, (source, target) in enumerate(pairs)
    ]
    for copy in copies:
        copy.start()
    for copy in copies:
        copy.wait()
    shard = stacked(weights_ref[...], jnp.zeros((BOX_ROWS - SHARD_ROWS, LANES), F32))
    for peer in range(PEERS):
        out_ref[peer * BOX_ROWS : (peer + 1) * BOX_ROWS, :] = shard
    index = index_ref[...]
    owner = lax.shift_right_logical(index, 8)
    row = lax.bitwise_and(index, CODE_ROWS - 1)
    sent = (rows_of_lanes(0, (DEVICES, POINTS_DEV)) == owner).astype(F32)
    sent_low = sent.astype(BF16)
    width = 256
    earlier = rows_of_lanes(0, (width, width)) < rows_of_lanes(1, (width, width))
    earlier = earlier.astype(F32).astype(BF16)
    ones = jnp.ones((width, width), BF16)
    ranks = [
        mm(sent_low[:, : (part + 1) * width], stacked(*([ones] * part + [earlier])))
        for part in range(POINTS_DEV // width)
    ]
    placed = jnp.sum(sent * beside(*ranks), axis=0, keepdims=True).astype(jnp.int32)
    at_slot = rows_of_lanes(0, (SLOTS, POINTS_DEV)) == placed
    values = [coords_ref[i : i + 1, :] for i in range(3)]
    values += [distances_ref[...], (row + 1).astype(F32)]
    pieces = [[], [], []]
    for value in values:
        for k, third in enumerate(thirds(value)):
            pieces[k].append(jnp.where(at_slot, third, 0.0))
    spare = jnp.zeros((LANES - SLOTS * len(values), POINTS_DEV), F32)
    boxes = mm_nt(
        beside(sent_low, sent_low, sent_low),
        beside(*[stacked(*piece, spare).astype(BF16) for piece in pieces]),
    )
    for z in range(4):
        for core in range(2):
            first = z * 32 + core * 16
            out_ref[pl.ds(z * 16 * BOX_ROWS + SHARD_ROWS + core, 16, stride=BOX_ROWS), :] = boxes[
                first : first + 16, :
            ]


def unit_groups(count, stride_rows, extra, first_entry):
    for group in range(count):
        entry = first_entry + group * 8 * (stride_rows * LANES + extra)
        yield group, entry // LANES, entry % LANES


def unpack_units(flat_ref, out_ref, count, stride_rows, extra, first_entry):
    lane = rows_of_lanes(1, (8, LANES))
    slope = rows_of_lanes(0, (8, LANES)) * extra
    for group, first, shift in unit_groups(count, stride_rows, extra, first_entry):
        start = slope + shift
        wraps = shift + 7 * extra >= LANES
        turn = lax.bitwise_and(lane + start, LANES - 1)
        tiles = []
        for a in range(stride_rows + 2 + wraps):
            tile = flat_ref[pl.ds(first + a, 8, stride=stride_rows), :]
            tiles.append(jnp.take_along_axis(tile, turn, axis=1, mode="promise_in_bounds"))
        for c in range(stride_rows + 1):
            value = jnp.where(lane + start < LANES, tiles[c], tiles[c + 1])
            if wraps:
                value = jnp.where(lane + start < 2 * LANES, value, tiles[c + 2])
            out_ref[group * 8 : group * 8 + 8, c * LANES : (c + 1) * LANES] = value


def pack_units(value_ref, flat_ref, count, stride_rows, extra, first_entry, adding):
    lane = rows_of_lanes(1, (8, LANES))
    slope = rows_of_lanes(0, (8, LANES)) * extra
    zero = jnp.zeros((8, LANES), F32)
    for group, first, shift in unit_groups(count, stride_rows, extra, first_entry):
        start = slope + shift
        wraps = shift + 7 * extra >= LANES
        wanted = range(stride_rows, stride_rows + 1 + wraps + 1) if adding else range(stride_rows)
        rolled = {}

        turn = lax.bitwise_and(lane - start, LANES - 1)

        def tile(c, rolled=rolled, group=group, turn=turn):
            if c < 0 or c > stride_rows:
                return zero
            if c not in rolled:
                value = value_ref[group * 8 : group * 8 + 8, c * LANES : (c + 1) * LANES]
                rolled[c] = jnp.take_along_axis(value, turn, axis=1, mode="promise_in_bounds")
            return rolled[c]

        for a in wanted:
            value = jnp.where(lane >= start, tile(a), tile(a - 1))
            if wraps:
                value = jnp.where(lane >= start - LANES, value, tile(a - 2))
            rows = pl.ds(first + a, 8, stride=stride_rows)
            if adding:
                flat_ref[rows, :] = flat_ref[rows, :] + value
            else:
                flat_ref[rows, :] = value


FIRST_UNITS = (32, 2, 5, 0)
SECOND_UNITS = (64, 4, 3, MIDDLE * (LATENT + 5))
HEAD_ENTRY = MIDDLE * (LATENT + 5) + HID * (HID + 3)


def across(column):
    return beside(*[column] * TILES)


def folded(v):
    return sum(v[:, i * LANES : (i + 1) * LANES] for i in range(TILES))


def silu_parts(half):
    gate = jnp.tanh(half)
    low = 0.5 * gate
    bend = 0.5 - gate * low
    bent = half * gate
    return half + bent, (0.5 + low) + half * bend, bend * (1.0 - bent)


def silu_parts_twice(half):
    gate = jnp.tanh(half)
    bend = 1.0 - gate * gate
    bent = half * gate
    return half + bent, (1.0 + gate) + half * bend, bend * (1.0 - bent)


def main_kernel(
    core_ref,
    mine_ref,
    other_ref,
    codes_ref,
    keep_ref,
    give_ref,
    code_grad_ref,
    flat,
    first_w,
    second_w,
    lhs_one,
    lhs_two,
    lhs_back,
    latent_w,
    coord_w,
    head_w,
    spots,
    sum_two,
    sum_codes,
    sum_coord,
    sum_head,
    sum_count,
    sum_loss,
    act_one,
    slope_one,
    curve_one,
    back_one,
    hid_hi,
    hid_lo,
    hot,
    act_two,
    slope_two,
    curve_two,
    act_tang,
    gate_hi,
    gate_lo,
    tang_hi,
    tang_lo,
    near_hi,
    near_lo,
    bar_hi,
    bar_lo,
    low_hi,
    low_lo,
):
    core = core_ref[0]

    for which in range(2):

        @pl.when(core == which)
        def _(which=which):
            for d in range(DEVICES):
                z, c, w = d // 32, d // 16 % 2, d % 16
                box = (z * 16 + w) * BOX_ROWS
                source = mine_ref if c == which else other_ref
                flat[d * SHARD_ROWS : d * SHARD_ROWS + BOX_ROWS, :] = source[box : box + BOX_ROWS, :]
            rows = pl.ds(SHARD_ROWS + which, PEERS, stride=BOX_ROWS)
            spots[...] = stacked(mine_ref[rows, :], other_ref[rows, :]).T

    unpack_units(flat, first_w, *FIRST_UNITS)
    unpack_units(flat, second_w, *SECOND_UNITS)
    head_bias = flat[HEAD_ENTRY // LANES : HEAD_ENTRY // LANES + 1, :][
        :, HEAD_ENTRY % LANES : HEAD_ENTRY % LANES + 1
    ]

    lane = rows_of_lanes(1, (256, LANES))
    unit = rows_of_lanes(0, (256, LANES))
    real = unit < MIDDLE

    first_low = jnp.where(beside(real, real), first_w[:, : 2 * LANES], 0.0)
    first_end = jnp.where(real, first_w[:, 2 * LANES :], 0.0)
    first_near = jnp.where(lane < 3, first_end, 0.0)
    first_gain = first_end[:, 3:4]
    first_bias = first_end[:, 4:5]
    first_w[:, : 2 * LANES] = first_low
    first_w[:, 2 * LANES :] = first_end
    first_root = lax.rsqrt(
        jnp.sum(first_low * first_low, axis=1, keepdims=True)
        + jnp.sum(first_near * first_near, axis=1, keepdims=True)
        + 1e-12
    )
    first_scale = first_gain * first_root
    first_low = first_low * first_scale
    first_near = first_near * first_scale
    latent_w[0:256, :] = first_low
    for i in range(3):
        coord_w[:, i * LANES : (i + 1) * LANES] = jnp.broadcast_to(
            first_near[:, i : i + 1], (256, LANES)
        )

    second_a = second_w[:, 0:256]
    second_b = second_w[:, 256:512]
    second_gain = second_w[:, 512:513]
    second_bias = second_w[:, 513:514]
    head = jnp.broadcast_to(second_w[:, 514:515], (HID, LANES))
    head_w[:, :LANES] = 0.5 * head
    head_w[:, LANES:] = head
    second_root = lax.rsqrt(
        jnp.sum(second_a * second_a + second_b * second_b, axis=1, keepdims=True) + 1e-12
    )
    second_scale = second_gain * second_root
    second_a = second_a * second_scale
    second_b = second_b * second_scale
    is_hidden = rows_of_lanes(1, (HID, 256)) < MIDDLE
    hidden_cols = jnp.where(is_hidden, second_a, second_b)
    latent_cols = pltpu.roll(jnp.where(is_hidden, second_b, second_a), 3, 1)
    latent_w[256:768, :] = latent_cols

    hidden_hi, hidden_lo = halves(0.5 * hidden_cols)
    lhs_two[:, 0:256] = hidden_hi
    lhs_two[:, 256:512] = hidden_hi
    lhs_two[:, 512:768] = hidden_lo
    back_hi, back_lo = halves(hidden_cols.T)
    lhs_back[:, 0:512] = back_hi
    lhs_back[:, 512:1024] = back_hi
    lhs_back[:, 1024:1536] = back_lo

    code_hi, code_lo = halves(codes_ref[...])
    weight_hi, weight_lo = halves(latent_w[...])
    by_code = mm_nt(
        beside(weight_hi, weight_hi, weight_lo), beside(code_hi, code_lo, code_hi)
    )
    one_hi, one_lo = halves(0.5 * (by_code[0:256, :] + first_bias))
    lhs_one[:, 0:256] = one_hi
    lhs_one[:, 256:512] = one_lo
    two_hi, two_lo = halves(0.5 * (by_code[256:768, :] + second_bias))
    lhs_two[:, 768:1024] = two_hi
    lhs_two[:, 1024:1280] = two_lo
    spread = jnp.where((unit - MIDDLE == lane) & (lane < 3), 1.0, first_near)
    near_parts = thirds(0.5 * spread)
    near_lhs = near_parts[0]
    for place, k in enumerate((0, 0, 1, 1, 2)):
        near_lhs = near_lhs + pltpu.roll(near_parts[k], 8 * (place + 1), 1)
    lhs_one[:, 512:640] = near_lhs.astype(BF16)

    for ref in (sum_two, sum_codes, sum_coord, sum_head, sum_count, sum_loss):
        ref[...] = jnp.zeros(ref.shape, F32)

    def feature(which, step, sub):
        first = which * SLOTS + (step * SUBS + sub) * TILES
        return beside(*[spots[pl.ds(first + i, 1), :] for i in range(TILES)])

    blank5 = jnp.zeros((5, BLOCK), F32)
    chunk = 8192 // BLOCK
    low_chunks = range(0, 256, chunk)
    high_chunks = range(0, HID, chunk)

    def block_stages(step, s):
        place = [feature(i, step, s) for i in range(3)]
        target = feature(3, step, s)
        code_row = feature(4, step, s)
        valid = (code_row > 0.5).astype(F32)
        near_pieces = thirds(stacked(*place, blank5))

        wanted = code_row - 1.0
        for r in range(0, CODE_ROWS, chunk):
            row = (rows_of_lanes(0, (chunk, BLOCK)) + r).astype(F32)
            mark = jnp.where(row == wanted, 1.0, 0.0)
            hot[s, r : r + chunk, :] = mark.astype(BF16)
            sum_count[r : r + chunk, :] += folded(mark)
        yield

        high, mid, low = near_pieces
        near_rhs = stacked(high, mid, low, high, mid, high, jnp.zeros((80, BLOCK), F32))
        act_one[s] = mm(lhs_one[...], stacked(hot[s], hot[s], near_rhs.astype(BF16)))
        yield
        for r in low_chunks:
            pre = act_one[s, r : r + chunk, :]
            value, slope, curve = silu_parts(pre)
            if r + chunk == 256:
                inside = rows_of_lanes(0, (chunk, BLOCK)) + r < MIDDLE
                value = jnp.where(inside, value, pre + pre)
                slope = jnp.where(inside, slope, 0.0)
                curve = jnp.where(inside, curve, 0.0)
            high, low = halves(value)
            hid_hi[s, r : r + chunk, :] = high
            hid_lo[s, r : r + chunk, :] = low
            slope_one[s, r : r + chunk, :] = slope
            curve_one[s, r : r + chunk, :] = curve
        yield

        act_two[s] = mm(lhs_two[...], stacked(hid_hi[s], hid_lo[s], hid_hi[s], hot[s], hot[s]))
        yield
        total = jnp.zeros((8, BLOCK), F32)
        for r in high_chunks:
            value, slope, curve = silu_parts_twice(act_two[s, r : r + chunk, :])
            head = across(head_w[r : r + chunk, :LANES])
            weighed = head * value
            for k in range(0, chunk, 8):
                total = total + weighed[k : k + 8, :]
            high, low = halves(head * slope)
            gate_hi[s, r : r + chunk, :] = high
            gate_lo[s, r : r + chunk, :] = low
            act_two[s, r : r + chunk, :] = value
            slope_two[s, r : r + chunk, :] = slope
            curve_two[s, r : r + chunk, :] = curve
        summed = jnp.sum(total, axis=0, keepdims=True)
        yield

        back_one[s] = mm(lhs_back[...], stacked(gate_hi[s], gate_lo[s], gate_hi[s]))
        yield
        totals = [jnp.zeros((8, BLOCK), F32) for _ in range(3)]
        for r in low_chunks:
            grad = back_one[s, r : r + chunk, :] * slope_one[s, r : r + chunk, :]
            high, low = halves(grad)
            near_hi[s, r : r + chunk, :] = high
            near_lo[s, r : r + chunk, :] = low
            for i in range(3):
                weighed = across(coord_w[r : r + chunk, i * LANES : (i + 1) * LANES]) * grad
                for k in range(0, chunk, 8):
                    totals[i] = totals[i] + weighed[k : k + 8, :]
        lead = [
            jnp.sum(totals[i], axis=0, keepdims=True)
            + back_one[s, MIDDLE + i : MIDDLE + i + 1, :]
            for i in range(3)
        ]

        predicted = jnp.tanh(2.0 * summed + head_bias)
        flank = 1.0 - predicted * predicted
        slope = [flank * q for q in lead]
        excess = slope[0] * slope[0] + slope[1] * slope[1] + slope[2] * slope[2] - 1.0
        capped = jnp.tanh(predicted / DELTA)
        misfit = DELTA * capped - DELTA * jnp.tanh(target / DELTA)
        fitting = jnp.sqrt(misfit * misfit + SMOOTH * SMOOTH)
        sum_loss[0:1, :] += valid * (fitting + EIK_WEIGHT * excess * excess)
        share = valid * (1.0 / ALL_POINTS)
        pull = [(4.0 * EIK_WEIGHT) * excess * v for v in slope]
        by_flank = sum(p * q for p, q in zip(pull, lead))
        by_predicted = misfit / fitting * (1.0 - capped * capped) - 2.0 * predicted * by_flank
        bar_out = share * by_predicted * flank
        sum_loss[1:2, :] += bar_out
        half_bar = 0.5 * bar_out
        pull = [share * flank * p for p in pull]

        last = stacked(blank5, *pull)
        for r in low_chunks:
            grad = 0.0
            for i in range(3):
                grad = grad + across(coord_w[r : r + chunk, i * LANES : (i + 1) * LANES]) * pull[i]
            through = grad * slope_one[s, r : r + chunk, :]
            if r + chunk == 256:
                inside = rows_of_lanes(0, (8, BLOCK)) < MIDDLE - 248
                end = jnp.where(inside, through[chunk - 8 :], last)
                through = stacked(through[: chunk - 8], end)
            high, low = halves(through)
            tang_hi[s, r : r + chunk, :] = high
            tang_lo[s, r : r + chunk, :] = low
            curve_one[s, r : r + chunk, :] = (
                grad * back_one[s, r : r + chunk, :] * curve_one[s, r : r + chunk, :]
            )
        yield
        act_tang[s] = mm(lhs_two[:, 0:768], stacked(tang_hi[s], tang_lo[s], tang_hi[s]))
        yield
        for r in high_chunks:
            tangent = act_tang[s, r : r + chunk, :]
            slope = slope_two[s, r : r + chunk, :]
            head = across(head_w[r : r + chunk, LANES:])
            bar = head * (half_bar * slope + tangent * curve_two[s, r : r + chunk, :])
            by_head = act_two[s, r : r + chunk, :] * bar_out + slope * tangent
            sum_head[r : r + chunk, :] += folded(by_head)
            high, low = halves(bar)
            bar_hi[s, r : r + chunk, :] = high
            bar_lo[s, r : r + chunk, :] = low
        yield

        back_one[s] = mm(lhs_back[...], stacked(bar_hi[s], bar_lo[s], bar_hi[s]))
        yield
        for r in low_chunks:
            bar = (
                back_one[s, r : r + chunk, :] * slope_one[s, r : r + chunk, :]
                + curve_one[s, r : r + chunk, :]
            )
            high, low = halves(bar)
            low_hi[s, r : r + chunk, :] = high
            low_lo[s, r : r + chunk, :] = low
        yield

        sum_two[...] += mm_nt(
            beside(bar_hi[s], bar_hi[s], bar_lo[s], gate_hi[s], gate_hi[s], gate_lo[s]),
            beside(hid_hi[s], hid_lo[s], hid_hi[s], tang_hi[s], tang_lo[s], tang_hi[s]),
        )
        hots = beside(hot[s], hot[s])
        sum_codes[256:768, :] += mm_nt(beside(bar_hi[s], bar_lo[s]), hots)
        sum_codes[0:256, :] += mm_nt(beside(low_hi[s], low_lo[s]), hots)
        seen = stacked(near_pieces[0], near_pieces[1]).astype(BF16)
        pulled = stacked(*pull, blank5)
        high = pulled.astype(BF16).astype(F32)
        pulled = stacked(high, pulled - high).astype(BF16)
        sum_coord[...] += mm_nt(
            beside(seen, seen, pulled, pulled),
            beside(low_hi[s], low_lo[s], near_hi[s], near_lo[s]),
        )

    def step_body(step, carry):
        waiting = [block_stages(step, s) for s in range(SUBS)]
        active = []
        while waiting or active:
            if waiting:
                active.append(waiting.pop(0))
            active = [work for work in active if next(work, work) is not work]
        return carry

    lax.fori_loop(0, SLOTS * DEVICES // (SUBS * BLOCK), step_body, 0)

    codes = codes_ref[...]
    count = jnp.sum(sum_count[...], axis=1, keepdims=True)
    by_code = sum_codes[...]
    turned_hi, turned_lo = halves(by_code.T)
    weight_hi, weight_lo = halves(latent_w[...])
    code_grad = mm(
        beside(turned_hi, turned_hi, turned_lo), stacked(weight_hi, weight_lo, weight_hi)
    )
    code_grad = code_grad + (2.0 * CODE_WEIGHT / ALL_POINTS) * count * codes
    code_grad_ref[...] = code_grad
    code_squares = total_of(code_grad * code_grad)
    loss = jnp.sum(sum_loss[0:1, :], axis=1, keepdims=True)
    loss = loss + CODE_WEIGHT * total_of(count * codes * codes)
    loss = loss / ALL_POINTS

    code_hi, code_lo = halves(codes)
    by_hi, by_lo = halves(by_code)
    latent_grad = mm(beside(by_hi, by_hi, by_lo), stacked(code_hi, code_lo, code_hi))
    bias_grad = jnp.sum(by_code, axis=1, keepdims=True)

    near_grad = sum_coord[0:8, :] + sum_coord[8:16, :]
    near_grad = stacked(near_grad, jnp.zeros((LANES - 8, 256), F32)).T
    near_grad = jnp.where(lane < 3, near_grad, 0.0)
    low_grad = latent_grad[0:256, :]
    first_low = first_w[:, : 2 * LANES]
    first_near = jnp.where(lane < 3, first_w[:, 2 * LANES :], 0.0)
    along = jnp.sum(first_low * low_grad, axis=1, keepdims=True)
    along = along + jnp.sum(first_near * near_grad, axis=1, keepdims=True)
    inward = first_scale * first_root * first_root * along
    end = first_scale * near_grad - first_near * inward
    end = jnp.where(lane == 3, first_root * along, end)
    end = jnp.where(lane == 4, bias_grad[0:256, :], end)
    low_grad = first_scale * low_grad - first_low * inward
    first_w[:, : 2 * LANES] = jnp.where(beside(real, real), low_grad, 0.0)
    first_w[:, 2 * LANES :] = jnp.where(real, end, 0.0)

    hidden_grad = sum_two[...]
    moved = pltpu.roll(latent_grad[256:768, :], 256 - 3, 1)
    grad_a = jnp.where(is_hidden, hidden_grad, moved)
    grad_b = jnp.where(is_hidden, moved, hidden_grad)
    second_a = second_w[:, 0:256]
    second_b = second_w[:, 256:512]
    along = jnp.sum(second_a * grad_a + second_b * grad_b, axis=1, keepdims=True)
    inward = second_scale * second_root * second_root * along
    second_w[:, 0:256] = second_scale * grad_a - second_a * inward
    second_w[:, 256:512] = second_scale * grad_b - second_b * inward
    head_grad = jnp.sum(sum_head[...], axis=1, keepdims=True)
    lane = rows_of_lanes(1, (HID, LANES))
    end = jnp.where(lane == 0, second_root * along, 0.0)
    end = jnp.where(lane == 1, bias_grad[256:768, :], end)
    second_w[:, 512:640] = jnp.where(lane == 2, head_grad, end)

    flat[...] = jnp.zeros(flat.shape, F32)
    for adding in (False, True):
        pack_units(first_w, flat, *FIRST_UNITS, adding)
        pack_units(second_w, flat, *SECOND_UNITS, adding)
    row = HEAD_ENTRY // LANES
    lane = rows_of_lanes(1, (1, LANES))
    bias_total = jnp.sum(sum_loss[1:2, :], axis=1, keepdims=True)
    flat[row : row + 1, :] = flat[row : row + 1, :] + jnp.where(
        lane == HEAD_ENTRY % LANES, bias_total, 0.0
    )
    sub = rows_of_lanes(0, (8, LANES))
    wide = rows_of_lanes(1, (8, LANES))
    info = jnp.where((sub == 5) & (wide == 0), loss, 0.0)
    info = jnp.where((sub == 5) & (wide == 1), code_squares, info)
    for which in range(2):

        @pl.when(core == which)
        def _(which=which):
            for d in range(DEVICES):
                z, c, w = d // 32, d // 16 % 2, d % 16
                target = keep_ref if c == which else give_ref
                box = (z * 16 + w) * BOX_ROWS
                first = d * SHARD_ROWS
                target[box : box + 16, :] = flat[first : first + 16, :]
                target[box + 16 : box + 24, :] = jnp.where(
                    sub < 5, flat[first + 16 : first + 24, :], info
                )


def vmem(count):
    return [pl.BlockSpec(memory_space=pltpu.VMEM)] * count


PARAMS = pltpu.CompilerParams(vmem_limit_bytes=48 * 1024 * 1024)


HBM = pl.BlockSpec(memory_space=pltpu.HBM)


def pack_boxes(weights, coords, distances, index):
    return pl.pallas_call(
        pack_kernel,
        out_shape=jax.ShapeDtypeStruct((PEERS * BOX_ROWS, LANES), F32),
        in_specs=[HBM] * 4,
        out_specs=vmem(1)[0],
        scratch_shapes=[
            pltpu.VMEM(weights.shape, F32),
            pltpu.VMEM(coords.shape, F32),
            pltpu.VMEM(distances.shape, F32),
            pltpu.VMEM(index.shape, jnp.int32),
            pltpu.SemaphoreType.DMA((4,)),
        ],
        compiler_params=pltpu.CompilerParams(vmem_limit_bytes=60 * 1024 * 1024),
    )(weights, coords, distances, index)


def main_call(core, mine, other, codes):
    pair = (SUBS, 256, BLOCK)
    pair_two = (SUBS, HID, BLOCK)
    scratch = [
        ((FLAT_ROWS + 8, LANES), F32),
        ((256, 3 * LANES), F32),
        ((HID, 5 * LANES), F32),
        ((256, 640), BF16),
        ((HID, 1280), BF16),
        ((256, 1536), BF16),
        ((768, 256), F32),
        ((256, 3 * LANES), F32),
        ((HID, 2 * LANES), F32),
        ((LANES, LANES), F32),
        ((HID, 256), F32),
        ((768, 256), F32),
        ((16, 256), F32),
        ((HID, LANES), F32),
        ((CODE_ROWS, LANES), F32),
        ((2, BLOCK), F32),
        (pair, F32),
        (pair, F32),
        (pair, F32),
        (pair, F32),
        (pair, BF16),
        (pair, BF16),
        (pair, BF16),
        (pair_two, F32),
        (pair_two, F32),
        (pair_two, F32),
        (pair_two, F32),
        (pair_two, BF16),
        (pair_two, BF16),
        (pair, BF16),
        (pair, BF16),
        (pair, BF16),
        (pair, BF16),
        (pair_two, BF16),
        (pair_two, BF16),
        (pair, BF16),
        (pair, BF16),
    ]
    return pl.pallas_call(
        main_kernel,
        out_shape=(
            jax.ShapeDtypeStruct((PEERS * BOX_ROWS, LANES), F32),
            jax.ShapeDtypeStruct((PEERS * BOX_ROWS, LANES), F32),
            jax.ShapeDtypeStruct((CODE_ROWS, LATENT), F32),
        ),
        in_specs=[pl.BlockSpec(memory_space=pltpu.SMEM)] + vmem(3),
        out_specs=tuple(vmem(3)),
        scratch_shapes=[pltpu.VMEM(shape, dtype) for shape, dtype in scratch],
        compiler_params=PARAMS,
    )(core, mine, other, codes)


def adam_update(value, first, second, grad, rate):
    first_new = BETA_ONE * first + (1.0 - BETA_ONE) * grad
    second_new = BETA_TWO * second + (1.0 - BETA_TWO) * grad * grad
    first_hat = first_new / (1.0 - BETA_ONE**STEP)
    second_hat = second_new / (1.0 - BETA_TWO**STEP)
    value_new = value - rate * (first_hat / (jnp.sqrt(second_hat) + ADAM_EPS) + DECAY * value)
    return (value_new, first_new, second_new)


def shard_kernel(parts_ref, shard_ref, squares_ref):
    total = parts_ref[0:BOX_ROWS, :]
    for peer in range(1, PEERS):
        total = total + parts_ref[peer * BOX_ROWS : (peer + 1) * BOX_ROWS, :]
    shard_ref[...] = total
    grad = total[:SHARD_ROWS, :]
    squares_ref[...] = jnp.broadcast_to(total_of(grad * grad), squares_ref.shape)


def sum_shards(parts):
    return pl.pallas_call(
        shard_kernel,
        out_shape=(
            jax.ShapeDtypeStruct((BOX_ROWS, LANES), F32),
            jax.ShapeDtypeStruct((8, LANES), F32),
        ),
        in_specs=vmem(1),
        out_specs=tuple(vmem(2)),
        compiler_params=PARAMS,
    )(parts)


def update_kernel(
    seen_ref,
    shard_ref,
    weights_ref,
    moment_one_ref,
    moment_two_ref,
    codes_ref,
    code_first_ref,
    code_second_ref,
    code_grad_ref,
    loss_out,
    norm_out,
    weights_out,
    moment_one_out,
    moment_two_out,
    weights_copy_out,
    codes_out,
    code_first_out,
    code_second_out,
    codes_copy_out,
):
    total = seen_ref[0:8, :]
    for peer in range(1, PEERS):
        total = total + seen_ref[peer * 8 : peer * 8 + 8, :]
    loss_out[...] = shard_ref[SHARD_ROWS : SHARD_ROWS + 1, 0:1]
    norm = jnp.sqrt(total[0:1, 0:1] + shard_ref[SHARD_ROWS : SHARD_ROWS + 1, 1:2])
    norm_out[...] = norm
    factor = jnp.minimum(1.0, CLIP / (norm + 1e-06))
    value, first, second = adam_update(
        weights_ref[...],
        moment_one_ref[...],
        moment_two_ref[...],
        factor * shard_ref[0:SHARD_ROWS, :],
        WEIGHT_RATE,
    )
    weights_out[...] = value
    moment_one_out[...] = first
    moment_two_out[...] = second
    weights_copy_out[...] = value.astype(BF16)
    for r in range(0, CODE_ROWS, 32):
        rows = slice(r, r + 32)
        value, first, second = adam_update(
            codes_ref[rows, :],
            code_first_ref[rows, :],
            code_second_ref[rows, :],
            factor * code_grad_ref[rows, :],
            CODE_RATE,
        )
        codes_out[rows, :] = value
        code_first_out[rows, :] = first
        code_second_out[rows, :] = second
        codes_copy_out[rows, :] = value.astype(BF16)


def update_all(*args):
    scalar = jax.ShapeDtypeStruct((1, 1), F32)
    shard = [jax.ShapeDtypeStruct((SHARD_ROWS, LANES), t) for t in (F32, F32, F32, BF16)]
    table = [jax.ShapeDtypeStruct((CODE_ROWS, LATENT), t) for t in (F32, F32, F32, BF16)]
    return pl.pallas_call(
        update_kernel,
        out_shape=(scalar, scalar, *shard, *table),
        in_specs=vmem(9),
        out_specs=tuple(vmem(10)),
        compiler_params=PARAMS,
    )(*args)


def swap_cores(v):
    return lax.ppermute(v, "core", [(0, 1), (1, 0)])


def exchange(v):
    return lax.all_to_all(v, ("z", "wide"), split_axis=0, concat_axis=0)


def body(
    weights_flat,
    moment_one,
    moment_two,
    codes,
    code_first,
    code_second,
    coords,
    distances,
    shape_index,
):
    boxes = pack_boxes(
        weights_flat.reshape(SHARD_ROWS, LANES),
        coords,
        distances.reshape(1, POINTS_DEV),
        shape_index.reshape(1, POINTS_DEV),
    )
    mine = exchange(boxes.reshape(PEERS, BOX_ROWS, LANES))
    other = swap_cores(mine)
    core = lax.axis_index("core").astype(jnp.int32).reshape(1)
    keep, give, code_grad = main_call(
        core,
        mine.reshape(PEERS * BOX_ROWS, LANES),
        other.reshape(PEERS * BOX_ROWS, LANES),
        codes,
    )
    pair_sum = (keep + swap_cores(give)).reshape(PEERS, BOX_ROWS, LANES)
    shard, squares = sum_shards(exchange(pair_sum).reshape(PEERS * BOX_ROWS, LANES))
    squares = squares + swap_cores(squares)
    seen = exchange(jnp.broadcast_to(squares, (PEERS, 8, LANES)))
    flat = lambda v: v.reshape(SHARD_ROWS, LANES)
    out = update_all(
        seen.reshape(PEERS * 8, LANES),
        shard,
        flat(weights_flat),
        flat(moment_one),
        flat(moment_two),
        codes,
        code_first,
        code_second,
        code_grad,
    )
    return (
        out[0].reshape(()),
        out[1].reshape(()),
        *[v.reshape(weights_flat.shape) for v in out[2:6]],
        *out[6:],
    )


def solution(mesh):
    parts = Mesh(mesh.devices.reshape(4, 2, 16), ALL)
    return jax.shard_map(
        body,
        mesh=parts,
        in_specs=(
            P(ALL),
            P(ALL),
            P(ALL),
            P(ALL, None),
            P(ALL, None),
            P(ALL, None),
            P(None, ALL),
            P(ALL),
            P(ALL),
        ),
        out_specs=(
            P(),
            P(),
            P(ALL),
            P(ALL),
            P(ALL),
            P(ALL),
            P(ALL, None),
            P(ALL, None),
            P(ALL, None),
            P(ALL, None),
        ),
        check_vma=False,
    )
```

```python
import jax
import jax.numpy as jnp
from jax import lax
from jax.experimental import pallas as pl
from jax.experimental.pallas import tpu as pltpu
from jax.sharding import Mesh
from jax.sharding import PartitionSpec as P

LATENT = 256
HID = 512
MIDDLE = HID - LATENT - 3
STEP = 10

DELTA = 0.1
SMOOTH = 0.01
CODE_WEIGHT = 0.001
EIK_WEIGHT = 0.1
CLIP = 0.001
WEIGHT_RATE = 0.02
CODE_RATE = 0.15
BETA_ONE = 0.9
BETA_TWO = 0.999
ADAM_EPS = 1e-08
DECAY = 0.01

LANES = 128
DEVICES = 128
PEERS = 64
SHARD_ROWS = 21
BOX_ROWS = 24
SLOTS = 16
POINTS_DEV = 1024
CODE_ROWS = 256
FLAT_ROWS = DEVICES * SHARD_ROWS
BLOCK = 256
SUBS = 4
TILES = BLOCK // LANES
ALL_POINTS = POINTS_DEV * DEVICES

F32 = jnp.float32
BF16 = jnp.bfloat16
ALL = ("z", "core", "wide")


def rows_of_lanes(lead, shape):
    return lax.broadcasted_iota(jnp.int32, shape, lead)


def halves(v):
    high = v.astype(BF16)
    return high, (v - high.astype(F32)).astype(BF16)


def thirds(v):
    high = v.astype(BF16).astype(F32)
    rest = v - high
    mid = rest.astype(BF16).astype(F32)
    return high, mid, rest - mid


def mm(a, b):
    return lax.dot_general(a, b, (((1,), (0,)), ((), ())), preferred_element_type=F32)


def mm_nt(a, b):
    return lax.dot_general(a, b, (((1,), (1,)), ((), ())), preferred_element_type=F32)


def beside(*parts):
    return jnp.concatenate(parts, axis=1)


def total_of(v):
    return jnp.sum(jnp.sum(v, axis=0, keepdims=True), axis=1, keepdims=True)


def stacked(*parts):
    return jnp.concatenate(parts, axis=0)


def pack_kernel(
    weights_hbm,
    coords_hbm,
    distances_hbm,
    index_hbm,
    out_ref,
    weights_ref,
    coords_ref,
    distances_ref,
    index_ref,
    sems,
):
    pairs = [
        (index_hbm, index_ref),
        (weights_hbm, weights_ref),
        (coords_hbm, coords_ref),
        (distances_hbm, distances_ref),
    ]
    copies = [
        pltpu.make_async_copy(source, target, sems.at[i])
        for i, (source, target) in enumerate(pairs)
    ]
    for copy in copies:
        copy.start()
    for copy in copies:
        copy.wait()
    shard = stacked(weights_ref[...], jnp.zeros((BOX_ROWS - SHARD_ROWS, LANES), F32))
    for peer in range(PEERS):
        out_ref[peer * BOX_ROWS : (peer + 1) * BOX_ROWS, :] = shard
    index = index_ref[...]
    owner = lax.shift_right_logical(index, 8)
    row = lax.bitwise_and(index, CODE_ROWS - 1)
    sent = (rows_of_lanes(0, (DEVICES, POINTS_DEV)) == owner).astype(F32)
    sent_low = sent.astype(BF16)
    width = 256
    earlier = rows_of_lanes(0, (width, width)) < rows_of_lanes(1, (width, width))
    earlier = earlier.astype(F32).astype(BF16)
    ones = jnp.ones((width, width), BF16)
    ranks = [
        mm(sent_low[:, : (part + 1) * width], stacked(*([ones] * part + [earlier])))
        for part in range(POINTS_DEV // width)
    ]
    placed = jnp.sum(sent * beside(*ranks), axis=0, keepdims=True).astype(jnp.int32)
    at_slot = rows_of_lanes(0, (SLOTS, POINTS_DEV)) == placed
    values = [coords_ref[i : i + 1, :] for i in range(3)]
    values += [distances_ref[...], (row + 1).astype(F32)]
    pieces = [[], [], []]
    for value in values:
        for k, third in enumerate(thirds(value)):
            pieces[k].append(jnp.where(at_slot, third, 0.0))
    spare = jnp.zeros((LANES - SLOTS * len(values), POINTS_DEV), F32)
    boxes = mm_nt(
        beside(sent_low, sent_low, sent_low),
        beside(*[stacked(*piece, spare).astype(BF16) for piece in pieces]),
    )
    for z in range(4):
        for core in range(2):
            first = z * 32 + core * 16
            out_ref[pl.ds(z * 16 * BOX_ROWS + SHARD_ROWS + core, 16, stride=BOX_ROWS), :] = boxes[
                first : first + 16, :
            ]


def unit_groups(count, stride_rows, extra, first_entry):
    for group in range(count):
        entry = first_entry + group * 8 * (stride_rows * LANES + extra)
        yield group, entry // LANES, entry % LANES


def unpack_units(flat_ref, out_ref, count, stride_rows, extra, first_entry):
    lane = rows_of_lanes(1, (8, LANES))
    slope = rows_of_lanes(0, (8, LANES)) * extra
    for group, first, shift in unit_groups(count, stride_rows, extra, first_entry):
        start = slope + shift
        wraps = shift + 7 * extra >= LANES
        turn = lax.bitwise_and(lane + start, LANES - 1)
        tiles = []
        for a in range(stride_rows + 2 + wraps):
            tile = flat_ref[pl.ds(first + a, 8, stride=stride_rows), :]
            tiles.append(jnp.take_along_axis(tile, turn, axis=1, mode="promise_in_bounds"))
        for c in range(stride_rows + 1):
            value = jnp.where(lane + start < LANES, tiles[c], tiles[c + 1])
            if wraps:
                value = jnp.where(lane + start < 2 * LANES, value, tiles[c + 2])
            out_ref[group * 8 : group * 8 + 8, c * LANES : (c + 1) * LANES] = value


def pack_units(value_ref, flat_ref, count, stride_rows, extra, first_entry, adding):
    lane = rows_of_lanes(1, (8, LANES))
    slope = rows_of_lanes(0, (8, LANES)) * extra
    zero = jnp.zeros((8, LANES), F32)
    for group, first, shift in unit_groups(count, stride_rows, extra, first_entry):
        start = slope + shift
        wraps = shift + 7 * extra >= LANES
        wanted = range(stride_rows, stride_rows + 1 + wraps + 1) if adding else range(stride_rows)
        rolled = {}

        turn = lax.bitwise_and(lane - start, LANES - 1)

        def tile(c, rolled=rolled, group=group, turn=turn):
            if c < 0 or c > stride_rows:
                return zero
            if c not in rolled:
                value = value_ref[group * 8 : group * 8 + 8, c * LANES : (c + 1) * LANES]
                rolled[c] = jnp.take_along_axis(value, turn, axis=1, mode="promise_in_bounds")
            return rolled[c]

        for a in wanted:
            value = jnp.where(lane >= start, tile(a), tile(a - 1))
            if wraps:
                value = jnp.where(lane >= start - LANES, value, tile(a - 2))
            rows = pl.ds(first + a, 8, stride=stride_rows)
            if adding:
                flat_ref[rows, :] = flat_ref[rows, :] + value
            else:
                flat_ref[rows, :] = value


FIRST_UNITS = (32, 2, 5, 0)
SECOND_UNITS = (64, 4, 3, MIDDLE * (LATENT + 5))
HEAD_ENTRY = MIDDLE * (LATENT + 5) + HID * (HID + 3)


def across(column):
    return beside(*[column] * TILES)


def folded(v):
    return sum(v[:, i * LANES : (i + 1) * LANES] for i in range(TILES))


def silu_parts(half):
    gate = jnp.tanh(half)
    low = 0.5 * gate
    bend = 0.5 - gate * low
    bent = half * gate
    return half + bent, (0.5 + low) + half * bend, bend * (1.0 - bent)


def silu_parts_twice(half):
    gate = jnp.tanh(half)
    bend = 1.0 - gate * gate
    bent = half * gate
    return half + bent, (1.0 + gate) + half * bend, bend * (1.0 - bent)


def loop_kernel(
    core_ref,
    mine_ref,
    other_ref,
    codes_ref,
    first_w,
    second_w,
    latent_w,
    sum_two,
    sum_codes,
    sum_coord,
    sum_head,
    sum_count,
    sum_loss,
    flat,
    lhs_one,
    lhs_two,
    lhs_back,
    coord_w,
    head_w,
    spots,
    act_one,
    slope_one,
    curve_one,
    back_one,
    hid_hi,
    hid_lo,
    hot,
    act_two,
    slope_two,
    curve_two,
    act_tang,
    gate_hi,
    gate_lo,
    tang_hi,
    tang_lo,
    near_hi,
    near_lo,
    bar_hi,
    bar_lo,
    low_hi,
    low_lo,
):
    core = core_ref[0]

    for which in range(2):

        @pl.when(core == which)
        def _(which=which):
            for d in range(DEVICES):
                z, c, w = d // 32, d // 16 % 2, d % 16
                box = (z * 16 + w) * BOX_ROWS
                source = mine_ref if c == which else other_ref
                flat[d * SHARD_ROWS : d * SHARD_ROWS + BOX_ROWS, :] = source[box : box + BOX_ROWS, :]
            rows = pl.ds(SHARD_ROWS + which, PEERS, stride=BOX_ROWS)
            spots[...] = stacked(mine_ref[rows, :], other_ref[rows, :]).T

    unpack_units(flat, first_w, *FIRST_UNITS)
    unpack_units(flat, second_w, *SECOND_UNITS)
    head_bias = flat[HEAD_ENTRY // LANES : HEAD_ENTRY // LANES + 1, :][
        :, HEAD_ENTRY % LANES : HEAD_ENTRY % LANES + 1
    ]

    lane = rows_of_lanes(1, (256, LANES))
    unit = rows_of_lanes(0, (256, LANES))
    real = unit < MIDDLE

    first_low = jnp.where(beside(real, real), first_w[:, : 2 * LANES], 0.0)
    first_end = jnp.where(real, first_w[:, 2 * LANES :], 0.0)
    first_near = jnp.where(lane < 3, first_end, 0.0)
    first_gain = first_end[:, 3:4]
    first_bias = first_end[:, 4:5]
    first_w[:, : 2 * LANES] = first_low
    first_w[:, 2 * LANES :] = first_end
    _, first_scale = norm_parts(beside(first_low, first_near), first_gain)
    first_low = first_low * first_scale
    first_near = first_near * first_scale
    latent_w[0:256, :] = first_low
    for i in range(3):
        coord_w[:, i * LANES : (i + 1) * LANES] = jnp.broadcast_to(
            first_near[:, i : i + 1], (256, LANES)
        )

    second_a = second_w[:, 0:256]
    second_b = second_w[:, 256:512]
    second_gain = second_w[:, 512:513]
    second_bias = second_w[:, 513:514]
    head = jnp.broadcast_to(second_w[:, 514:515], (HID, LANES))
    head_w[:, :LANES] = 0.5 * head
    head_w[:, LANES:] = head
    _, second_scale = norm_parts(second_w[:, 0:512], second_gain)
    second_a = second_a * second_scale
    second_b = second_b * second_scale
    is_hidden = rows_of_lanes(1, (HID, 256)) < MIDDLE
    hidden_cols = jnp.where(is_hidden, second_a, second_b)
    latent_cols = pltpu.roll(jnp.where(is_hidden, second_b, second_a), 3, 1)
    latent_w[256:768, :] = latent_cols

    hidden_hi, hidden_lo = halves(0.5 * hidden_cols)
    lhs_two[:, 0:256] = hidden_hi
    lhs_two[:, 256:512] = hidden_hi
    lhs_two[:, 512:768] = hidden_lo
    back_hi, back_lo = halves(hidden_cols.T)
    lhs_back[:, 0:512] = back_hi
    lhs_back[:, 512:1024] = back_hi
    lhs_back[:, 1024:1536] = back_lo

    code_hi, code_lo = halves(codes_ref[...])
    weight_hi, weight_lo = halves(latent_w[...])
    by_code = mm_nt(
        beside(weight_hi, weight_hi, weight_lo), beside(code_hi, code_lo, code_hi)
    )
    one_hi, one_lo = halves(0.5 * (by_code[0:256, :] + first_bias))
    lhs_one[:, 0:256] = one_hi
    lhs_one[:, 256:512] = one_lo
    two_hi, two_lo = halves(0.5 * (by_code[256:768, :] + second_bias))
    lhs_two[:, 768:1024] = two_hi
    lhs_two[:, 1024:1280] = two_lo
    spread = jnp.where((unit - MIDDLE == lane) & (lane < 3), 1.0, first_near)
    near_parts = thirds(0.5 * spread)
    near_lhs = near_parts[0]
    for place, k in enumerate((0, 0, 1, 1, 2)):
        near_lhs = near_lhs + pltpu.roll(near_parts[k], 8 * (place + 1), 1)
    lhs_one[:, 512:640] = near_lhs.astype(BF16)

    for ref in (sum_two, sum_codes, sum_coord, sum_head, sum_count, sum_loss):
        ref[...] = jnp.zeros(ref.shape, F32)

    def feature(which, step, sub):
        first = which * SLOTS + (step * SUBS + sub) * TILES
        return beside(*[spots[pl.ds(first + i, 1), :] for i in range(TILES)])

    blank5 = jnp.zeros((5, BLOCK), F32)
    chunk = 8192 // BLOCK
    low_chunks = range(0, 256, chunk)
    high_chunks = range(0, HID, chunk)

    def block_stages(step, s):
        place = [feature(i, step, s) for i in range(3)]
        target = feature(3, step, s)
        code_row = feature(4, step, s)
        valid = (code_row > 0.5).astype(F32)
        near_pieces = thirds(stacked(*place, blank5))

        wanted = code_row - 1.0
        for r in range(0, CODE_ROWS, chunk):
            row = (rows_of_lanes(0, (chunk, BLOCK)) + r).astype(F32)
            mark = jnp.where(row == wanted, 1.0, 0.0)
            hot[s, r : r + chunk, :] = mark.astype(BF16)
            sum_count[r : r + chunk, :] += folded(mark)
        yield

        high, mid, low = near_pieces
        near_rhs = stacked(high, mid, low, high, mid, high, jnp.zeros((80, BLOCK), F32))
        act_one[s] = mm(lhs_one[...], stacked(hot[s], hot[s], near_rhs.astype(BF16)))
        yield
        for r in low_chunks:
            pre = act_one[s, r : r + chunk, :]
            value, slope, curve = silu_parts(pre)
            if r + chunk == 256:
                inside = rows_of_lanes(0, (chunk, BLOCK)) + r < MIDDLE
                value = jnp.where(inside, value, pre + pre)
                slope = jnp.where(inside, slope, 0.0)
                curve = jnp.where(inside, curve, 0.0)
            high, low = halves(value)
            hid_hi[s, r : r + chunk, :] = high
            hid_lo[s, r : r + chunk, :] = low
            slope_one[s, r : r + chunk, :] = slope
            curve_one[s, r : r + chunk, :] = curve
        yield

        act_two[s] = mm(lhs_two[...], stacked(hid_hi[s], hid_lo[s], hid_hi[s], hot[s], hot[s]))
        yield
        total = jnp.zeros((8, BLOCK), F32)
        for r in high_chunks:
            value, slope, curve = silu_parts_twice(act_two[s, r : r + chunk, :])
            head = across(head_w[r : r + chunk, :LANES])
            weighed = head * value
            for k in range(0, chunk, 8):
                total = total + weighed[k : k + 8, :]
            high, low = halves(head * slope)
            gate_hi[s, r : r + chunk, :] = high
            gate_lo[s, r : r + chunk, :] = low
            act_two[s, r : r + chunk, :] = value
            slope_two[s, r : r + chunk, :] = slope
            curve_two[s, r : r + chunk, :] = curve
        summed = jnp.sum(total, axis=0, keepdims=True)
        yield

        back_one[s] = mm(lhs_back[...], stacked(gate_hi[s], gate_lo[s], gate_hi[s]))
        yield
        totals = [jnp.zeros((8, BLOCK), F32) for _ in range(3)]
        for r in low_chunks:
            grad = back_one[s, r : r + chunk, :] * slope_one[s, r : r + chunk, :]
            high, low = halves(grad)
            near_hi[s, r : r + chunk, :] = high
            near_lo[s, r : r + chunk, :] = low
            for i in range(3):
                weighed = across(coord_w[r : r + chunk, i * LANES : (i + 1) * LANES]) * grad
                for k in range(0, chunk, 8):
                    totals[i] = totals[i] + weighed[k : k + 8, :]
        lead = [
            jnp.sum(totals[i], axis=0, keepdims=True)
            + back_one[s, MIDDLE + i : MIDDLE + i + 1, :]
            for i in range(3)
        ]

        predicted = jnp.tanh(2.0 * summed + head_bias)
        flank = 1.0 - predicted * predicted
        slope = [flank * q for q in lead]
        excess = slope[0] * slope[0] + slope[1] * slope[1] + slope[2] * slope[2] - 1.0
        capped = jnp.tanh(predicted / DELTA)
        misfit = DELTA * capped - DELTA * jnp.tanh(target / DELTA)
        fitting = jnp.sqrt(misfit * misfit + SMOOTH * SMOOTH)
        sum_loss[0:1, :] += valid * (fitting + EIK_WEIGHT * excess * excess)
        share = valid * (1.0 / ALL_POINTS)
        pull = [(4.0 * EIK_WEIGHT) * excess * v for v in slope]
        by_flank = sum(p * q for p, q in zip(pull, lead))
        by_predicted = misfit / fitting * (1.0 - capped * capped) - 2.0 * predicted * by_flank
        bar_out = share * by_predicted * flank
        sum_loss[1:2, :] += bar_out
        half_bar = 0.5 * bar_out
        pull = [share * flank * p for p in pull]

        last = stacked(blank5, *pull)
        for r in low_chunks:
            grad = 0.0
            for i in range(3):
                grad = grad + across(coord_w[r : r + chunk, i * LANES : (i + 1) * LANES]) * pull[i]
            through = grad * slope_one[s, r : r + chunk, :]
            if r + chunk == 256:
                inside = rows_of_lanes(0, (8, BLOCK)) < MIDDLE - 248
                end = jnp.where(inside, through[chunk - 8 :], last)
                through = stacked(through[: chunk - 8], end)
            high, low = halves(through)
            tang_hi[s, r : r + chunk, :] = high
            tang_lo[s, r : r + chunk, :] = low
            curve_one[s, r : r + chunk, :] = (
                grad * back_one[s, r : r + chunk, :] * curve_one[s, r : r + chunk, :]
            )
        yield
        act_tang[s] = mm(lhs_two[:, 0:768], stacked(tang_hi[s], tang_lo[s], tang_hi[s]))
        yield
        for r in high_chunks:
            tangent = act_tang[s, r : r + chunk, :]
            slope = slope_two[s, r : r + chunk, :]
            head = across(head_w[r : r + chunk, LANES:])
            bar = head * (half_bar * slope + tangent * curve_two[s, r : r + chunk, :])
            by_head = act_two[s, r : r + chunk, :] * bar_out + slope * tangent
            sum_head[r : r + chunk, :] += folded(by_head)
            high, low = halves(bar)
            bar_hi[s, r : r + chunk, :] = high
            bar_lo[s, r : r + chunk, :] = low
        yield

        back_one[s] = mm(lhs_back[...], stacked(bar_hi[s], bar_lo[s], bar_hi[s]))
        yield
        for r in low_chunks:
            bar = (
                back_one[s, r : r + chunk, :] * slope_one[s, r : r + chunk, :]
                + curve_one[s, r : r + chunk, :]
            )
            high, low = halves(bar)
            low_hi[s, r : r + chunk, :] = high
            low_lo[s, r : r + chunk, :] = low
        yield

        sum_two[...] += mm_nt(
            beside(bar_hi[s], bar_hi[s], bar_lo[s], gate_hi[s], gate_hi[s], gate_lo[s]),
            beside(hid_hi[s], hid_lo[s], hid_hi[s], tang_hi[s], tang_lo[s], tang_hi[s]),
        )
        hots = beside(hot[s], hot[s])
        sum_codes[256:768, :] += mm_nt(beside(bar_hi[s], bar_lo[s]), hots)
        sum_codes[0:256, :] += mm_nt(beside(low_hi[s], low_lo[s]), hots)
        seen = stacked(near_pieces[0], near_pieces[1]).astype(BF16)
        pulled = stacked(*pull, blank5)
        high = pulled.astype(BF16).astype(F32)
        pulled = stacked(high, pulled - high).astype(BF16)
        sum_coord[...] += mm_nt(
            beside(seen, seen, pulled, pulled),
            beside(low_hi[s], low_lo[s], near_hi[s], near_lo[s]),
        )

    def step_body(step, carry):
        waiting = [block_stages(step, s) for s in range(SUBS)]
        active = []
        while waiting or active:
            if waiting:
                active.append(waiting.pop(0))
            active = [work for work in active if next(work, work) is not work]
        return carry

    lax.fori_loop(0, SLOTS * DEVICES // (SUBS * BLOCK), step_body, 0)


def code_kernel(codes_ref, latent_w, sum_codes, sum_count, code_grad_ref, squares_ref):
    codes = codes_ref[...]
    count = jnp.sum(sum_count[...], axis=1, keepdims=True)
    turned_hi, turned_lo = halves(sum_codes[...].T)
    weight_hi, weight_lo = halves(latent_w[...])
    code_grad = mm(
        beside(turned_hi, turned_hi, turned_lo), stacked(weight_hi, weight_lo, weight_hi)
    )
    code_grad = code_grad + (2.0 * CODE_WEIGHT / ALL_POINTS) * count * codes
    code_grad_ref[...] = code_grad
    squares_ref[...] = jnp.broadcast_to(total_of(code_grad * code_grad), squares_ref.shape)


def norm_parts(direction, gain):
    root = lax.rsqrt(jnp.sum(direction * direction, axis=1, keepdims=True) + 1e-12)
    return root, gain * root


def weight_kernel(
    core_ref,
    codes_ref,
    first_w,
    second_w,
    sum_two,
    sum_codes,
    sum_coord,
    sum_head,
    sum_count,
    sum_loss,
    keep_ref,
    give_ref,
    flat,
    first_grad,
    second_grad,
):
    core = core_ref[0]
    codes = codes_ref[...]
    by_code = sum_codes[...]
    count = jnp.sum(sum_count[...], axis=1, keepdims=True)
    loss = jnp.sum(sum_loss[0:1, :], axis=1, keepdims=True)
    loss = loss + CODE_WEIGHT * total_of(count * codes * codes)
    loss = loss / ALL_POINTS

    code_hi, code_lo = halves(codes)
    by_hi, by_lo = halves(by_code)
    latent_grad = mm(beside(by_hi, by_hi, by_lo), stacked(code_hi, code_lo, code_hi))
    bias_grad = jnp.sum(by_code, axis=1, keepdims=True)

    lane = rows_of_lanes(1, (256, LANES))
    real = rows_of_lanes(0, (256, LANES)) < MIDDLE
    near_grad = sum_coord[0:8, :] + sum_coord[8:16, :]
    near_grad = stacked(near_grad, jnp.zeros((LANES - 8, 256), F32)).T
    near_grad = jnp.where(lane < 3, near_grad, 0.0)
    low_grad = latent_grad[0:256, :]
    first_low = first_w[:, : 2 * LANES]
    first_near = jnp.where(lane < 3, first_w[:, 2 * LANES :], 0.0)
    root, scale = norm_parts(beside(first_low, first_near), first_w[:, 2 * LANES + 3 : 2 * LANES + 4])
    along = jnp.sum(first_low * low_grad, axis=1, keepdims=True)
    along = along + jnp.sum(first_near * near_grad, axis=1, keepdims=True)
    inward = scale * root * root * along
    end = scale * near_grad - first_near * inward
    end = jnp.where(lane == 3, root * along, end)
    end = jnp.where(lane == 4, bias_grad[0:256, :], end)
    low_grad = scale * low_grad - first_low * inward
    first_grad[:, : 2 * LANES] = jnp.where(beside(real, real), low_grad, 0.0)
    first_grad[:, 2 * LANES :] = jnp.where(real, end, 0.0)

    is_hidden = rows_of_lanes(1, (HID, 256)) < MIDDLE
    hidden_grad = sum_two[...]
    moved = pltpu.roll(latent_grad[256:768, :], 256 - 3, 1)
    grad_a = jnp.where(is_hidden, hidden_grad, moved)
    grad_b = jnp.where(is_hidden, moved, hidden_grad)
    second_a = second_w[:, 0:256]
    second_b = second_w[:, 256:512]
    root, scale = norm_parts(second_w[:, 0:512], second_w[:, 512:513])
    along = jnp.sum(second_a * grad_a + second_b * grad_b, axis=1, keepdims=True)
    inward = scale * root * root * along
    second_grad[:, 0:256] = scale * grad_a - second_a * inward
    second_grad[:, 256:512] = scale * grad_b - second_b * inward
    head_grad = jnp.sum(sum_head[...], axis=1, keepdims=True)
    lane = rows_of_lanes(1, (HID, LANES))
    end = jnp.where(lane == 0, root * along, 0.0)
    end = jnp.where(lane == 1, bias_grad[256:768, :], end)
    second_grad[:, 512:640] = jnp.where(lane == 2, head_grad, end)

    flat[...] = jnp.zeros(flat.shape, F32)
    for adding in (False, True):
        pack_units(first_grad, flat, *FIRST_UNITS, adding)
        pack_units(second_grad, flat, *SECOND_UNITS, adding)
    row = HEAD_ENTRY // LANES
    lane = rows_of_lanes(1, (1, LANES))
    bias_total = jnp.sum(sum_loss[1:2, :], axis=1, keepdims=True)
    flat[row : row + 1, :] = flat[row : row + 1, :] + jnp.where(
        lane == HEAD_ENTRY % LANES, bias_total, 0.0
    )
    sub = rows_of_lanes(0, (8, LANES))
    wide = rows_of_lanes(1, (8, LANES))
    info = jnp.where((sub == 5) & (wide == 0), loss, 0.0)
    for which in range(2):

        @pl.when(core == which)
        def _(which=which):
            for d in range(DEVICES):
                z, c, w = d // 32, d // 16 % 2, d % 16
                target = keep_ref if c == which else give_ref
                box = (z * 16 + w) * BOX_ROWS
                first = d * SHARD_ROWS
                target[box : box + 16, :] = flat[first : first + 16, :]
                target[box + 16 : box + 24, :] = jnp.where(
                    sub < 5, flat[first + 16 : first + 24, :], info
                )


def vmem(count):
    return [pl.BlockSpec(memory_space=pltpu.VMEM)] * count


PARAMS = pltpu.CompilerParams(vmem_limit_bytes=48 * 1024 * 1024)


HBM = pl.BlockSpec(memory_space=pltpu.HBM)
SMEM = pl.BlockSpec(memory_space=pltpu.SMEM)


def pack_boxes(weights, coords, distances, index):
    return pl.pallas_call(
        pack_kernel,
        out_shape=jax.ShapeDtypeStruct((PEERS * BOX_ROWS, LANES), F32),
        in_specs=[HBM] * 4,
        out_specs=vmem(1)[0],
        scratch_shapes=[
            pltpu.VMEM(weights.shape, F32),
            pltpu.VMEM(coords.shape, F32),
            pltpu.VMEM(distances.shape, F32),
            pltpu.VMEM(index.shape, jnp.int32),
            pltpu.SemaphoreType.DMA((4,)),
        ],
        compiler_params=pltpu.CompilerParams(vmem_limit_bytes=60 * 1024 * 1024),
    )(weights, coords, distances, index)


def f32(*shape):
    return jax.ShapeDtypeStruct(shape, F32)


def run_loop(core, mine, other, codes):
    pair = (SUBS, 256, BLOCK)
    pair_two = (SUBS, HID, BLOCK)
    scratch = [
        ((FLAT_ROWS + 8, LANES), F32),
        ((256, 640), BF16),
        ((HID, 1280), BF16),
        ((256, 1536), BF16),
        ((256, 3 * LANES), F32),
        ((HID, 2 * LANES), F32),
        ((LANES, LANES), F32),
        (pair, F32),
        (pair, F32),
        (pair, F32),
        (pair, F32),
        (pair, BF16),
        (pair, BF16),
        (pair, BF16),
        (pair_two, F32),
        (pair_two, F32),
        (pair_two, F32),
        (pair_two, F32),
        (pair_two, BF16),
        (pair_two, BF16),
        (pair, BF16),
        (pair, BF16),
        (pair, BF16),
        (pair, BF16),
        (pair_two, BF16),
        (pair_two, BF16),
        (pair, BF16),
        (pair, BF16),
    ]
    return pl.pallas_call(
        loop_kernel,
        out_shape=(
            f32(256, 3 * LANES),
            f32(HID, 5 * LANES),
            f32(768, 256),
            f32(HID, 256),
            f32(768, 256),
            f32(16, 256),
            f32(HID, LANES),
            f32(CODE_ROWS, LANES),
            f32(2, BLOCK),
        ),
        in_specs=[SMEM] + vmem(3),
        out_specs=tuple(vmem(9)),
        scratch_shapes=[pltpu.VMEM(shape, dtype) for shape, dtype in scratch],
        compiler_params=PARAMS,
    )(core, mine, other, codes)


def weight_boxes(core, codes, first_w, second_w, *sums):
    return pl.pallas_call(
        weight_kernel,
        out_shape=(f32(PEERS * BOX_ROWS, LANES),) * 2,
        in_specs=[SMEM] + vmem(9),
        out_specs=tuple(vmem(2)),
        scratch_shapes=[
            pltpu.VMEM((FLAT_ROWS + 8, LANES), F32),
            pltpu.VMEM((256, 3 * LANES), F32),
            pltpu.VMEM((HID, 5 * LANES), F32),
        ],
        compiler_params=PARAMS,
    )(core, codes, first_w, second_w, *sums)


def code_grads(*args):
    return pl.pallas_call(
        code_kernel,
        out_shape=(f32(CODE_ROWS, LATENT), f32(8, LANES)),
        in_specs=vmem(4),
        out_specs=tuple(vmem(2)),
        compiler_params=PARAMS,
        cost_estimate=pl.CostEstimate(
            flops=2 * 3 * 768 * 256 * 256, bytes_accessed=3 << 20, transcendentals=0
        ),
    )(*args)


def adam_update(value, first, second, grad, rate):
    first_new = BETA_ONE * first + (1.0 - BETA_ONE) * grad
    second_new = BETA_TWO * second + (1.0 - BETA_TWO) * grad * grad
    first_hat = first_new / (1.0 - BETA_ONE**STEP)
    second_hat = second_new / (1.0 - BETA_TWO**STEP)
    value_new = value - rate * (first_hat / (jnp.sqrt(second_hat) + ADAM_EPS) + DECAY * value)
    return (value_new, first_new, second_new)


def shard_kernel(parts_ref, code_squares_ref, shard_ref, squares_ref):
    total = parts_ref[0:BOX_ROWS, :]
    for peer in range(1, PEERS):
        total = total + parts_ref[peer * BOX_ROWS : (peer + 1) * BOX_ROWS, :]
    shard_ref[...] = total
    grad = total[:SHARD_ROWS, :]
    squares_ref[...] = code_squares_ref[...] + total_of(grad * grad)


def sum_shards(parts, code_squares):
    return pl.pallas_call(
        shard_kernel,
        out_shape=(
            jax.ShapeDtypeStruct((BOX_ROWS, LANES), F32),
            jax.ShapeDtypeStruct((8, LANES), F32),
        ),
        in_specs=vmem(2),
        out_specs=tuple(vmem(2)),
        compiler_params=PARAMS,
    )(parts, code_squares)


def update_kernel(
    seen_ref,
    shard_ref,
    weights_ref,
    moment_one_ref,
    moment_two_ref,
    codes_ref,
    code_first_ref,
    code_second_ref,
    code_grad_ref,
    loss_out,
    norm_out,
    weights_out,
    moment_one_out,
    moment_two_out,
    weights_copy_out,
    codes_out,
    code_first_out,
    code_second_out,
    codes_copy_out,
):
    total = seen_ref[0:8, :]
    for peer in range(1, PEERS):
        total = total + seen_ref[peer * 8 : peer * 8 + 8, :]
    loss_out[...] = shard_ref[SHARD_ROWS : SHARD_ROWS + 1, 0:1]
    norm = jnp.sqrt(total[0:1, 0:1])
    norm_out[...] = norm
    factor = jnp.minimum(1.0, CLIP / (norm + 1e-06))
    value, first, second = adam_update(
        weights_ref[...],
        moment_one_ref[...],
        moment_two_ref[...],
        factor * shard_ref[0:SHARD_ROWS, :],
        WEIGHT_RATE,
    )
    weights_out[...] = value
    moment_one_out[...] = first
    moment_two_out[...] = second
    weights_copy_out[...] = value.astype(BF16)
    for r in range(0, CODE_ROWS, 32):
        rows = slice(r, r + 32)
        value, first, second = adam_update(
            codes_ref[rows, :],
            code_first_ref[rows, :],
            code_second_ref[rows, :],
            factor * code_grad_ref[rows, :],
            CODE_RATE,
        )
        codes_out[rows, :] = value
        code_first_out[rows, :] = first
        code_second_out[rows, :] = second
        codes_copy_out[rows, :] = value.astype(BF16)


def update_all(*args):
    scalar = jax.ShapeDtypeStruct((1, 1), F32)
    shard = [jax.ShapeDtypeStruct((SHARD_ROWS, LANES), t) for t in (F32, F32, F32, BF16)]
    table = [jax.ShapeDtypeStruct((CODE_ROWS, LATENT), t) for t in (F32, F32, F32, BF16)]
    return pl.pallas_call(
        update_kernel,
        out_shape=(scalar, scalar, *shard, *table),
        in_specs=vmem(9),
        out_specs=tuple(vmem(10)),
        compiler_params=PARAMS,
    )(*args)


def swap_cores(v):
    return lax.ppermute(v, "core", [(0, 1), (1, 0)])


def exchange(v):
    return lax.all_to_all(v, ("z", "wide"), split_axis=0, concat_axis=0)


def body(
    weights_flat,
    moment_one,
    moment_two,
    codes,
    code_first,
    code_second,
    coords,
    distances,
    shape_index,
):
    boxes = pack_boxes(
        weights_flat.reshape(SHARD_ROWS, LANES),
        coords,
        distances.reshape(1, POINTS_DEV),
        shape_index.reshape(1, POINTS_DEV),
    )
    mine = exchange(boxes.reshape(PEERS, BOX_ROWS, LANES))
    other = swap_cores(mine)
    core = lax.axis_index("core").astype(jnp.int32).reshape(1)
    first_w, second_w, latent_w, *sums = run_loop(
        core,
        mine.reshape(PEERS * BOX_ROWS, LANES),
        other.reshape(PEERS * BOX_ROWS, LANES),
        codes,
    )
    keep, give = weight_boxes(core, codes, first_w, second_w, *sums)
    pair_sum = (keep + swap_cores(give)).reshape(PEERS, BOX_ROWS, LANES)
    code_grad, code_squares = code_grads(codes, latent_w, sums[1], sums[4])
    shard, squares = sum_shards(exchange(pair_sum).reshape(PEERS * BOX_ROWS, LANES), code_squares)
    squares = squares + swap_cores(squares)
    seen = exchange(jnp.broadcast_to(squares, (PEERS, 8, LANES)))
    flat = lambda v: v.reshape(SHARD_ROWS, LANES)
    out = update_all(
        seen.reshape(PEERS * 8, LANES),
        shard,
        flat(weights_flat),
        flat(moment_one),
        flat(moment_two),
        codes,
        code_first,
        code_second,
        code_grad,
    )
    return (
        out[0].reshape(()),
        out[1].reshape(()),
        *[v.reshape(weights_flat.shape) for v in out[2:6]],
        *out[6:],
    )


def solution(mesh):
    parts = Mesh(mesh.devices.reshape(4, 2, 16), ALL)
    return jax.shard_map(
        body,
        mesh=parts,
        in_specs=(
            P(ALL),
            P(ALL),
            P(ALL),
            P(ALL, None),
            P(ALL, None),
            P(ALL, None),
            P(None, ALL),
            P(ALL),
            P(ALL),
        ),
        out_specs=(
            P(),
            P(),
            P(ALL),
            P(ALL),
            P(ALL),
            P(ALL),
            P(ALL, None),
            P(ALL, None),
            P(ALL, None),
            P(ALL, None),
        ),
        check_vma=False,
    )
```

```python
import jax
import jax.numpy as jnp
from jax import lax
from jax.experimental import pallas as pl
from jax.experimental.pallas import tpu as pltpu
from jax.sharding import Mesh
from jax.sharding import PartitionSpec as P

LATENT = 256
HID = 512
MIDDLE = HID - LATENT - 3
STEP = 10

DELTA = 0.1
SMOOTH = 0.01
CODE_WEIGHT = 0.001
EIK_WEIGHT = 0.1
CLIP = 0.001
WEIGHT_RATE = 0.02
CODE_RATE = 0.15
BETA_ONE = 0.9
BETA_TWO = 0.999
ADAM_EPS = 1e-08
DECAY = 0.01

LANES = 128
DEVICES = 128
PEERS = 64
SHARD_ROWS = 21
BOX_ROWS = 24
SLOTS = 16
POINTS_DEV = 1024
CODE_ROWS = 256
FLAT_ROWS = DEVICES * SHARD_ROWS
BLOCK = 256
SUBS = 4
TILES = BLOCK // LANES
ALL_POINTS = POINTS_DEV * DEVICES

F32 = jnp.float32
BF16 = jnp.bfloat16
ALL = ("z", "core", "wide")


def rows_of_lanes(lead, shape):
    return lax.broadcasted_iota(jnp.int32, shape, lead)


def halves(v):
    high = v.astype(BF16)
    return high, (v - high.astype(F32)).astype(BF16)


def thirds(v):
    high = v.astype(BF16).astype(F32)
    rest = v - high
    mid = rest.astype(BF16).astype(F32)
    return high, mid, rest - mid


def mm(a, b):
    return lax.dot_general(a, b, (((1,), (0,)), ((), ())), preferred_element_type=F32)


def mm_nt(a, b):
    return lax.dot_general(a, b, (((1,), (1,)), ((), ())), preferred_element_type=F32)


def beside(*parts):
    return jnp.concatenate(parts, axis=1)


def total_of(v):
    return jnp.sum(jnp.sum(v, axis=0, keepdims=True), axis=1, keepdims=True)


def stacked(*parts):
    return jnp.concatenate(parts, axis=0)


def pack_kernel(
    weights_hbm,
    coords_hbm,
    distances_hbm,
    index_hbm,
    out_ref,
    weights_ref,
    coords_ref,
    distances_ref,
    index_ref,
    sems,
):
    pairs = [
        (index_hbm, index_ref),
        (weights_hbm, weights_ref),
        (coords_hbm, coords_ref),
        (distances_hbm, distances_ref),
    ]
    copies = [
        pltpu.make_async_copy(source, target, sems.at[i])
        for i, (source, target) in enumerate(pairs)
    ]
    for copy in copies:
        copy.start()
    for copy in copies:
        copy.wait()
    shard = stacked(weights_ref[...], jnp.zeros((BOX_ROWS - SHARD_ROWS, LANES), F32))
    for peer in range(PEERS):
        out_ref[peer * BOX_ROWS : (peer + 1) * BOX_ROWS, :] = shard
    index = index_ref[...]
    owner = lax.shift_right_logical(index, 8)
    row = lax.bitwise_and(index, CODE_ROWS - 1)
    sent = (rows_of_lanes(0, (DEVICES, POINTS_DEV)) == owner).astype(F32)
    sent_low = sent.astype(BF16)
    width = 256
    earlier = rows_of_lanes(0, (width, width)) < rows_of_lanes(1, (width, width))
    earlier = earlier.astype(F32).astype(BF16)
    ones = jnp.ones((width, width), BF16)
    ranks = [
        mm(sent_low[:, : (part + 1) * width], stacked(*([ones] * part + [earlier])))
        for part in range(POINTS_DEV // width)
    ]
    placed = jnp.sum(sent * beside(*ranks), axis=0, keepdims=True).astype(jnp.int32)
    at_slot = rows_of_lanes(0, (SLOTS, POINTS_DEV)) == placed
    values = [coords_ref[i : i + 1, :] for i in range(3)]
    values += [distances_ref[...], (row + 1).astype(F32)]
    pieces = [[], [], []]
    for value in values:
        for k, third in enumerate(thirds(value)):
            pieces[k].append(jnp.where(at_slot, third, 0.0))
    spare = jnp.zeros((LANES - SLOTS * len(values), POINTS_DEV), F32)
    boxes = mm_nt(
        beside(sent_low, sent_low, sent_low),
        beside(*[stacked(*piece, spare).astype(BF16) for piece in pieces]),
    )
    for z in range(4):
        for core in range(2):
            first = z * 32 + core * 16
            out_ref[pl.ds(z * 16 * BOX_ROWS + SHARD_ROWS + core, 16, stride=BOX_ROWS), :] = boxes[
                first : first + 16, :
            ]


def unit_groups(count, stride_rows, extra, first_entry):
    for group in range(count):
        entry = first_entry + group * 8 * (stride_rows * LANES + extra)
        yield group, entry // LANES, entry % LANES


def unpack_units(flat_ref, out_ref, count, stride_rows, extra, first_entry):
    lane = rows_of_lanes(1, (8, LANES))
    slope = rows_of_lanes(0, (8, LANES)) * extra
    for group, first, shift in unit_groups(count, stride_rows, extra, first_entry):
        start = slope + shift
        wraps = shift + 7 * extra >= LANES
        turn = lax.bitwise_and(lane + start, LANES - 1)
        tiles = []
        for a in range(stride_rows + 2 + wraps):
            tile = flat_ref[pl.ds(first + a, 8, stride=stride_rows), :]
            tiles.append(jnp.take_along_axis(tile, turn, axis=1, mode="promise_in_bounds"))
        for c in range(stride_rows + 1):
            value = jnp.where(lane + start < LANES, tiles[c], tiles[c + 1])
            if wraps:
                value = jnp.where(lane + start < 2 * LANES, value, tiles[c + 2])
            out_ref[group * 8 : group * 8 + 8, c * LANES : (c + 1) * LANES] = value


def pack_units(value_ref, flat_ref, count, stride_rows, extra, first_entry, adding):
    lane = rows_of_lanes(1, (8, LANES))
    slope = rows_of_lanes(0, (8, LANES)) * extra
    zero = jnp.zeros((8, LANES), F32)
    for group, first, shift in unit_groups(count, stride_rows, extra, first_entry):
        start = slope + shift
        wraps = shift + 7 * extra >= LANES
        wanted = range(stride_rows, stride_rows + 1 + wraps + 1) if adding else range(stride_rows)
        rolled = {}

        turn = lax.bitwise_and(lane - start, LANES - 1)

        def tile(c, rolled=rolled, group=group, turn=turn):
            if c < 0 or c > stride_rows:
                return zero
            if c not in rolled:
                value = value_ref[group * 8 : group * 8 + 8, c * LANES : (c + 1) * LANES]
                rolled[c] = jnp.take_along_axis(value, turn, axis=1, mode="promise_in_bounds")
            return rolled[c]

        for a in wanted:
            value = jnp.where(lane >= start, tile(a), tile(a - 1))
            if wraps:
                value = jnp.where(lane >= start - LANES, value, tile(a - 2))
            rows = pl.ds(first + a, 8, stride=stride_rows)
            if adding:
                flat_ref[rows, :] = flat_ref[rows, :] + value
            else:
                flat_ref[rows, :] = value


FIRST_UNITS = (32, 2, 5, 0)
SECOND_UNITS = (64, 4, 3, MIDDLE * (LATENT + 5))
HEAD_ENTRY = MIDDLE * (LATENT + 5) + HID * (HID + 3)


def across(column):
    return beside(*[column] * TILES)


def folded(v):
    return sum(v[:, i * LANES : (i + 1) * LANES] for i in range(TILES))


def silu_parts(half):
    gate = jnp.tanh(half)
    low = 0.5 * gate
    bend = 0.5 - gate * low
    bent = half * gate
    return half + bent, (0.5 + low) + half * bend, bend * (1.0 - bent)


def silu_parts_twice(half):
    gate = jnp.tanh(half)
    bend = 1.0 - gate * gate
    bent = half * gate
    return half + bent, (1.0 + gate) + half * bend, bend * (1.0 - bent)


def loop_kernel(
    core_ref,
    mine_ref,
    other_ref,
    codes_ref,
    first_w,
    second_w,
    latent_w,
    sum_two,
    sum_codes,
    sum_coord,
    sum_head,
    sum_count,
    sum_loss,
    flat,
    lhs_one,
    lhs_two,
    lhs_back,
    coord_w,
    head_w,
    spots,
    act_one,
    slope_one,
    curve_one,
    back_one,
    hid_hi,
    hid_lo,
    hot,
    hot_turned,
    act_two,
    slope_two,
    curve_two,
    act_tang,
    gate_hi,
    gate_lo,
    tang_hi,
    tang_lo,
    bar_hi,
    bar_lo,
    low_hi,
    low_lo,
):
    core = core_ref[0]

    for which in range(2):

        @pl.when(core == which)
        def _(which=which):
            for d in range(DEVICES):
                z, c, w = d // 32, d // 16 % 2, d % 16
                box = (z * 16 + w) * BOX_ROWS
                source = mine_ref if c == which else other_ref
                flat[d * SHARD_ROWS : d * SHARD_ROWS + BOX_ROWS, :] = source[box : box + BOX_ROWS, :]
            rows = pl.ds(SHARD_ROWS + which, PEERS, stride=BOX_ROWS)
            spots[...] = stacked(mine_ref[rows, :], other_ref[rows, :]).T

    unpack_units(flat, first_w, *FIRST_UNITS)
    unpack_units(flat, second_w, *SECOND_UNITS)
    head_bias = flat[HEAD_ENTRY // LANES : HEAD_ENTRY // LANES + 1, :][
        :, HEAD_ENTRY % LANES : HEAD_ENTRY % LANES + 1
    ]

    lane = rows_of_lanes(1, (256, LANES))
    unit = rows_of_lanes(0, (256, LANES))
    real = unit < MIDDLE

    first_low = jnp.where(beside(real, real), first_w[:, : 2 * LANES], 0.0)
    first_end = jnp.where(real, first_w[:, 2 * LANES :], 0.0)
    first_near = jnp.where(lane < 3, first_end, 0.0)
    first_gain = first_end[:, 3:4]
    first_bias = first_end[:, 4:5]
    first_w[:, : 2 * LANES] = first_low
    first_w[:, 2 * LANES :] = first_end
    _, first_scale = norm_parts(beside(first_low, first_near), first_gain)
    first_low = first_low * first_scale
    first_near = first_near * first_scale
    latent_w[0:256, :] = first_low
    for i in range(3):
        coord_w[:, i * LANES : (i + 1) * LANES] = jnp.broadcast_to(
            0.5 * first_near[:, i : i + 1], (256, LANES)
        )

    second_a = second_w[:, 0:256]
    second_b = second_w[:, 256:512]
    second_gain = second_w[:, 512:513]
    second_bias = second_w[:, 513:514]
    head = jnp.broadcast_to(second_w[:, 514:515], (HID, LANES))
    head_w[:, :LANES] = 0.5 * head
    head_w[:, LANES:] = head
    _, second_scale = norm_parts(second_w[:, 0:512], second_gain)
    second_a = second_a * second_scale
    second_b = second_b * second_scale
    is_hidden = rows_of_lanes(1, (HID, 256)) < MIDDLE
    hidden_cols = jnp.where(is_hidden, second_a, second_b)
    latent_cols = pltpu.roll(jnp.where(is_hidden, second_b, second_a), 3, 1)
    latent_w[256:768, :] = latent_cols

    hidden_hi, hidden_lo = halves(0.5 * hidden_cols)
    lhs_two[:, 0:256] = hidden_hi
    lhs_two[:, 256:512] = hidden_hi
    lhs_two[:, 512:768] = hidden_lo
    back_hi, back_lo = halves(hidden_cols.T)
    lhs_back[:, 0:512] = back_hi
    lhs_back[:, 512:1024] = back_hi
    lhs_back[:, 1024:1536] = back_lo

    code_hi, code_lo = halves(codes_ref[...])
    weight_hi, weight_lo = halves(latent_w[...])
    by_code = mm_nt(
        beside(weight_hi, weight_hi, weight_lo), beside(code_hi, code_lo, code_hi)
    )
    one_hi, one_lo = halves(0.5 * (by_code[0:256, :] + first_bias))
    lhs_one[:, 0:256] = one_hi
    lhs_one[:, 256:512] = one_lo
    two_hi, two_lo = halves(0.5 * (by_code[256:768, :] + second_bias))
    lhs_two[:, 768:1024] = two_hi
    lhs_two[:, 1024:1280] = two_lo

    for ref in (sum_two, sum_codes, sum_coord, sum_head, sum_count, sum_loss):
        ref[...] = jnp.zeros(ref.shape, F32)

    def feature(which, step, sub):
        first = which * SLOTS + (step * SUBS + sub) * TILES
        return beside(*[spots[pl.ds(first + i, 1), :] for i in range(TILES)])

    blank5 = jnp.zeros((5, BLOCK), F32)
    chunk = 8192 // BLOCK
    low_chunks = range(0, 256, chunk)
    high_chunks = range(0, HID, chunk)

    def block_stages(step, s):
        place = [feature(i, step, s) for i in range(3)]
        target = feature(3, step, s)
        code_row = feature(4, step, s)
        valid = (code_row > 0.5).astype(F32)

        wanted = code_row - 1.0
        for r in range(0, CODE_ROWS, chunk):
            row = (rows_of_lanes(0, (chunk, BLOCK)) + r).astype(F32)
            mark = jnp.where(row == wanted, 1.0, 0.0)
            hot[s, r : r + chunk, :] = mark.astype(BF16)
            sum_count[r : r + chunk, :] += folded(mark)
        for i in range(TILES):
            wanted = jnp.broadcast_to(code_row[:, i * LANES : (i + 1) * LANES] - 1.0, (LANES, LANES)).T
            for c in range(0, CODE_ROWS, LANES):
                code = (rows_of_lanes(1, (LANES, LANES)) + c).astype(F32)
                mark = jnp.where(code == wanted, 1.0, 0.0).astype(BF16)
                hot_turned[s, i * LANES : (i + 1) * LANES, c : c + LANES] = mark
        yield

        act_one[s] = mm(lhs_one[...], stacked(hot[s], hot[s]))
        yield
        last = stacked(blank5, *place)
        for r in low_chunks:
            pre = act_one[s, r : r + chunk, :]
            for i in range(3):
                pre = pre + across(coord_w[r : r + chunk, i * LANES : (i + 1) * LANES]) * place[i]
            value, slope, curve = silu_parts(pre)
            if r + chunk == 256:
                inside = rows_of_lanes(0, (chunk, BLOCK)) + r < MIDDLE
                end = jnp.where(inside[chunk - 8 :], value[chunk - 8 :], last)
                value = stacked(value[: chunk - 8], end)
                slope = jnp.where(inside, slope, 0.0)
                curve = jnp.where(inside, curve, 0.0)
            high, low = halves(value)
            hid_hi[s, r : r + chunk, :] = high
            hid_lo[s, r : r + chunk, :] = low
            slope_one[s, r : r + chunk, :] = slope
            curve_one[s, r : r + chunk, :] = curve
        yield

        act_two[s] = mm(lhs_two[...], stacked(hid_hi[s], hid_lo[s], hid_hi[s], hot[s], hot[s]))
        yield
        total = jnp.zeros((8, BLOCK), F32)
        for r in high_chunks:
            value, slope, curve = silu_parts_twice(act_two[s, r : r + chunk, :])
            head = across(head_w[r : r + chunk, :LANES])
            weighed = head * value
            for k in range(0, chunk, 8):
                total = total + weighed[k : k + 8, :]
            high, low = halves(head * slope)
            gate_hi[s, r : r + chunk, :] = high
            gate_lo[s, r : r + chunk, :] = low
            act_two[s, r : r + chunk, :] = value
            slope_two[s, r : r + chunk, :] = slope
            curve_two[s, r : r + chunk, :] = curve
        summed = jnp.sum(total, axis=0, keepdims=True)
        yield

        back_one[s] = mm(lhs_back[...], stacked(gate_hi[s], gate_lo[s], gate_hi[s]))
        yield
        totals = [jnp.zeros((8, BLOCK), F32) for _ in range(3)]
        for r in low_chunks:
            grad = back_one[s, r : r + chunk, :] * slope_one[s, r : r + chunk, :]
            for i in range(3):
                weighed = across(coord_w[r : r + chunk, i * LANES : (i + 1) * LANES]) * grad
                for k in range(0, chunk, 8):
                    totals[i] = totals[i] + weighed[k : k + 8, :]
        lead = [
            2.0 * jnp.sum(totals[i], axis=0, keepdims=True)
            + back_one[s, MIDDLE + i : MIDDLE + i + 1, :]
            for i in range(3)
        ]

        predicted = jnp.tanh(2.0 * summed + head_bias)
        flank = 1.0 - predicted * predicted
        slope = [flank * q for q in lead]
        excess = slope[0] * slope[0] + slope[1] * slope[1] + slope[2] * slope[2] - 1.0
        capped = jnp.tanh(predicted / DELTA)
        misfit = DELTA * capped - DELTA * jnp.tanh(target / DELTA)
        fitting = jnp.sqrt(misfit * misfit + SMOOTH * SMOOTH)
        sum_loss[0:1, :] += valid * (fitting + EIK_WEIGHT * excess * excess)
        share = valid * (1.0 / ALL_POINTS)
        pull = [(4.0 * EIK_WEIGHT) * excess * v for v in slope]
        by_flank = sum(p * q for p, q in zip(pull, lead))
        by_predicted = misfit / fitting * (1.0 - capped * capped) - 2.0 * predicted * by_flank
        bar_out = share * by_predicted * flank
        sum_loss[1:2, :] += bar_out
        half_bar = 0.5 * bar_out
        pull = [share * flank * p for p in pull]

        last = stacked(blank5, *pull)
        twice = [2.0 * p for p in pull]
        for r in low_chunks:
            grad = 0.0
            for i in range(3):
                grad = grad + across(coord_w[r : r + chunk, i * LANES : (i + 1) * LANES]) * twice[i]
            slope = slope_one[s, r : r + chunk, :]
            back = back_one[s, r : r + chunk, :]
            near = back * slope
            for i in range(3):
                sum_coord[r : r + chunk, i * LANES : (i + 1) * LANES] += folded(near * pull[i])
            through = grad * slope
            if r + chunk == 256:
                inside = rows_of_lanes(0, (8, BLOCK)) < MIDDLE - 248
                end = jnp.where(inside, through[chunk - 8 :], last)
                through = stacked(through[: chunk - 8], end)
            high, low = halves(through)
            tang_hi[s, r : r + chunk, :] = high
            tang_lo[s, r : r + chunk, :] = low
            curve_one[s, r : r + chunk, :] = (
                grad * back * curve_one[s, r : r + chunk, :]
            )
        yield
        act_tang[s] = mm(lhs_two[:, 0:768], stacked(tang_hi[s], tang_lo[s], tang_hi[s]))
        yield
        for r in high_chunks:
            tangent = act_tang[s, r : r + chunk, :]
            slope = slope_two[s, r : r + chunk, :]
            head = across(head_w[r : r + chunk, LANES:])
            bar = head * (half_bar * slope + tangent * curve_two[s, r : r + chunk, :])
            by_head = act_two[s, r : r + chunk, :] * bar_out + slope * tangent
            sum_head[r : r + chunk, :] += folded(by_head)
            high, low = halves(bar)
            bar_hi[s, r : r + chunk, :] = high
            bar_lo[s, r : r + chunk, :] = low
        yield

        back_one[s] = mm(lhs_back[...], stacked(bar_hi[s], bar_lo[s], bar_hi[s]))
        yield
        for r in low_chunks:
            bar = (
                back_one[s, r : r + chunk, :] * slope_one[s, r : r + chunk, :]
                + curve_one[s, r : r + chunk, :]
            )
            for i in range(3):
                sum_coord[r : r + chunk, i * LANES : (i + 1) * LANES] += folded(bar * place[i])
            high, low = halves(bar)
            low_hi[s, r : r + chunk, :] = high
            low_lo[s, r : r + chunk, :] = low
        yield

        sum_two[...] += mm_nt(
            beside(bar_hi[s], bar_hi[s], bar_lo[s], gate_hi[s], gate_hi[s], gate_lo[s]),
            beside(hid_hi[s], hid_lo[s], hid_hi[s], tang_hi[s], tang_lo[s], tang_hi[s]),
        )
        turned = stacked(hot_turned[s], hot_turned[s])
        sum_codes[256:768, :] += mm(beside(bar_hi[s], bar_lo[s]), turned)
        sum_codes[0:256, :] += mm(beside(low_hi[s], low_lo[s]), turned)

    def step_body(step, carry):
        waiting = [block_stages(step, s) for s in range(SUBS)]
        active = []
        while waiting or active:
            if waiting:
                active.append(waiting.pop(0))
            active = [work for work in active if next(work, work) is not work]
        return carry

    lax.fori_loop(0, SLOTS * DEVICES // (SUBS * BLOCK), step_body, 0)


def code_kernel(codes_ref, latent_w, sum_codes, sum_count, code_grad_ref, squares_ref):
    codes = codes_ref[...]
    count = jnp.sum(sum_count[...], axis=1, keepdims=True)
    turned_hi, turned_lo = halves(sum_codes[...].T)
    weight_hi, weight_lo = halves(latent_w[...])
    code_grad = mm(
        beside(turned_hi, turned_hi, turned_lo), stacked(weight_hi, weight_lo, weight_hi)
    )
    code_grad = code_grad + (2.0 * CODE_WEIGHT / ALL_POINTS) * count * codes
    code_grad_ref[...] = code_grad
    squares_ref[...] = jnp.broadcast_to(total_of(code_grad * code_grad), squares_ref.shape)


def norm_parts(direction, gain):
    root = lax.rsqrt(jnp.sum(direction * direction, axis=1, keepdims=True) + 1e-12)
    return root, gain * root


def weight_kernel(
    core_ref,
    codes_ref,
    first_w,
    second_w,
    sum_two,
    sum_codes,
    sum_coord,
    sum_head,
    sum_count,
    sum_loss,
    keep_ref,
    give_ref,
    flat,
    first_grad,
    second_grad,
):
    core = core_ref[0]
    codes = codes_ref[...]
    by_code = sum_codes[...]
    count = jnp.sum(sum_count[...], axis=1, keepdims=True)
    loss = jnp.sum(sum_loss[0:1, :], axis=1, keepdims=True)
    loss = loss + CODE_WEIGHT * total_of(count * codes * codes)
    loss = loss / ALL_POINTS

    code_hi, code_lo = halves(codes)
    by_hi, by_lo = halves(by_code)
    latent_grad = mm(beside(by_hi, by_hi, by_lo), stacked(code_hi, code_lo, code_hi))
    bias_grad = jnp.sum(by_code, axis=1, keepdims=True)

    lane = rows_of_lanes(1, (256, LANES))
    real = rows_of_lanes(0, (256, LANES)) < MIDDLE
    near_grad = 0.0
    for i in range(3):
        column = jnp.sum(sum_coord[:, i * LANES : (i + 1) * LANES], axis=1, keepdims=True)
        near_grad = jnp.where(lane == i, column, near_grad)
    low_grad = latent_grad[0:256, :]
    first_low = first_w[:, : 2 * LANES]
    first_near = jnp.where(lane < 3, first_w[:, 2 * LANES :], 0.0)
    root, scale = norm_parts(beside(first_low, first_near), first_w[:, 2 * LANES + 3 : 2 * LANES + 4])
    along = jnp.sum(first_low * low_grad, axis=1, keepdims=True)
    along = along + jnp.sum(first_near * near_grad, axis=1, keepdims=True)
    inward = scale * root * root * along
    end = scale * near_grad - first_near * inward
    end = jnp.where(lane == 3, root * along, end)
    end = jnp.where(lane == 4, bias_grad[0:256, :], end)
    low_grad = scale * low_grad - first_low * inward
    first_grad[:, : 2 * LANES] = jnp.where(beside(real, real), low_grad, 0.0)
    first_grad[:, 2 * LANES :] = jnp.where(real, end, 0.0)

    is_hidden = rows_of_lanes(1, (HID, 256)) < MIDDLE
    hidden_grad = sum_two[...]
    moved = pltpu.roll(latent_grad[256:768, :], 256 - 3, 1)
    grad_a = jnp.where(is_hidden, hidden_grad, moved)
    grad_b = jnp.where(is_hidden, moved, hidden_grad)
    second_a = second_w[:, 0:256]
    second_b = second_w[:, 256:512]
    root, scale = norm_parts(second_w[:, 0:512], second_w[:, 512:513])
    along = jnp.sum(second_a * grad_a + second_b * grad_b, axis=1, keepdims=True)
    inward = scale * root * root * along
    second_grad[:, 0:256] = scale * grad_a - second_a * inward
    second_grad[:, 256:512] = scale * grad_b - second_b * inward
    head_grad = jnp.sum(sum_head[...], axis=1, keepdims=True)
    lane = rows_of_lanes(1, (HID, LANES))
    end = jnp.where(lane == 0, root * along, 0.0)
    end = jnp.where(lane == 1, bias_grad[256:768, :], end)
    second_grad[:, 512:640] = jnp.where(lane == 2, head_grad, end)

    flat[...] = jnp.zeros(flat.shape, F32)
    for adding in (False, True):
        pack_units(first_grad, flat, *FIRST_UNITS, adding)
        pack_units(second_grad, flat, *SECOND_UNITS, adding)
    row = HEAD_ENTRY // LANES
    lane = rows_of_lanes(1, (1, LANES))
    bias_total = jnp.sum(sum_loss[1:2, :], axis=1, keepdims=True)
    flat[row : row + 1, :] = flat[row : row + 1, :] + jnp.where(
        lane == HEAD_ENTRY % LANES, bias_total, 0.0
    )
    sub = rows_of_lanes(0, (8, LANES))
    wide = rows_of_lanes(1, (8, LANES))
    info = jnp.where((sub == 5) & (wide == 0), loss, 0.0)
    for which in range(2):

        @pl.when(core == which)
        def _(which=which):
            for d in range(DEVICES):
                z, c, w = d // 32, d // 16 % 2, d % 16
                target = keep_ref if c == which else give_ref
                box = (z * 16 + w) * BOX_ROWS
                first = d * SHARD_ROWS
                target[box : box + 16, :] = flat[first : first + 16, :]
                target[box + 16 : box + 24, :] = jnp.where(
                    sub < 5, flat[first + 16 : first + 24, :], info
                )


def vmem(count):
    return [pl.BlockSpec(memory_space=pltpu.VMEM)] * count


PARAMS = pltpu.CompilerParams(vmem_limit_bytes=48 * 1024 * 1024)


HBM = pl.BlockSpec(memory_space=pltpu.HBM)
SMEM = pl.BlockSpec(memory_space=pltpu.SMEM)


def pack_boxes(weights, coords, distances, index):
    return pl.pallas_call(
        pack_kernel,
        out_shape=jax.ShapeDtypeStruct((PEERS * BOX_ROWS, LANES), F32),
        in_specs=[HBM] * 4,
        out_specs=vmem(1)[0],
        scratch_shapes=[
            pltpu.VMEM(weights.shape, F32),
            pltpu.VMEM(coords.shape, F32),
            pltpu.VMEM(distances.shape, F32),
            pltpu.VMEM(index.shape, jnp.int32),
            pltpu.SemaphoreType.DMA((4,)),
        ],
        compiler_params=pltpu.CompilerParams(vmem_limit_bytes=60 * 1024 * 1024),
    )(weights, coords, distances, index)


def f32(*shape):
    return jax.ShapeDtypeStruct(shape, F32)


def run_loop(core, mine, other, codes):
    pair = (SUBS, 256, BLOCK)
    pair_two = (SUBS, HID, BLOCK)
    scratch = [
        ((FLAT_ROWS + 8, LANES), F32),
        ((256, 512), BF16),
        ((HID, 1280), BF16),
        ((256, 1536), BF16),
        ((256, 3 * LANES), F32),
        ((HID, 2 * LANES), F32),
        ((LANES, LANES), F32),
        (pair, F32),
        (pair, F32),
        (pair, F32),
        (pair, F32),
        (pair, BF16),
        (pair, BF16),
        (pair, BF16),
        ((SUBS, BLOCK, CODE_ROWS), BF16),
        (pair_two, F32),
        (pair_two, F32),
        (pair_two, F32),
        (pair_two, F32),
        (pair_two, BF16),
        (pair_two, BF16),
        (pair, BF16),
        (pair, BF16),
        (pair_two, BF16),
        (pair_two, BF16),
        (pair, BF16),
        (pair, BF16),
    ]
    return pl.pallas_call(
        loop_kernel,
        out_shape=(
            f32(256, 3 * LANES),
            f32(HID, 5 * LANES),
            f32(768, 256),
            f32(HID, 256),
            f32(768, 256),
            f32(256, 3 * LANES),
            f32(HID, LANES),
            f32(CODE_ROWS, LANES),
            f32(2, BLOCK),
        ),
        in_specs=[SMEM] + vmem(3),
        out_specs=tuple(vmem(9)),
        scratch_shapes=[pltpu.VMEM(shape, dtype) for shape, dtype in scratch],
        compiler_params=PARAMS,
    )(core, mine, other, codes)


def weight_boxes(core, codes, first_w, second_w, *sums):
    return pl.pallas_call(
        weight_kernel,
        out_shape=(f32(PEERS * BOX_ROWS, LANES),) * 2,
        in_specs=[SMEM] + vmem(9),
        out_specs=tuple(vmem(2)),
        scratch_shapes=[
            pltpu.VMEM((FLAT_ROWS + 8, LANES), F32),
            pltpu.VMEM((256, 3 * LANES), F32),
            pltpu.VMEM((HID, 5 * LANES), F32),
        ],
        compiler_params=PARAMS,
    )(core, codes, first_w, second_w, *sums)


def code_grads(*args):
    return pl.pallas_call(
        code_kernel,
        out_shape=(f32(CODE_ROWS, LATENT), f32(8, LANES)),
        in_specs=vmem(4),
        out_specs=tuple(vmem(2)),
        compiler_params=PARAMS,
        cost_estimate=pl.CostEstimate(
            flops=2 * 3 * 768 * 256 * 256, bytes_accessed=3 << 20, transcendentals=0
        ),
    )(*args)


def adam_update(value, first, second, grad, rate):
    first_new = BETA_ONE * first + (1.0 - BETA_ONE) * grad
    second_new = BETA_TWO * second + (1.0 - BETA_TWO) * grad * grad
    first_hat = first_new / (1.0 - BETA_ONE**STEP)
    second_hat = second_new / (1.0 - BETA_TWO**STEP)
    value_new = value - rate * (first_hat / (jnp.sqrt(second_hat) + ADAM_EPS) + DECAY * value)
    return (value_new, first_new, second_new)


def shard_kernel(parts_ref, code_squares_ref, shard_ref, squares_ref):
    total = parts_ref[0:BOX_ROWS, :]
    for peer in range(1, PEERS):
        total = total + parts_ref[peer * BOX_ROWS : (peer + 1) * BOX_ROWS, :]
    shard_ref[...] = total
    grad = total[:SHARD_ROWS, :]
    squares_ref[...] = code_squares_ref[...] + total_of(grad * grad)


def sum_shards(parts, code_squares):
    return pl.pallas_call(
        shard_kernel,
        out_shape=(
            jax.ShapeDtypeStruct((BOX_ROWS, LANES), F32),
            jax.ShapeDtypeStruct((8, LANES), F32),
        ),
        in_specs=vmem(2),
        out_specs=tuple(vmem(2)),
        compiler_params=PARAMS,
    )(parts, code_squares)


def update_kernel(
    seen_ref,
    shard_ref,
    weights_ref,
    moment_one_ref,
    moment_two_ref,
    codes_ref,
    code_first_ref,
    code_second_ref,
    code_grad_ref,
    loss_out,
    norm_out,
    weights_out,
    moment_one_out,
    moment_two_out,
    weights_copy_out,
    codes_out,
    code_first_out,
    code_second_out,
    codes_copy_out,
):
    total = seen_ref[0:8, :]
    for peer in range(1, PEERS):
        total = total + seen_ref[peer * 8 : peer * 8 + 8, :]
    loss_out[...] = shard_ref[SHARD_ROWS : SHARD_ROWS + 1, 0:1]
    norm = jnp.sqrt(total[0:1, 0:1])
    norm_out[...] = norm
    factor = jnp.minimum(1.0, CLIP / (norm + 1e-06))
    value, first, second = adam_update(
        weights_ref[...],
        moment_one_ref[...],
        moment_two_ref[...],
        factor * shard_ref[0:SHARD_ROWS, :],
        WEIGHT_RATE,
    )
    weights_out[...] = value
    moment_one_out[...] = first
    moment_two_out[...] = second
    weights_copy_out[...] = value.astype(BF16)
    for r in range(0, CODE_ROWS, 32):
        rows = slice(r, r + 32)
        value, first, second = adam_update(
            codes_ref[rows, :],
            code_first_ref[rows, :],
            code_second_ref[rows, :],
            factor * code_grad_ref[rows, :],
            CODE_RATE,
        )
        codes_out[rows, :] = value
        code_first_out[rows, :] = first
        code_second_out[rows, :] = second
        codes_copy_out[rows, :] = value.astype(BF16)


def update_all(*args):
    scalar = jax.ShapeDtypeStruct((1, 1), F32)
    shard = [jax.ShapeDtypeStruct((SHARD_ROWS, LANES), t) for t in (F32, F32, F32, BF16)]
    table = [jax.ShapeDtypeStruct((CODE_ROWS, LATENT), t) for t in (F32, F32, F32, BF16)]
    return pl.pallas_call(
        update_kernel,
        out_shape=(scalar, scalar, *shard, *table),
        in_specs=vmem(9),
        out_specs=tuple(vmem(10)),
        compiler_params=PARAMS,
    )(*args)


def swap_cores(v):
    return lax.ppermute(v, "core", [(0, 1), (1, 0)])


def exchange(v):
    return lax.all_to_all(v, ("z", "wide"), split_axis=0, concat_axis=0)


def body(
    weights_flat,
    moment_one,
    moment_two,
    codes,
    code_first,
    code_second,
    coords,
    distances,
    shape_index,
):
    boxes = pack_boxes(
        weights_flat.reshape(SHARD_ROWS, LANES),
        coords,
        distances.reshape(1, POINTS_DEV),
        shape_index.reshape(1, POINTS_DEV),
    )
    mine = exchange(boxes.reshape(PEERS, BOX_ROWS, LANES))
    other = swap_cores(mine)
    core = lax.axis_index("core").astype(jnp.int32).reshape(1)
    first_w, second_w, latent_w, *sums = run_loop(
        core,
        mine.reshape(PEERS * BOX_ROWS, LANES),
        other.reshape(PEERS * BOX_ROWS, LANES),
        codes,
    )
    keep, give = weight_boxes(core, codes, first_w, second_w, *sums)
    pair_sum = (keep + swap_cores(give)).reshape(PEERS, BOX_ROWS, LANES)
    code_grad, code_squares = code_grads(codes, latent_w, sums[1], sums[4])
    pair_sum, code_grad, code_squares = lax.optimization_barrier((pair_sum, code_grad, code_squares))
    shard, squares = sum_shards(exchange(pair_sum).reshape(PEERS * BOX_ROWS, LANES), code_squares)
    squares = squares + swap_cores(squares)
    seen = exchange(jnp.broadcast_to(squares, (PEERS, 8, LANES)))
    flat = lambda v: v.reshape(SHARD_ROWS, LANES)
    out = update_all(
        seen.reshape(PEERS * 8, LANES),
        shard,
        flat(weights_flat),
        flat(moment_one),
        flat(moment_two),
        codes,
        code_first,
        code_second,
        code_grad,
    )
    return (
        out[0].reshape(()),
        out[1].reshape(()),
        *[v.reshape(weights_flat.shape) for v in out[2:6]],
        *out[6:],
    )


def solution(mesh):
    parts = Mesh(mesh.devices.reshape(4, 2, 16), ALL)
    return jax.shard_map(
        body,
        mesh=parts,
        in_specs=(
            P(ALL),
            P(ALL),
            P(ALL),
            P(ALL, None),
            P(ALL, None),
            P(ALL, None),
            P(None, ALL),
            P(ALL),
            P(ALL),
        ),
        out_specs=(
            P(),
            P(),
            P(ALL),
            P(ALL),
            P(ALL),
            P(ALL),
            P(ALL, None),
            P(ALL, None),
            P(ALL, None),
            P(ALL, None),
        ),
        check_vma=False,
    )
```

```python
import jax
import jax.numpy as jnp
from jax import lax
from jax.experimental import pallas as pl
from jax.experimental.pallas import tpu as pltpu
from jax.sharding import Mesh
from jax.sharding import PartitionSpec as P

LATENT = 256
HID = 512
MIDDLE = HID - LATENT - 3
STEP = 10

DELTA = 0.1
SMOOTH = 0.01
CODE_WEIGHT = 0.001
EIK_WEIGHT = 0.1
CLIP = 0.001
WEIGHT_RATE = 0.02
CODE_RATE = 0.15
BETA_ONE = 0.9
BETA_TWO = 0.999
ADAM_EPS = 1e-08
DECAY = 0.01

LANES = 128
DEVICES = 128
PEERS = 64
SHARD_ROWS = 21
BOX_ROWS = 24
SLOTS = 16
POINTS_DEV = 1024
CODE_ROWS = 256
FLAT_ROWS = DEVICES * SHARD_ROWS
BLOCK = 512
SUBS = 4
TILES = BLOCK // LANES
ALL_POINTS = POINTS_DEV * DEVICES

F32 = jnp.float32
BF16 = jnp.bfloat16
ALL = ("z", "core", "wide")


def rows_of_lanes(lead, shape):
    return lax.broadcasted_iota(jnp.int32, shape, lead)


def halves(v):
    high = v.astype(BF16)
    return high, (v - high.astype(F32)).astype(BF16)


def thirds(v):
    high = v.astype(BF16).astype(F32)
    rest = v - high
    mid = rest.astype(BF16).astype(F32)
    return high, mid, rest - mid


def mm(a, b):
    return lax.dot_general(a, b, (((1,), (0,)), ((), ())), preferred_element_type=F32)


def mm_nt(a, b):
    return lax.dot_general(a, b, (((1,), (1,)), ((), ())), preferred_element_type=F32)


def beside(*parts):
    return jnp.concatenate(parts, axis=1)


def total_of(v):
    return jnp.sum(jnp.sum(v, axis=0, keepdims=True), axis=1, keepdims=True)


def stacked(*parts):
    return jnp.concatenate(parts, axis=0)


def pack_kernel(
    weights_hbm,
    coords_hbm,
    distances_hbm,
    index_hbm,
    out_hbm,
    weights_ref,
    coords_ref,
    distances_ref,
    index_ref,
    staged,
    sems,
):
    pairs = [
        (index_hbm, index_ref),
        (weights_hbm, weights_ref),
        (coords_hbm, coords_ref),
        (distances_hbm, distances_ref),
    ]
    copies = [
        pltpu.make_async_copy(source, target, sems.at[i])
        for i, (source, target) in enumerate(pairs)
    ]
    for copy in copies:
        copy.start()
    copies[1].wait()
    shard = stacked(weights_ref[...], jnp.zeros((BOX_ROWS - SHARD_ROWS, LANES), F32))
    for peer in range(PEERS):
        staged[peer] = shard
    early = pltpu.make_async_copy(
        staged.at[:, pl.ds(0, 16), :], out_hbm.at[:, pl.ds(0, 16), :], sems.at[4]
    )
    early.start()
    for i in (0, 2, 3):
        copies[i].wait()
    index = index_ref[...]
    owner = lax.shift_right_logical(index, 8)
    row = lax.bitwise_and(index, CODE_ROWS - 1)
    sent = (rows_of_lanes(0, (DEVICES, POINTS_DEV)) == owner).astype(F32)
    sent_low = sent.astype(BF16)
    width = 256
    earlier = rows_of_lanes(0, (width, width)) < rows_of_lanes(1, (width, width))
    earlier = earlier.astype(F32).astype(BF16)
    ones = jnp.ones((width, width), BF16)
    ranks = [
        mm(sent_low[:, : (part + 1) * width], stacked(*([ones] * part + [earlier])))
        for part in range(POINTS_DEV // width)
    ]
    placed = jnp.sum(sent * beside(*ranks), axis=0, keepdims=True).astype(jnp.int32)
    at_slot = rows_of_lanes(0, (SLOTS, POINTS_DEV)) == placed
    values = [coords_ref[i : i + 1, :] for i in range(3)]
    values += [distances_ref[...], (row + 1).astype(F32)]
    pieces = [[], [], []]
    for value in values:
        for k, third in enumerate(thirds(value)):
            pieces[k].append(jnp.where(at_slot, third, 0.0))
    spare = jnp.zeros((LANES - SLOTS * len(values), POINTS_DEV), F32)
    boxes = mm_nt(
        beside(sent_low, sent_low, sent_low),
        beside(*[stacked(*piece, spare).astype(BF16) for piece in pieces]),
    )
    for d in range(DEVICES):
        z, core, w = d // 32, d // 16 % 2, d % 16
        row = SHARD_ROWS + core
        staged[z * 16 + w, row : row + 1, :] = boxes[d : d + 1, :]
    late = pltpu.make_async_copy(
        staged.at[:, pl.ds(16, 8), :], out_hbm.at[:, pl.ds(16, 8), :], sems.at[5]
    )
    late.start()
    early.wait()
    late.wait()


def unit_groups(count, stride_rows, extra, first_entry):
    for group in range(count):
        entry = first_entry + group * 8 * (stride_rows * LANES + extra)
        yield group, entry // LANES, entry % LANES


def unpack_units(flat_ref, out_ref, count, stride_rows, extra, first_entry):
    lane = rows_of_lanes(1, (8, LANES))
    slope = rows_of_lanes(0, (8, LANES)) * extra
    for group, first, shift in unit_groups(count, stride_rows, extra, first_entry):
        start = slope + shift
        wraps = shift + 7 * extra >= LANES
        turn = lax.bitwise_and(lane + start, LANES - 1)
        tiles = []
        for a in range(stride_rows + 2 + wraps):
            tile = flat_ref[pl.ds(first + a, 8, stride=stride_rows), :]
            tiles.append(jnp.take_along_axis(tile, turn, axis=1, mode="promise_in_bounds"))
        for c in range(stride_rows + 1):
            value = jnp.where(lane + start < LANES, tiles[c], tiles[c + 1])
            if wraps:
                value = jnp.where(lane + start < 2 * LANES, value, tiles[c + 2])
            out_ref[group * 8 : group * 8 + 8, c * LANES : (c + 1) * LANES] = value


def pack_units(value_ref, flat_ref, count, stride_rows, extra, first_entry, adding):
    lane = rows_of_lanes(1, (8, LANES))
    slope = rows_of_lanes(0, (8, LANES)) * extra
    zero = jnp.zeros((8, LANES), F32)
    for group, first, shift in unit_groups(count, stride_rows, extra, first_entry):
        start = slope + shift
        wraps = shift + 7 * extra >= LANES
        wanted = range(stride_rows, stride_rows + 1 + wraps + 1) if adding else range(stride_rows)
        rolled = {}

        turn = lax.bitwise_and(lane - start, LANES - 1)

        def tile(c, rolled=rolled, group=group, turn=turn):
            if c < 0 or c > stride_rows:
                return zero
            if c not in rolled:
                value = value_ref[group * 8 : group * 8 + 8, c * LANES : (c + 1) * LANES]
                rolled[c] = jnp.take_along_axis(value, turn, axis=1, mode="promise_in_bounds")
            return rolled[c]

        for a in wanted:
            value = jnp.where(lane >= start, tile(a), tile(a - 1))
            if wraps:
                value = jnp.where(lane >= start - LANES, value, tile(a - 2))
            rows = pl.ds(first + a, 8, stride=stride_rows)
            if adding:
                flat_ref[rows, :] = flat_ref[rows, :] + value
            else:
                flat_ref[rows, :] = value


FIRST_UNITS = (32, 2, 5, 0)
SECOND_UNITS = (64, 4, 3, MIDDLE * (LATENT + 5))
HEAD_ENTRY = MIDDLE * (LATENT + 5) + HID * (HID + 3)


def across(column):
    return beside(*[column] * TILES)


def folded(v):
    return sum(v[:, i * LANES : (i + 1) * LANES] for i in range(TILES))


def silu_parts(half):
    gate = jnp.tanh(half)
    low = 0.5 * gate
    bend = 0.5 - gate * low
    bent = half * gate
    return half + bent, (0.5 + low) + half * bend, bend * (1.0 - bent)


def silu_parts_twice(half):
    gate = jnp.tanh(half)
    bend = 1.0 - gate * gate
    bent = half * gate
    return half + bent, (1.0 + gate) + half * bend, bend * (1.0 - bent)


def loop_kernel(
    core_ref,
    mine_ref,
    other_ref,
    codes_ref,
    first_w,
    second_w,
    latent_w,
    sum_two,
    sum_codes,
    sum_coord,
    sum_head,
    sum_count,
    sum_loss,
    flat,
    lhs_one,
    lhs_two,
    lhs_back,
    coord_w,
    head_w,
    spots,
    act_one,
    slope_one,
    curve_one,
    back_one,
    hid_hi,
    hid_lo,
    hot,
    hot_turned,
    act_two,
    slope_two,
    curve_two,
    act_tang,
    gate_hi,
    gate_lo,
    tang_hi,
    tang_lo,
    bar_hi,
    bar_lo,
    low_hi,
    low_lo,
):
    core = core_ref[0]

    for which in range(2):

        @pl.when(core == which)
        def _(which=which):
            for d in range(DEVICES):
                z, c, w = d // 32, d // 16 % 2, d % 16
                box = (z * 16 + w) * BOX_ROWS
                source = mine_ref if c == which else other_ref
                flat[d * SHARD_ROWS : d * SHARD_ROWS + BOX_ROWS, :] = source[box : box + BOX_ROWS, :]
            rows = pl.ds(SHARD_ROWS + which, PEERS, stride=BOX_ROWS)
            spots[...] = stacked(mine_ref[rows, :], other_ref[rows, :]).T

    unpack_units(flat, first_w, *FIRST_UNITS)
    unpack_units(flat, second_w, *SECOND_UNITS)
    head_bias = flat[HEAD_ENTRY // LANES : HEAD_ENTRY // LANES + 1, :][
        :, HEAD_ENTRY % LANES : HEAD_ENTRY % LANES + 1
    ]

    lane = rows_of_lanes(1, (256, LANES))
    unit = rows_of_lanes(0, (256, LANES))
    real = unit < MIDDLE

    first_low = jnp.where(beside(real, real), first_w[:, : 2 * LANES], 0.0)
    first_end = jnp.where(real, first_w[:, 2 * LANES :], 0.0)
    first_near = jnp.where(lane < 3, first_end, 0.0)
    first_gain = first_end[:, 3:4]
    first_bias = first_end[:, 4:5]
    first_w[:, : 2 * LANES] = first_low
    first_w[:, 2 * LANES :] = first_end
    _, first_scale = norm_parts(beside(first_low, first_near), first_gain)
    first_low = first_low * first_scale
    first_near = first_near * first_scale
    latent_w[0:256, :] = first_low
    for i in range(3):
        coord_w[:, i * LANES : (i + 1) * LANES] = jnp.broadcast_to(
            0.5 * first_near[:, i : i + 1], (256, LANES)
        )

    second_a = second_w[:, 0:256]
    second_b = second_w[:, 256:512]
    second_gain = second_w[:, 512:513]
    second_bias = second_w[:, 513:514]
    head = jnp.broadcast_to(second_w[:, 514:515], (HID, LANES))
    head_w[:, :LANES] = 0.5 * head
    head_w[:, LANES:] = head
    _, second_scale = norm_parts(second_w[:, 0:512], second_gain)
    second_a = second_a * second_scale
    second_b = second_b * second_scale
    is_hidden = rows_of_lanes(1, (HID, 256)) < MIDDLE
    hidden_cols = jnp.where(is_hidden, second_a, second_b)
    latent_cols = pltpu.roll(jnp.where(is_hidden, second_b, second_a), 3, 1)
    latent_w[256:768, :] = latent_cols

    hidden_hi, hidden_lo = halves(0.5 * hidden_cols)
    lhs_two[:, 0:256] = hidden_hi
    lhs_two[:, 256:512] = hidden_hi
    lhs_two[:, 512:768] = hidden_lo
    back_hi, back_lo = halves(hidden_cols.T)
    lhs_back[:, 0:512] = back_hi
    lhs_back[:, 512:1024] = back_hi
    lhs_back[:, 1024:1536] = back_lo

    code_hi, code_lo = halves(codes_ref[...])
    weight_hi, weight_lo = halves(latent_w[...])
    by_code = mm_nt(
        beside(weight_hi, weight_hi, weight_lo), beside(code_hi, code_lo, code_hi)
    )
    one_hi, one_lo = halves(0.5 * (by_code[0:256, :] + first_bias))
    lhs_one[:, 0:256] = one_hi
    lhs_one[:, 256:512] = one_lo
    two_hi, two_lo = halves(0.5 * (by_code[256:768, :] + second_bias))
    lhs_two[:, 768:1024] = two_hi
    lhs_two[:, 1024:1280] = two_lo

    for ref in (sum_two, sum_codes, sum_coord, sum_head, sum_count, sum_loss):
        ref[...] = jnp.zeros(ref.shape, F32)

    def feature(which, step, sub):
        first = which * SLOTS + (step * SUBS + sub) * TILES
        return beside(*[spots[pl.ds(first + i, 1), :] for i in range(TILES)])

    blank5 = jnp.zeros((5, BLOCK), F32)
    chunk = 8192 // BLOCK
    low_chunks = range(0, 256, chunk)
    high_chunks = range(0, HID, chunk)

    def block_stages(step, s):
        place = [feature(i, step, s) for i in range(3)]
        target = feature(3, step, s)
        code_row = feature(4, step, s)
        valid = (code_row > 0.5).astype(F32)

        wanted = code_row - 1.0
        for r in range(0, CODE_ROWS, chunk):
            row = (rows_of_lanes(0, (chunk, BLOCK)) + r).astype(F32)
            mark = jnp.where(row == wanted, 1.0, 0.0)
            hot[s, r : r + chunk, :] = mark.astype(BF16)
            sum_count[r : r + chunk, :] += folded(mark)
        for i in range(TILES):
            wanted = jnp.broadcast_to(code_row[:, i * LANES : (i + 1) * LANES] - 1.0, (LANES, LANES)).T
            for c in range(0, CODE_ROWS, LANES):
                code = (rows_of_lanes(1, (LANES, LANES)) + c).astype(F32)
                mark = jnp.where(code == wanted, 1.0, 0.0).astype(BF16)
                hot_turned[s, i * LANES : (i + 1) * LANES, c : c + LANES] = mark
        yield

        act_one[s] = mm(lhs_one[...], stacked(hot[s], hot[s]))
        yield
        last = stacked(blank5, *place)
        for r in low_chunks:
            pre = act_one[s, r : r + chunk, :]
            for i in range(3):
                pre = pre + across(coord_w[r : r + chunk, i * LANES : (i + 1) * LANES]) * place[i]
            value, slope, curve = silu_parts(pre)
            if r + chunk == 256:
                inside = rows_of_lanes(0, (chunk, BLOCK)) + r < MIDDLE
                end = jnp.where(inside[chunk - 8 :], value[chunk - 8 :], last)
                value = stacked(value[: chunk - 8], end)
                slope = jnp.where(inside, slope, 0.0)
                curve = jnp.where(inside, curve, 0.0)
            high, low = halves(value)
            hid_hi[s, r : r + chunk, :] = high
            hid_lo[s, r : r + chunk, :] = low
            slope_one[s, r : r + chunk, :] = slope
            curve_one[s, r : r + chunk, :] = curve
        yield

        act_two[s] = mm(lhs_two[...], stacked(hid_hi[s], hid_lo[s], hid_hi[s], hot[s], hot[s]))
        yield
        total = jnp.zeros((8, BLOCK), F32)
        for r in high_chunks:
            value, slope, curve = silu_parts_twice(act_two[s, r : r + chunk, :])
            head = across(head_w[r : r + chunk, :LANES])
            weighed = head * value
            for k in range(0, chunk, 8):
                total = total + weighed[k : k + 8, :]
            high, low = halves(head * slope)
            gate_hi[s, r : r + chunk, :] = high
            gate_lo[s, r : r + chunk, :] = low
            act_two[s, r : r + chunk, :] = value
            slope_two[s, r : r + chunk, :] = slope
            curve_two[s, r : r + chunk, :] = curve
        summed = jnp.sum(total, axis=0, keepdims=True)
        yield

        back_one[s] = mm(lhs_back[...], stacked(gate_hi[s], gate_lo[s], gate_hi[s]))
        yield
        totals = [jnp.zeros((8, BLOCK), F32) for _ in range(3)]
        for r in low_chunks:
            grad = back_one[s, r : r + chunk, :] * slope_one[s, r : r + chunk, :]
            for i in range(3):
                weighed = across(coord_w[r : r + chunk, i * LANES : (i + 1) * LANES]) * grad
                for k in range(0, chunk, 8):
                    totals[i] = totals[i] + weighed[k : k + 8, :]
        lead = [
            2.0 * jnp.sum(totals[i], axis=0, keepdims=True)
            + back_one[s, MIDDLE + i : MIDDLE + i + 1, :]
            for i in range(3)
        ]

        predicted = jnp.tanh(2.0 * summed + head_bias)
        flank = 1.0 - predicted * predicted
        slope = [flank * q for q in lead]
        excess = slope[0] * slope[0] + slope[1] * slope[1] + slope[2] * slope[2] - 1.0
        capped = jnp.tanh(predicted / DELTA)
        misfit = DELTA * capped - DELTA * jnp.tanh(target / DELTA)
        fitting = jnp.sqrt(misfit * misfit + SMOOTH * SMOOTH)
        sum_loss[0:1, :] += valid * (fitting + EIK_WEIGHT * excess * excess)
        share = valid * (1.0 / ALL_POINTS)
        pull = [(4.0 * EIK_WEIGHT) * excess * v for v in slope]
        by_flank = sum(p * q for p, q in zip(pull, lead))
        by_predicted = misfit / fitting * (1.0 - capped * capped) - 2.0 * predicted * by_flank
        bar_out = share * by_predicted * flank
        sum_loss[1:2, :] += bar_out
        half_bar = 0.5 * bar_out
        pull = [share * flank * p for p in pull]

        last = stacked(blank5, *pull)
        twice = [2.0 * p for p in pull]
        for r in low_chunks:
            grad = 0.0
            for i in range(3):
                grad = grad + across(coord_w[r : r + chunk, i * LANES : (i + 1) * LANES]) * twice[i]
            slope = slope_one[s, r : r + chunk, :]
            back = back_one[s, r : r + chunk, :]
            near = back * slope
            for i in range(3):
                sum_coord[r : r + chunk, i * LANES : (i + 1) * LANES] += folded(near * pull[i])
            through = grad * slope
            if r + chunk == 256:
                inside = rows_of_lanes(0, (8, BLOCK)) < MIDDLE - 248
                end = jnp.where(inside, through[chunk - 8 :], last)
                through = stacked(through[: chunk - 8], end)
            high, low = halves(through)
            tang_hi[s, r : r + chunk, :] = high
            tang_lo[s, r : r + chunk, :] = low
            curve_one[s, r : r + chunk, :] = (
                grad * back * curve_one[s, r : r + chunk, :]
            )
        yield
        act_tang[s] = mm(lhs_two[:, 0:768], stacked(tang_hi[s], tang_lo[s], tang_hi[s]))
        yield
        for r in high_chunks:
            tangent = act_tang[s, r : r + chunk, :]
            slope = slope_two[s, r : r + chunk, :]
            head = across(head_w[r : r + chunk, LANES:])
            bar = head * (half_bar * slope + tangent * curve_two[s, r : r + chunk, :])
            by_head = act_two[s, r : r + chunk, :] * bar_out + slope * tangent
            sum_head[r : r + chunk, :] += folded(by_head)
            high, low = halves(bar)
            bar_hi[s, r : r + chunk, :] = high
            bar_lo[s, r : r + chunk, :] = low
        yield

        back_one[s] = mm(lhs_back[...], stacked(bar_hi[s], bar_lo[s], bar_hi[s]))
        yield
        for r in low_chunks:
            bar = (
                back_one[s, r : r + chunk, :] * slope_one[s, r : r + chunk, :]
                + curve_one[s, r : r + chunk, :]
            )
            for i in range(3):
                sum_coord[r : r + chunk, i * LANES : (i + 1) * LANES] += folded(bar * place[i])
            high, low = halves(bar)
            low_hi[s, r : r + chunk, :] = high
            low_lo[s, r : r + chunk, :] = low
        yield

        sum_two[...] += mm_nt(
            beside(bar_hi[s], bar_hi[s], bar_lo[s], gate_hi[s], gate_hi[s], gate_lo[s]),
            beside(hid_hi[s], hid_lo[s], hid_hi[s], tang_hi[s], tang_lo[s], tang_hi[s]),
        )
        turned = stacked(hot_turned[s], hot_turned[s])
        sum_codes[256:768, :] += mm(beside(bar_hi[s], bar_lo[s]), turned)
        sum_codes[0:256, :] += mm(beside(low_hi[s], low_lo[s]), turned)

    def step_body(step, carry):
        waiting = [block_stages(step, s) for s in range(SUBS)]
        active = []
        while waiting or active:
            if waiting:
                active.append(waiting.pop(0))
            active = [work for work in active if next(work, work) is not work]
        return carry

    steps = SLOTS * DEVICES // (SUBS * BLOCK)
    if steps == 1:
        step_body(0, 0)
    else:
        lax.fori_loop(0, steps, step_body, 0)


def code_kernel(codes_ref, latent_w, sum_codes, sum_count, code_grad_ref, squares_ref):
    codes = codes_ref[...]
    count = jnp.sum(sum_count[...], axis=1, keepdims=True)
    turned_hi, turned_lo = halves(sum_codes[...].T)
    weight_hi, weight_lo = halves(latent_w[...])
    code_grad = mm(
        beside(turned_hi, turned_hi, turned_lo), stacked(weight_hi, weight_lo, weight_hi)
    )
    code_grad = code_grad + (2.0 * CODE_WEIGHT / ALL_POINTS) * count * codes
    code_grad_ref[...] = code_grad
    squares_ref[...] = jnp.broadcast_to(total_of(code_grad * code_grad), squares_ref.shape)


def norm_parts(direction, gain):
    root = lax.rsqrt(jnp.sum(direction * direction, axis=1, keepdims=True) + 1e-12)
    return root, gain * root


def weight_kernel(
    core_ref,
    codes_ref,
    first_w,
    second_w,
    sum_two,
    sum_codes,
    sum_coord,
    sum_head,
    sum_count,
    sum_loss,
    keep_ref,
    give_ref,
    flat,
    first_grad,
    second_grad,
):
    core = core_ref[0]
    codes = codes_ref[...]
    by_code = sum_codes[...]
    count = jnp.sum(sum_count[...], axis=1, keepdims=True)
    loss = jnp.sum(sum_loss[0:1, :], axis=1, keepdims=True)
    loss = loss + CODE_WEIGHT * total_of(count * codes * codes)
    loss = loss / ALL_POINTS

    code_hi, code_lo = halves(codes)
    by_hi, by_lo = halves(by_code)
    latent_grad = mm(beside(by_hi, by_hi, by_lo), stacked(code_hi, code_lo, code_hi))
    bias_grad = jnp.sum(by_code, axis=1, keepdims=True)

    lane = rows_of_lanes(1, (256, LANES))
    real = rows_of_lanes(0, (256, LANES)) < MIDDLE
    near_grad = 0.0
    for i in range(3):
        column = jnp.sum(sum_coord[:, i * LANES : (i + 1) * LANES], axis=1, keepdims=True)
        near_grad = jnp.where(lane == i, column, near_grad)
    low_grad = latent_grad[0:256, :]
    first_low = first_w[:, : 2 * LANES]
    first_near = jnp.where(lane < 3, first_w[:, 2 * LANES :], 0.0)
    root, scale = norm_parts(beside(first_low, first_near), first_w[:, 2 * LANES + 3 : 2 * LANES + 4])
    along = jnp.sum(first_low * low_grad, axis=1, keepdims=True)
    along = along + jnp.sum(first_near * near_grad, axis=1, keepdims=True)
    inward = scale * root * root * along
    end = scale * near_grad - first_near * inward
    end = jnp.where(lane == 3, root * along, end)
    end = jnp.where(lane == 4, bias_grad[0:256, :], end)
    low_grad = scale * low_grad - first_low * inward
    first_grad[:, : 2 * LANES] = jnp.where(beside(real, real), low_grad, 0.0)
    first_grad[:, 2 * LANES :] = jnp.where(real, end, 0.0)

    is_hidden = rows_of_lanes(1, (HID, 256)) < MIDDLE
    hidden_grad = sum_two[...]
    moved = pltpu.roll(latent_grad[256:768, :], 256 - 3, 1)
    grad_a = jnp.where(is_hidden, hidden_grad, moved)
    grad_b = jnp.where(is_hidden, moved, hidden_grad)
    second_a = second_w[:, 0:256]
    second_b = second_w[:, 256:512]
    root, scale = norm_parts(second_w[:, 0:512], second_w[:, 512:513])
    along = jnp.sum(second_a * grad_a + second_b * grad_b, axis=1, keepdims=True)
    inward = scale * root * root * along
    second_grad[:, 0:256] = scale * grad_a - second_a * inward
    second_grad[:, 256:512] = scale * grad_b - second_b * inward
    head_grad = jnp.sum(sum_head[...], axis=1, keepdims=True)
    lane = rows_of_lanes(1, (HID, LANES))
    end = jnp.where(lane == 0, root * along, 0.0)
    end = jnp.where(lane == 1, bias_grad[256:768, :], end)
    second_grad[:, 512:640] = jnp.where(lane == 2, head_grad, end)

    flat[...] = jnp.zeros(flat.shape, F32)
    for adding in (False, True):
        pack_units(first_grad, flat, *FIRST_UNITS, adding)
        pack_units(second_grad, flat, *SECOND_UNITS, adding)
    row = HEAD_ENTRY // LANES
    lane = rows_of_lanes(1, (1, LANES))
    bias_total = jnp.sum(sum_loss[1:2, :], axis=1, keepdims=True)
    flat[row : row + 1, :] = flat[row : row + 1, :] + jnp.where(
        lane == HEAD_ENTRY % LANES, bias_total, 0.0
    )
    sub = rows_of_lanes(0, (8, LANES))
    wide = rows_of_lanes(1, (8, LANES))
    info = jnp.where((sub == 5) & (wide == 0), loss, 0.0)
    for which in range(2):

        @pl.when(core == which)
        def _(which=which):
            for d in range(DEVICES):
                z, c, w = d // 32, d // 16 % 2, d % 16
                target = keep_ref if c == which else give_ref
                box = (z * 16 + w) * BOX_ROWS
                first = d * SHARD_ROWS
                target[box : box + 16, :] = flat[first : first + 16, :]
                target[box + 16 : box + 24, :] = jnp.where(
                    sub < 5, flat[first + 16 : first + 24, :], info
                )


def vmem(count):
    return [pl.BlockSpec(memory_space=pltpu.VMEM)] * count


PARAMS = pltpu.CompilerParams(vmem_limit_bytes=48 * 1024 * 1024)


HBM = pl.BlockSpec(memory_space=pltpu.HBM)
SMEM = pl.BlockSpec(memory_space=pltpu.SMEM)


def f32(*shape):
    return jax.ShapeDtypeStruct(shape, F32)


def pack_boxes(weights, coords, distances, index):
    return pl.pallas_call(
        pack_kernel,
        out_shape=f32(PEERS, BOX_ROWS, LANES),
        in_specs=[HBM] * 4,
        out_specs=HBM,
        scratch_shapes=[
            pltpu.VMEM(weights.shape, F32),
            pltpu.VMEM(coords.shape, F32),
            pltpu.VMEM(distances.shape, F32),
            pltpu.VMEM(index.shape, jnp.int32),
            pltpu.VMEM((PEERS, BOX_ROWS, LANES), F32),
            pltpu.SemaphoreType.DMA((6,)),
        ],
        compiler_params=pltpu.CompilerParams(vmem_limit_bytes=60 * 1024 * 1024),
    )(weights, coords, distances, index)


def main_kernel(
    core_ref, mine_ref, other_ref, codes_ref, keep_ref, give_ref, code_grad_ref, squares_ref, *scratch
):
    first_w, second_w, latent_w, *sums = scratch[:9]
    flat, first_grad, second_grad = scratch[9:12]
    loop_kernel(core_ref, mine_ref, other_ref, codes_ref, *scratch[:9], flat, *scratch[12:])
    code_kernel(codes_ref, latent_w, sums[1], sums[4], code_grad_ref, squares_ref)
    weight_kernel(
        core_ref, codes_ref, first_w, second_w, *sums, keep_ref, give_ref, flat, first_grad, second_grad
    )


def main_call(core, mine, other, codes):
    pair = (SUBS, 256, BLOCK)
    pair_two = (SUBS, HID, BLOCK)
    scratch = [
        ((256, 3 * LANES), F32),
        ((HID, 5 * LANES), F32),
        ((768, 256), F32),
        ((HID, 256), F32),
        ((768, 256), F32),
        ((256, 3 * LANES), F32),
        ((HID, LANES), F32),
        ((CODE_ROWS, LANES), F32),
        ((2, BLOCK), F32),
        ((FLAT_ROWS + 8, LANES), F32),
        ((256, 3 * LANES), F32),
        ((HID, 5 * LANES), F32),
        ((256, 512), BF16),
        ((HID, 1280), BF16),
        ((256, 1536), BF16),
        ((256, 3 * LANES), F32),
        ((HID, 2 * LANES), F32),
        ((LANES, LANES), F32),
        (pair, F32),
        (pair, F32),
        (pair, F32),
        (pair, F32),
        (pair, BF16),
        (pair, BF16),
        (pair, BF16),
        ((SUBS, BLOCK, CODE_ROWS), BF16),
        (pair_two, F32),
        (pair_two, F32),
        (pair_two, F32),
        (pair_two, F32),
        (pair_two, BF16),
        (pair_two, BF16),
        (pair, BF16),
        (pair, BF16),
        (pair_two, BF16),
        (pair_two, BF16),
        (pair, BF16),
        (pair, BF16),
    ]
    boxes = f32(PEERS * BOX_ROWS, LANES)
    return pl.pallas_call(
        main_kernel,
        out_shape=(boxes, boxes, f32(CODE_ROWS, LATENT), f32(8, LANES)),
        in_specs=[SMEM] + vmem(3),
        out_specs=tuple(vmem(4)),
        scratch_shapes=[pltpu.VMEM(shape, dtype) for shape, dtype in scratch],
        compiler_params=PARAMS,
    )(core, mine, other, codes)


def adam_update(value, first, second, grad, rate):
    first_new = BETA_ONE * first + (1.0 - BETA_ONE) * grad
    second_new = BETA_TWO * second + (1.0 - BETA_TWO) * grad * grad
    first_hat = first_new / (1.0 - BETA_ONE**STEP)
    second_hat = second_new / (1.0 - BETA_TWO**STEP)
    value_new = value - rate * (first_hat / (jnp.sqrt(second_hat) + ADAM_EPS) + DECAY * value)
    return (value_new, first_new, second_new)


def shard_kernel(parts_ref, code_squares_ref, shard_ref, squares_ref):
    total = parts_ref[0:BOX_ROWS, :]
    for peer in range(1, PEERS):
        total = total + parts_ref[peer * BOX_ROWS : (peer + 1) * BOX_ROWS, :]
    shard_ref[...] = total
    grad = total[:SHARD_ROWS, :]
    squares_ref[...] = code_squares_ref[...] + total_of(grad * grad)


def sum_shards(parts, code_squares):
    return pl.pallas_call(
        shard_kernel,
        out_shape=(
            jax.ShapeDtypeStruct((BOX_ROWS, LANES), F32),
            jax.ShapeDtypeStruct((8, LANES), F32),
        ),
        in_specs=vmem(2),
        out_specs=tuple(vmem(2)),
        compiler_params=PARAMS,
    )(parts, code_squares)


def update_kernel(
    squares_ref,
    shard_ref,
    weights_ref,
    moment_one_ref,
    moment_two_ref,
    codes_ref,
    code_first_ref,
    code_second_ref,
    code_grad_ref,
    loss_out,
    norm_out,
    weights_out,
    moment_one_out,
    moment_two_out,
    weights_copy_out,
    codes_out,
    code_first_out,
    code_second_out,
    codes_copy_out,
):
    loss_out[...] = shard_ref[SHARD_ROWS : SHARD_ROWS + 1, 0:1]
    norm = jnp.sqrt(squares_ref[0:1, 0:1])
    norm_out[...] = norm
    factor = jnp.minimum(1.0, CLIP / (norm + 1e-06))
    value, first, second = adam_update(
        weights_ref[...],
        moment_one_ref[...],
        moment_two_ref[...],
        factor * shard_ref[0:SHARD_ROWS, :],
        WEIGHT_RATE,
    )
    weights_out[...] = value
    moment_one_out[...] = first
    moment_two_out[...] = second
    weights_copy_out[...] = value.astype(BF16)
    for r in range(0, CODE_ROWS, 32):
        rows = slice(r, r + 32)
        value, first, second = adam_update(
            codes_ref[rows, :],
            code_first_ref[rows, :],
            code_second_ref[rows, :],
            factor * code_grad_ref[rows, :],
            CODE_RATE,
        )
        codes_out[rows, :] = value
        code_first_out[rows, :] = first
        code_second_out[rows, :] = second
        codes_copy_out[rows, :] = value.astype(BF16)


def update_all(*args):
    scalar = jax.ShapeDtypeStruct((1, 1), F32)
    shard = [jax.ShapeDtypeStruct((SHARD_ROWS, LANES), t) for t in (F32, F32, F32, BF16)]
    table = [jax.ShapeDtypeStruct((CODE_ROWS, LATENT), t) for t in (F32, F32, F32, BF16)]
    return pl.pallas_call(
        update_kernel,
        out_shape=(scalar, scalar, *shard, *table),
        in_specs=vmem(9),
        out_specs=tuple(vmem(10)),
        compiler_params=PARAMS,
    )(*args)


def swap_cores(v):
    return lax.ppermute(v, "core", [(0, 1), (1, 0)])


def exchange(v):
    return lax.all_to_all(v, ("z", "wide"), split_axis=0, concat_axis=0)


def sum_everywhere(v):
    v = v + swap_cores(v)
    flip = [1, 0, 3, 2], [3, 2, 1, 0]
    for pairs in flip:
        v = v + lax.ppermute(v, "z", list(enumerate(pairs)))
    for stride in (4, 1):
        for pairs in flip:
            moves = [(d, d + (pairs[d // stride % 4] - d // stride % 4) * stride) for d in range(16)]
            v = v + lax.ppermute(v, "wide", moves)
    return v


def body(
    weights_flat,
    moment_one,
    moment_two,
    codes,
    code_first,
    code_second,
    coords,
    distances,
    shape_index,
):
    boxes = pack_boxes(
        weights_flat.reshape(SHARD_ROWS, LANES),
        coords,
        distances.reshape(1, POINTS_DEV),
        shape_index.reshape(1, POINTS_DEV),
    )
    mine = exchange(boxes)
    other = swap_cores(mine)
    core = lax.axis_index("core").astype(jnp.int32).reshape(1)
    keep, give, code_grad, code_squares = main_call(
        core,
        mine.reshape(PEERS * BOX_ROWS, LANES),
        other.reshape(PEERS * BOX_ROWS, LANES),
        codes,
    )
    pair_sum = (keep + swap_cores(give)).reshape(PEERS, BOX_ROWS, LANES)
    shard, squares = sum_shards(exchange(pair_sum).reshape(PEERS * BOX_ROWS, LANES), code_squares)
    squares = sum_everywhere(squares)
    flat = lambda v: v.reshape(SHARD_ROWS, LANES)
    out = update_all(
        squares,
        shard,
        flat(weights_flat),
        flat(moment_one),
        flat(moment_two),
        codes,
        code_first,
        code_second,
        code_grad,
    )
    return (
        out[0].reshape(()),
        out[1].reshape(()),
        *[v.reshape(weights_flat.shape) for v in out[2:6]],
        *out[6:],
    )


def solution(mesh):
    parts = Mesh(mesh.devices.reshape(4, 2, 16), ALL)
    return jax.shard_map(
        body,
        mesh=parts,
        in_specs=(
            P(ALL),
            P(ALL),
            P(ALL),
            P(ALL, None),
            P(ALL, None),
            P(ALL, None),
            P(None, ALL),
            P(ALL),
            P(ALL),
        ),
        out_specs=(
            P(),
            P(),
            P(ALL),
            P(ALL),
            P(ALL),
            P(ALL),
            P(ALL, None),
            P(ALL, None),
            P(ALL, None),
            P(ALL, None),
        ),
        check_vma=False,
    )
```

```python
import jax
import jax.numpy as jnp
from jax import lax
from jax.experimental import pallas as pl
from jax.experimental.pallas import tpu as pltpu
from jax.sharding import Mesh
from jax.sharding import PartitionSpec as P

LATENT = 256
HID = 512
MIDDLE = HID - LATENT - 3
STEP = 10

DELTA = 0.1
SMOOTH = 0.01
CODE_WEIGHT = 0.001
EIK_WEIGHT = 0.1
CLIP = 0.001
WEIGHT_RATE = 0.02
CODE_RATE = 0.15
BETA_ONE = 0.9
BETA_TWO = 0.999
ADAM_EPS = 1e-08
DECAY = 0.01

LANES = 128
DEVICES = 128
PEERS = 64
SHARD_ROWS = 21
BOX_ROWS = 24
SLOTS = 16
POINTS_DEV = 1024
CODE_ROWS = 256
FLAT_ROWS = DEVICES * SHARD_ROWS
BLOCK = 256
SUBS = 4
TILES = BLOCK // LANES
ALL_POINTS = POINTS_DEV * DEVICES

F32 = jnp.float32
BF16 = jnp.bfloat16
ALL = ("z", "core", "wide")


def rows_of_lanes(lead, shape):
    return lax.broadcasted_iota(jnp.int32, shape, lead)


def halves(v):
    high = v.astype(BF16)
    return high, (v - high.astype(F32)).astype(BF16)


def thirds(v):
    high = v.astype(BF16).astype(F32)
    rest = v - high
    mid = rest.astype(BF16).astype(F32)
    return high, mid, rest - mid


def mm(a, b):
    return lax.dot_general(a, b, (((1,), (0,)), ((), ())), preferred_element_type=F32)


def mm_nt(a, b):
    return lax.dot_general(a, b, (((1,), (1,)), ((), ())), preferred_element_type=F32)


def beside(*parts):
    return jnp.concatenate(parts, axis=1)


def total_of(v):
    return jnp.sum(jnp.sum(v, axis=0, keepdims=True), axis=1, keepdims=True)


def stacked(*parts):
    return jnp.concatenate(parts, axis=0)


def pack_kernel(
    weights_hbm,
    coords_hbm,
    distances_hbm,
    index_hbm,
    out_hbm,
    weights_ref,
    coords_ref,
    distances_ref,
    index_ref,
    staged,
    sems,
):
    pairs = [
        (index_hbm, index_ref),
        (weights_hbm, weights_ref),
        (coords_hbm, coords_ref),
        (distances_hbm, distances_ref),
    ]
    copies = [
        pltpu.make_async_copy(source, target, sems.at[i])
        for i, (source, target) in enumerate(pairs)
    ]
    for copy in copies:
        copy.start()
    copies[1].wait()
    shard = stacked(weights_ref[...], jnp.zeros((BOX_ROWS - SHARD_ROWS, LANES), F32))
    for peer in range(PEERS):
        staged[peer] = shard
    early = pltpu.make_async_copy(
        staged.at[:, pl.ds(0, 16), :], out_hbm.at[:, pl.ds(0, 16), :], sems.at[4]
    )
    early.start()
    for i in (0, 2, 3):
        copies[i].wait()
    index = index_ref[...]
    owner = lax.shift_right_logical(index, 8)
    row = lax.bitwise_and(index, CODE_ROWS - 1)
    sent = (rows_of_lanes(0, (DEVICES, POINTS_DEV)) == owner).astype(F32)
    sent_low = sent.astype(BF16)
    width = 256
    earlier = rows_of_lanes(0, (width, width)) < rows_of_lanes(1, (width, width))
    earlier = earlier.astype(F32).astype(BF16)
    ones = jnp.ones((width, width), BF16)
    ranks = [
        mm(sent_low[:, : (part + 1) * width], stacked(*([ones] * part + [earlier])))
        for part in range(POINTS_DEV // width)
    ]
    placed = jnp.sum(sent * beside(*ranks), axis=0, keepdims=True).astype(jnp.int32)
    at_slot = rows_of_lanes(0, (SLOTS, POINTS_DEV)) == placed
    values = [coords_ref[i : i + 1, :] for i in range(3)]
    values += [distances_ref[...], (row + 1).astype(F32)]
    pieces = [[], [], []]
    for value in values:
        for k, third in enumerate(thirds(value)):
            pieces[k].append(jnp.where(at_slot, third, 0.0))
    spare = jnp.zeros((LANES - SLOTS * len(values), POINTS_DEV), F32)
    boxes = mm_nt(
        beside(sent_low, sent_low, sent_low),
        beside(*[stacked(*piece, spare).astype(BF16) for piece in pieces]),
    )
    for d in range(DEVICES):
        z, core, w = d // 32, d // 16 % 2, d % 16
        row = SHARD_ROWS + core
        staged[z * 16 + w, row : row + 1, :] = boxes[d : d + 1, :]
    late = pltpu.make_async_copy(
        staged.at[:, pl.ds(16, 8), :], out_hbm.at[:, pl.ds(16, 8), :], sems.at[5]
    )
    late.start()
    early.wait()
    late.wait()


def unit_groups(count, stride_rows, extra, first_entry):
    for group in range(count):
        entry = first_entry + group * 8 * (stride_rows * LANES + extra)
        yield group, entry // LANES, entry % LANES


def unpack_units(flat_ref, out_ref, count, stride_rows, extra, first_entry):
    lane = rows_of_lanes(1, (8, LANES))
    slope = rows_of_lanes(0, (8, LANES)) * extra
    for group, first, shift in unit_groups(count, stride_rows, extra, first_entry):
        start = slope + shift
        wraps = shift + 7 * extra >= LANES
        turn = lax.bitwise_and(lane + start, LANES - 1)
        tiles = []
        for a in range(stride_rows + 2 + wraps):
            tile = flat_ref[pl.ds(first + a, 8, stride=stride_rows), :]
            tiles.append(jnp.take_along_axis(tile, turn, axis=1, mode="promise_in_bounds"))
        for c in range(stride_rows + 1):
            value = jnp.where(lane + start < LANES, tiles[c], tiles[c + 1])
            if wraps:
                value = jnp.where(lane + start < 2 * LANES, value, tiles[c + 2])
            out_ref[group * 8 : group * 8 + 8, c * LANES : (c + 1) * LANES] = value


def pack_group(flat_ref, tiles, first, shift, stride_rows, extra):
    lane = rows_of_lanes(1, (8, LANES))
    start = rows_of_lanes(0, (8, LANES)) * extra + shift
    wraps = shift + 7 * extra >= LANES
    turn = lax.bitwise_and(lane - start, LANES - 1)
    zero = jnp.zeros((8, LANES), F32)
    turned = [jnp.take_along_axis(v, turn, axis=1, mode="promise_in_bounds") for v in tiles]
    turned = [zero, zero] + turned + [zero, zero]
    for a in range(stride_rows + 2 + wraps):
        value = jnp.where(lane >= start, turned[a + 2], turned[a + 1])
        if wraps:
            value = jnp.where(lane >= start - LANES, value, turned[a])
        rows = pl.ds(first + a, 8, stride=stride_rows)
        if 1 + wraps <= a < stride_rows:
            flat_ref[rows, :] = value
        else:
            flat_ref[rows, :] = flat_ref[rows, :] + value


FIRST_UNITS = (32, 2, 5, 0)
SECOND_UNITS = (64, 4, 3, MIDDLE * (LATENT + 5))
HEAD_ENTRY = MIDDLE * (LATENT + 5) + HID * (HID + 3)


def across(column):
    return beside(*[column] * TILES)


def folded(v):
    return sum(v[:, i * LANES : (i + 1) * LANES] for i in range(TILES))


def silu_parts(half):
    gate = jnp.tanh(half)
    low = 0.5 * gate
    bend = 0.5 - gate * low
    bent = half * gate
    return half + bent, (0.5 + low) + half * bend, bend * (1.0 - bent)


def silu_parts_twice(half):
    gate = jnp.tanh(half)
    bend = 1.0 - gate * gate
    bent = half * gate
    return half + bent, (1.0 + gate) + half * bend, bend * (1.0 - bent)


def loop_kernel(
    core_ref,
    mine_ref,
    other_ref,
    codes_ref,
    first_w,
    second_w,
    latent_w,
    sum_two,
    sum_codes,
    sum_coord,
    sum_head,
    sum_count,
    sum_loss,
    flat,
    lhs_one,
    lhs_two,
    lhs_back,
    coord_w,
    head_w,
    spots,
    act_one,
    slope_one,
    curve_one,
    back_one,
    hid_hi,
    hid_lo,
    hot,
    hot_turned,
    act_two,
    slope_two,
    curve_two,
    act_tang,
    gate_hi,
    gate_lo,
    tang_hi,
    tang_lo,
    bar_hi,
    bar_lo,
    low_hi,
    low_lo,
):
    core = core_ref[0]

    for which in range(2):

        @pl.when(core == which)
        def _(which=which):
            for d in range(DEVICES):
                z, c, w = d // 32, d // 16 % 2, d % 16
                box = (z * 16 + w) * BOX_ROWS
                source = mine_ref if c == which else other_ref
                flat[d * SHARD_ROWS : d * SHARD_ROWS + BOX_ROWS, :] = source[box : box + BOX_ROWS, :]
            rows = pl.ds(SHARD_ROWS + which, PEERS, stride=BOX_ROWS)
            spots[...] = stacked(mine_ref[rows, :], other_ref[rows, :]).T

    unpack_units(flat, first_w, *FIRST_UNITS)
    unpack_units(flat, second_w, *SECOND_UNITS)
    head_bias = flat[HEAD_ENTRY // LANES : HEAD_ENTRY // LANES + 1, :][
        :, HEAD_ENTRY % LANES : HEAD_ENTRY % LANES + 1
    ]

    lane = rows_of_lanes(1, (256, LANES))
    unit = rows_of_lanes(0, (256, LANES))
    real = unit < MIDDLE

    first_low = jnp.where(beside(real, real), first_w[:, : 2 * LANES], 0.0)
    first_end = jnp.where(real, first_w[:, 2 * LANES :], 0.0)
    first_near = jnp.where(lane < 3, first_end, 0.0)
    first_gain = first_end[:, 3:4]
    first_bias = first_end[:, 4:5]
    first_w[:, : 2 * LANES] = first_low
    first_w[:, 2 * LANES :] = first_end
    _, first_scale = norm_parts(beside(first_low, first_near), first_gain)
    first_low = first_low * first_scale
    first_near = first_near * first_scale
    latent_w[0:256, :] = first_low
    for i in range(3):
        coord_w[:, i * LANES : (i + 1) * LANES] = jnp.broadcast_to(
            0.5 * first_near[:, i : i + 1], (256, LANES)
        )

    second_a = second_w[:, 0:256]
    second_b = second_w[:, 256:512]
    second_gain = second_w[:, 512:513]
    second_bias = second_w[:, 513:514]
    head = jnp.broadcast_to(second_w[:, 514:515], (HID, LANES))
    head_w[:, :LANES] = 0.5 * head
    head_w[:, LANES:] = head
    _, second_scale = norm_parts(second_w[:, 0:512], second_gain)
    second_a = second_a * second_scale
    second_b = second_b * second_scale
    is_hidden = rows_of_lanes(1, (HID, 256)) < MIDDLE
    hidden_cols = jnp.where(is_hidden, second_a, second_b)
    latent_cols = pltpu.roll(jnp.where(is_hidden, second_b, second_a), 3, 1)
    latent_w[256:768, :] = latent_cols

    hidden_hi, hidden_lo = halves(0.5 * hidden_cols)
    lhs_two[:, 0:256] = hidden_hi
    lhs_two[:, 256:512] = hidden_hi
    lhs_two[:, 512:768] = hidden_lo
    back_hi, back_lo = halves(hidden_cols.T)
    lhs_back[:, 0:512] = back_hi
    lhs_back[:, 512:1024] = back_hi
    lhs_back[:, 1024:1536] = back_lo

    code_hi, code_lo = halves(codes_ref[...])
    weight_hi, weight_lo = halves(latent_w[...])
    by_code = mm_nt(
        beside(weight_hi, weight_hi, weight_lo), beside(code_hi, code_lo, code_hi)
    )
    one_hi, one_lo = halves(0.5 * (by_code[0:256, :] + first_bias))
    lhs_one[:, 0:256] = one_hi
    lhs_one[:, 256:512] = one_lo
    two_hi, two_lo = halves(0.5 * (by_code[256:768, :] + second_bias))
    lhs_two[:, 768:1024] = two_hi
    lhs_two[:, 1024:1280] = two_lo

    for ref in (sum_two, sum_codes, sum_coord, sum_head, sum_count, sum_loss):
        ref[...] = jnp.zeros(ref.shape, F32)

    def feature(which, step, sub):
        first = which * SLOTS + (step * SUBS + sub) * TILES
        return beside(*[spots[pl.ds(first + i, 1), :] for i in range(TILES)])

    blank5 = jnp.zeros((5, BLOCK), F32)
    chunk = 8192 // BLOCK
    low_chunks = range(0, 256, chunk)
    high_chunks = range(0, HID, chunk)

    def block_stages(step, s):
        place = [feature(i, step, s) for i in range(3)]
        target = feature(3, step, s)
        code_row = feature(4, step, s)
        valid = (code_row > 0.5).astype(F32)

        wanted = code_row - 1.0
        for r in range(0, CODE_ROWS, chunk):
            row = (rows_of_lanes(0, (chunk, BLOCK)) + r).astype(F32)
            mark = jnp.where(row == wanted, 1.0, 0.0)
            hot[s, r : r + chunk, :] = mark.astype(BF16)
            sum_count[r : r + chunk, :] += folded(mark)
        for i in range(TILES):
            wanted = jnp.broadcast_to(code_row[:, i * LANES : (i + 1) * LANES] - 1.0, (LANES, LANES)).T
            for c in range(0, CODE_ROWS, LANES):
                code = (rows_of_lanes(1, (LANES, LANES)) + c).astype(F32)
                mark = jnp.where(code == wanted, 1.0, 0.0).astype(BF16)
                hot_turned[s, i * LANES : (i + 1) * LANES, c : c + LANES] = mark
        yield

        act_one[s] = mm(lhs_one[...], stacked(hot[s], hot[s]))
        yield
        last = stacked(blank5, *place)
        for r in low_chunks:
            pre = act_one[s, r : r + chunk, :]
            for i in range(3):
                pre = pre + across(coord_w[r : r + chunk, i * LANES : (i + 1) * LANES]) * place[i]
            value, slope, curve = silu_parts(pre)
            if r + chunk == 256:
                inside = rows_of_lanes(0, (chunk, BLOCK)) + r < MIDDLE
                end = jnp.where(inside[chunk - 8 :], value[chunk - 8 :], last)
                value = stacked(value[: chunk - 8], end)
                slope = jnp.where(inside, slope, 0.0)
                curve = jnp.where(inside, curve, 0.0)
            high, low = halves(value)
            hid_hi[s, r : r + chunk, :] = high
            hid_lo[s, r : r + chunk, :] = low
            slope_one[s, r : r + chunk, :] = slope
            curve_one[s, r : r + chunk, :] = curve
        yield

        act_two[s] = mm(lhs_two[...], stacked(hid_hi[s], hid_lo[s], hid_hi[s], hot[s], hot[s]))
        yield
        total = jnp.zeros((8, BLOCK), F32)
        for r in high_chunks:
            value, slope, curve = silu_parts_twice(act_two[s, r : r + chunk, :])
            head = across(head_w[r : r + chunk, :LANES])
            weighed = head * value
            for k in range(0, chunk, 8):
                total = total + weighed[k : k + 8, :]
            high, low = halves(head * slope)
            gate_hi[s, r : r + chunk, :] = high
            gate_lo[s, r : r + chunk, :] = low
            act_two[s, r : r + chunk, :] = value
            slope_two[s, r : r + chunk, :] = slope
            curve_two[s, r : r + chunk, :] = curve
        summed = jnp.sum(total, axis=0, keepdims=True)
        yield

        back_one[s] = mm(lhs_back[...], stacked(gate_hi[s], gate_lo[s], gate_hi[s]))
        yield
        totals = [jnp.zeros((8, BLOCK), F32) for _ in range(3)]
        for r in low_chunks:
            grad = back_one[s, r : r + chunk, :] * slope_one[s, r : r + chunk, :]
            for i in range(3):
                weighed = across(coord_w[r : r + chunk, i * LANES : (i + 1) * LANES]) * grad
                for k in range(0, chunk, 8):
                    totals[i] = totals[i] + weighed[k : k + 8, :]
        lead = [
            2.0 * jnp.sum(totals[i], axis=0, keepdims=True)
            + back_one[s, MIDDLE + i : MIDDLE + i + 1, :]
            for i in range(3)
        ]

        predicted = jnp.tanh(2.0 * summed + head_bias)
        flank = 1.0 - predicted * predicted
        slope = [flank * q for q in lead]
        excess = slope[0] * slope[0] + slope[1] * slope[1] + slope[2] * slope[2] - 1.0
        capped = jnp.tanh(predicted / DELTA)
        misfit = DELTA * capped - DELTA * jnp.tanh(target / DELTA)
        fitting = jnp.sqrt(misfit * misfit + SMOOTH * SMOOTH)
        sum_loss[0:1, :] += valid * (fitting + EIK_WEIGHT * excess * excess)
        share = valid * (1.0 / ALL_POINTS)
        pull = [(4.0 * EIK_WEIGHT) * excess * v for v in slope]
        by_flank = sum(p * q for p, q in zip(pull, lead))
        by_predicted = misfit / fitting * (1.0 - capped * capped) - 2.0 * predicted * by_flank
        bar_out = share * by_predicted * flank
        sum_loss[1:2, :] += bar_out
        half_bar = 0.5 * bar_out
        pull = [share * flank * p for p in pull]

        last = stacked(blank5, *pull)
        twice = [2.0 * p for p in pull]
        for r in low_chunks:
            grad = 0.0
            for i in range(3):
                grad = grad + across(coord_w[r : r + chunk, i * LANES : (i + 1) * LANES]) * twice[i]
            slope = slope_one[s, r : r + chunk, :]
            back = back_one[s, r : r + chunk, :]
            near = back * slope
            for i in range(3):
                sum_coord[r : r + chunk, i * LANES : (i + 1) * LANES] += folded(near * pull[i])
            through = grad * slope
            if r + chunk == 256:
                inside = rows_of_lanes(0, (8, BLOCK)) < MIDDLE - 248
                end = jnp.where(inside, through[chunk - 8 :], last)
                through = stacked(through[: chunk - 8], end)
            high, low = halves(through)
            tang_hi[s, r : r + chunk, :] = high
            tang_lo[s, r : r + chunk, :] = low
            curve_one[s, r : r + chunk, :] = (
                grad * back * curve_one[s, r : r + chunk, :]
            )
        yield
        act_tang[s] = mm(lhs_two[:, 0:768], stacked(tang_hi[s], tang_lo[s], tang_hi[s]))
        yield
        for r in high_chunks:
            tangent = act_tang[s, r : r + chunk, :]
            slope = slope_two[s, r : r + chunk, :]
            head = across(head_w[r : r + chunk, LANES:])
            bar = head * (half_bar * slope + tangent * curve_two[s, r : r + chunk, :])
            by_head = act_two[s, r : r + chunk, :] * bar_out + slope * tangent
            sum_head[r : r + chunk, :] += folded(by_head)
            high, low = halves(bar)
            bar_hi[s, r : r + chunk, :] = high
            bar_lo[s, r : r + chunk, :] = low
        yield

        back_one[s] = mm(lhs_back[...], stacked(bar_hi[s], bar_lo[s], bar_hi[s]))
        yield
        for r in low_chunks:
            bar = (
                back_one[s, r : r + chunk, :] * slope_one[s, r : r + chunk, :]
                + curve_one[s, r : r + chunk, :]
            )
            for i in range(3):
                sum_coord[r : r + chunk, i * LANES : (i + 1) * LANES] += folded(bar * place[i])
            high, low = halves(bar)
            low_hi[s, r : r + chunk, :] = high
            low_lo[s, r : r + chunk, :] = low
        yield

        sum_two[...] += mm_nt(
            beside(bar_hi[s], bar_hi[s], bar_lo[s], gate_hi[s], gate_hi[s], gate_lo[s]),
            beside(hid_hi[s], hid_lo[s], hid_hi[s], tang_hi[s], tang_lo[s], tang_hi[s]),
        )
        turned = stacked(hot_turned[s], hot_turned[s])
        sum_codes[256:768, :] += mm(beside(bar_hi[s], bar_lo[s]), turned)
        sum_codes[0:256, :] += mm(beside(low_hi[s], low_lo[s]), turned)

    def step_body(step, carry):
        waiting = [block_stages(step, s) for s in range(SUBS)]
        active = []
        while waiting or active:
            if waiting:
                active.append(waiting.pop(0))
            active = [work for work in active if next(work, work) is not work]
        return carry

    steps = SLOTS * DEVICES // (SUBS * BLOCK)
    if steps == 1:
        step_body(0, 0)
    else:
        lax.fori_loop(0, steps, step_body, 0)


def code_kernel(codes_ref, latent_w, sum_codes, sum_count, sum_loss, code_grad_ref, facts_ref):
    codes = codes_ref[...]
    count = jnp.sum(sum_count[...], axis=1, keepdims=True)
    turned_hi, turned_lo = halves(sum_codes[...].T)
    weight_hi, weight_lo = halves(latent_w[...])
    code_grad = mm(
        beside(turned_hi, turned_hi, turned_lo), stacked(weight_hi, weight_lo, weight_hi)
    )
    code_grad = code_grad + (2.0 * CODE_WEIGHT / ALL_POINTS) * count * codes
    code_grad_ref[...] = code_grad
    loss = jnp.sum(sum_loss[0:1, :], axis=1, keepdims=True)
    loss = (loss + CODE_WEIGHT * total_of(count * codes * codes)) / ALL_POINTS
    left = rows_of_lanes(1, facts_ref.shape) < LANES // 2
    facts_ref[...] = jnp.where(left, total_of(code_grad * code_grad), loss)


def norm_parts(direction, gain):
    root = lax.rsqrt(jnp.sum(direction * direction, axis=1, keepdims=True) + 1e-12)
    return root, gain * root


def weight_kernel(
    core_ref,
    codes_ref,
    first_w,
    second_w,
    sum_two,
    sum_codes,
    sum_coord,
    sum_head,
    _,
    sum_loss,
    keep_ref,
    give_ref,
    flat,
):
    core = core_ref[0]
    codes = codes_ref[...]
    by_code = sum_codes[...]
    code_hi, code_lo = halves(codes)
    by_hi, by_lo = halves(by_code)
    latent_grad = mm(beside(by_hi, by_hi, by_lo), stacked(code_hi, code_lo, code_hi))

    flat[...] = jnp.zeros(flat.shape, F32)
    lane = rows_of_lanes(1, (8, LANES))
    line = rows_of_lanes(0, (8, LANES))

    def lane_sum(v):
        return jnp.sum(v, axis=1, keepdims=True)

    for group, first, shift in unit_groups(*FIRST_UNITS):
        rows = slice(group * 8, group * 8 + 8)
        raw = [first_w[rows, c * LANES : (c + 1) * LANES] for c in range(3)]
        gain = raw[2][:, 3:4]
        raw[2] = jnp.where(lane < 3, raw[2], 0.0)
        grad = [latent_grad[rows, c * LANES : (c + 1) * LANES] for c in range(2)]
        near = 0.0
        for i in range(3):
            near = jnp.where(
                lane == i, lane_sum(sum_coord[rows, i * LANES : (i + 1) * LANES]), near
            )
        grad.append(near)
        root = lax.rsqrt(lane_sum(sum(v * v for v in raw)) + 1e-12)
        scale = gain * root
        along = lane_sum(sum(v * g for v, g in zip(raw, grad)))
        inward = scale * root * root * along
        tiles = [scale * g - v * inward for v, g in zip(raw, grad)]
        tiles[2] = jnp.where(lane == 3, root * along, tiles[2])
        bias = lane_sum(by_code[rows, :LANES] + by_code[rows, LANES:])
        tiles[2] = jnp.where(lane == 4, bias, tiles[2])
        if group * 8 + 8 > MIDDLE:
            tiles = [jnp.where(line < MIDDLE - group * 8, v, 0.0) for v in tiles]
        pack_group(flat, tiles, first, shift, *FIRST_UNITS[1:3])

    edge = lane < MIDDLE - LANES
    for group, first, shift in unit_groups(*SECOND_UNITS):
        rows = slice(group * 8, group * 8 + 8)
        low = slice(256 + group * 8, 256 + group * 8 + 8)
        raw = [second_w[rows, c * LANES : (c + 1) * LANES] for c in range(4)]
        gain = second_w[rows, 512:513]
        hidden = [sum_two[rows, c * LANES : (c + 1) * LANES] for c in range(2)]
        moved = pltpu.roll(latent_grad[low, :], 256 - 3, 1)
        moved = [moved[:, :LANES], moved[:, LANES:]]
        grad = [
            hidden[0],
            jnp.where(edge, hidden[1], moved[1]),
            moved[0],
            jnp.where(edge, moved[1], hidden[1]),
        ]
        root = lax.rsqrt(lane_sum(sum(v * v for v in raw)) + 1e-12)
        scale = gain * root
        along = lane_sum(sum(v * g for v, g in zip(raw, grad)))
        inward = scale * root * root * along
        tiles = [scale * g - v * inward for v, g in zip(raw, grad)]
        end = jnp.where(lane == 0, root * along, 0.0)
        end = jnp.where(lane == 1, lane_sum(by_code[low, :LANES] + by_code[low, LANES:]), end)
        tiles.append(jnp.where(lane == 2, lane_sum(sum_head[rows, :]), end))
        pack_group(flat, tiles, first, shift, *SECOND_UNITS[1:3])

    row = HEAD_ENTRY // LANES
    lane = rows_of_lanes(1, (1, LANES))
    bias_total = jnp.sum(sum_loss[1:2, :], axis=1, keepdims=True)
    flat[row : row + 1, :] = flat[row : row + 1, :] + jnp.where(
        lane == HEAD_ENTRY % LANES, bias_total, 0.0
    )
    size = 16 * SHARD_ROWS
    for which in range(2):

        @pl.when(core == which)
        def _(which=which):
            for z in range(4):
                for c in range(2):
                    target = keep_ref if c == which else give_ref
                    first = (z * 2 + c) * size
                    target[z * size : (z + 1) * size, :] = flat[first : first + size, :]


def vmem(count):
    return [pl.BlockSpec(memory_space=pltpu.VMEM)] * count


PARAMS = pltpu.CompilerParams(vmem_limit_bytes=48 * 1024 * 1024)


HBM = pl.BlockSpec(memory_space=pltpu.HBM)
SMEM = pl.BlockSpec(memory_space=pltpu.SMEM)


def f32(*shape):
    return jax.ShapeDtypeStruct(shape, F32)


def pack_boxes(weights, coords, distances, index):
    return pl.pallas_call(
        pack_kernel,
        out_shape=f32(PEERS, BOX_ROWS, LANES),
        in_specs=[HBM] * 4,
        out_specs=HBM,
        scratch_shapes=[
            pltpu.VMEM(weights.shape, F32),
            pltpu.VMEM(coords.shape, F32),
            pltpu.VMEM(distances.shape, F32),
            pltpu.VMEM(index.shape, jnp.int32),
            pltpu.VMEM((PEERS, BOX_ROWS, LANES), F32),
            pltpu.SemaphoreType.DMA((6,)),
        ],
        compiler_params=pltpu.CompilerParams(vmem_limit_bytes=60 * 1024 * 1024),
    )(weights, coords, distances, index)


def main_kernel(
    core_ref, mine_ref, other_ref, codes_ref, keep_ref, give_ref, code_grad_ref, facts_ref, *scratch
):
    first_w, second_w, latent_w, *sums = scratch[:9]
    flat = scratch[9]
    loop_kernel(core_ref, mine_ref, other_ref, codes_ref, *scratch)
    code_kernel(codes_ref, latent_w, sums[1], sums[4], sums[5], code_grad_ref, facts_ref)
    weight_kernel(core_ref, codes_ref, first_w, second_w, *sums, keep_ref, give_ref, flat)


def main_call(core, mine, other, codes):
    pair = (SUBS, 256, BLOCK)
    pair_two = (SUBS, HID, BLOCK)
    scratch = [
        ((256, 3 * LANES), F32),
        ((HID, 5 * LANES), F32),
        ((768, 256), F32),
        ((HID, 256), F32),
        ((768, 256), F32),
        ((256, 3 * LANES), F32),
        ((HID, LANES), F32),
        ((CODE_ROWS, LANES), F32),
        ((2, BLOCK), F32),
        ((FLAT_ROWS + 8, LANES), F32),
        ((256, 512), BF16),
        ((HID, 1280), BF16),
        ((256, 1536), BF16),
        ((256, 3 * LANES), F32),
        ((HID, 2 * LANES), F32),
        ((LANES, LANES), F32),
        (pair, F32),
        (pair, F32),
        (pair, F32),
        (pair, F32),
        (pair, BF16),
        (pair, BF16),
        (pair, BF16),
        ((SUBS, BLOCK, CODE_ROWS), BF16),
        (pair_two, F32),
        (pair_two, F32),
        (pair_two, F32),
        (pair_two, F32),
        (pair_two, BF16),
        (pair_two, BF16),
        (pair, BF16),
        (pair, BF16),
        (pair_two, BF16),
        (pair_two, BF16),
        (pair, BF16),
        (pair, BF16),
    ]
    boxes = f32(PEERS * SHARD_ROWS, LANES)
    return pl.pallas_call(
        main_kernel,
        out_shape=(boxes, boxes, f32(CODE_ROWS, LATENT), f32(8, LANES)),
        in_specs=[SMEM] + vmem(3),
        out_specs=tuple(vmem(4)),
        scratch_shapes=[pltpu.VMEM(shape, dtype) for shape, dtype in scratch],
        compiler_params=PARAMS,
    )(core, mine, other, codes)


def adam_update(value, first, second, grad, rate):
    first_new = BETA_ONE * first + (1.0 - BETA_ONE) * grad
    second_new = BETA_TWO * second + (1.0 - BETA_TWO) * grad * grad
    first_hat = first_new / (1.0 - BETA_ONE**STEP)
    second_hat = second_new / (1.0 - BETA_TWO**STEP)
    value_new = value - rate * (first_hat / (jnp.sqrt(second_hat) + ADAM_EPS) + DECAY * value)
    return (value_new, first_new, second_new)


def shard_kernel(parts_ref, facts_ref, shard_ref, all_facts_ref):
    total = parts_ref[0:SHARD_ROWS, :]
    for peer in range(1, PEERS):
        total = total + parts_ref[peer * SHARD_ROWS : (peer + 1) * SHARD_ROWS, :]
    shard_ref[...] = total
    facts = facts_ref[...]
    left = rows_of_lanes(1, facts.shape) < LANES // 2
    all_facts_ref[...] = facts + jnp.where(left, total_of(total * total), 0.0)


def sum_shards(parts, facts):
    return pl.pallas_call(
        shard_kernel,
        out_shape=(f32(SHARD_ROWS, LANES), f32(8, LANES)),
        in_specs=vmem(2),
        out_specs=tuple(vmem(2)),
        compiler_params=PARAMS,
    )(parts, facts)


def update_kernel(
    seen_ref,
    shard_ref,
    weights_ref,
    moment_one_ref,
    moment_two_ref,
    codes_ref,
    code_first_ref,
    code_second_ref,
    code_grad_ref,
    loss_out,
    norm_out,
    weights_out,
    moment_one_out,
    moment_two_out,
    weights_copy_out,
    codes_out,
    code_first_out,
    code_second_out,
    codes_copy_out,
):
    total = jnp.sum(seen_ref[...], axis=0, keepdims=True)
    loss_out[...] = total[:, LANES // 2 : LANES // 2 + 1]
    norm = jnp.sqrt(total[:, 0:1])
    norm_out[...] = norm
    factor = jnp.minimum(1.0, CLIP / (norm + 1e-06))
    value, first, second = adam_update(
        weights_ref[...],
        moment_one_ref[...],
        moment_two_ref[...],
        factor * shard_ref[...],
        WEIGHT_RATE,
    )
    weights_out[...] = value
    moment_one_out[...] = first
    moment_two_out[...] = second
    weights_copy_out[...] = value.astype(BF16)
    for r in range(0, CODE_ROWS, 32):
        rows = slice(r, r + 32)
        value, first, second = adam_update(
            codes_ref[rows, :],
            code_first_ref[rows, :],
            code_second_ref[rows, :],
            factor * code_grad_ref[rows, :],
            CODE_RATE,
        )
        codes_out[rows, :] = value
        code_first_out[rows, :] = first
        code_second_out[rows, :] = second
        codes_copy_out[rows, :] = value.astype(BF16)


def update_all(*args):
    scalar = jax.ShapeDtypeStruct((1, 1), F32)
    shard = [jax.ShapeDtypeStruct((SHARD_ROWS, LANES), t) for t in (F32, F32, F32, BF16)]
    table = [jax.ShapeDtypeStruct((CODE_ROWS, LATENT), t) for t in (F32, F32, F32, BF16)]
    return pl.pallas_call(
        update_kernel,
        out_shape=(scalar, scalar, *shard, *table),
        in_specs=vmem(9),
        out_specs=tuple(vmem(10)),
        compiler_params=PARAMS,
    )(*args)


def swap_cores(v):
    return lax.ppermute(v, "core", [(0, 1), (1, 0)])


def exchange(v):
    return lax.all_to_all(v, ("z", "wide"), split_axis=0, concat_axis=0)


def body(
    weights_flat,
    moment_one,
    moment_two,
    codes,
    code_first,
    code_second,
    coords,
    distances,
    shape_index,
):
    boxes = pack_boxes(
        weights_flat.reshape(SHARD_ROWS, LANES),
        coords,
        distances.reshape(1, POINTS_DEV),
        shape_index.reshape(1, POINTS_DEV),
    )
    mine = exchange(boxes)
    other = swap_cores(mine)
    core = lax.axis_index("core").astype(jnp.int32).reshape(1)
    keep, give, code_grad, facts = main_call(
        core,
        mine.reshape(PEERS * BOX_ROWS, LANES),
        other.reshape(PEERS * BOX_ROWS, LANES),
        codes,
    )
    pair_sum = (keep + swap_cores(give)).reshape(PEERS, 1, SHARD_ROWS * LANES)
    parts = exchange(pair_sum).reshape(PEERS * SHARD_ROWS, LANES)
    shard, facts = sum_shards(parts, facts)
    facts = facts + swap_cores(facts)
    facts = jnp.broadcast_to(facts[0:1], (PEERS, LANES)).reshape(PEERS, 1, LANES)
    flat = lambda v: v.reshape(SHARD_ROWS, LANES)
    out = update_all(
        exchange(facts).reshape(PEERS, LANES),
        shard,
        flat(weights_flat),
        flat(moment_one),
        flat(moment_two),
        codes,
        code_first,
        code_second,
        code_grad,
    )
    return (
        out[0].reshape(()),
        out[1].reshape(()),
        *[v.reshape(weights_flat.shape) for v in out[2:6]],
        *out[6:],
    )


def solution(mesh):
    parts = Mesh(mesh.devices.reshape(4, 2, 16), ALL)
    return jax.shard_map(
        body,
        mesh=parts,
        in_specs=(
            P(ALL),
            P(ALL),
            P(ALL),
            P(ALL, None),
            P(ALL, None),
            P(ALL, None),
            P(None, ALL),
            P(ALL),
            P(ALL),
        ),
        out_specs=(
            P(),
            P(),
            P(ALL),
            P(ALL),
            P(ALL),
            P(ALL),
            P(ALL, None),
            P(ALL, None),
            P(ALL, None),
            P(ALL, None),
        ),
        check_vma=False,
    )
```

```python
import jax
import jax.numpy as jnp
from jax import lax
from jax.experimental import pallas as pl
from jax.experimental.pallas import tpu as pltpu
from jax.sharding import Mesh
from jax.sharding import PartitionSpec as P

LATENT = 256
HID = 512
MIDDLE = HID - LATENT - 3
STEP = 10

DELTA = 0.1
SMOOTH = 0.01
CODE_WEIGHT = 0.001
EIK_WEIGHT = 0.1
CLIP = 0.001
WEIGHT_RATE = 0.02
CODE_RATE = 0.15
BETA_ONE = 0.9
BETA_TWO = 0.999
ADAM_EPS = 1e-08
DECAY = 0.01

LANES = 128
DEVICES = 128
PEERS = 64
SHARD_ROWS = 21
BOX_ROWS = 24
SLOTS = 16
POINTS_DEV = 1024
CODE_ROWS = 256
FLAT_ROWS = DEVICES * SHARD_ROWS
BLOCK = 256
SUBS = 4
TILES = BLOCK // LANES
ALL_POINTS = POINTS_DEV * DEVICES

F32 = jnp.float32
BF16 = jnp.bfloat16
ALL = ("z", "core", "wide")


def rows_of_lanes(lead, shape):
    return lax.broadcasted_iota(jnp.int32, shape, lead)


def halves(v):
    high = v.astype(BF16)
    return high, (v - high.astype(F32)).astype(BF16)


def thirds(v):
    high = v.astype(BF16).astype(F32)
    rest = v - high
    mid = rest.astype(BF16).astype(F32)
    return high, mid, rest - mid


def mm(a, b):
    return lax.dot_general(a, b, (((1,), (0,)), ((), ())), preferred_element_type=F32)


def mm_nt(a, b):
    return lax.dot_general(a, b, (((1,), (1,)), ((), ())), preferred_element_type=F32)


def beside(*parts):
    return jnp.concatenate(parts, axis=1)


def total_of(v):
    return jnp.sum(jnp.sum(v, axis=0, keepdims=True), axis=1, keepdims=True)


def stacked(*parts):
    return jnp.concatenate(parts, axis=0)


def pack_kernel(
    weights_hbm,
    coords_hbm,
    distances_hbm,
    index_hbm,
    out_hbm,
    weights_ref,
    coords_ref,
    distances_ref,
    index_ref,
    staged,
    sems,
):
    pairs = [
        (index_hbm, index_ref),
        (weights_hbm, weights_ref),
        (coords_hbm, coords_ref),
        (distances_hbm, distances_ref),
    ]
    copies = [
        pltpu.make_async_copy(source, target, sems.at[i])
        for i, (source, target) in enumerate(pairs)
    ]
    for copy in copies:
        copy.start()
    copies[1].wait()
    shard = stacked(weights_ref[...], jnp.zeros((BOX_ROWS - SHARD_ROWS, LANES), F32))
    for peer in range(PEERS):
        staged[peer] = shard
    early = pltpu.make_async_copy(
        staged.at[:, pl.ds(0, 16), :], out_hbm.at[:, pl.ds(0, 16), :], sems.at[4]
    )
    early.start()
    for i in (0, 2, 3):
        copies[i].wait()
    index = index_ref[...]
    owner = lax.shift_right_logical(index, 8)
    row = lax.bitwise_and(index, CODE_ROWS - 1)
    sent = (rows_of_lanes(0, (DEVICES, POINTS_DEV)) == owner).astype(F32)
    sent_low = sent.astype(BF16)
    width = 256
    earlier = rows_of_lanes(0, (width, width)) < rows_of_lanes(1, (width, width))
    earlier = earlier.astype(F32).astype(BF16)
    ones = jnp.ones((width, width), BF16)
    ranks = [
        mm(sent_low[:, : (part + 1) * width], stacked(*([ones] * part + [earlier])))
        for part in range(POINTS_DEV // width)
    ]
    placed = jnp.sum(sent * beside(*ranks), axis=0, keepdims=True).astype(jnp.int32)
    at_slot = rows_of_lanes(0, (SLOTS, POINTS_DEV)) == placed
    values = [coords_ref[i : i + 1, :] for i in range(3)]
    values += [distances_ref[...], (row + 1).astype(F32)]
    pieces = [[], [], []]
    for value in values:
        for k, third in enumerate(thirds(value)):
            pieces[k].append(jnp.where(at_slot, third, 0.0))
    spare = jnp.zeros((LANES - SLOTS * len(values), POINTS_DEV), F32)
    boxes = mm_nt(
        beside(sent_low, sent_low, sent_low),
        beside(*[stacked(*piece, spare).astype(BF16) for piece in pieces]),
    )
    for d in range(DEVICES):
        z, core, w = d // 32, d // 16 % 2, d % 16
        row = SHARD_ROWS + core
        staged[z * 16 + w, row : row + 1, :] = boxes[d : d + 1, :]
    late = pltpu.make_async_copy(
        staged.at[:, pl.ds(16, 8), :], out_hbm.at[:, pl.ds(16, 8), :], sems.at[5]
    )
    late.start()
    early.wait()
    late.wait()


def unit_groups(count, stride_rows, extra, first_entry):
    for group in range(count):
        entry = first_entry + group * 8 * (stride_rows * LANES + extra)
        yield group, entry // LANES, entry % LANES


def unpack_units(flat_ref, out_ref, count, stride_rows, extra, first_entry):
    lane = rows_of_lanes(1, (8, LANES))
    slope = rows_of_lanes(0, (8, LANES)) * extra
    for group, first, shift in unit_groups(count, stride_rows, extra, first_entry):
        start = slope + shift
        wraps = shift + 7 * extra >= LANES
        turn = lax.bitwise_and(lane + start, LANES - 1)
        tiles = []
        for a in range(stride_rows + 2 + wraps):
            tile = flat_ref[pl.ds(first + a, 8, stride=stride_rows), :]
            tiles.append(jnp.take_along_axis(tile, turn, axis=1, mode="promise_in_bounds"))
        for c in range(stride_rows + 1):
            value = jnp.where(lane + start < LANES, tiles[c], tiles[c + 1])
            if wraps:
                value = jnp.where(lane + start < 2 * LANES, value, tiles[c + 2])
            out_ref[group * 8 : group * 8 + 8, c * LANES : (c + 1) * LANES] = value


def pack_units(value_ref, flat_ref, count, stride_rows, extra, first_entry, tails):
    lane = rows_of_lanes(1, (8, LANES))
    slope = rows_of_lanes(0, (8, LANES)) * extra
    zero = jnp.zeros((8, LANES), F32)
    for group, first, shift in unit_groups(count, stride_rows, extra, first_entry):
        start = slope + shift
        wraps = shift + 7 * extra >= LANES
        turn = lax.bitwise_and(lane - start, LANES - 1)
        rolled = {}

        def tile(c, rolled=rolled, group=group, turn=turn):
            if c < 0 or c > stride_rows:
                return zero
            if c not in rolled:
                value = value_ref[group * 8 : group * 8 + 8, c * LANES : (c + 1) * LANES]
                rolled[c] = jnp.take_along_axis(value, turn, axis=1, mode="promise_in_bounds")
            return rolled[c]

        for a in range(stride_rows, stride_rows + 2) if tails else range(stride_rows):
            value = jnp.where(lane >= start, tile(a), tile(a - 1))
            if wraps:
                value = jnp.where(lane >= start - LANES, value, tile(a - 2))
            flat_ref[pl.ds(first + a, 8, stride=stride_rows), :] = value


FIRST_UNITS = (32, 2, 5, 0)
SECOND_UNITS = (64, 4, 3, MIDDLE * (LATENT + 5))
HEAD_ENTRY = MIDDLE * (LATENT + 5) + HID * (HID + 3)


def across(column):
    return beside(*[column] * TILES)


def folded(v):
    return sum(v[:, i * LANES : (i + 1) * LANES] for i in range(TILES))


def silu_parts(half):
    gate = jnp.tanh(half)
    low = 0.5 * gate
    bend = 0.5 - gate * low
    bent = half * gate
    return half + bent, (0.5 + low) + half * bend, bend * (1.0 - bent)


def silu_parts_twice(half):
    gate = jnp.tanh(half)
    bend = 1.0 - gate * gate
    bent = half * gate
    return half + bent, (1.0 + gate) + half * bend, bend * (1.0 - bent)


def loop_kernel(
    core_ref,
    mine_ref,
    other_ref,
    codes_ref,
    first_w,
    second_w,
    latent_w,
    sum_two,
    sum_codes,
    sum_coord,
    sum_head,
    sum_count,
    sum_loss,
    flat,
    lhs_one,
    lhs_two,
    lhs_back,
    coord_w,
    head_w,
    spots,
    act_one,
    slope_one,
    curve_one,
    back_one,
    hid_hi,
    hid_lo,
    hot,
    hot_turned,
    act_two,
    slope_two,
    curve_two,
    act_tang,
    gate_hi,
    gate_lo,
    tang_hi,
    tang_lo,
    bar_hi,
    bar_lo,
    low_hi,
    low_lo,
):
    core = core_ref[0]

    for which in range(2):

        @pl.when(core == which)
        def _(which=which):
            for d in range(DEVICES):
                z, c, w = d // 32, d // 16 % 2, d % 16
                box = (z * 16 + w) * BOX_ROWS
                source = mine_ref if c == which else other_ref
                flat[d * SHARD_ROWS : d * SHARD_ROWS + BOX_ROWS, :] = source[box : box + BOX_ROWS, :]
            rows = pl.ds(SHARD_ROWS + which, PEERS, stride=BOX_ROWS)
            spots[...] = stacked(mine_ref[rows, :], other_ref[rows, :]).T

    unpack_units(flat, first_w, *FIRST_UNITS)
    unpack_units(flat, second_w, *SECOND_UNITS)
    head_bias = flat[HEAD_ENTRY // LANES : HEAD_ENTRY // LANES + 1, :][
        :, HEAD_ENTRY % LANES : HEAD_ENTRY % LANES + 1
    ]

    lane = rows_of_lanes(1, (256, LANES))
    unit = rows_of_lanes(0, (256, LANES))
    real = unit < MIDDLE

    first_low = jnp.where(beside(real, real), first_w[:, : 2 * LANES], 0.0)
    first_end = jnp.where(real, first_w[:, 2 * LANES :], 0.0)
    first_near = jnp.where(lane < 3, first_end, 0.0)
    first_gain = first_end[:, 3:4]
    first_bias = first_end[:, 4:5]
    first_w[:, : 2 * LANES] = first_low
    first_w[:, 2 * LANES :] = first_end
    _, first_scale = norm_parts(beside(first_low, first_near), first_gain)
    first_low = first_low * first_scale
    first_near = first_near * first_scale
    latent_w[0:256, :] = first_low
    for i in range(3):
        coord_w[:, i * LANES : (i + 1) * LANES] = jnp.broadcast_to(
            0.5 * first_near[:, i : i + 1], (256, LANES)
        )

    second_a = second_w[:, 0:256]
    second_b = second_w[:, 256:512]
    second_gain = second_w[:, 512:513]
    second_bias = second_w[:, 513:514]
    head = jnp.broadcast_to(second_w[:, 514:515], (HID, LANES))
    head_w[:, :LANES] = 0.5 * head
    head_w[:, LANES:] = head
    _, second_scale = norm_parts(second_w[:, 0:512], second_gain)
    second_a = second_a * second_scale
    second_b = second_b * second_scale
    is_hidden = rows_of_lanes(1, (HID, 256)) < MIDDLE
    hidden_cols = jnp.where(is_hidden, second_a, second_b)
    latent_cols = pltpu.roll(jnp.where(is_hidden, second_b, second_a), 3, 1)
    latent_w[256:768, :] = latent_cols

    hidden_hi, hidden_lo = halves(0.5 * hidden_cols)
    lhs_two[:, 0:256] = hidden_hi
    lhs_two[:, 256:512] = hidden_hi
    lhs_two[:, 512:768] = hidden_lo
    back_hi, back_lo = halves(hidden_cols.T)
    lhs_back[:, 0:512] = back_hi
    lhs_back[:, 512:1024] = back_hi
    lhs_back[:, 1024:1536] = back_lo

    code_hi, code_lo = halves(codes_ref[...])
    weight_hi, weight_lo = halves(latent_w[...])
    by_code = mm_nt(
        beside(weight_hi, weight_hi, weight_lo), beside(code_hi, code_lo, code_hi)
    )
    one_hi, one_lo = halves(0.5 * (by_code[0:256, :] + first_bias))
    lhs_one[:, 0:256] = one_hi
    lhs_one[:, 256:512] = one_lo
    two_hi, two_lo = halves(0.5 * (by_code[256:768, :] + second_bias))
    lhs_two[:, 768:1024] = two_hi
    lhs_two[:, 1024:1280] = two_lo

    for ref in (sum_two, sum_codes, sum_coord, sum_head, sum_count, sum_loss):
        ref[...] = jnp.zeros(ref.shape, F32)

    def feature(which, step, sub):
        first = which * SLOTS + (step * SUBS + sub) * TILES
        return beside(*[spots[pl.ds(first + i, 1), :] for i in range(TILES)])

    blank5 = jnp.zeros((5, BLOCK), F32)
    chunk = 8192 // BLOCK
    low_chunks = range(0, 256, chunk)
    high_chunks = range(0, HID, chunk)

    def block_stages(step, s):
        place = [feature(i, step, s) for i in range(3)]
        target = feature(3, step, s)
        code_row = feature(4, step, s)
        valid = (code_row > 0.5).astype(F32)

        wanted = code_row - 1.0
        for r in range(0, CODE_ROWS, chunk):
            row = (rows_of_lanes(0, (chunk, BLOCK)) + r).astype(F32)
            mark = jnp.where(row == wanted, 1.0, 0.0)
            hot[s, r : r + chunk, :] = mark.astype(BF16)
            sum_count[r : r + chunk, :] += folded(mark)
        for i in range(TILES):
            wanted = jnp.broadcast_to(code_row[:, i * LANES : (i + 1) * LANES] - 1.0, (LANES, LANES)).T
            for c in range(0, CODE_ROWS, LANES):
                code = (rows_of_lanes(1, (LANES, LANES)) + c).astype(F32)
                mark = jnp.where(code == wanted, 1.0, 0.0).astype(BF16)
                hot_turned[s, i * LANES : (i + 1) * LANES, c : c + LANES] = mark
        yield

        act_one[s] = mm(lhs_one[...], stacked(hot[s], hot[s]))
        yield
        last = stacked(blank5, *place)
        for r in low_chunks:
            pre = act_one[s, r : r + chunk, :]
            for i in range(3):
                pre = pre + across(coord_w[r : r + chunk, i * LANES : (i + 1) * LANES]) * place[i]
            value, slope, curve = silu_parts(pre)
            if r + chunk == 256:
                inside = rows_of_lanes(0, (chunk, BLOCK)) + r < MIDDLE
                end = jnp.where(inside[chunk - 8 :], value[chunk - 8 :], last)
                value = stacked(value[: chunk - 8], end)
                slope = jnp.where(inside, slope, 0.0)
                curve = jnp.where(inside, curve, 0.0)
            high, low = halves(value)
            hid_hi[s, r : r + chunk, :] = high
            hid_lo[s, r : r + chunk, :] = low
            slope_one[s, r : r + chunk, :] = slope
            curve_one[s, r : r + chunk, :] = curve
        yield

        act_two[s] = mm(lhs_two[...], stacked(hid_hi[s], hid_lo[s], hid_hi[s], hot[s], hot[s]))
        yield
        total = jnp.zeros((8, BLOCK), F32)
        for r in high_chunks:
            value, slope, curve = silu_parts_twice(act_two[s, r : r + chunk, :])
            head = across(head_w[r : r + chunk, :LANES])
            weighed = head * value
            for k in range(0, chunk, 8):
                total = total + weighed[k : k + 8, :]
            high, low = halves(head * slope)
            gate_hi[s, r : r + chunk, :] = high
            gate_lo[s, r : r + chunk, :] = low
            act_two[s, r : r + chunk, :] = value
            slope_two[s, r : r + chunk, :] = slope
            curve_two[s, r : r + chunk, :] = curve
        summed = jnp.sum(total, axis=0, keepdims=True)
        yield

        back_one[s] = mm(lhs_back[...], stacked(gate_hi[s], gate_lo[s], gate_hi[s]))
        yield
        totals = [jnp.zeros((8, BLOCK), F32) for _ in range(3)]
        for r in low_chunks:
            grad = back_one[s, r : r + chunk, :] * slope_one[s, r : r + chunk, :]
            for i in range(3):
                weighed = across(coord_w[r : r + chunk, i * LANES : (i + 1) * LANES]) * grad
                for k in range(0, chunk, 8):
                    totals[i] = totals[i] + weighed[k : k + 8, :]
        lead = [
            2.0 * jnp.sum(totals[i], axis=0, keepdims=True)
            + back_one[s, MIDDLE + i : MIDDLE + i + 1, :]
            for i in range(3)
        ]

        predicted = jnp.tanh(2.0 * summed + head_bias)
        flank = 1.0 - predicted * predicted
        slope = [flank * q for q in lead]
        excess = slope[0] * slope[0] + slope[1] * slope[1] + slope[2] * slope[2] - 1.0
        capped = jnp.tanh(predicted / DELTA)
        misfit = DELTA * capped - DELTA * jnp.tanh(target / DELTA)
        fitting = jnp.sqrt(misfit * misfit + SMOOTH * SMOOTH)
        sum_loss[0:1, :] += valid * (fitting + EIK_WEIGHT * excess * excess)
        share = valid * (1.0 / ALL_POINTS)
        pull = [(4.0 * EIK_WEIGHT) * excess * v for v in slope]
        by_flank = sum(p * q for p, q in zip(pull, lead))
        by_predicted = misfit / fitting * (1.0 - capped * capped) - 2.0 * predicted * by_flank
        bar_out = share * by_predicted * flank
        sum_loss[1:2, :] += bar_out
        half_bar = 0.5 * bar_out
        pull = [share * flank * p for p in pull]

        last = stacked(blank5, *pull)
        twice = [2.0 * p for p in pull]
        for r in low_chunks:
            grad = 0.0
            for i in range(3):
                grad = grad + across(coord_w[r : r + chunk, i * LANES : (i + 1) * LANES]) * twice[i]
            slope = slope_one[s, r : r + chunk, :]
            back = back_one[s, r : r + chunk, :]
            near = back * slope
            for i in range(3):
                sum_coord[r : r + chunk, i * LANES : (i + 1) * LANES] += folded(near * pull[i])
            through = grad * slope
            if r + chunk == 256:
                inside = rows_of_lanes(0, (8, BLOCK)) < MIDDLE - 248
                end = jnp.where(inside, through[chunk - 8 :], last)
                through = stacked(through[: chunk - 8], end)
            high, low = halves(through)
            tang_hi[s, r : r + chunk, :] = high
            tang_lo[s, r : r + chunk, :] = low
            curve_one[s, r : r + chunk, :] = (
                grad * back * curve_one[s, r : r + chunk, :]
            )
        yield
        act_tang[s] = mm(lhs_two[:, 0:768], stacked(tang_hi[s], tang_lo[s], tang_hi[s]))
        yield
        for r in high_chunks:
            tangent = act_tang[s, r : r + chunk, :]
            slope = slope_two[s, r : r + chunk, :]
            head = across(head_w[r : r + chunk, LANES:])
            bar = head * (half_bar * slope + tangent * curve_two[s, r : r + chunk, :])
            by_head = act_two[s, r : r + chunk, :] * bar_out + slope * tangent
            sum_head[r : r + chunk, :] += folded(by_head)
            high, low = halves(bar)
            bar_hi[s, r : r + chunk, :] = high
            bar_lo[s, r : r + chunk, :] = low
        yield

        back_one[s] = mm(lhs_back[...], stacked(bar_hi[s], bar_lo[s], bar_hi[s]))
        yield
        for r in low_chunks:
            bar = (
                back_one[s, r : r + chunk, :] * slope_one[s, r : r + chunk, :]
                + curve_one[s, r : r + chunk, :]
            )
            for i in range(3):
                sum_coord[r : r + chunk, i * LANES : (i + 1) * LANES] += folded(bar * place[i])
            high, low = halves(bar)
            low_hi[s, r : r + chunk, :] = high
            low_lo[s, r : r + chunk, :] = low
        yield

        sum_two[...] += mm_nt(
            beside(bar_hi[s], bar_hi[s], bar_lo[s], gate_hi[s], gate_hi[s], gate_lo[s]),
            beside(hid_hi[s], hid_lo[s], hid_hi[s], tang_hi[s], tang_lo[s], tang_hi[s]),
        )
        turned = stacked(hot_turned[s], hot_turned[s])
        sum_codes[256:768, :] += mm(beside(bar_hi[s], bar_lo[s]), turned)
        sum_codes[0:256, :] += mm(beside(low_hi[s], low_lo[s]), turned)

    def step_body(step, carry):
        waiting = [block_stages(step, s) for s in range(SUBS)]
        active = []
        while waiting or active:
            if waiting:
                active.append(waiting.pop(0))
            active = [work for work in active if next(work, work) is not work]
        return carry

    steps = SLOTS * DEVICES // (SUBS * BLOCK)
    if steps == 1:
        step_body(0, 0)
    else:
        lax.fori_loop(0, steps, step_body, 0)


def code_kernel(codes_ref, latent_w, sum_codes, sum_count, sum_loss, code_grad_ref, facts_ref):
    codes = codes_ref[...]
    count = jnp.sum(sum_count[...], axis=1, keepdims=True)
    turned_hi, turned_lo = halves(sum_codes[...].T)
    weight_hi, weight_lo = halves(latent_w[...])
    code_grad = mm(
        beside(turned_hi, turned_hi, turned_lo), stacked(weight_hi, weight_lo, weight_hi)
    )
    code_grad = code_grad + (2.0 * CODE_WEIGHT / ALL_POINTS) * count * codes
    code_grad_ref[...] = code_grad
    loss = jnp.sum(sum_loss[0:1, :], axis=1, keepdims=True)
    loss = (loss + CODE_WEIGHT * total_of(count * codes * codes)) / ALL_POINTS
    left = rows_of_lanes(1, facts_ref.shape) < LANES // 2
    facts_ref[...] = jnp.where(left, total_of(code_grad * code_grad), loss)


def norm_parts(direction, gain):
    root = lax.rsqrt(jnp.sum(direction * direction, axis=1, keepdims=True) + 1e-12)
    return root, gain * root


def weight_kernel(
    core_ref,
    codes_ref,
    first_w,
    second_w,
    sum_two,
    sum_codes,
    sum_coord,
    sum_head,
    _,
    sum_loss,
    keep_ref,
    give_ref,
    flat,
    tails,
    first_grad,
    second_grad,
):
    core = core_ref[0]
    codes = codes_ref[...]
    by_code = sum_codes[...]
    code_hi, code_lo = halves(codes)
    by_hi, by_lo = halves(by_code)
    latent_grad = mm(beside(by_hi, by_hi, by_lo), stacked(code_hi, code_lo, code_hi))

    bias_grad = jnp.sum(by_code, axis=1, keepdims=True)
    lane = rows_of_lanes(1, (256, LANES))
    real = rows_of_lanes(0, (256, LANES)) < MIDDLE
    near_grad = 0.0
    for i in range(3):
        column = jnp.sum(sum_coord[:, i * LANES : (i + 1) * LANES], axis=1, keepdims=True)
        near_grad = jnp.where(lane == i, column, near_grad)
    low_grad = latent_grad[0:256, :]
    first_low = first_w[:, : 2 * LANES]
    first_near = jnp.where(lane < 3, first_w[:, 2 * LANES :], 0.0)
    root, scale = norm_parts(beside(first_low, first_near), first_w[:, 2 * LANES + 3 : 2 * LANES + 4])
    along = jnp.sum(first_low * low_grad, axis=1, keepdims=True)
    along = along + jnp.sum(first_near * near_grad, axis=1, keepdims=True)
    inward = scale * root * root * along
    end = scale * near_grad - first_near * inward
    end = jnp.where(lane == 3, root * along, end)
    end = jnp.where(lane == 4, bias_grad[0:256, :], end)
    low_grad = scale * low_grad - first_low * inward
    first_grad[:, : 2 * LANES] = jnp.where(beside(real, real), low_grad, 0.0)
    first_grad[:, 2 * LANES :] = jnp.where(real, end, 0.0)

    is_hidden = rows_of_lanes(1, (HID, 256)) < MIDDLE
    hidden_grad = sum_two[...]
    moved = pltpu.roll(latent_grad[256:768, :], 256 - 3, 1)
    grad_a = jnp.where(is_hidden, hidden_grad, moved)
    grad_b = jnp.where(is_hidden, moved, hidden_grad)
    second_a = second_w[:, 0:256]
    second_b = second_w[:, 256:512]
    root, scale = norm_parts(second_w[:, 0:512], second_w[:, 512:513])
    along = jnp.sum(second_a * grad_a + second_b * grad_b, axis=1, keepdims=True)
    inward = scale * root * root * along
    second_grad[:, 0:256] = scale * grad_a - second_a * inward
    second_grad[:, 256:512] = scale * grad_b - second_b * inward
    head_grad = jnp.sum(sum_head[...], axis=1, keepdims=True)
    lane = rows_of_lanes(1, (HID, LANES))
    end = jnp.where(lane == 0, root * along, 0.0)
    end = jnp.where(lane == 1, bias_grad[256:768, :], end)
    second_grad[:, 512:640] = jnp.where(lane == 2, head_grad, end)

    for ref in (flat, tails):
        ref[...] = jnp.zeros(ref.shape, F32)
    pack_units(first_grad, flat, *FIRST_UNITS, False)
    pack_units(second_grad, flat, *SECOND_UNITS, False)
    pack_units(first_grad, tails, *FIRST_UNITS, True)
    pack_units(second_grad, tails, *SECOND_UNITS, True)
    row = HEAD_ENTRY // LANES
    lane = rows_of_lanes(1, (1, LANES))
    bias_total = jnp.sum(sum_loss[1:2, :], axis=1, keepdims=True)
    flat[row : row + 1, :] += jnp.where(lane == HEAD_ENTRY % LANES, bias_total, 0.0)
    size = 16 * SHARD_ROWS
    for which in range(2):

        @pl.when(core == which)
        def _(which=which):
            for z in range(4):
                for c in range(2):
                    target = keep_ref if c == which else give_ref
                    first = (z * 2 + c) * size
                    target[z * size : (z + 1) * size, :] = (
                        flat[first : first + size, :] + tails[first : first + size, :]
                    )


def vmem(count):
    return [pl.BlockSpec(memory_space=pltpu.VMEM)] * count


PARAMS = pltpu.CompilerParams(vmem_limit_bytes=48 * 1024 * 1024)


HBM = pl.BlockSpec(memory_space=pltpu.HBM)
SMEM = pl.BlockSpec(memory_space=pltpu.SMEM)


def f32(*shape):
    return jax.ShapeDtypeStruct(shape, F32)


def pack_boxes(weights, coords, distances, index):
    return pl.pallas_call(
        pack_kernel,
        out_shape=f32(PEERS, BOX_ROWS, LANES),
        in_specs=[HBM] * 4,
        out_specs=HBM,
        scratch_shapes=[
            pltpu.VMEM(weights.shape, F32),
            pltpu.VMEM(coords.shape, F32),
            pltpu.VMEM(distances.shape, F32),
            pltpu.VMEM(index.shape, jnp.int32),
            pltpu.VMEM((PEERS, BOX_ROWS, LANES), F32),
            pltpu.SemaphoreType.DMA((6,)),
        ],
        compiler_params=pltpu.CompilerParams(vmem_limit_bytes=60 * 1024 * 1024),
    )(weights, coords, distances, index)


def main_kernel(
    core_ref, mine_ref, other_ref, codes_ref, keep_ref, give_ref, code_grad_ref, facts_ref, *scratch
):
    first_w, second_w, latent_w, *sums = scratch[:9]
    flat = scratch[9]
    loop_kernel(core_ref, mine_ref, other_ref, codes_ref, *scratch[:-3])
    code_kernel(codes_ref, latent_w, sums[1], sums[4], sums[5], code_grad_ref, facts_ref)
    weight_kernel(core_ref, codes_ref, first_w, second_w, *sums, keep_ref, give_ref, flat, *scratch[-3:])


def main_call(core, mine, other, codes):
    pair = (SUBS, 256, BLOCK)
    pair_two = (SUBS, HID, BLOCK)
    scratch = [
        ((256, 3 * LANES), F32),
        ((HID, 5 * LANES), F32),
        ((768, 256), F32),
        ((HID, 256), F32),
        ((768, 256), F32),
        ((256, 3 * LANES), F32),
        ((HID, LANES), F32),
        ((CODE_ROWS, LANES), F32),
        ((2, BLOCK), F32),
        ((FLAT_ROWS + 8, LANES), F32),
        ((256, 512), BF16),
        ((HID, 1280), BF16),
        ((256, 1536), BF16),
        ((256, 3 * LANES), F32),
        ((HID, 2 * LANES), F32),
        ((LANES, LANES), F32),
        (pair, F32),
        (pair, F32),
        (pair, F32),
        (pair, F32),
        (pair, BF16),
        (pair, BF16),
        (pair, BF16),
        ((SUBS, BLOCK, CODE_ROWS), BF16),
        (pair_two, F32),
        (pair_two, F32),
        (pair_two, F32),
        (pair_two, F32),
        (pair_two, BF16),
        (pair_two, BF16),
        (pair, BF16),
        (pair, BF16),
        (pair_two, BF16),
        (pair_two, BF16),
        (pair, BF16),
        (pair, BF16),
        ((FLAT_ROWS + 8, LANES), F32),
        ((256, 3 * LANES), F32),
        ((HID, 5 * LANES), F32),
    ]
    boxes = f32(PEERS * SHARD_ROWS, LANES)
    return pl.pallas_call(
        main_kernel,
        out_shape=(boxes, boxes, f32(CODE_ROWS, LATENT), f32(8, LANES)),
        in_specs=[SMEM] + vmem(3),
        out_specs=tuple(vmem(4)),
        scratch_shapes=[pltpu.VMEM(shape, dtype) for shape, dtype in scratch],
        compiler_params=PARAMS,
    )(core, mine, other, codes)


def adam_update(value, first, second, grad, rate):
    first_new = BETA_ONE * first + (1.0 - BETA_ONE) * grad
    second_new = BETA_TWO * second + (1.0 - BETA_TWO) * grad * grad
    first_hat = first_new / (1.0 - BETA_ONE**STEP)
    second_hat = second_new / (1.0 - BETA_TWO**STEP)
    value_new = value - rate * (first_hat / (jnp.sqrt(second_hat) + ADAM_EPS) + DECAY * value)
    return (value_new, first_new, second_new)


def shard_kernel(parts_ref, facts_ref, shard_ref, all_facts_ref):
    total = parts_ref[0:SHARD_ROWS, :]
    for peer in range(1, PEERS):
        total = total + parts_ref[peer * SHARD_ROWS : (peer + 1) * SHARD_ROWS, :]
    shard_ref[...] = total
    facts = facts_ref[...]
    left = rows_of_lanes(1, facts.shape) < LANES // 2
    all_facts_ref[...] = facts + jnp.where(left, total_of(total * total), 0.0)


def sum_shards(parts, facts):
    return pl.pallas_call(
        shard_kernel,
        out_shape=(f32(SHARD_ROWS, LANES), f32(8, LANES)),
        in_specs=vmem(2),
        out_specs=tuple(vmem(2)),
        compiler_params=PARAMS,
    )(parts, facts)


def update_kernel(
    seen_ref,
    shard_ref,
    weights_ref,
    moment_one_ref,
    moment_two_ref,
    codes_ref,
    code_first_ref,
    code_second_ref,
    code_grad_ref,
    loss_out,
    norm_out,
    weights_out,
    moment_one_out,
    moment_two_out,
    weights_copy_out,
    codes_out,
    code_first_out,
    code_second_out,
    codes_copy_out,
):
    total = jnp.sum(seen_ref[...], axis=0, keepdims=True)
    loss_out[...] = total[:, LANES // 2 : LANES // 2 + 1]
    norm = jnp.sqrt(total[:, 0:1])
    norm_out[...] = norm
    factor = jnp.minimum(1.0, CLIP / (norm + 1e-06))
    value, first, second = adam_update(
        weights_ref[...],
        moment_one_ref[...],
        moment_two_ref[...],
        factor * shard_ref[...],
        WEIGHT_RATE,
    )
    weights_out[...] = value
    moment_one_out[...] = first
    moment_two_out[...] = second
    weights_copy_out[...] = value.astype(BF16)
    for r in range(0, CODE_ROWS, 32):
        rows = slice(r, r + 32)
        value, first, second = adam_update(
            codes_ref[rows, :],
            code_first_ref[rows, :],
            code_second_ref[rows, :],
            factor * code_grad_ref[rows, :],
            CODE_RATE,
        )
        codes_out[rows, :] = value
        code_first_out[rows, :] = first
        code_second_out[rows, :] = second
        codes_copy_out[rows, :] = value.astype(BF16)


def update_all(*args):
    scalar = jax.ShapeDtypeStruct((1, 1), F32)
    shard = [jax.ShapeDtypeStruct((SHARD_ROWS, LANES), t) for t in (F32, F32, F32, BF16)]
    table = [jax.ShapeDtypeStruct((CODE_ROWS, LATENT), t) for t in (F32, F32, F32, BF16)]
    return pl.pallas_call(
        update_kernel,
        out_shape=(scalar, scalar, *shard, *table),
        in_specs=vmem(9),
        out_specs=tuple(vmem(10)),
        compiler_params=PARAMS,
    )(*args)


def swap_cores(v):
    return lax.ppermute(v, "core", [(0, 1), (1, 0)])


def exchange(v):
    return lax.all_to_all(v, ("z", "wide"), split_axis=0, concat_axis=0)


def body(
    weights_flat,
    moment_one,
    moment_two,
    codes,
    code_first,
    code_second,
    coords,
    distances,
    shape_index,
):
    boxes = pack_boxes(
        weights_flat.reshape(SHARD_ROWS, LANES),
        coords,
        distances.reshape(1, POINTS_DEV),
        shape_index.reshape(1, POINTS_DEV),
    )
    mine = exchange(boxes)
    other = swap_cores(mine)
    core = lax.axis_index("core").astype(jnp.int32).reshape(1)
    keep, give, code_grad, facts = main_call(
        core,
        mine.reshape(PEERS * BOX_ROWS, LANES),
        other.reshape(PEERS * BOX_ROWS, LANES),
        codes,
    )
    pair_sum = (keep + swap_cores(give)).reshape(PEERS, 1, SHARD_ROWS * LANES)
    parts = exchange(pair_sum).reshape(PEERS * SHARD_ROWS, LANES)
    shard, facts = sum_shards(parts, facts)
    facts = facts + swap_cores(facts)
    facts = jnp.broadcast_to(facts[0:1], (PEERS, LANES)).reshape(PEERS, 1, LANES)
    flat = lambda v: v.reshape(SHARD_ROWS, LANES)
    out = update_all(
        exchange(facts).reshape(PEERS, LANES),
        shard,
        flat(weights_flat),
        flat(moment_one),
        flat(moment_two),
        codes,
        code_first,
        code_second,
        code_grad,
    )
    return (
        out[0].reshape(()),
        out[1].reshape(()),
        *[v.reshape(weights_flat.shape) for v in out[2:6]],
        *out[6:],
    )


def solution(mesh):
    parts = Mesh(mesh.devices.reshape(4, 2, 16), ALL)
    return jax.shard_map(
        body,
        mesh=parts,
        in_specs=(
            P(ALL),
            P(ALL),
            P(ALL),
            P(ALL, None),
            P(ALL, None),
            P(ALL, None),
            P(None, ALL),
            P(ALL),
            P(ALL),
        ),
        out_specs=(
            P(),
            P(),
            P(ALL),
            P(ALL),
            P(ALL),
            P(ALL),
            P(ALL, None),
            P(ALL, None),
            P(ALL, None),
            P(ALL, None),
        ),
        check_vma=False,
    )
```

```python
import jax
import jax.numpy as jnp
from jax import lax
from jax.experimental import pallas as pl
from jax.experimental.pallas import tpu as pltpu
from jax.sharding import Mesh
from jax.sharding import PartitionSpec as P

LATENT = 256
HID = 512
MIDDLE = HID - LATENT - 3
STEP = 10

DELTA = 0.1
SMOOTH = 0.01
CODE_WEIGHT = 0.001
EIK_WEIGHT = 0.1
CLIP = 0.001
WEIGHT_RATE = 0.02
CODE_RATE = 0.15
BETA_ONE = 0.9
BETA_TWO = 0.999
ADAM_EPS = 1e-08
DECAY = 0.01

LANES = 128
DEVICES = 128
PEERS = 64
SHARD_ROWS = 21
BOX_ROWS = 24
SLOTS = 16
POINTS_DEV = 1024
CODE_ROWS = 256
FLAT_ROWS = DEVICES * SHARD_ROWS
BLOCK = 256
SUBS = 4
TILES = BLOCK // LANES
ALL_POINTS = POINTS_DEV * DEVICES

F32 = jnp.float32
BF16 = jnp.bfloat16
ALL = ("z", "core", "wide")


def rows_of_lanes(lead, shape):
    return lax.broadcasted_iota(jnp.int32, shape, lead)


def halves(v):
    high = v.astype(BF16)
    return high, (v - high.astype(F32)).astype(BF16)


def thirds(v):
    high = v.astype(BF16).astype(F32)
    rest = v - high
    mid = rest.astype(BF16).astype(F32)
    return high, mid, rest - mid


def mm(a, b):
    return lax.dot_general(a, b, (((1,), (0,)), ((), ())), preferred_element_type=F32)


def mm_nt(a, b):
    return lax.dot_general(a, b, (((1,), (1,)), ((), ())), preferred_element_type=F32)


def beside(*parts):
    return jnp.concatenate(parts, axis=1)


def total_of(v):
    return jnp.sum(jnp.sum(v, axis=0, keepdims=True), axis=1, keepdims=True)


def stacked(*parts):
    return jnp.concatenate(parts, axis=0)


def pack_kernel(
    weights_hbm,
    coords_hbm,
    distances_hbm,
    index_hbm,
    out_hbm,
    weights_ref,
    coords_ref,
    distances_ref,
    index_ref,
    staged,
    sems,
):
    pairs = [
        (index_hbm, index_ref),
        (weights_hbm, weights_ref),
        (coords_hbm, coords_ref),
        (distances_hbm, distances_ref),
    ]
    copies = [
        pltpu.make_async_copy(source, target, sems.at[i])
        for i, (source, target) in enumerate(pairs)
    ]
    for copy in copies:
        copy.start()
    copies[1].wait()
    shard = stacked(weights_ref[...], jnp.zeros((BOX_ROWS - SHARD_ROWS, LANES), F32))
    for peer in range(PEERS):
        staged[peer] = shard
    early = pltpu.make_async_copy(
        staged.at[:, pl.ds(0, 16), :], out_hbm.at[:, pl.ds(0, 16), :], sems.at[4]
    )
    early.start()
    for i in (0, 2, 3):
        copies[i].wait()
    index = index_ref[...]
    owner = lax.shift_right_logical(index, 8)
    row = lax.bitwise_and(index, CODE_ROWS - 1)
    sent = (rows_of_lanes(0, (DEVICES, POINTS_DEV)) == owner).astype(F32)
    sent_low = sent.astype(BF16)
    width = 256
    earlier = rows_of_lanes(0, (width, width)) < rows_of_lanes(1, (width, width))
    earlier = earlier.astype(F32).astype(BF16)
    ones = jnp.ones((width, width), BF16)
    ranks = [
        mm(sent_low[:, : (part + 1) * width], stacked(*([ones] * part + [earlier])))
        for part in range(POINTS_DEV // width)
    ]
    placed = jnp.sum(sent * beside(*ranks), axis=0, keepdims=True).astype(jnp.int32)
    at_slot = rows_of_lanes(0, (SLOTS, POINTS_DEV)) == placed
    values = [coords_ref[i : i + 1, :] for i in range(3)]
    values += [distances_ref[...], (row + 1).astype(F32)]
    pieces = [[], [], []]
    for value in values:
        for k, third in enumerate(thirds(value)):
            pieces[k].append(jnp.where(at_slot, third, 0.0))
    spare = jnp.zeros((LANES - SLOTS * len(values), POINTS_DEV), F32)
    boxes = mm_nt(
        beside(sent_low, sent_low, sent_low),
        beside(*[stacked(*piece, spare).astype(BF16) for piece in pieces]),
    )
    for d in range(DEVICES):
        z, core, w = d // 32, d // 16 % 2, d % 16
        row = SHARD_ROWS + core
        staged[z * 16 + w, row : row + 1, :] = boxes[d : d + 1, :]
    late = pltpu.make_async_copy(
        staged.at[:, pl.ds(16, 8), :], out_hbm.at[:, pl.ds(16, 8), :], sems.at[5]
    )
    late.start()
    early.wait()
    late.wait()


def unit_groups(count, stride_rows, extra, first_entry):
    for group in range(count):
        entry = first_entry + group * 8 * (stride_rows * LANES + extra)
        yield group, entry // LANES, entry % LANES


def unpack_units(flat_ref, out_ref, count, stride_rows, extra, first_entry):
    lane = rows_of_lanes(1, (8, LANES))
    slope = rows_of_lanes(0, (8, LANES)) * extra
    for group, first, shift in unit_groups(count, stride_rows, extra, first_entry):
        start = slope + shift
        wraps = shift + 7 * extra >= LANES
        turn = lax.bitwise_and(lane + start, LANES - 1)
        tiles = []
        for a in range(stride_rows + 2 + wraps):
            tile = flat_ref[pl.ds(first + a, 8, stride=stride_rows), :]
            tiles.append(jnp.take_along_axis(tile, turn, axis=1, mode="promise_in_bounds"))
        for c in range(stride_rows + 1):
            value = jnp.where(lane + start < LANES, tiles[c], tiles[c + 1])
            if wraps:
                value = jnp.where(lane + start < 2 * LANES, value, tiles[c + 2])
            out_ref[group * 8 : group * 8 + 8, c * LANES : (c + 1) * LANES] = value


def pack_units(value_ref, flat_ref, count, stride_rows, extra, first_entry, tails):
    lane = rows_of_lanes(1, (8, LANES))
    slope = rows_of_lanes(0, (8, LANES)) * extra
    zero = jnp.zeros((8, LANES), F32)
    for group, first, shift in unit_groups(count, stride_rows, extra, first_entry):
        start = slope + shift
        wraps = shift + 7 * extra >= LANES
        turn = lax.bitwise_and(lane - start, LANES - 1)
        rolled = {}

        def tile(c, rolled=rolled, group=group, turn=turn):
            if c < 0 or c > stride_rows:
                return zero
            if c not in rolled:
                value = value_ref[group * 8 : group * 8 + 8, c * LANES : (c + 1) * LANES]
                rolled[c] = jnp.take_along_axis(value, turn, axis=1, mode="promise_in_bounds")
            return rolled[c]

        for a in range(stride_rows, stride_rows + 2) if tails else range(stride_rows):
            value = jnp.where(lane >= start, tile(a), tile(a - 1))
            if wraps:
                value = jnp.where(lane >= start - LANES, value, tile(a - 2))
            flat_ref[pl.ds(first + a, 8, stride=stride_rows), :] = value


FIRST_UNITS = (32, 2, 5, 0)
SECOND_UNITS = (64, 4, 3, MIDDLE * (LATENT + 5))
HEAD_ENTRY = MIDDLE * (LATENT + 5) + HID * (HID + 3)


def across(column):
    return beside(*[column] * TILES)


def folded(v):
    return sum(v[:, i * LANES : (i + 1) * LANES] for i in range(TILES))


def silu_parts(half):
    gate = jnp.tanh(half)
    low = 0.5 * gate
    bend = 0.5 - gate * low
    bent = half * gate
    return half + bent, (0.5 + low) + half * bend, bend * (1.0 - bent)


def silu_parts_twice(half):
    gate = jnp.tanh(half)
    bend = 1.0 - gate * gate
    bent = half * gate
    return half + bent, (1.0 + gate) + half * bend, bend * (1.0 - bent)


def loop_kernel(
    core_ref,
    mine_ref,
    other_ref,
    codes_ref,
    first_w,
    second_w,
    latent_w,
    sum_two,
    sum_codes,
    sum_coord,
    sum_head,
    sum_count,
    sum_loss,
    flat,
    table,
    lhs_two,
    lhs_back,
    coord_w,
    head_w,
    spots,
    slope_one,
    curve_one,
    back_one,
    hid_hi,
    hid_lo,
    hot,
    act_two,
    slope_two,
    curve_two,
    act_tang,
    gate_hi,
    gate_lo,
    tang_hi,
    tang_lo,
    bar_hi,
    bar_lo,
    low_hi,
    low_lo,
):
    core = core_ref[0]

    for which in range(2):

        @pl.when(core == which)
        def _(which=which):
            for d in range(DEVICES):
                z, c, w = d // 32, d // 16 % 2, d % 16
                box = (z * 16 + w) * BOX_ROWS
                source = mine_ref if c == which else other_ref
                flat[d * SHARD_ROWS : d * SHARD_ROWS + BOX_ROWS, :] = source[box : box + BOX_ROWS, :]
            rows = pl.ds(SHARD_ROWS + which, PEERS, stride=BOX_ROWS)
            spots[...] = stacked(mine_ref[rows, :], other_ref[rows, :]).T

    unpack_units(flat, first_w, *FIRST_UNITS)
    unpack_units(flat, second_w, *SECOND_UNITS)
    head_bias = flat[HEAD_ENTRY // LANES : HEAD_ENTRY // LANES + 1, :][
        :, HEAD_ENTRY % LANES : HEAD_ENTRY % LANES + 1
    ]

    lane = rows_of_lanes(1, (256, LANES))
    unit = rows_of_lanes(0, (256, LANES))
    real = unit < MIDDLE

    first_low = jnp.where(beside(real, real), first_w[:, : 2 * LANES], 0.0)
    first_end = jnp.where(real, first_w[:, 2 * LANES :], 0.0)
    first_near = jnp.where(lane < 3, first_end, 0.0)
    first_gain = first_end[:, 3:4]
    first_bias = first_end[:, 4:5]
    first_w[:, : 2 * LANES] = first_low
    first_w[:, 2 * LANES :] = first_end
    _, first_scale = norm_parts(beside(first_low, first_near), first_gain)
    first_low = first_low * first_scale
    first_near = first_near * first_scale
    latent_w[0:256, :] = first_low
    for i in range(3):
        coord_w[:, i * LANES : (i + 1) * LANES] = jnp.broadcast_to(
            0.5 * first_near[:, i : i + 1], (256, LANES)
        )

    second_a = second_w[:, 0:256]
    second_b = second_w[:, 256:512]
    second_gain = second_w[:, 512:513]
    second_bias = second_w[:, 513:514]
    head = jnp.broadcast_to(second_w[:, 514:515], (HID, LANES))
    head_w[:, :LANES] = 0.5 * head
    head_w[:, LANES:] = head
    _, second_scale = norm_parts(second_w[:, 0:512], second_gain)
    second_a = second_a * second_scale
    second_b = second_b * second_scale
    is_hidden = rows_of_lanes(1, (HID, 256)) < MIDDLE
    hidden_cols = jnp.where(is_hidden, second_a, second_b)
    latent_cols = pltpu.roll(jnp.where(is_hidden, second_b, second_a), 3, 1)
    latent_w[256:768, :] = latent_cols

    hidden_hi, hidden_lo = halves(0.5 * hidden_cols)
    lhs_two[:, 0:256] = hidden_hi
    lhs_two[:, 256:512] = hidden_hi
    lhs_two[:, 512:768] = hidden_lo
    back_hi, back_lo = halves(hidden_cols.T)
    lhs_back[:, 0:512] = back_hi
    lhs_back[:, 512:1024] = back_hi
    lhs_back[:, 1024:1536] = back_lo

    code_hi, code_lo = halves(codes_ref[...])
    weight_hi, weight_lo = halves(latent_w[...])
    by_code = mm_nt(
        beside(weight_hi, weight_hi, weight_lo), beside(code_hi, code_lo, code_hi)
    )
    table[0:256, :] = 0.5 * (by_code[0:256, :] + first_bias)
    table[256:768, :] = 0.5 * (by_code[256:768, :] + second_bias)

    for ref in (sum_two, sum_codes, sum_coord, sum_head, sum_count, sum_loss):
        ref[...] = jnp.zeros(ref.shape, F32)

    def feature(which, step, sub):
        first = which * SLOTS + (step * SUBS + sub) * TILES
        return beside(*[spots[pl.ds(first + i, 1), :] for i in range(TILES)])

    blank5 = jnp.zeros((5, BLOCK), F32)
    chunk = 8192 // BLOCK
    low_chunks = range(0, 256, chunk)
    high_chunks = range(0, HID, chunk)

    def block_stages(step, s):
        place = [feature(i, step, s) for i in range(3)]
        target = feature(3, step, s)
        code_row = feature(4, step, s)
        valid = (code_row > 0.5).astype(F32)

        for c in range(0, CODE_ROWS, LANES):
            code = (rows_of_lanes(1, (LANES, LANES)) + c).astype(F32)
            seen = jnp.zeros((8, LANES), F32)
            for i in range(TILES):
                wanted = code_row[:, i * LANES : (i + 1) * LANES] - 1.0
                mark = jnp.where(code == jnp.broadcast_to(wanted, (LANES, LANES)).T, 1.0, 0.0)
                hot[s, i * LANES : (i + 1) * LANES, c : c + LANES] = mark.astype(BF16)
                for k in range(0, LANES, 8):
                    seen = seen + mark[k : k + 8, :]
            sum_count[:, c : c + LANES] += seen

        code = jnp.broadcast_to(jnp.maximum(code_row - 1.0, 0.0).astype(jnp.int32), (chunk, BLOCK))
        upper = code >= LANES
        code = lax.bitwise_and(code, LANES - 1)

        def picked(first):
            rows = slice(first, first + chunk)
            tiles = []
            for i in range(TILES):
                part = slice(i * LANES, (i + 1) * LANES)
                both = [
                    jnp.take_along_axis(
                        table[rows, c : c + LANES], code[:, part], axis=1, mode="promise_in_bounds"
                    )
                    for c in (0, LANES)
                ]
                tiles.append(jnp.where(upper[:, part], both[1], both[0]))
            return beside(*tiles)

        last = stacked(blank5, *place)
        for r in low_chunks:
            pre = picked(r)
            for i in range(3):
                pre = pre + across(coord_w[r : r + chunk, i * LANES : (i + 1) * LANES]) * place[i]
            value, slope, curve = silu_parts(pre)
            if r + chunk == 256:
                inside = rows_of_lanes(0, (chunk, BLOCK)) + r < MIDDLE
                end = jnp.where(inside[chunk - 8 :], value[chunk - 8 :], last)
                value = stacked(value[: chunk - 8], end)
                slope = jnp.where(inside, slope, 0.0)
                curve = jnp.where(inside, curve, 0.0)
            high, low = halves(value)
            hid_hi[s, r : r + chunk, :] = high
            hid_lo[s, r : r + chunk, :] = low
            slope_one[s, r : r + chunk, :] = slope
            curve_one[s, r : r + chunk, :] = curve
        yield

        act_two[s] = mm(lhs_two[...], stacked(hid_hi[s], hid_lo[s], hid_hi[s]))
        yield
        total = jnp.zeros((8, BLOCK), F32)
        for r in high_chunks:
            value, slope, curve = silu_parts_twice(act_two[s, r : r + chunk, :] + picked(256 + r))
            head = across(head_w[r : r + chunk, :LANES])
            weighed = head * value
            for k in range(0, chunk, 8):
                total = total + weighed[k : k + 8, :]
            high, low = halves(head * slope)
            gate_hi[s, r : r + chunk, :] = high
            gate_lo[s, r : r + chunk, :] = low
            act_two[s, r : r + chunk, :] = value
            slope_two[s, r : r + chunk, :] = slope
            curve_two[s, r : r + chunk, :] = curve
        summed = jnp.sum(total, axis=0, keepdims=True)
        yield

        back_one[s] = mm(lhs_back[...], stacked(gate_hi[s], gate_lo[s], gate_hi[s]))
        yield
        totals = [jnp.zeros((8, BLOCK), F32) for _ in range(3)]
        for r in low_chunks:
            grad = back_one[s, r : r + chunk, :] * slope_one[s, r : r + chunk, :]
            for i in range(3):
                weighed = across(coord_w[r : r + chunk, i * LANES : (i + 1) * LANES]) * grad
                for k in range(0, chunk, 8):
                    totals[i] = totals[i] + weighed[k : k + 8, :]
        lead = [
            2.0 * jnp.sum(totals[i], axis=0, keepdims=True)
            + back_one[s, MIDDLE + i : MIDDLE + i + 1, :]
            for i in range(3)
        ]

        predicted = jnp.tanh(2.0 * summed + head_bias)
        flank = 1.0 - predicted * predicted
        slope = [flank * q for q in lead]
        excess = slope[0] * slope[0] + slope[1] * slope[1] + slope[2] * slope[2] - 1.0
        capped = jnp.tanh(predicted / DELTA)
        misfit = DELTA * capped - DELTA * jnp.tanh(target / DELTA)
        fitting = jnp.sqrt(misfit * misfit + SMOOTH * SMOOTH)
        sum_loss[0:1, :] += valid * (fitting + EIK_WEIGHT * excess * excess)
        share = valid * (1.0 / ALL_POINTS)
        pull = [(4.0 * EIK_WEIGHT) * excess * v for v in slope]
        by_flank = sum(p * q for p, q in zip(pull, lead))
        by_predicted = misfit / fitting * (1.0 - capped * capped) - 2.0 * predicted * by_flank
        bar_out = share * by_predicted * flank
        sum_loss[1:2, :] += bar_out
        half_bar = 0.5 * bar_out
        pull = [share * flank * p for p in pull]

        last = stacked(blank5, *pull)
        twice = [2.0 * p for p in pull]
        for r in low_chunks:
            grad = 0.0
            for i in range(3):
                grad = grad + across(coord_w[r : r + chunk, i * LANES : (i + 1) * LANES]) * twice[i]
            slope = slope_one[s, r : r + chunk, :]
            back = back_one[s, r : r + chunk, :]
            near = back * slope
            for i in range(3):
                sum_coord[r : r + chunk, i * LANES : (i + 1) * LANES] += folded(near * pull[i])
            through = grad * slope
            if r + chunk == 256:
                inside = rows_of_lanes(0, (8, BLOCK)) < MIDDLE - 248
                end = jnp.where(inside, through[chunk - 8 :], last)
                through = stacked(through[: chunk - 8], end)
            high, low = halves(through)
            tang_hi[s, r : r + chunk, :] = high
            tang_lo[s, r : r + chunk, :] = low
            curve_one[s, r : r + chunk, :] = (
                grad * back * curve_one[s, r : r + chunk, :]
            )
        yield
        act_tang[s] = mm(lhs_two[...], stacked(tang_hi[s], tang_lo[s], tang_hi[s]))
        yield
        for r in high_chunks:
            tangent = act_tang[s, r : r + chunk, :]
            slope = slope_two[s, r : r + chunk, :]
            head = across(head_w[r : r + chunk, LANES:])
            bar = head * (half_bar * slope + tangent * curve_two[s, r : r + chunk, :])
            by_head = act_two[s, r : r + chunk, :] * bar_out + slope * tangent
            sum_head[r : r + chunk, :] += folded(by_head)
            high, low = halves(bar)
            bar_hi[s, r : r + chunk, :] = high
            bar_lo[s, r : r + chunk, :] = low
        yield

        back_one[s] = mm(lhs_back[...], stacked(bar_hi[s], bar_lo[s], bar_hi[s]))
        yield
        for r in low_chunks:
            bar = (
                back_one[s, r : r + chunk, :] * slope_one[s, r : r + chunk, :]
                + curve_one[s, r : r + chunk, :]
            )
            for i in range(3):
                sum_coord[r : r + chunk, i * LANES : (i + 1) * LANES] += folded(bar * place[i])
            high, low = halves(bar)
            low_hi[s, r : r + chunk, :] = high
            low_lo[s, r : r + chunk, :] = low
        yield

        sum_two[...] += mm_nt(
            beside(bar_hi[s], bar_hi[s], bar_lo[s], gate_hi[s], gate_hi[s], gate_lo[s]),
            beside(hid_hi[s], hid_lo[s], hid_hi[s], tang_hi[s], tang_lo[s], tang_hi[s]),
        )
        marks = stacked(hot[s], hot[s])
        sum_codes[256:768, :] += mm(beside(bar_hi[s], bar_lo[s]), marks)
        sum_codes[0:256, :] += mm(beside(low_hi[s], low_lo[s]), marks)

    def step_body(step, carry):
        waiting = [block_stages(step, s) for s in range(SUBS)]
        active = []
        while waiting or active:
            if waiting:
                active.append(waiting.pop(0))
            active = [work for work in active if next(work, work) is not work]
        return carry

    steps = SLOTS * DEVICES // (SUBS * BLOCK)
    if steps == 1:
        step_body(0, 0)
    else:
        lax.fori_loop(0, steps, step_body, 0)


def code_kernel(codes_ref, latent_w, sum_codes, sum_count, sum_loss, code_grad_ref, facts_ref):
    codes = codes_ref[...]
    count = jnp.sum(sum_count[...], axis=0, keepdims=True)
    count = jnp.broadcast_to(count, (LANES, CODE_ROWS)).T[:, 0:1]
    turned_hi, turned_lo = halves(sum_codes[...].T)
    weight_hi, weight_lo = halves(latent_w[...])
    code_grad = mm(
        beside(turned_hi, turned_hi, turned_lo), stacked(weight_hi, weight_lo, weight_hi)
    )
    code_grad = code_grad + (2.0 * CODE_WEIGHT / ALL_POINTS) * count * codes
    code_grad_ref[...] = code_grad
    loss = jnp.sum(sum_loss[0:1, :], axis=1, keepdims=True)
    loss = (loss + CODE_WEIGHT * total_of(count * codes * codes)) / ALL_POINTS
    left = rows_of_lanes(1, facts_ref.shape) < LANES // 2
    facts_ref[...] = jnp.where(left, total_of(code_grad * code_grad), loss)


def norm_parts(direction, gain):
    root = lax.rsqrt(jnp.sum(direction * direction, axis=1, keepdims=True) + 1e-12)
    return root, gain * root


def weight_kernel(
    core_ref,
    codes_ref,
    first_w,
    second_w,
    sum_two,
    sum_codes,
    sum_coord,
    sum_head,
    _,
    sum_loss,
    keep_ref,
    give_ref,
    flat,
    tails,
    first_grad,
    second_grad,
):
    core = core_ref[0]
    codes = codes_ref[...]
    by_code = sum_codes[...]
    code_hi, code_lo = halves(codes)
    by_hi, by_lo = halves(by_code)
    latent_grad = mm(beside(by_hi, by_hi, by_lo), stacked(code_hi, code_lo, code_hi))

    bias_grad = jnp.sum(by_code, axis=1, keepdims=True)
    lane = rows_of_lanes(1, (256, LANES))
    real = rows_of_lanes(0, (256, LANES)) < MIDDLE
    near_grad = 0.0
    for i in range(3):
        column = jnp.sum(sum_coord[:, i * LANES : (i + 1) * LANES], axis=1, keepdims=True)
        near_grad = jnp.where(lane == i, column, near_grad)
    low_grad = latent_grad[0:256, :]
    first_low = first_w[:, : 2 * LANES]
    first_near = jnp.where(lane < 3, first_w[:, 2 * LANES :], 0.0)
    root, scale = norm_parts(beside(first_low, first_near), first_w[:, 2 * LANES + 3 : 2 * LANES + 4])
    along = jnp.sum(first_low * low_grad, axis=1, keepdims=True)
    along = along + jnp.sum(first_near * near_grad, axis=1, keepdims=True)
    inward = scale * root * root * along
    end = scale * near_grad - first_near * inward
    end = jnp.where(lane == 3, root * along, end)
    end = jnp.where(lane == 4, bias_grad[0:256, :], end)
    low_grad = scale * low_grad - first_low * inward
    first_grad[:, : 2 * LANES] = jnp.where(beside(real, real), low_grad, 0.0)
    first_grad[:, 2 * LANES :] = jnp.where(real, end, 0.0)

    is_hidden = rows_of_lanes(1, (HID, 256)) < MIDDLE
    hidden_grad = sum_two[...]
    moved = pltpu.roll(latent_grad[256:768, :], 256 - 3, 1)
    grad_a = jnp.where(is_hidden, hidden_grad, moved)
    grad_b = jnp.where(is_hidden, moved, hidden_grad)
    second_a = second_w[:, 0:256]
    second_b = second_w[:, 256:512]
    root, scale = norm_parts(second_w[:, 0:512], second_w[:, 512:513])
    along = jnp.sum(second_a * grad_a + second_b * grad_b, axis=1, keepdims=True)
    inward = scale * root * root * along
    second_grad[:, 0:256] = scale * grad_a - second_a * inward
    second_grad[:, 256:512] = scale * grad_b - second_b * inward
    head_grad = jnp.sum(sum_head[...], axis=1, keepdims=True)
    lane = rows_of_lanes(1, (HID, LANES))
    end = jnp.where(lane == 0, root * along, 0.0)
    end = jnp.where(lane == 1, bias_grad[256:768, :], end)
    second_grad[:, 512:640] = jnp.where(lane == 2, head_grad, end)

    for ref in (flat, tails):
        ref[...] = jnp.zeros(ref.shape, F32)
    pack_units(first_grad, flat, *FIRST_UNITS, False)
    pack_units(second_grad, flat, *SECOND_UNITS, False)
    pack_units(first_grad, tails, *FIRST_UNITS, True)
    pack_units(second_grad, tails, *SECOND_UNITS, True)
    row = HEAD_ENTRY // LANES
    lane = rows_of_lanes(1, (1, LANES))
    bias_total = jnp.sum(sum_loss[1:2, :], axis=1, keepdims=True)
    flat[row : row + 1, :] += jnp.where(lane == HEAD_ENTRY % LANES, bias_total, 0.0)
    size = 16 * SHARD_ROWS
    for which in range(2):

        @pl.when(core == which)
        def _(which=which):
            for z in range(4):
                for c in range(2):
                    target = keep_ref if c == which else give_ref
                    first = (z * 2 + c) * size
                    target[z * size : (z + 1) * size, :] = (
                        flat[first : first + size, :] + tails[first : first + size, :]
                    )


def vmem(count):
    return [pl.BlockSpec(memory_space=pltpu.VMEM)] * count


PARAMS = pltpu.CompilerParams(vmem_limit_bytes=48 * 1024 * 1024)


HBM = pl.BlockSpec(memory_space=pltpu.HBM)
SMEM = pl.BlockSpec(memory_space=pltpu.SMEM)


def f32(*shape):
    return jax.ShapeDtypeStruct(shape, F32)


def pack_boxes(weights, coords, distances, index):
    return pl.pallas_call(
        pack_kernel,
        out_shape=f32(PEERS, BOX_ROWS, LANES),
        in_specs=[HBM] * 4,
        out_specs=HBM,
        scratch_shapes=[
            pltpu.VMEM(weights.shape, F32),
            pltpu.VMEM(coords.shape, F32),
            pltpu.VMEM(distances.shape, F32),
            pltpu.VMEM(index.shape, jnp.int32),
            pltpu.VMEM((PEERS, BOX_ROWS, LANES), F32),
            pltpu.SemaphoreType.DMA((6,)),
        ],
        compiler_params=pltpu.CompilerParams(vmem_limit_bytes=60 * 1024 * 1024),
    )(weights, coords, distances, index)


def main_kernel(
    core_ref, mine_ref, other_ref, codes_ref, keep_ref, give_ref, code_grad_ref, facts_ref, *scratch
):
    first_w, second_w, latent_w, *sums = scratch[:9]
    flat = scratch[9]
    loop_kernel(core_ref, mine_ref, other_ref, codes_ref, *scratch[:-3])
    code_kernel(codes_ref, latent_w, sums[1], sums[4], sums[5], code_grad_ref, facts_ref)
    weight_kernel(core_ref, codes_ref, first_w, second_w, *sums, keep_ref, give_ref, flat, *scratch[-3:])


def main_call(core, mine, other, codes):
    pair = (SUBS, 256, BLOCK)
    pair_two = (SUBS, HID, BLOCK)
    scratch = [
        ((256, 3 * LANES), F32),
        ((HID, 5 * LANES), F32),
        ((768, 256), F32),
        ((HID, 256), F32),
        ((768, 256), F32),
        ((256, 3 * LANES), F32),
        ((HID, LANES), F32),
        ((8, CODE_ROWS), F32),
        ((2, BLOCK), F32),
        ((FLAT_ROWS + 8, LANES), F32),
        ((768, CODE_ROWS), F32),
        ((HID, 768), BF16),
        ((256, 1536), BF16),
        ((256, 3 * LANES), F32),
        ((HID, 2 * LANES), F32),
        ((LANES, LANES), F32),
        (pair, F32),
        (pair, F32),
        (pair, F32),
        (pair, BF16),
        (pair, BF16),
        ((SUBS, BLOCK, CODE_ROWS), BF16),
        (pair_two, F32),
        (pair_two, F32),
        (pair_two, F32),
        (pair_two, F32),
        (pair_two, BF16),
        (pair_two, BF16),
        (pair, BF16),
        (pair, BF16),
        (pair_two, BF16),
        (pair_two, BF16),
        (pair, BF16),
        (pair, BF16),
        ((FLAT_ROWS + 8, LANES), F32),
        ((256, 3 * LANES), F32),
        ((HID, 5 * LANES), F32),
    ]
    boxes = f32(PEERS * SHARD_ROWS, LANES)
    return pl.pallas_call(
        main_kernel,
        out_shape=(boxes, boxes, f32(CODE_ROWS, LATENT), f32(8, LANES)),
        in_specs=[SMEM] + vmem(3),
        out_specs=tuple(vmem(4)),
        scratch_shapes=[pltpu.VMEM(shape, dtype) for shape, dtype in scratch],
        compiler_params=PARAMS,
    )(core, mine, other, codes)


def adam_update(value, first, second, grad, rate):
    first_new = BETA_ONE * first + (1.0 - BETA_ONE) * grad
    second_new = BETA_TWO * second + (1.0 - BETA_TWO) * grad * grad
    first_hat = first_new / (1.0 - BETA_ONE**STEP)
    second_hat = second_new / (1.0 - BETA_TWO**STEP)
    value_new = value - rate * (first_hat / (jnp.sqrt(second_hat) + ADAM_EPS) + DECAY * value)
    return (value_new, first_new, second_new)


def shard_kernel(parts_ref, facts_ref, shard_ref, all_facts_ref):
    total = parts_ref[0:SHARD_ROWS, :]
    for peer in range(1, PEERS):
        total = total + parts_ref[peer * SHARD_ROWS : (peer + 1) * SHARD_ROWS, :]
    shard_ref[...] = total
    facts = facts_ref[...]
    left = rows_of_lanes(1, facts.shape) < LANES // 2
    all_facts_ref[...] = facts + jnp.where(left, total_of(total * total), 0.0)


def sum_shards(parts, facts):
    return pl.pallas_call(
        shard_kernel,
        out_shape=(f32(SHARD_ROWS, LANES), f32(8, LANES)),
        in_specs=vmem(2),
        out_specs=tuple(vmem(2)),
        compiler_params=PARAMS,
    )(parts, facts)


def update_kernel(
    seen_ref,
    shard_ref,
    weights_ref,
    moment_one_ref,
    moment_two_ref,
    codes_ref,
    code_first_ref,
    code_second_ref,
    code_grad_ref,
    loss_out,
    norm_out,
    weights_out,
    moment_one_out,
    moment_two_out,
    weights_copy_out,
    codes_out,
    code_first_out,
    code_second_out,
    codes_copy_out,
):
    total = jnp.sum(seen_ref[...], axis=0, keepdims=True)
    loss_out[...] = total[:, LANES // 2 : LANES // 2 + 1]
    norm = jnp.sqrt(total[:, 0:1])
    norm_out[...] = norm
    factor = jnp.minimum(1.0, CLIP / (norm + 1e-06))
    value, first, second = adam_update(
        weights_ref[...],
        moment_one_ref[...],
        moment_two_ref[...],
        factor * shard_ref[...],
        WEIGHT_RATE,
    )
    weights_out[...] = value
    moment_one_out[...] = first
    moment_two_out[...] = second
    weights_copy_out[...] = value.astype(BF16)
    for r in range(0, CODE_ROWS, 32):
        rows = slice(r, r + 32)
        value, first, second = adam_update(
            codes_ref[rows, :],
            code_first_ref[rows, :],
            code_second_ref[rows, :],
            factor * code_grad_ref[rows, :],
            CODE_RATE,
        )
        codes_out[rows, :] = value
        code_first_out[rows, :] = first
        code_second_out[rows, :] = second
        codes_copy_out[rows, :] = value.astype(BF16)


def update_all(*args):
    scalar = jax.ShapeDtypeStruct((1, 1), F32)
    shard = [jax.ShapeDtypeStruct((SHARD_ROWS, LANES), t) for t in (F32, F32, F32, BF16)]
    table = [jax.ShapeDtypeStruct((CODE_ROWS, LATENT), t) for t in (F32, F32, F32, BF16)]
    return pl.pallas_call(
        update_kernel,
        out_shape=(scalar, scalar, *shard, *table),
        in_specs=vmem(9),
        out_specs=tuple(vmem(10)),
        compiler_params=PARAMS,
    )(*args)


def swap_cores(v):
    return lax.ppermute(v, "core", [(0, 1), (1, 0)])


def exchange(v):
    return lax.all_to_all(v, ("z", "wide"), split_axis=0, concat_axis=0)


def body(
    weights_flat,
    moment_one,
    moment_two,
    codes,
    code_first,
    code_second,
    coords,
    distances,
    shape_index,
):
    boxes = pack_boxes(
        weights_flat.reshape(SHARD_ROWS, LANES),
        coords,
        distances.reshape(1, POINTS_DEV),
        shape_index.reshape(1, POINTS_DEV),
    )
    mine = exchange(boxes)
    other = swap_cores(mine)
    core = lax.axis_index("core").astype(jnp.int32).reshape(1)
    keep, give, code_grad, facts = main_call(
        core,
        mine.reshape(PEERS * BOX_ROWS, LANES),
        other.reshape(PEERS * BOX_ROWS, LANES),
        codes,
    )
    pair_sum = (keep + swap_cores(give)).reshape(PEERS, 1, SHARD_ROWS * LANES)
    parts = exchange(pair_sum).reshape(PEERS * SHARD_ROWS, LANES)
    shard, facts = sum_shards(parts, facts)
    facts = facts + swap_cores(facts)
    facts = jnp.broadcast_to(facts[0:1], (PEERS, LANES)).reshape(PEERS, 1, LANES)
    flat = lambda v: v.reshape(SHARD_ROWS, LANES)
    out = update_all(
        exchange(facts).reshape(PEERS, LANES),
        shard,
        flat(weights_flat),
        flat(moment_one),
        flat(moment_two),
        codes,
        code_first,
        code_second,
        code_grad,
    )
    return (
        out[0].reshape(()),
        out[1].reshape(()),
        *[v.reshape(weights_flat.shape) for v in out[2:6]],
        *out[6:],
    )


def solution(mesh):
    parts = Mesh(mesh.devices.reshape(4, 2, 16), ALL)
    return jax.shard_map(
        body,
        mesh=parts,
        in_specs=(
            P(ALL),
            P(ALL),
            P(ALL),
            P(ALL, None),
            P(ALL, None),
            P(ALL, None),
            P(None, ALL),
            P(ALL),
            P(ALL),
        ),
        out_specs=(
            P(),
            P(),
            P(ALL),
            P(ALL),
            P(ALL),
            P(ALL),
            P(ALL, None),
            P(ALL, None),
            P(ALL, None),
            P(ALL, None),
        ),
        check_vma=False,
    )
```

```python
import jax
import jax.numpy as jnp
from jax import lax
from jax.experimental import pallas as pl
from jax.experimental.pallas import tpu as pltpu
from jax.sharding import Mesh
from jax.sharding import PartitionSpec as P

LATENT = 256
HID = 512
MIDDLE = HID - LATENT - 3
STEP = 10

DELTA = 0.1
SMOOTH = 0.01
CODE_WEIGHT = 0.001
EIK_WEIGHT = 0.1
CLIP = 0.001
WEIGHT_RATE = 0.02
CODE_RATE = 0.15
BETA_ONE = 0.9
BETA_TWO = 0.999
ADAM_EPS = 1e-08
DECAY = 0.01

LANES = 128
DEVICES = 128
PEERS = 64
SHARD_ROWS = 21
BOX_ROWS = 24
SLOTS = 16
POINTS_DEV = 1024
CODE_ROWS = 256
FLAT_ROWS = DEVICES * SHARD_ROWS
BLOCK = 256
SUBS = 8
TILES = BLOCK // LANES
ALL_POINTS = POINTS_DEV * DEVICES

F32 = jnp.float32
BF16 = jnp.bfloat16
ALL = ("z", "core", "wide")


def rows_of_lanes(lead, shape):
    return lax.broadcasted_iota(jnp.int32, shape, lead)


def halves(v):
    high = v.astype(BF16)
    return high, (v - high.astype(F32)).astype(BF16)


def thirds(v):
    high = v.astype(BF16).astype(F32)
    rest = v - high
    mid = rest.astype(BF16).astype(F32)
    return high, mid, rest - mid


def mm(a, b):
    return lax.dot_general(a, b, (((1,), (0,)), ((), ())), preferred_element_type=F32)


def mm_nt(a, b):
    return lax.dot_general(a, b, (((1,), (1,)), ((), ())), preferred_element_type=F32)


def beside(*parts):
    return jnp.concatenate(parts, axis=1)


def total_of(v):
    return jnp.sum(jnp.sum(v, axis=0, keepdims=True), axis=1, keepdims=True)


def stacked(*parts):
    return jnp.concatenate(parts, axis=0)


def pack_kernel(
    weights_hbm,
    coords_hbm,
    distances_hbm,
    index_hbm,
    out_hbm,
    weights_ref,
    coords_ref,
    distances_ref,
    index_ref,
    staged,
    sems,
):
    pairs = [
        (index_hbm, index_ref),
        (weights_hbm, weights_ref),
        (coords_hbm, coords_ref),
        (distances_hbm, distances_ref),
    ]
    copies = [
        pltpu.make_async_copy(source, target, sems.at[i])
        for i, (source, target) in enumerate(pairs)
    ]
    for copy in copies:
        copy.start()
    copies[1].wait()
    shard = stacked(weights_ref[...], jnp.zeros((BOX_ROWS - SHARD_ROWS, LANES), F32))
    for peer in range(PEERS):
        staged[peer] = shard
    early = pltpu.make_async_copy(
        staged.at[:, pl.ds(0, 16), :], out_hbm.at[:, pl.ds(0, 16), :], sems.at[4]
    )
    early.start()
    for i in (0, 2, 3):
        copies[i].wait()
    index = index_ref[...]
    owner = lax.shift_right_logical(index, 8)
    row = lax.bitwise_and(index, CODE_ROWS - 1)
    sent = (rows_of_lanes(0, (DEVICES, POINTS_DEV)) == owner).astype(F32)
    sent_low = sent.astype(BF16)
    width = 256
    earlier = rows_of_lanes(0, (width, width)) < rows_of_lanes(1, (width, width))
    earlier = earlier.astype(F32).astype(BF16)
    ones = jnp.ones((width, width), BF16)
    ranks = [
        mm(sent_low[:, : (part + 1) * width], stacked(*([ones] * part + [earlier])))
        for part in range(POINTS_DEV // width)
    ]
    placed = jnp.sum(sent * beside(*ranks), axis=0, keepdims=True).astype(jnp.int32)
    at_slot = rows_of_lanes(0, (SLOTS, POINTS_DEV)) == placed
    values = [coords_ref[i : i + 1, :] for i in range(3)]
    values += [distances_ref[...], (row + 1).astype(F32)]
    pieces = [[], [], []]
    for value in values:
        for k, third in enumerate(thirds(value)):
            pieces[k].append(jnp.where(at_slot, third, 0.0))
    spare = jnp.zeros((LANES - SLOTS * len(values), POINTS_DEV), F32)
    boxes = mm_nt(
        beside(sent_low, sent_low, sent_low),
        beside(*[stacked(*piece, spare).astype(BF16) for piece in pieces]),
    )
    for d in range(DEVICES):
        z, core, w = d // 32, d // 16 % 2, d % 16
        row = SHARD_ROWS + core
        staged[z * 16 + w, row : row + 1, :] = boxes[d : d + 1, :]
    late = pltpu.make_async_copy(
        staged.at[:, pl.ds(16, 8), :], out_hbm.at[:, pl.ds(16, 8), :], sems.at[5]
    )
    late.start()
    early.wait()
    late.wait()


def unit_groups(count, stride_rows, extra, first_entry):
    for group in range(count):
        entry = first_entry + group * 8 * (stride_rows * LANES + extra)
        yield group, entry // LANES, entry % LANES


def unpack_units(flat_ref, out_ref, count, stride_rows, extra, first_entry):
    lane = rows_of_lanes(1, (8, LANES))
    slope = rows_of_lanes(0, (8, LANES)) * extra
    for group, first, shift in unit_groups(count, stride_rows, extra, first_entry):
        start = slope + shift
        wraps = shift + 7 * extra >= LANES
        turn = lax.bitwise_and(lane + start, LANES - 1)
        tiles = []
        for a in range(stride_rows + 2 + wraps):
            tile = flat_ref[pl.ds(first + a, 8, stride=stride_rows), :]
            tiles.append(jnp.take_along_axis(tile, turn, axis=1, mode="promise_in_bounds"))
        for c in range(stride_rows + 1):
            value = jnp.where(lane + start < LANES, tiles[c], tiles[c + 1])
            if wraps:
                value = jnp.where(lane + start < 2 * LANES, value, tiles[c + 2])
            out_ref[group * 8 : group * 8 + 8, c * LANES : (c + 1) * LANES] = value


def pack_units(value_ref, flat_ref, count, stride_rows, extra, first_entry, tails):
    lane = rows_of_lanes(1, (8, LANES))
    slope = rows_of_lanes(0, (8, LANES)) * extra
    zero = jnp.zeros((8, LANES), F32)
    for group, first, shift in unit_groups(count, stride_rows, extra, first_entry):
        start = slope + shift
        wraps = shift + 7 * extra >= LANES
        turn = lax.bitwise_and(lane - start, LANES - 1)
        rolled = {}

        def tile(c, rolled=rolled, group=group, turn=turn):
            if c < 0 or c > stride_rows:
                return zero
            if c not in rolled:
                value = value_ref[group * 8 : group * 8 + 8, c * LANES : (c + 1) * LANES]
                rolled[c] = jnp.take_along_axis(value, turn, axis=1, mode="promise_in_bounds")
            return rolled[c]

        for a in range(stride_rows, stride_rows + 2) if tails else range(stride_rows):
            value = jnp.where(lane >= start, tile(a), tile(a - 1))
            if wraps:
                value = jnp.where(lane >= start - LANES, value, tile(a - 2))
            flat_ref[pl.ds(first + a, 8, stride=stride_rows), :] = value


FIRST_UNITS = (32, 2, 5, 0)
SECOND_UNITS = (64, 4, 3, MIDDLE * (LATENT + 5))
HEAD_ENTRY = MIDDLE * (LATENT + 5) + HID * (HID + 3)


def across(column):
    return beside(*[column] * TILES)


def folded(v):
    return sum(v[:, i * LANES : (i + 1) * LANES] for i in range(TILES))


def silu_parts(half):
    gate = jnp.tanh(half)
    low = 0.5 * gate
    bend = 0.5 - gate * low
    bent = half * gate
    return half + bent, (0.5 + low) + half * bend, bend * (1.0 - bent)


def silu_parts_twice(half):
    gate = jnp.tanh(half)
    bend = 1.0 - gate * gate
    bent = half * gate
    return half + bent, (1.0 + gate) + half * bend, bend * (1.0 - bent)


def loop_kernel(
    core_ref,
    mine_ref,
    other_ref,
    codes_ref,
    first_w,
    second_w,
    latent_w,
    sum_two,
    sum_codes,
    sum_coord,
    sum_head,
    sum_count,
    sum_loss,
    flat,
    table,
    lhs_two,
    lhs_back,
    coord_w,
    head_w,
    spots,
    slope_one,
    curve_one,
    back_one,
    hid_hi,
    hid_lo,
    hot,
    act_two,
    slope_two,
    curve_two,
    act_tang,
    gate_hi,
    gate_lo,
    tang_hi,
    tang_lo,
    bar_hi,
    bar_lo,
    low_hi,
    low_lo,
):
    core = core_ref[0]

    for which in range(2):

        @pl.when(core == which)
        def _(which=which):
            for d in range(DEVICES):
                z, c, w = d // 32, d // 16 % 2, d % 16
                box = (z * 16 + w) * BOX_ROWS
                source = mine_ref if c == which else other_ref
                flat[d * SHARD_ROWS : d * SHARD_ROWS + BOX_ROWS, :] = source[box : box + BOX_ROWS, :]
            rows = pl.ds(SHARD_ROWS + which, PEERS, stride=BOX_ROWS)
            spots[...] = stacked(mine_ref[rows, :], other_ref[rows, :]).T

    unpack_units(flat, first_w, *FIRST_UNITS)
    unpack_units(flat, second_w, *SECOND_UNITS)
    head_bias = flat[HEAD_ENTRY // LANES : HEAD_ENTRY // LANES + 1, :][
        :, HEAD_ENTRY % LANES : HEAD_ENTRY % LANES + 1
    ]

    lane = rows_of_lanes(1, (256, LANES))
    unit = rows_of_lanes(0, (256, LANES))
    real = unit < MIDDLE

    first_low = jnp.where(beside(real, real), first_w[:, : 2 * LANES], 0.0)
    first_end = jnp.where(real, first_w[:, 2 * LANES :], 0.0)
    first_near = jnp.where(lane < 3, first_end, 0.0)
    first_gain = first_end[:, 3:4]
    first_bias = first_end[:, 4:5]
    first_w[:, : 2 * LANES] = first_low
    first_w[:, 2 * LANES :] = first_end
    _, first_scale = norm_parts(beside(first_low, first_near), first_gain)
    first_low = first_low * first_scale
    first_near = first_near * first_scale
    latent_w[0:256, :] = first_low
    for i in range(3):
        coord_w[:, i * LANES : (i + 1) * LANES] = jnp.broadcast_to(
            0.5 * first_near[:, i : i + 1], (256, LANES)
        )

    second_a = second_w[:, 0:256]
    second_b = second_w[:, 256:512]
    second_gain = second_w[:, 512:513]
    second_bias = second_w[:, 513:514]
    head = jnp.broadcast_to(second_w[:, 514:515], (HID, LANES))
    head_w[:, :LANES] = 0.5 * head
    head_w[:, LANES:] = head
    _, second_scale = norm_parts(second_w[:, 0:512], second_gain)
    second_a = second_a * second_scale
    second_b = second_b * second_scale
    is_hidden = rows_of_lanes(1, (HID, 256)) < MIDDLE
    hidden_cols = jnp.where(is_hidden, second_a, second_b)
    latent_cols = pltpu.roll(jnp.where(is_hidden, second_b, second_a), 3, 1)
    latent_w[256:768, :] = latent_cols

    hidden_hi, hidden_lo = halves(0.5 * hidden_cols)
    lhs_two[:, 0:256] = hidden_hi
    lhs_two[:, 256:512] = hidden_hi
    lhs_two[:, 512:768] = hidden_lo
    back_hi, back_lo = halves(hidden_cols.T)
    lhs_back[:, 0:512] = back_hi
    lhs_back[:, 512:1024] = back_hi
    lhs_back[:, 1024:1536] = back_lo

    code_hi, code_lo = halves(codes_ref[...])
    weight_hi, weight_lo = halves(latent_w[...])
    by_code = mm_nt(
        beside(weight_hi, weight_hi, weight_lo), beside(code_hi, code_lo, code_hi)
    )
    table[0:256, :] = 0.5 * (by_code[0:256, :] + first_bias)
    table[256:768, :] = 0.5 * (by_code[256:768, :] + second_bias)

    for ref in (sum_two, sum_codes, sum_coord, sum_head, sum_count, sum_loss):
        ref[...] = jnp.zeros(ref.shape, F32)

    def feature(which, step, sub):
        first = which * SLOTS + (step * SUBS + sub) * TILES
        return beside(*[spots[pl.ds(first + i, 1), :] for i in range(TILES)])

    blank5 = jnp.zeros((5, BLOCK), F32)
    chunk = 8192 // BLOCK
    low_chunks = range(0, 256, chunk)
    high_chunks = range(0, HID, chunk)

    def block_stages(step, s):
        place = [feature(i, step, s) for i in range(3)]
        target = feature(3, step, s)
        code_row = feature(4, step, s)
        valid = (code_row > 0.5).astype(F32)

        for c in range(0, CODE_ROWS, LANES):
            code = (rows_of_lanes(1, (LANES, LANES)) + c).astype(F32)
            seen = jnp.zeros((8, LANES), F32)
            for i in range(TILES):
                wanted = code_row[:, i * LANES : (i + 1) * LANES] - 1.0
                mark = jnp.where(code == jnp.broadcast_to(wanted, (LANES, LANES)).T, 1.0, 0.0)
                hot[s, i * LANES : (i + 1) * LANES, c : c + LANES] = mark.astype(BF16)
                for k in range(0, LANES, 8):
                    seen = seen + mark[k : k + 8, :]
            sum_count[:, c : c + LANES] += seen

        code = jnp.broadcast_to(jnp.maximum(code_row - 1.0, 0.0).astype(jnp.int32), (chunk, BLOCK))
        upper = code >= LANES
        code = lax.bitwise_and(code, LANES - 1)

        def picked(first):
            rows = slice(first, first + chunk)
            tiles = []
            for i in range(TILES):
                part = slice(i * LANES, (i + 1) * LANES)
                both = [
                    jnp.take_along_axis(
                        table[rows, c : c + LANES], code[:, part], axis=1, mode="promise_in_bounds"
                    )
                    for c in (0, LANES)
                ]
                tiles.append(jnp.where(upper[:, part], both[1], both[0]))
            return beside(*tiles)

        last = stacked(blank5, *place)
        for r in low_chunks:
            pre = picked(r)
            for i in range(3):
                pre = pre + across(coord_w[r : r + chunk, i * LANES : (i + 1) * LANES]) * place[i]
            value, slope, curve = silu_parts(pre)
            if r + chunk == 256:
                inside = rows_of_lanes(0, (chunk, BLOCK)) + r < MIDDLE
                end = jnp.where(inside[chunk - 8 :], value[chunk - 8 :], last)
                value = stacked(value[: chunk - 8], end)
                slope = jnp.where(inside, slope, 0.0)
                curve = jnp.where(inside, curve, 0.0)
            high, low = halves(value)
            hid_hi[s, r : r + chunk, :] = high
            hid_lo[s, r : r + chunk, :] = low
            slope_one[s, r : r + chunk, :] = slope
            curve_one[s, r : r + chunk, :] = curve
        yield

        act_two[s] = mm(lhs_two[...], stacked(hid_hi[s], hid_lo[s], hid_hi[s]))
        yield
        total = jnp.zeros((8, BLOCK), F32)
        for r in high_chunks:
            value, slope, curve = silu_parts_twice(act_two[s, r : r + chunk, :] + picked(256 + r))
            head = across(head_w[r : r + chunk, :LANES])
            weighed = head * value
            for k in range(0, chunk, 8):
                total = total + weighed[k : k + 8, :]
            high, low = halves(head * slope)
            gate_hi[s, r : r + chunk, :] = high
            gate_lo[s, r : r + chunk, :] = low
            act_two[s, r : r + chunk, :] = value
            slope_two[s, r : r + chunk, :] = slope
            curve_two[s, r : r + chunk, :] = curve
        summed = jnp.sum(total, axis=0, keepdims=True)
        yield

        back_one[s] = mm(lhs_back[...], stacked(gate_hi[s], gate_lo[s], gate_hi[s]))
        yield
        totals = [jnp.zeros((8, BLOCK), F32) for _ in range(3)]
        for r in low_chunks:
            grad = back_one[s, r : r + chunk, :] * slope_one[s, r : r + chunk, :]
            for i in range(3):
                weighed = across(coord_w[r : r + chunk, i * LANES : (i + 1) * LANES]) * grad
                for k in range(0, chunk, 8):
                    totals[i] = totals[i] + weighed[k : k + 8, :]
        lead = [
            2.0 * jnp.sum(totals[i], axis=0, keepdims=True)
            + back_one[s, MIDDLE + i : MIDDLE + i + 1, :]
            for i in range(3)
        ]

        predicted = jnp.tanh(2.0 * summed + head_bias)
        flank = 1.0 - predicted * predicted
        slope = [flank * q for q in lead]
        excess = slope[0] * slope[0] + slope[1] * slope[1] + slope[2] * slope[2] - 1.0
        capped = jnp.tanh(predicted / DELTA)
        misfit = DELTA * capped - DELTA * jnp.tanh(target / DELTA)
        fitting = jnp.sqrt(misfit * misfit + SMOOTH * SMOOTH)
        sum_loss[0:1, :] += valid * (fitting + EIK_WEIGHT * excess * excess)
        share = valid * (1.0 / ALL_POINTS)
        pull = [(4.0 * EIK_WEIGHT) * excess * v for v in slope]
        by_flank = sum(p * q for p, q in zip(pull, lead))
        by_predicted = misfit / fitting * (1.0 - capped * capped) - 2.0 * predicted * by_flank
        bar_out = share * by_predicted * flank
        sum_loss[1:2, :] += bar_out
        half_bar = 0.5 * bar_out
        pull = [share * flank * p for p in pull]

        last = stacked(blank5, *pull)
        twice = [2.0 * p for p in pull]
        for r in low_chunks:
            grad = 0.0
            for i in range(3):
                grad = grad + across(coord_w[r : r + chunk, i * LANES : (i + 1) * LANES]) * twice[i]
            slope = slope_one[s, r : r + chunk, :]
            back = back_one[s, r : r + chunk, :]
            near = back * slope
            for i in range(3):
                sum_coord[r : r + chunk, i * LANES : (i + 1) * LANES] += folded(near * pull[i])
            through = grad * slope
            if r + chunk == 256:
                inside = rows_of_lanes(0, (8, BLOCK)) < MIDDLE - 248
                end = jnp.where(inside, through[chunk - 8 :], last)
                through = stacked(through[: chunk - 8], end)
            high, low = halves(through)
            tang_hi[s, r : r + chunk, :] = high
            tang_lo[s, r : r + chunk, :] = low
            curve_one[s, r : r + chunk, :] = (
                grad * back * curve_one[s, r : r + chunk, :]
            )
        yield
        act_tang[s] = mm(lhs_two[...], stacked(tang_hi[s], tang_lo[s], tang_hi[s]))
        yield
        for r in high_chunks:
            tangent = act_tang[s, r : r + chunk, :]
            slope = slope_two[s, r : r + chunk, :]
            head = across(head_w[r : r + chunk, LANES:])
            bar = head * (half_bar * slope + tangent * curve_two[s, r : r + chunk, :])
            by_head = act_two[s, r : r + chunk, :] * bar_out + slope * tangent
            sum_head[r : r + chunk, :] += folded(by_head)
            high, low = halves(bar)
            bar_hi[s, r : r + chunk, :] = high
            bar_lo[s, r : r + chunk, :] = low
        yield

        back_one[s] = mm(lhs_back[...], stacked(bar_hi[s], bar_lo[s], bar_hi[s]))
        yield
        for r in low_chunks:
            bar = (
                back_one[s, r : r + chunk, :] * slope_one[s, r : r + chunk, :]
                + curve_one[s, r : r + chunk, :]
            )
            for i in range(3):
                sum_coord[r : r + chunk, i * LANES : (i + 1) * LANES] += folded(bar * place[i])
            high, low = halves(bar)
            low_hi[s, r : r + chunk, :] = high
            low_lo[s, r : r + chunk, :] = low
        yield

        sum_two[...] += mm_nt(
            beside(bar_hi[s], bar_hi[s], bar_lo[s], gate_hi[s], gate_hi[s], gate_lo[s]),
            beside(hid_hi[s], hid_lo[s], hid_hi[s], tang_hi[s], tang_lo[s], tang_hi[s]),
        )
        marks = stacked(hot[s], hot[s])
        sum_codes[256:768, :] += mm(beside(bar_hi[s], bar_lo[s]), marks)
        sum_codes[0:256, :] += mm(beside(low_hi[s], low_lo[s]), marks)

    def step_body(step, carry):
        waiting = [block_stages(step, s) for s in range(SUBS)]
        active = []
        while waiting or active:
            if waiting:
                active.append(waiting.pop(0))
            active = [work for work in active if next(work, work) is not work]
        return carry

    steps = SLOTS * DEVICES // (SUBS * BLOCK)
    if steps == 1:
        step_body(0, 0)
    else:
        lax.fori_loop(0, steps, step_body, 0)


def code_kernel(codes_ref, latent_w, sum_codes, sum_count, sum_loss, code_grad_ref, facts_ref):
    codes = codes_ref[...]
    count = jnp.sum(sum_count[...], axis=0, keepdims=True)
    count = jnp.broadcast_to(count, (LANES, CODE_ROWS)).T[:, 0:1]
    turned_hi, turned_lo = halves(sum_codes[...].T)
    weight_hi, weight_lo = halves(latent_w[...])
    code_grad = mm(
        beside(turned_hi, turned_hi, turned_lo), stacked(weight_hi, weight_lo, weight_hi)
    )
    code_grad = code_grad + (2.0 * CODE_WEIGHT / ALL_POINTS) * count * codes
    code_grad_ref[...] = code_grad
    loss = jnp.sum(sum_loss[0:1, :], axis=1, keepdims=True)
    loss = (loss + CODE_WEIGHT * total_of(count * codes * codes)) / ALL_POINTS
    left = rows_of_lanes(1, facts_ref.shape) < LANES // 2
    facts_ref[...] = jnp.where(left, total_of(code_grad * code_grad), loss)


def norm_parts(direction, gain):
    root = lax.rsqrt(jnp.sum(direction * direction, axis=1, keepdims=True) + 1e-12)
    return root, gain * root


def weight_kernel(
    core_ref,
    codes_ref,
    first_w,
    second_w,
    sum_two,
    sum_codes,
    sum_coord,
    sum_head,
    _,
    sum_loss,
    keep_ref,
    give_ref,
    flat,
    tails,
    first_grad,
    second_grad,
):
    core = core_ref[0]
    codes = codes_ref[...]
    by_code = sum_codes[...]
    code_hi, code_lo = halves(codes)
    by_hi, by_lo = halves(by_code)
    latent_grad = mm(beside(by_hi, by_hi, by_lo), stacked(code_hi, code_lo, code_hi))

    bias_grad = jnp.sum(by_code, axis=1, keepdims=True)
    lane = rows_of_lanes(1, (256, LANES))
    real = rows_of_lanes(0, (256, LANES)) < MIDDLE
    near_grad = 0.0
    for i in range(3):
        column = jnp.sum(sum_coord[:, i * LANES : (i + 1) * LANES], axis=1, keepdims=True)
        near_grad = jnp.where(lane == i, column, near_grad)
    low_grad = latent_grad[0:256, :]
    first_low = first_w[:, : 2 * LANES]
    first_near = jnp.where(lane < 3, first_w[:, 2 * LANES :], 0.0)
    root, scale = norm_parts(beside(first_low, first_near), first_w[:, 2 * LANES + 3 : 2 * LANES + 4])
    along = jnp.sum(first_low * low_grad, axis=1, keepdims=True)
    along = along + jnp.sum(first_near * near_grad, axis=1, keepdims=True)
    inward = scale * root * root * along
    end = scale * near_grad - first_near * inward
    end = jnp.where(lane == 3, root * along, end)
    end = jnp.where(lane == 4, bias_grad[0:256, :], end)
    low_grad = scale * low_grad - first_low * inward
    first_grad[:, : 2 * LANES] = jnp.where(beside(real, real), low_grad, 0.0)
    first_grad[:, 2 * LANES :] = jnp.where(real, end, 0.0)

    is_hidden = rows_of_lanes(1, (HID, 256)) < MIDDLE
    hidden_grad = sum_two[...]
    moved = pltpu.roll(latent_grad[256:768, :], 256 - 3, 1)
    grad_a = jnp.where(is_hidden, hidden_grad, moved)
    grad_b = jnp.where(is_hidden, moved, hidden_grad)
    second_a = second_w[:, 0:256]
    second_b = second_w[:, 256:512]
    root, scale = norm_parts(second_w[:, 0:512], second_w[:, 512:513])
    along = jnp.sum(second_a * grad_a + second_b * grad_b, axis=1, keepdims=True)
    inward = scale * root * root * along
    second_grad[:, 0:256] = scale * grad_a - second_a * inward
    second_grad[:, 256:512] = scale * grad_b - second_b * inward
    head_grad = jnp.sum(sum_head[...], axis=1, keepdims=True)
    lane = rows_of_lanes(1, (HID, LANES))
    end = jnp.where(lane == 0, root * along, 0.0)
    end = jnp.where(lane == 1, bias_grad[256:768, :], end)
    second_grad[:, 512:640] = jnp.where(lane == 2, head_grad, end)

    for ref in (flat, tails):
        ref[...] = jnp.zeros(ref.shape, F32)
    pack_units(first_grad, flat, *FIRST_UNITS, False)
    pack_units(second_grad, flat, *SECOND_UNITS, False)
    pack_units(first_grad, tails, *FIRST_UNITS, True)
    pack_units(second_grad, tails, *SECOND_UNITS, True)
    row = HEAD_ENTRY // LANES
    lane = rows_of_lanes(1, (1, LANES))
    bias_total = jnp.sum(sum_loss[1:2, :], axis=1, keepdims=True)
    flat[row : row + 1, :] += jnp.where(lane == HEAD_ENTRY % LANES, bias_total, 0.0)
    size = 16 * SHARD_ROWS
    for which in range(2):

        @pl.when(core == which)
        def _(which=which):
            for z in range(4):
                for c in range(2):
                    target = keep_ref if c == which else give_ref
                    first = (z * 2 + c) * size
                    target[z * size : (z + 1) * size, :] = (
                        flat[first : first + size, :] + tails[first : first + size, :]
                    )


def vmem(count):
    return [pl.BlockSpec(memory_space=pltpu.VMEM)] * count


PARAMS = pltpu.CompilerParams(vmem_limit_bytes=48 * 1024 * 1024)


HBM = pl.BlockSpec(memory_space=pltpu.HBM)
SMEM = pl.BlockSpec(memory_space=pltpu.SMEM)


def f32(*shape):
    return jax.ShapeDtypeStruct(shape, F32)


def pack_boxes(weights, coords, distances, index):
    return pl.pallas_call(
        pack_kernel,
        out_shape=f32(PEERS, BOX_ROWS, LANES),
        in_specs=[HBM] * 4,
        out_specs=HBM,
        scratch_shapes=[
            pltpu.VMEM(weights.shape, F32),
            pltpu.VMEM(coords.shape, F32),
            pltpu.VMEM(distances.shape, F32),
            pltpu.VMEM(index.shape, jnp.int32),
            pltpu.VMEM((PEERS, BOX_ROWS, LANES), F32),
            pltpu.SemaphoreType.DMA((6,)),
        ],
        compiler_params=pltpu.CompilerParams(vmem_limit_bytes=60 * 1024 * 1024),
    )(weights, coords, distances, index)


def main_kernel(
    core_ref, mine_ref, other_ref, codes_ref, keep_ref, give_ref, code_grad_ref, facts_ref, *scratch
):
    first_w, second_w, latent_w, *sums = scratch[:9]
    flat = scratch[9]
    loop_kernel(core_ref, mine_ref, other_ref, codes_ref, *scratch[:-3])
    code_kernel(codes_ref, latent_w, sums[1], sums[4], sums[5], code_grad_ref, facts_ref)
    weight_kernel(core_ref, codes_ref, first_w, second_w, *sums, keep_ref, give_ref, flat, *scratch[-3:])


def main_call(core, mine, other, codes):
    pair = (SUBS, 256, BLOCK)
    pair_two = (SUBS, HID, BLOCK)
    scratch = [
        ((256, 3 * LANES), F32),
        ((HID, 5 * LANES), F32),
        ((768, 256), F32),
        ((HID, 256), F32),
        ((768, 256), F32),
        ((256, 3 * LANES), F32),
        ((HID, LANES), F32),
        ((8, CODE_ROWS), F32),
        ((2, BLOCK), F32),
        ((FLAT_ROWS + 8, LANES), F32),
        ((768, CODE_ROWS), F32),
        ((HID, 768), BF16),
        ((256, 1536), BF16),
        ((256, 3 * LANES), F32),
        ((HID, 2 * LANES), F32),
        ((LANES, LANES), F32),
        (pair, F32),
        (pair, F32),
        (pair, F32),
        (pair, BF16),
        (pair, BF16),
        ((SUBS, BLOCK, CODE_ROWS), BF16),
        (pair_two, F32),
        (pair_two, F32),
        (pair_two, F32),
        (pair_two, F32),
        (pair_two, BF16),
        (pair_two, BF16),
        (pair, BF16),
        (pair, BF16),
        (pair_two, BF16),
        (pair_two, BF16),
        (pair, BF16),
        (pair, BF16),
        ((FLAT_ROWS + 8, LANES), F32),
        ((256, 3 * LANES), F32),
        ((HID, 5 * LANES), F32),
    ]
    boxes = f32(PEERS * SHARD_ROWS, LANES)
    return pl.pallas_call(
        main_kernel,
        out_shape=(boxes, boxes, f32(CODE_ROWS, LATENT), f32(8, LANES)),
        in_specs=[SMEM] + vmem(3),
        out_specs=tuple(vmem(4)),
        scratch_shapes=[pltpu.VMEM(shape, dtype) for shape, dtype in scratch],
        compiler_params=PARAMS,
    )(core, mine, other, codes)


def adam_update(value, first, second, grad, rate):
    first_new = BETA_ONE * first + (1.0 - BETA_ONE) * grad
    second_new = BETA_TWO * second + (1.0 - BETA_TWO) * grad * grad
    first_hat = first_new / (1.0 - BETA_ONE**STEP)
    second_hat = second_new / (1.0 - BETA_TWO**STEP)
    value_new = value - rate * (first_hat / (jnp.sqrt(second_hat) + ADAM_EPS) + DECAY * value)
    return (value_new, first_new, second_new)


def shard_kernel(parts_ref, facts_ref, shard_ref, all_facts_ref):
    total = parts_ref[0:SHARD_ROWS, :]
    for peer in range(1, PEERS):
        total = total + parts_ref[peer * SHARD_ROWS : (peer + 1) * SHARD_ROWS, :]
    shard_ref[...] = total
    facts = facts_ref[...]
    left = rows_of_lanes(1, facts.shape) < LANES // 2
    all_facts_ref[...] = facts + jnp.where(left, total_of(total * total), 0.0)


def sum_shards(parts, facts):
    return pl.pallas_call(
        shard_kernel,
        out_shape=(f32(SHARD_ROWS, LANES), f32(8, LANES)),
        in_specs=vmem(2),
        out_specs=tuple(vmem(2)),
        compiler_params=PARAMS,
    )(parts, facts)


def update_kernel(
    seen_ref,
    shard_ref,
    weights_ref,
    moment_one_ref,
    moment_two_ref,
    codes_ref,
    code_first_ref,
    code_second_ref,
    code_grad_ref,
    loss_out,
    norm_out,
    weights_out,
    moment_one_out,
    moment_two_out,
    weights_copy_out,
    codes_out,
    code_first_out,
    code_second_out,
    codes_copy_out,
):
    total = jnp.sum(seen_ref[...], axis=0, keepdims=True)
    loss_out[...] = total[:, LANES // 2 : LANES // 2 + 1]
    norm = jnp.sqrt(total[:, 0:1])
    norm_out[...] = norm
    factor = jnp.minimum(1.0, CLIP / (norm + 1e-06))
    value, first, second = adam_update(
        weights_ref[...],
        moment_one_ref[...],
        moment_two_ref[...],
        factor * shard_ref[...],
        WEIGHT_RATE,
    )
    weights_out[...] = value
    moment_one_out[...] = first
    moment_two_out[...] = second
    weights_copy_out[...] = value.astype(BF16)
    for r in range(0, CODE_ROWS, 32):
        rows = slice(r, r + 32)
        value, first, second = adam_update(
            codes_ref[rows, :],
            code_first_ref[rows, :],
            code_second_ref[rows, :],
            factor * code_grad_ref[rows, :],
            CODE_RATE,
        )
        codes_out[rows, :] = value
        code_first_out[rows, :] = first
        code_second_out[rows, :] = second
        codes_copy_out[rows, :] = value.astype(BF16)


def update_all(*args):
    scalar = jax.ShapeDtypeStruct((1, 1), F32)
    shard = [jax.ShapeDtypeStruct((SHARD_ROWS, LANES), t) for t in (F32, F32, F32, BF16)]
    table = [jax.ShapeDtypeStruct((CODE_ROWS, LATENT), t) for t in (F32, F32, F32, BF16)]
    return pl.pallas_call(
        update_kernel,
        out_shape=(scalar, scalar, *shard, *table),
        in_specs=vmem(9),
        out_specs=tuple(vmem(10)),
        compiler_params=PARAMS,
    )(*args)


def swap_cores(v):
    return lax.ppermute(v, "core", [(0, 1), (1, 0)])


def exchange(v):
    return lax.all_to_all(v, ("z", "wide"), split_axis=0, concat_axis=0)


def body(
    weights_flat,
    moment_one,
    moment_two,
    codes,
    code_first,
    code_second,
    coords,
    distances,
    shape_index,
):
    boxes = pack_boxes(
        weights_flat.reshape(SHARD_ROWS, LANES),
        coords,
        distances.reshape(1, POINTS_DEV),
        shape_index.reshape(1, POINTS_DEV),
    )
    mine = exchange(boxes)
    other = swap_cores(mine)
    core = lax.axis_index("core").astype(jnp.int32).reshape(1)
    keep, give, code_grad, facts = main_call(
        core,
        mine.reshape(PEERS * BOX_ROWS, LANES),
        other.reshape(PEERS * BOX_ROWS, LANES),
        codes,
    )
    pair_sum = (keep + swap_cores(give)).reshape(PEERS, 1, SHARD_ROWS * LANES)
    parts = exchange(pair_sum).reshape(PEERS * SHARD_ROWS, LANES)
    shard, facts = sum_shards(parts, facts)
    facts = facts + swap_cores(facts)
    facts = jnp.broadcast_to(facts[0:1], (PEERS, LANES)).reshape(PEERS, 1, LANES)
    flat = lambda v: v.reshape(SHARD_ROWS, LANES)
    out = update_all(
        exchange(facts).reshape(PEERS, LANES),
        shard,
        flat(weights_flat),
        flat(moment_one),
        flat(moment_two),
        codes,
        code_first,
        code_second,
        code_grad,
    )
    return (
        out[0].reshape(()),
        out[1].reshape(()),
        *[v.reshape(weights_flat.shape) for v in out[2:6]],
        *out[6:],
    )


def solution(mesh):
    parts = Mesh(mesh.devices.reshape(4, 2, 16), ALL)
    return jax.shard_map(
        body,
        mesh=parts,
        in_specs=(
            P(ALL),
            P(ALL),
            P(ALL),
            P(ALL, None),
            P(ALL, None),
            P(ALL, None),
            P(None, ALL),
            P(ALL),
            P(ALL),
        ),
        out_specs=(
            P(),
            P(),
            P(ALL),
            P(ALL),
            P(ALL),
            P(ALL),
            P(ALL, None),
            P(ALL, None),
            P(ALL, None),
            P(ALL, None),
        ),
        check_vma=False,
    )
```

```python
import jax
import jax.numpy as jnp
from jax import lax
from jax.experimental import pallas as pl
from jax.experimental.pallas import tpu as pltpu
from jax.sharding import Mesh
from jax.sharding import PartitionSpec as P

LATENT = 256
HID = 512
MIDDLE = HID - LATENT - 3
STEP = 10

DELTA = 0.1
SMOOTH = 0.01
CODE_WEIGHT = 0.001
EIK_WEIGHT = 0.1
CLIP = 0.001
WEIGHT_RATE = 0.02
CODE_RATE = 0.15
BETA_ONE = 0.9
BETA_TWO = 0.999
ADAM_EPS = 1e-08
DECAY = 0.01

LANES = 128
DEVICES = 128
PEERS = 64
SHARD_ROWS = 21
BOX_ROWS = 24
SLOTS = 16
POINTS_DEV = 1024
CODE_ROWS = 256
FLAT_ROWS = DEVICES * SHARD_ROWS
BLOCK = 256
SUBS = 2
TILES = BLOCK // LANES
ALL_POINTS = POINTS_DEV * DEVICES

F32 = jnp.float32
BF16 = jnp.bfloat16
ALL = ("z", "core", "wide")


def rows_of_lanes(lead, shape):
    return lax.broadcasted_iota(jnp.int32, shape, lead)


def halves(v):
    high = v.astype(BF16)
    return high, (v - high.astype(F32)).astype(BF16)


def thirds(v):
    high = v.astype(BF16).astype(F32)
    rest = v - high
    mid = rest.astype(BF16).astype(F32)
    return high, mid, rest - mid


def mm(a, b):
    return lax.dot_general(a, b, (((1,), (0,)), ((), ())), preferred_element_type=F32)


def mm_nt(a, b):
    return lax.dot_general(a, b, (((1,), (1,)), ((), ())), preferred_element_type=F32)


def beside(*parts):
    return jnp.concatenate(parts, axis=1)


def total_of(v):
    return jnp.sum(jnp.sum(v, axis=0, keepdims=True), axis=1, keepdims=True)


def stacked(*parts):
    return jnp.concatenate(parts, axis=0)


def pack_kernel(
    weights_hbm,
    coords_hbm,
    distances_hbm,
    index_hbm,
    out_hbm,
    weights_ref,
    coords_ref,
    distances_ref,
    index_ref,
    staged,
    sems,
):
    pairs = [
        (index_hbm, index_ref),
        (weights_hbm, weights_ref),
        (coords_hbm, coords_ref),
        (distances_hbm, distances_ref),
    ]
    copies = [
        pltpu.make_async_copy(source, target, sems.at[i])
        for i, (source, target) in enumerate(pairs)
    ]
    for copy in copies:
        copy.start()
    copies[1].wait()
    shard = stacked(weights_ref[...], jnp.zeros((BOX_ROWS - SHARD_ROWS, LANES), F32))
    for peer in range(PEERS):
        staged[peer] = shard
    early = pltpu.make_async_copy(
        staged.at[:, pl.ds(0, 16), :], out_hbm.at[:, pl.ds(0, 16), :], sems.at[4]
    )
    early.start()
    for i in (0, 2, 3):
        copies[i].wait()
    index = index_ref[...]
    owner = lax.shift_right_logical(index, 8)
    row = lax.bitwise_and(index, CODE_ROWS - 1)
    sent = (rows_of_lanes(0, (DEVICES, POINTS_DEV)) == owner).astype(F32)
    sent_low = sent.astype(BF16)
    width = 256
    earlier = rows_of_lanes(0, (width, width)) < rows_of_lanes(1, (width, width))
    earlier = earlier.astype(F32).astype(BF16)
    ones = jnp.ones((width, width), BF16)
    ranks = [
        mm(sent_low[:, : (part + 1) * width], stacked(*([ones] * part + [earlier])))
        for part in range(POINTS_DEV // width)
    ]
    placed = jnp.sum(sent * beside(*ranks), axis=0, keepdims=True).astype(jnp.int32)
    at_slot = rows_of_lanes(0, (SLOTS, POINTS_DEV)) == placed
    values = [coords_ref[i : i + 1, :] for i in range(3)]
    values += [distances_ref[...], (row + 1).astype(F32)]
    pieces = [[], [], []]
    for value in values:
        for k, third in enumerate(thirds(value)):
            pieces[k].append(jnp.where(at_slot, third, 0.0))
    spare = jnp.zeros((LANES - SLOTS * len(values), POINTS_DEV), F32)
    boxes = mm_nt(
        beside(sent_low, sent_low, sent_low),
        beside(*[stacked(*piece, spare).astype(BF16) for piece in pieces]),
    )
    for d in range(DEVICES):
        z, core, w = d // 32, d // 16 % 2, d % 16
        row = SHARD_ROWS + core
        staged[z * 16 + w, row : row + 1, :] = boxes[d : d + 1, :]
    late = pltpu.make_async_copy(
        staged.at[:, pl.ds(16, 8), :], out_hbm.at[:, pl.ds(16, 8), :], sems.at[5]
    )
    late.start()
    early.wait()
    late.wait()


def unit_groups(count, stride_rows, extra, first_entry):
    for group in range(count):
        entry = first_entry + group * 8 * (stride_rows * LANES + extra)
        yield group, entry // LANES, entry % LANES


def unpack_units(flat_ref, out_ref, count, stride_rows, extra, first_entry):
    lane = rows_of_lanes(1, (8, LANES))
    slope = rows_of_lanes(0, (8, LANES)) * extra
    for group, first, shift in unit_groups(count, stride_rows, extra, first_entry):
        start = slope + shift
        wraps = shift + 7 * extra >= LANES
        turn = lax.bitwise_and(lane + start, LANES - 1)
        tiles = []
        for a in range(stride_rows + 2 + wraps):
            tile = flat_ref[pl.ds(first + a, 8, stride=stride_rows), :]
            tiles.append(jnp.take_along_axis(tile, turn, axis=1, mode="promise_in_bounds"))
        for c in range(stride_rows + 1):
            value = jnp.where(lane + start < LANES, tiles[c], tiles[c + 1])
            if wraps:
                value = jnp.where(lane + start < 2 * LANES, value, tiles[c + 2])
            out_ref[group * 8 : group * 8 + 8, c * LANES : (c + 1) * LANES] = value


def pack_units(value_ref, heads_ref, tails_ref, count, stride_rows, extra, first_entry):
    lane = rows_of_lanes(1, (8, LANES))
    slope = rows_of_lanes(0, (8, LANES)) * extra
    zero = jnp.zeros((8, LANES), F32)
    for group, first, shift in unit_groups(count, stride_rows, extra, first_entry):
        start = slope + shift
        wraps = shift + 7 * extra >= LANES
        turn = lax.bitwise_and(lane - start, LANES - 1)
        tiles = [zero, zero]
        for c in range(stride_rows + 1):
            value = value_ref[group * 8 : group * 8 + 8, c * LANES : (c + 1) * LANES]
            tiles.append(jnp.take_along_axis(value, turn, axis=1, mode="promise_in_bounds"))
        tiles.append(zero)
        for a in range(stride_rows + 2):
            value = jnp.where(lane >= start, tiles[a + 2], tiles[a + 1])
            if wraps:
                value = jnp.where(lane >= start - LANES, value, tiles[a])
            target = heads_ref if a < stride_rows else tails_ref
            target[pl.ds(first + a, 8, stride=stride_rows), :] = value


def clear(ref, rows):
    def step(i, carry):
        place = pl.ds(pl.multiple_of(i * rows, 8), rows)
        ref[place, :] = jnp.zeros((rows, ref.shape[1]), F32)
        return carry

    lax.fori_loop(0, ref.shape[0] // rows, step, 0)


FIRST_UNITS = (32, 2, 5, 0)
SECOND_UNITS = (64, 4, 3, MIDDLE * (LATENT + 5))
HEAD_ENTRY = MIDDLE * (LATENT + 5) + HID * (HID + 3)


def across(column):
    return beside(*[column] * TILES)


def folded(v):
    return sum(v[:, i * LANES : (i + 1) * LANES] for i in range(TILES))


def silu_parts(half):
    gate = jnp.tanh(half)
    low = 0.5 * gate
    bend = 0.5 - gate * low
    bent = half * gate
    return half + bent, (0.5 + low) + half * bend, bend * (1.0 - bent)


def silu_parts_twice(half):
    gate = jnp.tanh(half)
    bend = 1.0 - gate * gate
    bent = half * gate
    return half + bent, (1.0 + gate) + half * bend, bend * (1.0 - bent)


def loop_kernel(
    core_ref,
    mine_ref,
    other_ref,
    codes_ref,
    first_w,
    second_w,
    latent_w,
    sum_two,
    sum_codes,
    sum_coord,
    sum_head,
    sum_count,
    sum_loss,
    flat,
    table,
    lhs_two,
    lhs_back,
    coord_w,
    head_w,
    spots,
    slope_one,
    curve_one,
    back_one,
    hid_hi,
    hid_lo,
    hot,
    act_two,
    slope_two,
    curve_two,
    act_tang,
    gate_hi,
    gate_lo,
    tang_hi,
    tang_lo,
    bar_hi,
    bar_lo,
    low_hi,
    low_lo,
):
    core = core_ref[0]

    for which in range(2):

        @pl.when(core == which)
        def _(which=which):
            for d in range(DEVICES):
                z, c, w = d // 32, d // 16 % 2, d % 16
                box = (z * 16 + w) * BOX_ROWS
                source = mine_ref if c == which else other_ref
                flat[d * SHARD_ROWS : d * SHARD_ROWS + BOX_ROWS, :] = source[box : box + BOX_ROWS, :]
            rows = pl.ds(SHARD_ROWS + which, PEERS, stride=BOX_ROWS)
            spots[...] = stacked(mine_ref[rows, :], other_ref[rows, :]).T

    unpack_units(flat, first_w, *FIRST_UNITS)
    unpack_units(flat, second_w, *SECOND_UNITS)
    head_bias = flat[HEAD_ENTRY // LANES : HEAD_ENTRY // LANES + 1, :][
        :, HEAD_ENTRY % LANES : HEAD_ENTRY % LANES + 1
    ]

    lane = rows_of_lanes(1, (256, LANES))
    unit = rows_of_lanes(0, (256, LANES))
    real = unit < MIDDLE

    first_low = jnp.where(beside(real, real), first_w[:, : 2 * LANES], 0.0)
    first_end = jnp.where(real, first_w[:, 2 * LANES :], 0.0)
    first_near = jnp.where(lane < 3, first_end, 0.0)
    first_gain = first_end[:, 3:4]
    first_bias = first_end[:, 4:5]
    first_w[:, : 2 * LANES] = first_low
    first_w[:, 2 * LANES :] = first_end
    _, first_scale = norm_parts(beside(first_low, first_near), first_gain)
    first_low = first_low * first_scale
    first_near = first_near * first_scale
    latent_w[0:256, :] = first_low
    for i in range(3):
        coord_w[:, i * LANES : (i + 1) * LANES] = jnp.broadcast_to(
            0.5 * first_near[:, i : i + 1], (256, LANES)
        )

    second_a = second_w[:, 0:256]
    second_b = second_w[:, 256:512]
    second_gain = second_w[:, 512:513]
    second_bias = second_w[:, 513:514]
    head = jnp.broadcast_to(second_w[:, 514:515], (HID, LANES))
    head_w[:, :LANES] = 0.5 * head
    head_w[:, LANES:] = head
    _, second_scale = norm_parts(second_w[:, 0:512], second_gain)
    second_a = second_a * second_scale
    second_b = second_b * second_scale
    is_hidden = rows_of_lanes(1, (HID, 256)) < MIDDLE
    hidden_cols = jnp.where(is_hidden, second_a, second_b)
    latent_cols = pltpu.roll(jnp.where(is_hidden, second_b, second_a), 3, 1)
    latent_w[256:768, :] = latent_cols

    hidden_hi, hidden_lo = halves(0.5 * hidden_cols)
    lhs_two[:, 0:256] = hidden_hi
    lhs_two[:, 256:512] = hidden_hi
    lhs_two[:, 512:768] = hidden_lo
    back_hi, back_lo = halves(hidden_cols.T)
    lhs_back[:, 0:512] = back_hi
    lhs_back[:, 512:1024] = back_hi
    lhs_back[:, 1024:1536] = back_lo

    code_hi, code_lo = halves(codes_ref[...])
    weight_hi, weight_lo = halves(latent_w[...])
    by_code = mm_nt(
        beside(weight_hi, weight_hi, weight_lo), beside(code_hi, code_lo, code_hi)
    )
    table[0:256, :] = 0.5 * (by_code[0:256, :] + first_bias)
    table[256:768, :] = 0.5 * (by_code[256:768, :] + second_bias)

    for ref in (sum_two, sum_codes, sum_coord, sum_head):
        clear(ref, 64)
    sum_count[...] = jnp.zeros(sum_count.shape, F32)
    sum_loss[...] = jnp.zeros(sum_loss.shape, F32)

    def feature(which, step, sub):
        first = which * SLOTS + (step * SUBS + sub) * TILES
        return beside(*[spots[pl.ds(first + i, 1), :] for i in range(TILES)])

    blank5 = jnp.zeros((5, BLOCK), F32)
    chunk = 8192 // BLOCK
    low_chunks = range(0, 256, chunk)
    high_chunks = range(0, HID, chunk)

    def block_stages(step, s):
        place = [feature(i, step, s) for i in range(3)]
        target = feature(3, step, s)
        code_row = feature(4, step, s)
        valid = (code_row > 0.5).astype(F32)

        for c in range(0, CODE_ROWS, LANES):
            code = (rows_of_lanes(1, (LANES, LANES)) + c).astype(F32)
            seen = jnp.zeros((8, LANES), F32)
            for i in range(TILES):
                wanted = code_row[:, i * LANES : (i + 1) * LANES] - 1.0
                mark = jnp.where(code == jnp.broadcast_to(wanted, (LANES, LANES)).T, 1.0, 0.0)
                hot[s, i * LANES : (i + 1) * LANES, c : c + LANES] = mark.astype(BF16)
                for k in range(0, LANES, 8):
                    seen = seen + mark[k : k + 8, :]
            sum_count[:, c : c + LANES] += seen

        code = jnp.broadcast_to(jnp.maximum(code_row - 1.0, 0.0).astype(jnp.int32), (chunk, BLOCK))
        upper = code >= LANES
        code = lax.bitwise_and(code, LANES - 1)

        def picked(first):
            rows = slice(first, first + chunk)
            tiles = []
            for i in range(TILES):
                part = slice(i * LANES, (i + 1) * LANES)
                both = [
                    jnp.take_along_axis(
                        table[rows, c : c + LANES], code[:, part], axis=1, mode="promise_in_bounds"
                    )
                    for c in (0, LANES)
                ]
                tiles.append(jnp.where(upper[:, part], both[1], both[0]))
            return beside(*tiles)

        last = stacked(blank5, *place)
        for r in low_chunks:
            pre = picked(r)
            for i in range(3):
                pre = pre + across(coord_w[r : r + chunk, i * LANES : (i + 1) * LANES]) * place[i]
            value, slope, curve = silu_parts(pre)
            if r + chunk == 256:
                inside = rows_of_lanes(0, (chunk, BLOCK)) + r < MIDDLE
                end = jnp.where(inside[chunk - 8 :], value[chunk - 8 :], last)
                value = stacked(value[: chunk - 8], end)
                slope = jnp.where(inside, slope, 0.0)
                curve = jnp.where(inside, curve, 0.0)
            high, low = halves(value)
            hid_hi[s, r : r + chunk, :] = high
            hid_lo[s, r : r + chunk, :] = low
            slope_one[s, r : r + chunk, :] = slope
            curve_one[s, r : r + chunk, :] = curve
        yield

        act_two[s] = mm(lhs_two[...], stacked(hid_hi[s], hid_lo[s], hid_hi[s]))
        yield
        total = jnp.zeros((8, BLOCK), F32)
        for r in high_chunks:
            value, slope, curve = silu_parts_twice(act_two[s, r : r + chunk, :] + picked(256 + r))
            head = across(head_w[r : r + chunk, :LANES])
            weighed = head * value
            for k in range(0, chunk, 8):
                total = total + weighed[k : k + 8, :]
            high, low = halves(head * slope)
            gate_hi[s, r : r + chunk, :] = high
            gate_lo[s, r : r + chunk, :] = low
            act_two[s, r : r + chunk, :] = value
            slope_two[s, r : r + chunk, :] = slope
            curve_two[s, r : r + chunk, :] = curve
        summed = jnp.sum(total, axis=0, keepdims=True)
        yield

        back_one[s] = mm(lhs_back[...], stacked(gate_hi[s], gate_lo[s], gate_hi[s]))
        yield
        totals = [jnp.zeros((8, BLOCK), F32) for _ in range(3)]
        for r in low_chunks:
            grad = back_one[s, r : r + chunk, :] * slope_one[s, r : r + chunk, :]
            for i in range(3):
                weighed = across(coord_w[r : r + chunk, i * LANES : (i + 1) * LANES]) * grad
                for k in range(0, chunk, 8):
                    totals[i] = totals[i] + weighed[k : k + 8, :]
        lead = [
            2.0 * jnp.sum(totals[i], axis=0, keepdims=True)
            + back_one[s, MIDDLE + i : MIDDLE + i + 1, :]
            for i in range(3)
        ]

        predicted = jnp.tanh(2.0 * summed + head_bias)
        flank = 1.0 - predicted * predicted
        slope = [flank * q for q in lead]
        excess = slope[0] * slope[0] + slope[1] * slope[1] + slope[2] * slope[2] - 1.0
        capped = jnp.tanh(predicted / DELTA)
        misfit = DELTA * capped - DELTA * jnp.tanh(target / DELTA)
        fitting = jnp.sqrt(misfit * misfit + SMOOTH * SMOOTH)
        sum_loss[0:1, :] += valid * (fitting + EIK_WEIGHT * excess * excess)
        share = valid * (1.0 / ALL_POINTS)
        pull = [(4.0 * EIK_WEIGHT) * excess * v for v in slope]
        by_flank = sum(p * q for p, q in zip(pull, lead))
        by_predicted = misfit / fitting * (1.0 - capped * capped) - 2.0 * predicted * by_flank
        bar_out = share * by_predicted * flank
        sum_loss[1:2, :] += bar_out
        half_bar = 0.5 * bar_out
        pull = [share * flank * p for p in pull]

        last = stacked(blank5, *pull)
        twice = [2.0 * p for p in pull]
        for r in low_chunks:
            grad = 0.0
            for i in range(3):
                grad = grad + across(coord_w[r : r + chunk, i * LANES : (i + 1) * LANES]) * twice[i]
            slope = slope_one[s, r : r + chunk, :]
            back = back_one[s, r : r + chunk, :]
            near = back * slope
            for i in range(3):
                sum_coord[r : r + chunk, i * LANES : (i + 1) * LANES] += folded(near * pull[i])
            through = grad * slope
            if r + chunk == 256:
                inside = rows_of_lanes(0, (8, BLOCK)) < MIDDLE - 248
                end = jnp.where(inside, through[chunk - 8 :], last)
                through = stacked(through[: chunk - 8], end)
            high, low = halves(through)
            tang_hi[s, r : r + chunk, :] = high
            tang_lo[s, r : r + chunk, :] = low
            curve_one[s, r : r + chunk, :] = (
                grad * back * curve_one[s, r : r + chunk, :]
            )
        yield
        act_tang[s] = mm(lhs_two[...], stacked(tang_hi[s], tang_lo[s], tang_hi[s]))
        yield
        for r in high_chunks:
            tangent = act_tang[s, r : r + chunk, :]
            slope = slope_two[s, r : r + chunk, :]
            head = across(head_w[r : r + chunk, LANES:])
            bar = head * (half_bar * slope + tangent * curve_two[s, r : r + chunk, :])
            by_head = act_two[s, r : r + chunk, :] * bar_out + slope * tangent
            sum_head[r : r + chunk, :] += folded(by_head)
            high, low = halves(bar)
            bar_hi[s, r : r + chunk, :] = high
            bar_lo[s, r : r + chunk, :] = low
        yield

        back_one[s] = mm(lhs_back[...], stacked(bar_hi[s], bar_lo[s], bar_hi[s]))
        yield
        for r in low_chunks:
            bar = (
                back_one[s, r : r + chunk, :] * slope_one[s, r : r + chunk, :]
                + curve_one[s, r : r + chunk, :]
            )
            for i in range(3):
                sum_coord[r : r + chunk, i * LANES : (i + 1) * LANES] += folded(bar * place[i])
            high, low = halves(bar)
            low_hi[s, r : r + chunk, :] = high
            low_lo[s, r : r + chunk, :] = low
        yield

        sum_two[...] += mm_nt(
            beside(bar_hi[s], bar_hi[s], bar_lo[s], gate_hi[s], gate_hi[s], gate_lo[s]),
            beside(hid_hi[s], hid_lo[s], hid_hi[s], tang_hi[s], tang_lo[s], tang_hi[s]),
        )
        marks = stacked(hot[s], hot[s])
        sum_codes[256:768, :] += mm(beside(bar_hi[s], bar_lo[s]), marks)
        sum_codes[0:256, :] += mm(beside(low_hi[s], low_lo[s]), marks)

    def step_body(step, carry):
        waiting = [block_stages(step, s) for s in range(SUBS)]
        active = []
        while waiting or active:
            if waiting:
                active.append(waiting.pop(0))
            active = [work for work in active if next(work, work) is not work]
        return carry

    steps = SLOTS * DEVICES // (SUBS * BLOCK)
    if steps == 1:
        step_body(0, 0)
    else:
        lax.fori_loop(0, steps, step_body, 0)


def code_kernel(codes_ref, latent_w, sum_codes, sum_count, sum_loss, code_grad_ref, facts_ref):
    codes = codes_ref[...]
    count = jnp.sum(sum_count[...], axis=0, keepdims=True)
    count = jnp.broadcast_to(count, (LANES, CODE_ROWS)).T[:, 0:1]
    turned_hi, turned_lo = halves(sum_codes[...].T)
    weight_hi, weight_lo = halves(latent_w[...])
    code_grad = mm(
        beside(turned_hi, turned_hi, turned_lo), stacked(weight_hi, weight_lo, weight_hi)
    )
    code_grad = code_grad + (2.0 * CODE_WEIGHT / ALL_POINTS) * count * codes
    code_grad_ref[...] = code_grad
    loss = jnp.sum(sum_loss[0:1, :], axis=1, keepdims=True)
    loss = (loss + CODE_WEIGHT * total_of(count * codes * codes)) / ALL_POINTS
    left = rows_of_lanes(1, facts_ref.shape) < LANES // 2
    facts_ref[...] = jnp.where(left, total_of(code_grad * code_grad), loss)


def norm_parts(direction, gain):
    root = lax.rsqrt(jnp.sum(direction * direction, axis=1, keepdims=True) + 1e-12)
    return root, gain * root


def weight_kernel(
    core_ref,
    codes_ref,
    first_w,
    second_w,
    sum_two,
    sum_codes,
    sum_coord,
    sum_head,
    _,
    sum_loss,
    keep_ref,
    give_ref,
    flat,
    tails,
    first_grad,
    second_grad,
):
    core = core_ref[0]
    codes = codes_ref[...]
    by_code = sum_codes[...]
    code_hi, code_lo = halves(codes)
    by_hi, by_lo = halves(by_code)
    latent_grad = mm(beside(by_hi, by_hi, by_lo), stacked(code_hi, code_lo, code_hi))

    bias_grad = jnp.sum(by_code, axis=1, keepdims=True)
    lane = rows_of_lanes(1, (256, LANES))
    real = rows_of_lanes(0, (256, LANES)) < MIDDLE
    near_grad = 0.0
    for i in range(3):
        column = jnp.sum(sum_coord[:, i * LANES : (i + 1) * LANES], axis=1, keepdims=True)
        near_grad = jnp.where(lane == i, column, near_grad)
    low_grad = latent_grad[0:256, :]
    first_low = first_w[:, : 2 * LANES]
    first_near = jnp.where(lane < 3, first_w[:, 2 * LANES :], 0.0)
    root, scale = norm_parts(beside(first_low, first_near), first_w[:, 2 * LANES + 3 : 2 * LANES + 4])
    along = jnp.sum(first_low * low_grad, axis=1, keepdims=True)
    along = along + jnp.sum(first_near * near_grad, axis=1, keepdims=True)
    inward = scale * root * root * along
    end = scale * near_grad - first_near * inward
    end = jnp.where(lane == 3, root * along, end)
    end = jnp.where(lane == 4, bias_grad[0:256, :], end)
    low_grad = scale * low_grad - first_low * inward
    first_grad[:, : 2 * LANES] = jnp.where(beside(real, real), low_grad, 0.0)
    first_grad[:, 2 * LANES :] = jnp.where(real, end, 0.0)

    is_hidden = rows_of_lanes(1, (HID, 256)) < MIDDLE
    hidden_grad = sum_two[...]
    moved = pltpu.roll(latent_grad[256:768, :], 256 - 3, 1)
    grad_a = jnp.where(is_hidden, hidden_grad, moved)
    grad_b = jnp.where(is_hidden, moved, hidden_grad)
    second_a = second_w[:, 0:256]
    second_b = second_w[:, 256:512]
    root, scale = norm_parts(second_w[:, 0:512], second_w[:, 512:513])
    along = jnp.sum(second_a * grad_a + second_b * grad_b, axis=1, keepdims=True)
    inward = scale * root * root * along
    second_grad[:, 0:256] = scale * grad_a - second_a * inward
    second_grad[:, 256:512] = scale * grad_b - second_b * inward
    head_grad = jnp.sum(sum_head[...], axis=1, keepdims=True)
    lane = rows_of_lanes(1, (HID, LANES))
    end = jnp.where(lane == 0, root * along, 0.0)
    end = jnp.where(lane == 1, bias_grad[256:768, :], end)
    second_grad[:, 512:640] = jnp.where(lane == 2, head_grad, end)

    for ref in (flat, tails):
        clear(ref, 128)
    pack_units(first_grad, flat, tails, *FIRST_UNITS)
    pack_units(second_grad, flat, tails, *SECOND_UNITS)
    row = HEAD_ENTRY // LANES
    lane = rows_of_lanes(1, (1, LANES))
    bias_total = jnp.sum(sum_loss[1:2, :], axis=1, keepdims=True)
    flat[row : row + 1, :] += jnp.where(lane == HEAD_ENTRY % LANES, bias_total, 0.0)
    size = 16 * SHARD_ROWS
    for which in range(2):

        @pl.when(core == which)
        def _(which=which):
            for z in range(4):
                for c in range(2):
                    target = keep_ref if c == which else give_ref
                    first = (z * 2 + c) * size
                    target[z * size : (z + 1) * size, :] = (
                        flat[first : first + size, :] + tails[first : first + size, :]
                    )


def vmem(count):
    return [pl.BlockSpec(memory_space=pltpu.VMEM)] * count


PARAMS = pltpu.CompilerParams(vmem_limit_bytes=48 * 1024 * 1024)


HBM = pl.BlockSpec(memory_space=pltpu.HBM)
SMEM = pl.BlockSpec(memory_space=pltpu.SMEM)


def f32(*shape):
    return jax.ShapeDtypeStruct(shape, F32)


def pack_boxes(weights, coords, distances, index):
    return pl.pallas_call(
        pack_kernel,
        out_shape=f32(PEERS, BOX_ROWS, LANES),
        in_specs=[HBM] * 4,
        out_specs=HBM,
        scratch_shapes=[
            pltpu.VMEM(weights.shape, F32),
            pltpu.VMEM(coords.shape, F32),
            pltpu.VMEM(distances.shape, F32),
            pltpu.VMEM(index.shape, jnp.int32),
            pltpu.VMEM((PEERS, BOX_ROWS, LANES), F32),
            pltpu.SemaphoreType.DMA((6,)),
        ],
        compiler_params=pltpu.CompilerParams(vmem_limit_bytes=60 * 1024 * 1024),
    )(weights, coords, distances, index)


def main_kernel(
    core_ref, mine_ref, other_ref, codes_ref, keep_ref, give_ref, code_grad_ref, facts_ref, *scratch
):
    first_w, second_w, latent_w, *sums = scratch[:9]
    flat = scratch[9]
    loop_kernel(core_ref, mine_ref, other_ref, codes_ref, *scratch[:-3])
    code_kernel(codes_ref, latent_w, sums[1], sums[4], sums[5], code_grad_ref, facts_ref)
    weight_kernel(core_ref, codes_ref, first_w, second_w, *sums, keep_ref, give_ref, flat, *scratch[-3:])


def main_call(core, mine, other, codes):
    pair = (SUBS, 256, BLOCK)
    pair_two = (SUBS, HID, BLOCK)
    scratch = [
        ((256, 3 * LANES), F32),
        ((HID, 5 * LANES), F32),
        ((768, 256), F32),
        ((HID, 256), F32),
        ((768, 256), F32),
        ((256, 3 * LANES), F32),
        ((HID, LANES), F32),
        ((8, CODE_ROWS), F32),
        ((2, BLOCK), F32),
        ((FLAT_ROWS + 8, LANES), F32),
        ((768, CODE_ROWS), F32),
        ((HID, 768), BF16),
        ((256, 1536), BF16),
        ((256, 3 * LANES), F32),
        ((HID, 2 * LANES), F32),
        ((LANES, LANES), F32),
        (pair, F32),
        (pair, F32),
        (pair, F32),
        (pair, BF16),
        (pair, BF16),
        ((SUBS, BLOCK, CODE_ROWS), BF16),
        (pair_two, F32),
        (pair_two, F32),
        (pair_two, F32),
        (pair_two, F32),
        (pair_two, BF16),
        (pair_two, BF16),
        (pair, BF16),
        (pair, BF16),
        (pair_two, BF16),
        (pair_two, BF16),
        (pair, BF16),
        (pair, BF16),
        ((FLAT_ROWS + 8, LANES), F32),
        ((256, 3 * LANES), F32),
        ((HID, 5 * LANES), F32),
    ]
    boxes = f32(PEERS * SHARD_ROWS, LANES)
    return pl.pallas_call(
        main_kernel,
        out_shape=(boxes, boxes, f32(CODE_ROWS, LATENT), f32(8, LANES)),
        in_specs=[SMEM] + vmem(3),
        out_specs=tuple(vmem(4)),
        scratch_shapes=[pltpu.VMEM(shape, dtype) for shape, dtype in scratch],
        compiler_params=PARAMS,
    )(core, mine, other, codes)


def adam_update(value, first, second, grad, rate):
    first_new = BETA_ONE * first + (1.0 - BETA_ONE) * grad
    second_new = BETA_TWO * second + (1.0 - BETA_TWO) * grad * grad
    first_hat = first_new / (1.0 - BETA_ONE**STEP)
    second_hat = second_new / (1.0 - BETA_TWO**STEP)
    value_new = value - rate * (first_hat / (jnp.sqrt(second_hat) + ADAM_EPS) + DECAY * value)
    return (value_new, first_new, second_new)


def shard_kernel(parts_ref, facts_ref, shard_ref, all_facts_ref):
    total = parts_ref[0:SHARD_ROWS, :]
    for peer in range(1, PEERS):
        total = total + parts_ref[peer * SHARD_ROWS : (peer + 1) * SHARD_ROWS, :]
    shard_ref[...] = total
    facts = facts_ref[...]
    left = rows_of_lanes(1, facts.shape) < LANES // 2
    all_facts_ref[...] = facts + jnp.where(left, total_of(total * total), 0.0)


def sum_shards(parts, facts):
    return pl.pallas_call(
        shard_kernel,
        out_shape=(f32(SHARD_ROWS, LANES), f32(8, LANES)),
        in_specs=vmem(2),
        out_specs=tuple(vmem(2)),
        compiler_params=PARAMS,
    )(parts, facts)


def update_kernel(
    seen_ref,
    shard_ref,
    weights_ref,
    moment_one_ref,
    moment_two_ref,
    codes_ref,
    code_first_ref,
    code_second_ref,
    code_grad_ref,
    loss_out,
    norm_out,
    weights_out,
    moment_one_out,
    moment_two_out,
    weights_copy_out,
    codes_out,
    code_first_out,
    code_second_out,
    codes_copy_out,
):
    total = jnp.sum(seen_ref[...], axis=0, keepdims=True)
    loss_out[...] = total[:, LANES // 2 : LANES // 2 + 1]
    norm = jnp.sqrt(total[:, 0:1])
    norm_out[...] = norm
    factor = jnp.minimum(1.0, CLIP / (norm + 1e-06))
    value, first, second = adam_update(
        weights_ref[...],
        moment_one_ref[...],
        moment_two_ref[...],
        factor * shard_ref[...],
        WEIGHT_RATE,
    )
    weights_out[...] = value
    moment_one_out[...] = first
    moment_two_out[...] = second
    weights_copy_out[...] = value.astype(BF16)
    for r in range(0, CODE_ROWS, 32):
        rows = slice(r, r + 32)
        value, first, second = adam_update(
            codes_ref[rows, :],
            code_first_ref[rows, :],
            code_second_ref[rows, :],
            factor * code_grad_ref[rows, :],
            CODE_RATE,
        )
        codes_out[rows, :] = value
        code_first_out[rows, :] = first
        code_second_out[rows, :] = second
        codes_copy_out[rows, :] = value.astype(BF16)


def update_all(*args):
    scalar = jax.ShapeDtypeStruct((1, 1), F32)
    shard = [jax.ShapeDtypeStruct((SHARD_ROWS, LANES), t) for t in (F32, F32, F32, BF16)]
    table = [jax.ShapeDtypeStruct((CODE_ROWS, LATENT), t) for t in (F32, F32, F32, BF16)]
    return pl.pallas_call(
        update_kernel,
        out_shape=(scalar, scalar, *shard, *table),
        in_specs=vmem(9),
        out_specs=tuple(vmem(10)),
        compiler_params=PARAMS,
    )(*args)


def swap_cores(v):
    return lax.ppermute(v, "core", [(0, 1), (1, 0)])


def exchange(v):
    return lax.all_to_all(v, ("z", "wide"), split_axis=0, concat_axis=0)


def body(
    weights_flat,
    moment_one,
    moment_two,
    codes,
    code_first,
    code_second,
    coords,
    distances,
    shape_index,
):
    boxes = pack_boxes(
        weights_flat.reshape(SHARD_ROWS, LANES),
        coords,
        distances.reshape(1, POINTS_DEV),
        shape_index.reshape(1, POINTS_DEV),
    )
    mine = exchange(boxes)
    other = swap_cores(mine)
    core = lax.axis_index("core").astype(jnp.int32).reshape(1)
    keep, give, code_grad, facts = main_call(
        core,
        mine.reshape(PEERS * BOX_ROWS, LANES),
        other.reshape(PEERS * BOX_ROWS, LANES),
        codes,
    )
    pair_sum = (keep + swap_cores(give)).reshape(PEERS, 1, SHARD_ROWS * LANES)
    parts = exchange(pair_sum).reshape(PEERS * SHARD_ROWS, LANES)
    shard, facts = sum_shards(parts, facts)
    facts = facts + swap_cores(facts)
    facts = jnp.broadcast_to(facts[0:1], (PEERS, LANES)).reshape(PEERS, 1, LANES)
    flat = lambda v: v.reshape(SHARD_ROWS, LANES)
    out = update_all(
        exchange(facts).reshape(PEERS, LANES),
        shard,
        flat(weights_flat),
        flat(moment_one),
        flat(moment_two),
        codes,
        code_first,
        code_second,
        code_grad,
    )
    return (
        out[0].reshape(()),
        out[1].reshape(()),
        *[v.reshape(weights_flat.shape) for v in out[2:6]],
        *out[6:],
    )


def solution(mesh):
    parts = Mesh(mesh.devices.reshape(4, 2, 16), ALL)
    return jax.shard_map(
        body,
        mesh=parts,
        in_specs=(
            P(ALL),
            P(ALL),
            P(ALL),
            P(ALL, None),
            P(ALL, None),
            P(ALL, None),
            P(None, ALL),
            P(ALL),
            P(ALL),
        ),
        out_specs=(
            P(),
            P(),
            P(ALL),
            P(ALL),
            P(ALL),
            P(ALL),
            P(ALL, None),
            P(ALL, None),
            P(ALL, None),
            P(ALL, None),
        ),
        check_vma=False,
    )
```

```python
import jax
import jax.numpy as jnp
from jax import lax
from jax.experimental import pallas as pl
from jax.experimental.pallas import tpu as pltpu
from jax.sharding import Mesh
from jax.sharding import PartitionSpec as P

LATENT = 256
HID = 512
MIDDLE = HID - LATENT - 3
STEP = 10

DELTA = 0.1
SMOOTH = 0.01
CODE_WEIGHT = 0.001
EIK_WEIGHT = 0.1
CLIP = 0.001
WEIGHT_RATE = 0.02
CODE_RATE = 0.15
BETA_ONE = 0.9
BETA_TWO = 0.999
ADAM_EPS = 1e-08
DECAY = 0.01

LANES = 128
DEVICES = 128
PEERS = 64
SHARD_ROWS = 21
BOX_ROWS = 24
SLOTS = 16
POINTS_DEV = 1024
CODE_ROWS = 256
FLAT_ROWS = DEVICES * SHARD_ROWS
BLOCK = 256
SUBS = 4
TILES = BLOCK // LANES
ALL_POINTS = POINTS_DEV * DEVICES

F32 = jnp.float32
BF16 = jnp.bfloat16
ALL = ("z", "core", "wide")


def rows_of_lanes(lead, shape):
    return lax.broadcasted_iota(jnp.int32, shape, lead)


def halves(v):
    high = v.astype(BF16)
    return high, (v - high.astype(F32)).astype(BF16)


def thirds(v):
    high = v.astype(BF16).astype(F32)
    rest = v - high
    mid = rest.astype(BF16).astype(F32)
    return high, mid, rest - mid


def mm(a, b):
    return lax.dot_general(a, b, (((1,), (0,)), ((), ())), preferred_element_type=F32)


def mm_nt(a, b):
    return lax.dot_general(a, b, (((1,), (1,)), ((), ())), preferred_element_type=F32)


def beside(*parts):
    return jnp.concatenate(parts, axis=1)


def total_of(v):
    return jnp.sum(jnp.sum(v, axis=0, keepdims=True), axis=1, keepdims=True)


def stacked(*parts):
    return jnp.concatenate(parts, axis=0)


def pack_kernel(
    weights_hbm,
    coords_hbm,
    distances_hbm,
    index_hbm,
    out_hbm,
    weights_ref,
    coords_ref,
    distances_ref,
    index_ref,
    staged,
    sems,
):
    pairs = [
        (index_hbm, index_ref),
        (weights_hbm, weights_ref),
        (coords_hbm, coords_ref),
        (distances_hbm, distances_ref),
    ]
    copies = [
        pltpu.make_async_copy(source, target, sems.at[i])
        for i, (source, target) in enumerate(pairs)
    ]
    for copy in copies:
        copy.start()
    copies[1].wait()
    shard = stacked(weights_ref[...], jnp.zeros((BOX_ROWS - SHARD_ROWS, LANES), F32))

    def fill(i, carry):
        for k in range(8):
            place = pl.ds(pl.multiple_of((i * 8 + k) * BOX_ROWS, 8), BOX_ROWS)
            staged[place, :] = shard
        return carry

    lax.fori_loop(0, PEERS // 8, fill, 0)
    for i in (0, 2, 3):
        copies[i].wait()
    index = index_ref[...]
    owner = lax.shift_right_logical(index, 8)
    row = lax.bitwise_and(index, CODE_ROWS - 1)
    sent = (rows_of_lanes(0, (DEVICES, POINTS_DEV)) == owner).astype(F32)
    sent_low = sent.astype(BF16)
    width = 256
    earlier = rows_of_lanes(0, (width, width)) < rows_of_lanes(1, (width, width))
    earlier = earlier.astype(F32).astype(BF16)
    ones = jnp.ones((width, width), BF16)
    ranks = [
        mm(sent_low[:, : (part + 1) * width], stacked(*([ones] * part + [earlier])))
        for part in range(POINTS_DEV // width)
    ]
    placed = jnp.sum(sent * beside(*ranks), axis=0, keepdims=True).astype(jnp.int32)
    at_slot = rows_of_lanes(0, (SLOTS, POINTS_DEV)) == placed
    values = [coords_ref[i : i + 1, :] for i in range(3)]
    values += [distances_ref[...], (row + 1).astype(F32)]
    pieces = [[], [], []]
    for value in values:
        for k, third in enumerate(thirds(value)):
            pieces[k].append(jnp.where(at_slot, third, 0.0))
    spare = jnp.zeros((LANES - SLOTS * len(values), POINTS_DEV), F32)
    boxes = mm_nt(
        beside(sent_low, sent_low, sent_low),
        beside(*[stacked(*piece, spare).astype(BF16) for piece in pieces]),
    )
    for z in range(4):
        for core in range(2):
            place = pl.ds(z * 16 * BOX_ROWS + SHARD_ROWS + core, 16, stride=BOX_ROWS)
            first = z * 32 + core * 16
            staged[place, :] = boxes[first : first + 16, :]
    out = pltpu.make_async_copy(staged, out_hbm, sems.at[4])
    out.start()
    out.wait()


def unit_groups(count, stride_rows, extra, first_entry):
    for group in range(count):
        entry = first_entry + group * 8 * (stride_rows * LANES + extra)
        yield group, entry // LANES, entry % LANES


def unpack_units(flat_ref, out_ref, count, stride_rows, extra, first_entry):
    lane = rows_of_lanes(1, (8, LANES))
    slope = rows_of_lanes(0, (8, LANES)) * extra
    for group, first, shift in unit_groups(count, stride_rows, extra, first_entry):
        start = slope + shift
        wraps = shift + 7 * extra >= LANES
        turn = lax.bitwise_and(lane + start, LANES - 1)
        tiles = []
        for a in range(stride_rows + 2 + wraps):
            tile = flat_ref[pl.ds(first + a, 8, stride=stride_rows), :]
            tiles.append(jnp.take_along_axis(tile, turn, axis=1, mode="promise_in_bounds"))
        for c in range(stride_rows + 1):
            value = jnp.where(lane + start < LANES, tiles[c], tiles[c + 1])
            if wraps:
                value = jnp.where(lane + start < 2 * LANES, value, tiles[c + 2])
            out_ref[group * 8 : group * 8 + 8, c * LANES : (c + 1) * LANES] = value


def pack_units(value_ref, heads_ref, tails_ref, count, stride_rows, extra, first_entry):
    lane = rows_of_lanes(1, (8, LANES))
    slope = rows_of_lanes(0, (8, LANES)) * extra
    zero = jnp.zeros((8, LANES), F32)
    for group, first, shift in unit_groups(count, stride_rows, extra, first_entry):
        start = slope + shift
        wraps = shift + 7 * extra >= LANES
        turn = lax.bitwise_and(lane - start, LANES - 1)
        tiles = [zero, zero]
        for c in range(stride_rows + 1):
            value = value_ref[group * 8 : group * 8 + 8, c * LANES : (c + 1) * LANES]
            tiles.append(jnp.take_along_axis(value, turn, axis=1, mode="promise_in_bounds"))
        tiles.append(zero)
        for a in range(stride_rows + 2):
            value = jnp.where(lane >= start, tiles[a + 2], tiles[a + 1])
            if wraps:
                value = jnp.where(lane >= start - LANES, value, tiles[a])
            target = heads_ref if a < stride_rows else tails_ref
            target[pl.ds(first + a, 8, stride=stride_rows), :] = value


def clear(ref, rows):
    def step(i, carry):
        place = pl.ds(pl.multiple_of(i * rows, 8), rows)
        ref[place, :] = jnp.zeros((rows, ref.shape[1]), F32)
        return carry

    lax.fori_loop(0, ref.shape[0] // rows, step, 0)


FIRST_UNITS = (32, 2, 5, 0)
SECOND_UNITS = (64, 4, 3, MIDDLE * (LATENT + 5))
HEAD_ENTRY = MIDDLE * (LATENT + 5) + HID * (HID + 3)


def across(column):
    return beside(*[column] * TILES)


def folded(v):
    return sum(v[:, i * LANES : (i + 1) * LANES] for i in range(TILES))


def silu_parts(half):
    gate = jnp.tanh(half)
    low = 0.5 * gate
    bend = 0.5 - gate * low
    bent = half * gate
    return half + bent, (0.5 + low) + half * bend, bend * (1.0 - bent)


def silu_parts_twice(half):
    gate = jnp.tanh(half)
    bend = 1.0 - gate * gate
    bent = half * gate
    return half + bent, (1.0 + gate) + half * bend, bend * (1.0 - bent)


def loop_kernel(
    core_ref,
    mine_ref,
    other_ref,
    codes_ref,
    first_w,
    second_w,
    latent_w,
    sum_two,
    sum_codes,
    sum_coord,
    sum_head,
    sum_count,
    sum_loss,
    flat,
    table,
    lhs_two,
    lhs_back,
    coord_w,
    head_w,
    spots,
    slope_one,
    curve_one,
    back_one,
    hid_hi,
    hid_lo,
    hot,
    act_two,
    slope_two,
    curve_two,
    act_tang,
    gate_hi,
    gate_lo,
    tang_hi,
    tang_lo,
    bar_hi,
    bar_lo,
    low_hi,
    low_lo,
):
    core = core_ref[0]

    for which in range(2):

        @pl.when(core == which)
        def _(which=which):
            for d in range(DEVICES):
                z, c, w = d // 32, d // 16 % 2, d % 16
                box = (z * 16 + w) * BOX_ROWS
                source = mine_ref if c == which else other_ref
                flat[d * SHARD_ROWS : d * SHARD_ROWS + BOX_ROWS, :] = source[box : box + BOX_ROWS, :]
            rows = pl.ds(SHARD_ROWS + which, PEERS, stride=BOX_ROWS)
            spots[...] = stacked(mine_ref[rows, :], other_ref[rows, :]).T

    unpack_units(flat, first_w, *FIRST_UNITS)
    unpack_units(flat, second_w, *SECOND_UNITS)
    head_bias = flat[HEAD_ENTRY // LANES : HEAD_ENTRY // LANES + 1, :][
        :, HEAD_ENTRY % LANES : HEAD_ENTRY % LANES + 1
    ]

    lane = rows_of_lanes(1, (256, LANES))
    unit = rows_of_lanes(0, (256, LANES))
    real = unit < MIDDLE

    first_low = jnp.where(beside(real, real), first_w[:, : 2 * LANES], 0.0)
    first_end = jnp.where(real, first_w[:, 2 * LANES :], 0.0)
    first_near = jnp.where(lane < 3, first_end, 0.0)
    first_gain = first_end[:, 3:4]
    first_bias = first_end[:, 4:5]
    first_w[:, : 2 * LANES] = first_low
    first_w[:, 2 * LANES :] = first_end
    _, first_scale = norm_parts(beside(first_low, first_near), first_gain)
    first_low = first_low * first_scale
    first_near = first_near * first_scale
    latent_w[0:256, :] = first_low
    for i in range(3):
        coord_w[:, i * LANES : (i + 1) * LANES] = jnp.broadcast_to(
            0.5 * first_near[:, i : i + 1], (256, LANES)
        )

    second_a = second_w[:, 0:256]
    second_b = second_w[:, 256:512]
    second_gain = second_w[:, 512:513]
    second_bias = second_w[:, 513:514]
    head = jnp.broadcast_to(second_w[:, 514:515], (HID, LANES))
    head_w[:, :LANES] = 0.5 * head
    head_w[:, LANES:] = head
    _, second_scale = norm_parts(second_w[:, 0:512], second_gain)
    second_a = second_a * second_scale
    second_b = second_b * second_scale
    is_hidden = rows_of_lanes(1, (HID, 256)) < MIDDLE
    hidden_cols = jnp.where(is_hidden, second_a, second_b)
    latent_cols = pltpu.roll(jnp.where(is_hidden, second_b, second_a), 3, 1)
    latent_w[256:768, :] = latent_cols

    hidden_hi, hidden_lo = halves(0.5 * hidden_cols)
    lhs_two[:, 0:256] = hidden_hi
    lhs_two[:, 256:512] = hidden_hi
    lhs_two[:, 512:768] = hidden_lo
    back_hi, back_lo = halves(hidden_cols.T)
    lhs_back[:, 0:512] = back_hi
    lhs_back[:, 512:1024] = back_hi
    lhs_back[:, 1024:1536] = back_lo

    code_hi, code_lo = halves(codes_ref[...])
    weight_hi, weight_lo = halves(latent_w[...])
    by_code = mm_nt(
        beside(weight_hi, weight_hi, weight_lo), beside(code_hi, code_lo, code_hi)
    )
    table[0:256, :] = 0.5 * (by_code[0:256, :] + first_bias)
    table[256:768, :] = 0.5 * (by_code[256:768, :] + second_bias)

    for ref in (sum_two, sum_codes, sum_coord, sum_head):
        clear(ref, 64)
    sum_count[...] = jnp.zeros(sum_count.shape, F32)
    sum_loss[...] = jnp.zeros(sum_loss.shape, F32)

    def feature(which, step, sub):
        first = which * SLOTS + (step * SUBS + sub) * TILES
        return beside(*[spots[pl.ds(first + i, 1), :] for i in range(TILES)])

    blank5 = jnp.zeros((5, BLOCK), F32)
    chunk = 8192 // BLOCK
    low_chunks = range(0, 256, chunk)
    high_chunks = range(0, HID, chunk)

    def block_stages(step, s):
        place = [feature(i, step, s) for i in range(3)]
        target = feature(3, step, s)
        code_row = feature(4, step, s)
        valid = (code_row > 0.5).astype(F32)

        code = jnp.broadcast_to(jnp.maximum(code_row - 1.0, 0.0).astype(jnp.int32), (chunk, BLOCK))
        upper = code >= LANES
        code = lax.bitwise_and(code, LANES - 1)

        def picked(first):
            rows = slice(first, first + chunk)
            tiles = []
            for i in range(TILES):
                part = slice(i * LANES, (i + 1) * LANES)
                both = [
                    jnp.take_along_axis(
                        table[rows, c : c + LANES], code[:, part], axis=1, mode="promise_in_bounds"
                    )
                    for c in (0, LANES)
                ]
                tiles.append(jnp.where(upper[:, part], both[1], both[0]))
            return beside(*tiles)

        last = stacked(blank5, *place)
        for r in low_chunks:
            pre = picked(r)
            for i in range(3):
                pre = pre + across(coord_w[r : r + chunk, i * LANES : (i + 1) * LANES]) * place[i]
            value, slope, curve = silu_parts(pre)
            if r + chunk == 256:
                inside = rows_of_lanes(0, (chunk, BLOCK)) + r < MIDDLE
                end = jnp.where(inside[chunk - 8 :], value[chunk - 8 :], last)
                value = stacked(value[: chunk - 8], end)
                slope = jnp.where(inside, slope, 0.0)
                curve = jnp.where(inside, curve, 0.0)
            high, low = halves(value)
            hid_hi[s, r : r + chunk, :] = high
            hid_lo[s, r : r + chunk, :] = low
            slope_one[s, r : r + chunk, :] = slope
            curve_one[s, r : r + chunk, :] = curve
        yield

        act_two[s] = mm(lhs_two[...], stacked(hid_hi[s], hid_lo[s], hid_hi[s]))
        yield
        total = jnp.zeros((8, BLOCK), F32)
        for r in high_chunks:
            value, slope, curve = silu_parts_twice(act_two[s, r : r + chunk, :] + picked(256 + r))
            head = across(head_w[r : r + chunk, :LANES])
            weighed = head * value
            for k in range(0, chunk, 8):
                total = total + weighed[k : k + 8, :]
            high, low = halves(head * slope)
            gate_hi[s, r : r + chunk, :] = high
            gate_lo[s, r : r + chunk, :] = low
            act_two[s, r : r + chunk, :] = value
            slope_two[s, r : r + chunk, :] = slope
            curve_two[s, r : r + chunk, :] = curve
        summed = jnp.sum(total, axis=0, keepdims=True)
        yield

        back_one[s] = mm(lhs_back[...], stacked(gate_hi[s], gate_lo[s], gate_hi[s]))
        yield
        totals = [jnp.zeros((8, BLOCK), F32) for _ in range(3)]
        for r in low_chunks:
            grad = back_one[s, r : r + chunk, :] * slope_one[s, r : r + chunk, :]
            for i in range(3):
                weighed = across(coord_w[r : r + chunk, i * LANES : (i + 1) * LANES]) * grad
                for k in range(0, chunk, 8):
                    totals[i] = totals[i] + weighed[k : k + 8, :]
        lead = [
            2.0 * jnp.sum(totals[i], axis=0, keepdims=True)
            + back_one[s, MIDDLE + i : MIDDLE + i + 1, :]
            for i in range(3)
        ]

        predicted = jnp.tanh(2.0 * summed + head_bias)
        flank = 1.0 - predicted * predicted
        slope = [flank * q for q in lead]
        excess = slope[0] * slope[0] + slope[1] * slope[1] + slope[2] * slope[2] - 1.0
        capped = jnp.tanh(predicted / DELTA)
        misfit = DELTA * capped - DELTA * jnp.tanh(target / DELTA)
        fitting = jnp.sqrt(misfit * misfit + SMOOTH * SMOOTH)
        sum_loss[0:1, :] += valid * (fitting + EIK_WEIGHT * excess * excess)
        share = valid * (1.0 / ALL_POINTS)
        pull = [(4.0 * EIK_WEIGHT) * excess * v for v in slope]
        by_flank = sum(p * q for p, q in zip(pull, lead))
        by_predicted = misfit / fitting * (1.0 - capped * capped) - 2.0 * predicted * by_flank
        bar_out = share * by_predicted * flank
        sum_loss[1:2, :] += bar_out
        half_bar = 0.5 * bar_out
        pull = [share * flank * p for p in pull]

        last = stacked(blank5, *pull)
        twice = [2.0 * p for p in pull]
        for r in low_chunks:
            grad = 0.0
            for i in range(3):
                grad = grad + across(coord_w[r : r + chunk, i * LANES : (i + 1) * LANES]) * twice[i]
            slope = slope_one[s, r : r + chunk, :]
            back = back_one[s, r : r + chunk, :]
            near = back * slope
            for i in range(3):
                sum_coord[r : r + chunk, i * LANES : (i + 1) * LANES] += folded(near * pull[i])
            through = grad * slope
            if r + chunk == 256:
                inside = rows_of_lanes(0, (8, BLOCK)) < MIDDLE - 248
                end = jnp.where(inside, through[chunk - 8 :], last)
                through = stacked(through[: chunk - 8], end)
            high, low = halves(through)
            tang_hi[s, r : r + chunk, :] = high
            tang_lo[s, r : r + chunk, :] = low
            curve_one[s, r : r + chunk, :] = (
                grad * back * curve_one[s, r : r + chunk, :]
            )
        yield
        act_tang[s] = mm(lhs_two[...], stacked(tang_hi[s], tang_lo[s], tang_hi[s]))

        for c in range(0, CODE_ROWS, LANES):
            code = (rows_of_lanes(1, (LANES, LANES)) + c).astype(F32)
            seen = jnp.zeros((8, LANES), F32)
            for i in range(TILES):
                wanted = code_row[:, i * LANES : (i + 1) * LANES] - 1.0
                mark = jnp.where(code == jnp.broadcast_to(wanted, (LANES, LANES)).T, 1.0, 0.0)
                hot[s, i * LANES : (i + 1) * LANES, c : c + LANES] = mark.astype(BF16)
                for k in range(0, LANES, 8):
                    seen = seen + mark[k : k + 8, :]
            sum_count[:, c : c + LANES] += seen
        yield
        for r in high_chunks:
            tangent = act_tang[s, r : r + chunk, :]
            slope = slope_two[s, r : r + chunk, :]
            head = across(head_w[r : r + chunk, LANES:])
            bar = head * (half_bar * slope + tangent * curve_two[s, r : r + chunk, :])
            by_head = act_two[s, r : r + chunk, :] * bar_out + slope * tangent
            sum_head[r : r + chunk, :] += folded(by_head)
            high, low = halves(bar)
            bar_hi[s, r : r + chunk, :] = high
            bar_lo[s, r : r + chunk, :] = low
        yield

        back_one[s] = mm(lhs_back[...], stacked(bar_hi[s], bar_lo[s], bar_hi[s]))
        yield
        for r in low_chunks:
            bar = (
                back_one[s, r : r + chunk, :] * slope_one[s, r : r + chunk, :]
                + curve_one[s, r : r + chunk, :]
            )
            for i in range(3):
                sum_coord[r : r + chunk, i * LANES : (i + 1) * LANES] += folded(bar * place[i])
            high, low = halves(bar)
            low_hi[s, r : r + chunk, :] = high
            low_lo[s, r : r + chunk, :] = low
        yield

        sum_two[...] += mm_nt(
            beside(bar_hi[s], bar_hi[s], bar_lo[s], gate_hi[s], gate_hi[s], gate_lo[s]),
            beside(hid_hi[s], hid_lo[s], hid_hi[s], tang_hi[s], tang_lo[s], tang_hi[s]),
        )
        marks = stacked(hot[s], hot[s])
        sum_codes[256:768, :] += mm(beside(bar_hi[s], bar_lo[s]), marks)
        sum_codes[0:256, :] += mm(beside(low_hi[s], low_lo[s]), marks)

    def step_body(step, carry):
        waiting = [block_stages(step, s) for s in range(SUBS)]
        active = []
        while waiting or active:
            if waiting:
                active.append(waiting.pop(0))
            active = [work for work in active if next(work, work) is not work]
        return carry

    steps = SLOTS * DEVICES // (SUBS * BLOCK)
    if steps == 1:
        step_body(0, 0)
    else:
        lax.fori_loop(0, steps, step_body, 0)


def code_kernel(codes_ref, latent_w, sum_codes, sum_count, sum_loss, code_grad_ref, facts_ref):
    codes = codes_ref[...]
    count = jnp.sum(sum_count[...], axis=0, keepdims=True)
    count = jnp.broadcast_to(count, (LANES, CODE_ROWS)).T[:, 0:1]
    turned_hi, turned_lo = halves(sum_codes[...].T)
    weight_hi, weight_lo = halves(latent_w[...])
    code_grad = mm(
        beside(turned_hi, turned_hi, turned_lo), stacked(weight_hi, weight_lo, weight_hi)
    )
    code_grad = code_grad + (2.0 * CODE_WEIGHT / ALL_POINTS) * count * codes
    code_grad_ref[...] = code_grad
    loss = jnp.sum(sum_loss[0:1, :], axis=1, keepdims=True)
    loss = (loss + CODE_WEIGHT * total_of(count * codes * codes)) / ALL_POINTS
    left = rows_of_lanes(1, facts_ref.shape) < LANES // 2
    facts_ref[...] = jnp.where(left, total_of(code_grad * code_grad), loss)


def norm_parts(direction, gain):
    root = lax.rsqrt(jnp.sum(direction * direction, axis=1, keepdims=True) + 1e-12)
    return root, gain * root


def weight_kernel(
    core_ref,
    codes_ref,
    first_w,
    second_w,
    sum_two,
    sum_codes,
    sum_coord,
    sum_head,
    _,
    sum_loss,
    keep_ref,
    give_ref,
    flat,
    tails,
    first_grad,
    second_grad,
):
    core = core_ref[0]
    codes = codes_ref[...]
    by_code = sum_codes[...]
    code_hi, code_lo = halves(codes)
    by_hi, by_lo = halves(by_code)
    latent_grad = mm(beside(by_hi, by_hi, by_lo), stacked(code_hi, code_lo, code_hi))

    bias_grad = jnp.sum(by_code, axis=1, keepdims=True)
    lane = rows_of_lanes(1, (256, LANES))
    real = rows_of_lanes(0, (256, LANES)) < MIDDLE
    near_grad = 0.0
    for i in range(3):
        column = jnp.sum(sum_coord[:, i * LANES : (i + 1) * LANES], axis=1, keepdims=True)
        near_grad = jnp.where(lane == i, column, near_grad)
    low_grad = latent_grad[0:256, :]
    first_low = first_w[:, : 2 * LANES]
    first_near = jnp.where(lane < 3, first_w[:, 2 * LANES :], 0.0)
    root, scale = norm_parts(beside(first_low, first_near), first_w[:, 2 * LANES + 3 : 2 * LANES + 4])
    along = jnp.sum(first_low * low_grad, axis=1, keepdims=True)
    along = along + jnp.sum(first_near * near_grad, axis=1, keepdims=True)
    inward = scale * root * root * along
    end = scale * near_grad - first_near * inward
    end = jnp.where(lane == 3, root * along, end)
    end = jnp.where(lane == 4, bias_grad[0:256, :], end)
    low_grad = scale * low_grad - first_low * inward
    first_grad[:, : 2 * LANES] = jnp.where(beside(real, real), low_grad, 0.0)
    first_grad[:, 2 * LANES :] = jnp.where(real, end, 0.0)

    is_hidden = rows_of_lanes(1, (HID, 256)) < MIDDLE
    hidden_grad = sum_two[...]
    moved = pltpu.roll(latent_grad[256:768, :], 256 - 3, 1)
    grad_a = jnp.where(is_hidden, hidden_grad, moved)
    grad_b = jnp.where(is_hidden, moved, hidden_grad)
    second_a = second_w[:, 0:256]
    second_b = second_w[:, 256:512]
    root, scale = norm_parts(second_w[:, 0:512], second_w[:, 512:513])
    along = jnp.sum(second_a * grad_a + second_b * grad_b, axis=1, keepdims=True)
    inward = scale * root * root * along
    second_grad[:, 0:256] = scale * grad_a - second_a * inward
    second_grad[:, 256:512] = scale * grad_b - second_b * inward
    head_grad = jnp.sum(sum_head[...], axis=1, keepdims=True)
    lane = rows_of_lanes(1, (HID, LANES))
    end = jnp.where(lane == 0, root * along, 0.0)
    end = jnp.where(lane == 1, bias_grad[256:768, :], end)
    second_grad[:, 512:640] = jnp.where(lane == 2, head_grad, end)

    for ref in (flat, tails):
        clear(ref, 128)
    pack_units(first_grad, flat, tails, *FIRST_UNITS)
    pack_units(second_grad, flat, tails, *SECOND_UNITS)
    row = HEAD_ENTRY // LANES
    lane = rows_of_lanes(1, (1, LANES))
    bias_total = jnp.sum(sum_loss[1:2, :], axis=1, keepdims=True)
    flat[row : row + 1, :] += jnp.where(lane == HEAD_ENTRY % LANES, bias_total, 0.0)
    size = 16 * SHARD_ROWS
    for which in range(2):

        @pl.when(core == which)
        def _(which=which):
            for z in range(4):
                for c in range(2):
                    target = keep_ref if c == which else give_ref
                    first = (z * 2 + c) * size
                    target[z * size : (z + 1) * size, :] = (
                        flat[first : first + size, :] + tails[first : first + size, :]
                    )


def vmem(count):
    return [pl.BlockSpec(memory_space=pltpu.VMEM)] * count


PARAMS = pltpu.CompilerParams(vmem_limit_bytes=48 * 1024 * 1024)


HBM = pl.BlockSpec(memory_space=pltpu.HBM)
SMEM = pl.BlockSpec(memory_space=pltpu.SMEM)


def f32(*shape):
    return jax.ShapeDtypeStruct(shape, F32)


def pack_boxes(weights, coords, distances, index):
    return pl.pallas_call(
        pack_kernel,
        out_shape=f32(PEERS * BOX_ROWS, LANES),
        in_specs=[HBM] * 4,
        out_specs=HBM,
        scratch_shapes=[
            pltpu.VMEM(weights.shape, F32),
            pltpu.VMEM(coords.shape, F32),
            pltpu.VMEM(distances.shape, F32),
            pltpu.VMEM(index.shape, jnp.int32),
            pltpu.VMEM((PEERS * BOX_ROWS, LANES), F32),
            pltpu.SemaphoreType.DMA((5,)),
        ],
        compiler_params=pltpu.CompilerParams(vmem_limit_bytes=60 * 1024 * 1024),
    )(weights, coords, distances, index)


def main_kernel(
    core_ref, mine_ref, other_ref, codes_ref, keep_ref, give_ref, code_grad_ref, facts_ref, *scratch
):
    first_w, second_w, latent_w, *sums = scratch[:9]
    flat = scratch[9]
    loop_kernel(core_ref, mine_ref, other_ref, codes_ref, *scratch[:-3])
    code_kernel(codes_ref, latent_w, sums[1], sums[4], sums[5], code_grad_ref, facts_ref)
    weight_kernel(core_ref, codes_ref, first_w, second_w, *sums, keep_ref, give_ref, flat, *scratch[-3:])


def main_call(core, mine, other, codes):
    pair = (SUBS, 256, BLOCK)
    pair_two = (SUBS, HID, BLOCK)
    scratch = [
        ((256, 3 * LANES), F32),
        ((HID, 5 * LANES), F32),
        ((768, 256), F32),
        ((HID, 256), F32),
        ((768, 256), F32),
        ((256, 3 * LANES), F32),
        ((HID, LANES), F32),
        ((8, CODE_ROWS), F32),
        ((2, BLOCK), F32),
        ((FLAT_ROWS + 8, LANES), F32),
        ((768, CODE_ROWS), F32),
        ((HID, 768), BF16),
        ((256, 1536), BF16),
        ((256, 3 * LANES), F32),
        ((HID, 2 * LANES), F32),
        ((LANES, LANES), F32),
        (pair, F32),
        (pair, F32),
        (pair, F32),
        (pair, BF16),
        (pair, BF16),
        ((SUBS, BLOCK, CODE_ROWS), BF16),
        (pair_two, F32),
        (pair_two, F32),
        (pair_two, F32),
        (pair_two, F32),
        (pair_two, BF16),
        (pair_two, BF16),
        (pair, BF16),
        (pair, BF16),
        (pair_two, BF16),
        (pair_two, BF16),
        (pair, BF16),
        (pair, BF16),
        ((FLAT_ROWS + 8, LANES), F32),
        ((256, 3 * LANES), F32),
        ((HID, 5 * LANES), F32),
    ]
    boxes = f32(PEERS * SHARD_ROWS, LANES)
    return pl.pallas_call(
        main_kernel,
        out_shape=(boxes, boxes, f32(CODE_ROWS, LATENT), f32(8, LANES)),
        in_specs=[SMEM] + vmem(3),
        out_specs=tuple(vmem(4)),
        scratch_shapes=[pltpu.VMEM(shape, dtype) for shape, dtype in scratch],
        compiler_params=PARAMS,
    )(core, mine, other, codes)


def adam_update(value, first, second, grad, rate):
    first_new = BETA_ONE * first + (1.0 - BETA_ONE) * grad
    second_new = BETA_TWO * second + (1.0 - BETA_TWO) * grad * grad
    first_hat = first_new / (1.0 - BETA_ONE**STEP)
    second_hat = second_new / (1.0 - BETA_TWO**STEP)
    value_new = value - rate * (first_hat / (jnp.sqrt(second_hat) + ADAM_EPS) + DECAY * value)
    return (value_new, first_new, second_new)


def shard_kernel(parts_ref, facts_ref, shard_ref, all_facts_ref):
    total = parts_ref[0:SHARD_ROWS, :]
    for peer in range(1, PEERS):
        total = total + parts_ref[peer * SHARD_ROWS : (peer + 1) * SHARD_ROWS, :]
    shard_ref[...] = total
    facts = facts_ref[...]
    left = rows_of_lanes(1, facts.shape) < LANES // 2
    all_facts_ref[...] = facts + jnp.where(left, total_of(total * total), 0.0)


def sum_shards(parts, facts):
    return pl.pallas_call(
        shard_kernel,
        out_shape=(f32(SHARD_ROWS, LANES), f32(8, LANES)),
        in_specs=vmem(2),
        out_specs=tuple(vmem(2)),
        compiler_params=PARAMS,
    )(parts, facts)


def update_kernel(
    seen_ref,
    shard_ref,
    weights_ref,
    moment_one_ref,
    moment_two_ref,
    codes_ref,
    code_first_ref,
    code_second_ref,
    code_grad_ref,
    loss_out,
    norm_out,
    weights_out,
    moment_one_out,
    moment_two_out,
    weights_copy_out,
    codes_out,
    code_first_out,
    code_second_out,
    codes_copy_out,
):
    total = jnp.sum(seen_ref[...], axis=0, keepdims=True)
    loss_out[...] = total[:, LANES // 2 : LANES // 2 + 1]
    norm = jnp.sqrt(total[:, 0:1])
    norm_out[...] = norm
    factor = jnp.minimum(1.0, CLIP / (norm + 1e-06))
    value, first, second = adam_update(
        weights_ref[...],
        moment_one_ref[...],
        moment_two_ref[...],
        factor * shard_ref[...],
        WEIGHT_RATE,
    )
    weights_out[...] = value
    moment_one_out[...] = first
    moment_two_out[...] = second
    weights_copy_out[...] = value.astype(BF16)

    def step(i, carry):
        rows = pl.ds(pl.multiple_of(i * 64, 8), 64)
        value, first, second = adam_update(
            codes_ref[rows, :],
            code_first_ref[rows, :],
            code_second_ref[rows, :],
            factor * code_grad_ref[rows, :],
            CODE_RATE,
        )
        codes_out[rows, :] = value
        code_first_out[rows, :] = first
        code_second_out[rows, :] = second
        codes_copy_out[rows, :] = value.astype(BF16)
        return carry

    lax.fori_loop(0, CODE_ROWS // 64, step, 0)


def update_all(*args):
    scalar = jax.ShapeDtypeStruct((1, 1), F32)
    shard = [jax.ShapeDtypeStruct((SHARD_ROWS, LANES), t) for t in (F32, F32, F32, BF16)]
    table = [jax.ShapeDtypeStruct((CODE_ROWS, LATENT), t) for t in (F32, F32, F32, BF16)]
    return pl.pallas_call(
        update_kernel,
        out_shape=(scalar, scalar, *shard, *table),
        in_specs=vmem(9),
        out_specs=tuple(vmem(10)),
        compiler_params=PARAMS,
    )(*args)


def swap_cores(v):
    return lax.ppermute(v, "core", [(0, 1), (1, 0)])


def exchange(v):
    return lax.all_to_all(v, ("z", "wide"), split_axis=0, concat_axis=0)


def body(
    weights_flat,
    moment_one,
    moment_two,
    codes,
    code_first,
    code_second,
    coords,
    distances,
    shape_index,
):
    boxes = pack_boxes(
        weights_flat.reshape(SHARD_ROWS, LANES),
        coords,
        distances.reshape(1, POINTS_DEV),
        shape_index.reshape(1, POINTS_DEV),
    )
    mine = exchange(boxes.reshape(PEERS, BOX_ROWS, LANES))
    other = swap_cores(mine)
    core = lax.axis_index("core").astype(jnp.int32).reshape(1)
    keep, give, code_grad, facts = main_call(
        core,
        mine.reshape(PEERS * BOX_ROWS, LANES),
        other.reshape(PEERS * BOX_ROWS, LANES),
        codes,
    )
    pair_sum = (keep + swap_cores(give)).reshape(PEERS, 1, SHARD_ROWS * LANES)
    parts = exchange(pair_sum).reshape(PEERS * SHARD_ROWS, LANES)
    shard, facts = sum_shards(parts, facts)
    facts = facts + swap_cores(facts)
    facts = jnp.broadcast_to(facts[0:1], (PEERS, LANES)).reshape(PEERS, 1, LANES)
    flat = lambda v: v.reshape(SHARD_ROWS, LANES)
    out = update_all(
        exchange(facts).reshape(PEERS, LANES),
        shard,
        flat(weights_flat),
        flat(moment_one),
        flat(moment_two),
        codes,
        code_first,
        code_second,
        code_grad,
    )
    return (
        out[0].reshape(()),
        out[1].reshape(()),
        *[v.reshape(weights_flat.shape) for v in out[2:6]],
        *out[6:],
    )


def solution(mesh):
    parts = Mesh(mesh.devices.reshape(4, 2, 16), ALL)
    return jax.shard_map(
        body,
        mesh=parts,
        in_specs=(
            P(ALL),
            P(ALL),
            P(ALL),
            P(ALL, None),
            P(ALL, None),
            P(ALL, None),
            P(None, ALL),
            P(ALL),
            P(ALL),
        ),
        out_specs=(
            P(),
            P(),
            P(ALL),
            P(ALL),
            P(ALL),
            P(ALL),
            P(ALL, None),
            P(ALL, None),
            P(ALL, None),
            P(ALL, None),
        ),
        check_vma=False,
    )
```

```python
import jax
import jax.numpy as jnp
from jax import lax
from jax.experimental import pallas as pl
from jax.experimental.pallas import tpu as pltpu
from jax.sharding import Mesh
from jax.sharding import PartitionSpec as P

LATENT = 256
HID = 512
MIDDLE = HID - LATENT - 3
STEP = 10

DELTA = 0.1
SMOOTH = 0.01
CODE_WEIGHT = 0.001
EIK_WEIGHT = 0.1
CLIP = 0.001
WEIGHT_RATE = 0.02
CODE_RATE = 0.15
BETA_ONE = 0.9
BETA_TWO = 0.999
ADAM_EPS = 1e-08
DECAY = 0.01

LANES = 128
DEVICES = 128
PEERS = 64
SHARD_ROWS = 21
BOX_ROWS = 24
SLOTS = 16
POINTS_DEV = 1024
CODE_ROWS = 256
FLAT_ROWS = DEVICES * SHARD_ROWS
BLOCK = 256
SUBS = 4
TILES = BLOCK // LANES
ALL_POINTS = POINTS_DEV * DEVICES

F32 = jnp.float32
BF16 = jnp.bfloat16
ALL = ("z", "core", "wide")


def rows_of_lanes(lead, shape):
    return lax.broadcasted_iota(jnp.int32, shape, lead)


def halves(v):
    high = v.astype(BF16)
    return high, (v - high.astype(F32)).astype(BF16)


def thirds(v):
    high = v.astype(BF16).astype(F32)
    rest = v - high
    mid = rest.astype(BF16).astype(F32)
    return high, mid, rest - mid


def mm(a, b):
    return lax.dot_general(a, b, (((1,), (0,)), ((), ())), preferred_element_type=F32)


def mm_nt(a, b):
    return lax.dot_general(a, b, (((1,), (1,)), ((), ())), preferred_element_type=F32)


def beside(*parts):
    return jnp.concatenate(parts, axis=1)


def row_sums(v):
    high, low = halves(v)
    return mm(beside(high, low), jnp.ones((2 * v.shape[1], LANES), BF16))


def picked_lanes(v, count):
    shape = (LANES, count * LANES)
    row, column = rows_of_lanes(0, shape), rows_of_lanes(1, shape)
    chosen = jnp.where(column >> 7 == row, 1.0, 0.0).astype(BF16)
    parts = beside(*[part.astype(BF16) for part in thirds(v)])
    wide = mm(parts, stacked(chosen, chosen, chosen))
    return [wide[:, i * LANES : (i + 1) * LANES] for i in range(count)]


def twice(v):
    return beside(v, v)


def total_of(v):
    return jnp.sum(jnp.sum(v, axis=0, keepdims=True), axis=1, keepdims=True)


def stacked(*parts):
    return jnp.concatenate(parts, axis=0)


def pack_kernel(
    weights_hbm,
    coords_hbm,
    distances_hbm,
    index_hbm,
    out_hbm,
    weights_ref,
    coords_ref,
    distances_ref,
    index_ref,
    staged,
    sems,
):
    pairs = [
        (index_hbm, index_ref),
        (weights_hbm, weights_ref),
        (coords_hbm, coords_ref),
        (distances_hbm, distances_ref),
    ]
    copies = [
        pltpu.make_async_copy(source, target, sems.at[i])
        for i, (source, target) in enumerate(pairs)
    ]
    for copy in copies:
        copy.start()
    copies[1].wait()
    shard = stacked(weights_ref[...], jnp.zeros((BOX_ROWS - SHARD_ROWS, LANES), F32))

    def fill(i, carry):
        for k in range(8):
            place = pl.ds(pl.multiple_of((i * 8 + k) * BOX_ROWS, 8), BOX_ROWS)
            staged[place, :] = shard
        return carry

    lax.fori_loop(0, PEERS // 8, fill, 0)
    for i in (0, 2, 3):
        copies[i].wait()
    index = index_ref[...]
    owner = lax.shift_right_logical(index, 8)
    row = lax.bitwise_and(index, CODE_ROWS - 1)
    sent = (rows_of_lanes(0, (DEVICES, POINTS_DEV)) == owner).astype(F32)
    sent_low = sent.astype(BF16)
    width = 256
    earlier = rows_of_lanes(0, (width, width)) < rows_of_lanes(1, (width, width))
    earlier = earlier.astype(F32).astype(BF16)
    ones = jnp.ones((width, width), BF16)
    ranks = [
        mm(sent_low[:, : (part + 1) * width], stacked(*([ones] * part + [earlier])))
        for part in range(POINTS_DEV // width)
    ]
    placed = jnp.sum(sent * beside(*ranks), axis=0, keepdims=True).astype(jnp.int32)
    at_slot = rows_of_lanes(0, (SLOTS, POINTS_DEV)) == placed
    values = [coords_ref[i : i + 1, :] for i in range(3)]
    values += [distances_ref[...], (row + 1).astype(F32)]
    pieces = [[], [], []]
    for value in values:
        for k, third in enumerate(thirds(value)):
            pieces[k].append(jnp.where(at_slot, third, 0.0))
    spare = jnp.zeros((LANES - SLOTS * len(values), POINTS_DEV), F32)
    boxes = mm_nt(
        beside(sent_low, sent_low, sent_low),
        beside(*[stacked(*piece, spare).astype(BF16) for piece in pieces]),
    )
    for z in range(4):
        for core in range(2):
            place = pl.ds(z * 16 * BOX_ROWS + SHARD_ROWS + core, 16, stride=BOX_ROWS)
            first = z * 32 + core * 16
            staged[place, :] = boxes[first : first + 16, :]
    out = pltpu.make_async_copy(staged, out_hbm, sems.at[4])
    out.start()
    out.wait()


def unit_groups(count, stride_rows, extra, first_entry):
    for group in range(count):
        entry = first_entry + group * 8 * (stride_rows * LANES + extra)
        yield group, entry // LANES, entry % LANES


def unpack_units(flat_ref, out_ref, count, stride_rows, extra, first_entry):
    lane = rows_of_lanes(1, (8, LANES))
    slope = rows_of_lanes(0, (8, LANES)) * extra
    for group, first, shift in unit_groups(count, stride_rows, extra, first_entry):
        start = slope + shift
        wraps = shift + 7 * extra >= LANES
        turn = lax.bitwise_and(lane + start, LANES - 1)
        tiles = []
        for a in range(stride_rows + 2 + wraps):
            tile = flat_ref[pl.ds(first + a, 8, stride=stride_rows), :]
            tiles.append(jnp.take_along_axis(tile, turn, axis=1, mode="promise_in_bounds"))
        for c in range(stride_rows + 1):
            value = jnp.where(lane + start < LANES, tiles[c], tiles[c + 1])
            if wraps:
                value = jnp.where(lane + start < 2 * LANES, value, tiles[c + 2])
            out_ref[group * 8 : group * 8 + 8, c * LANES : (c + 1) * LANES] = value


def pack_units(value_ref, heads_ref, tails_ref, count, stride_rows, extra, first_entry):
    lane = rows_of_lanes(1, (8, LANES))
    slope = rows_of_lanes(0, (8, LANES)) * extra
    zero = jnp.zeros((8, LANES), F32)
    for group, first, shift in unit_groups(count, stride_rows, extra, first_entry):
        start = slope + shift
        wraps = shift + 7 * extra >= LANES
        turn = lax.bitwise_and(lane - start, LANES - 1)
        tiles = [zero, zero]
        for c in range(stride_rows + 1):
            value = value_ref[group * 8 : group * 8 + 8, c * LANES : (c + 1) * LANES]
            tiles.append(jnp.take_along_axis(value, turn, axis=1, mode="promise_in_bounds"))
        tiles.append(zero)
        for a in range(stride_rows + 2):
            value = jnp.where(lane >= start, tiles[a + 2], tiles[a + 1])
            if wraps:
                value = jnp.where(lane >= start - LANES, value, tiles[a])
            target = heads_ref if a < stride_rows else tails_ref
            target[pl.ds(first + a, 8, stride=stride_rows), :] = value


def clear(ref, rows):
    def step(i, carry):
        place = pl.ds(pl.multiple_of(i * rows, 8), rows)
        ref[place, :] = jnp.zeros((rows, ref.shape[1]), F32)
        return carry

    lax.fori_loop(0, ref.shape[0] // rows, step, 0)


FIRST_UNITS = (32, 2, 5, 0)
SECOND_UNITS = (64, 4, 3, MIDDLE * (LATENT + 5))
HEAD_ENTRY = MIDDLE * (LATENT + 5) + HID * (HID + 3)


def across(column):
    return beside(*[column] * TILES)


def folded(v):
    return sum(v[:, i * LANES : (i + 1) * LANES] for i in range(TILES))


def silu_parts(half):
    gate = jnp.tanh(half)
    low = 0.5 * gate
    bend = 0.5 - gate * low
    bent = half * gate
    return half + bent, (0.5 + low) + half * bend, bend * (1.0 - bent)


def silu_parts_twice(half):
    gate = jnp.tanh(half)
    bend = 1.0 - gate * gate
    bent = half * gate
    return half + bent, (1.0 + gate) + half * bend, bend * (1.0 - bent)


def loop_kernel(
    core_ref,
    mine_ref,
    other_ref,
    codes_ref,
    first_w,
    second_w,
    latent_w,
    roots,
    scales,
    sum_two,
    sum_codes,
    sum_coord,
    sum_head,
    sum_count,
    sum_loss,
    flat,
    table,
    lhs_two,
    lhs_back,
    coord_w,
    head_w,
    spots,
    slope_one,
    curve_one,
    back_one,
    hid_hi,
    hid_lo,
    hot,
    act_two,
    slope_two,
    curve_two,
    act_tang,
    gate_hi,
    gate_lo,
    tang_hi,
    tang_lo,
    bar_hi,
    bar_lo,
    low_hi,
    low_lo,
):
    core = core_ref[0]

    for which in range(2):

        @pl.when(core == which)
        def _(which=which):
            for d in range(DEVICES):
                z, c, w = d // 32, d // 16 % 2, d % 16
                box = (z * 16 + w) * BOX_ROWS
                source = mine_ref if c == which else other_ref
                flat[d * SHARD_ROWS : d * SHARD_ROWS + BOX_ROWS, :] = source[box : box + BOX_ROWS, :]
            rows = pl.ds(SHARD_ROWS + which, PEERS, stride=BOX_ROWS)
            spots[...] = stacked(mine_ref[rows, :], other_ref[rows, :]).T

    unpack_units(flat, first_w, *FIRST_UNITS)
    unpack_units(flat, second_w, *SECOND_UNITS)
    head_bias = flat[HEAD_ENTRY // LANES : HEAD_ENTRY // LANES + 1, :][
        :, HEAD_ENTRY % LANES : HEAD_ENTRY % LANES + 1
    ]

    lane = rows_of_lanes(1, (256, LANES))
    unit = rows_of_lanes(0, (256, LANES))
    real = unit < MIDDLE

    first_low = jnp.where(beside(real, real), first_w[:, : 2 * LANES], 0.0)
    first_end = jnp.where(real, first_w[:, 2 * LANES :], 0.0)
    first_near = jnp.where(lane < 3, first_end, 0.0)
    first_w[:, : 2 * LANES] = first_low
    first_w[:, 2 * LANES :] = first_end
    *near_columns, gain, first_bias = picked_lanes(first_end, 5)
    square = first_low * first_low
    square = square[:, :LANES] + square[:, LANES:] + first_near * first_near
    root = lax.rsqrt(row_sums(square) + 1e-12)
    scale = gain * root
    roots[0:256, :] = root
    scales[0:256, :] = scale
    latent_w[0:256, :] = first_low * twice(scale)
    for i in range(3):
        coord_w[:, i * LANES : (i + 1) * LANES] = 0.5 * near_columns[i] * scale

    second_a = second_w[:, 0:256]
    second_b = second_w[:, 256:512]
    gain, second_bias, head = picked_lanes(second_w[:, 512:640], 3)
    head_w[:, :LANES] = 0.5 * head
    head_w[:, LANES:] = head
    square = second_a * second_a + second_b * second_b
    root = lax.rsqrt(row_sums(square[:, :LANES] + square[:, LANES:]) + 1e-12)
    scale = gain * root
    roots[256:768, :] = root
    scales[256:768, :] = scale
    second_a = second_a * twice(scale)
    second_b = second_b * twice(scale)
    is_hidden = rows_of_lanes(1, (HID, 256)) < MIDDLE
    hidden_cols = jnp.where(is_hidden, second_a, second_b)
    latent_cols = pltpu.roll(jnp.where(is_hidden, second_b, second_a), 3, 1)
    latent_w[256:768, :] = latent_cols

    hidden_hi, hidden_lo = halves(0.5 * hidden_cols)
    lhs_two[:, 0:256] = hidden_hi
    lhs_two[:, 256:512] = hidden_hi
    lhs_two[:, 512:768] = hidden_lo
    back_hi, back_lo = halves(hidden_cols.T)
    lhs_back[:, 0:512] = back_hi
    lhs_back[:, 512:1024] = back_hi
    lhs_back[:, 1024:1536] = back_lo

    code_hi, code_lo = halves(codes_ref[...])
    weight_hi, weight_lo = halves(latent_w[...])
    by_code = mm_nt(
        beside(weight_hi, weight_hi, weight_lo), beside(code_hi, code_lo, code_hi)
    )
    table[0:256, :] = 0.5 * (by_code[0:256, :] + twice(first_bias))
    table[256:768, :] = 0.5 * (by_code[256:768, :] + twice(second_bias))

    for ref in (sum_two, sum_codes, sum_coord, sum_head):
        clear(ref, 64)
    sum_count[...] = jnp.zeros(sum_count.shape, F32)
    sum_loss[...] = jnp.zeros(sum_loss.shape, F32)

    def feature(which, step, sub):
        first = which * SLOTS + (step * SUBS + sub) * TILES
        return beside(*[spots[pl.ds(first + i, 1), :] for i in range(TILES)])

    blank5 = jnp.zeros((5, BLOCK), F32)
    chunk = 8192 // BLOCK
    low_chunks = range(0, 256, chunk)
    high_chunks = range(0, HID, chunk)

    def block_stages(step, s):
        place = [feature(i, step, s) for i in range(3)]
        target = feature(3, step, s)
        code_row = feature(4, step, s)
        valid = (code_row > 0.5).astype(F32)

        code = jnp.broadcast_to(jnp.maximum(code_row - 1.0, 0.0).astype(jnp.int32), (chunk, BLOCK))
        upper = code >= LANES
        code = lax.bitwise_and(code, LANES - 1)

        def picked(first):
            rows = slice(first, first + chunk)
            tiles = []
            for i in range(TILES):
                part = slice(i * LANES, (i + 1) * LANES)
                both = [
                    jnp.take_along_axis(
                        table[rows, c : c + LANES], code[:, part], axis=1, mode="promise_in_bounds"
                    )
                    for c in (0, LANES)
                ]
                tiles.append(jnp.where(upper[:, part], both[1], both[0]))
            return beside(*tiles)

        last = stacked(blank5, *place)
        for r in low_chunks:
            pre = picked(r)
            for i in range(3):
                pre = pre + across(coord_w[r : r + chunk, i * LANES : (i + 1) * LANES]) * place[i]
            value, slope, curve = silu_parts(pre)
            if r + chunk == 256:
                inside = rows_of_lanes(0, (chunk, BLOCK)) + r < MIDDLE
                end = jnp.where(inside[chunk - 8 :], value[chunk - 8 :], last)
                value = stacked(value[: chunk - 8], end)
                slope = jnp.where(inside, slope, 0.0)
                curve = jnp.where(inside, curve, 0.0)
            high, low = halves(value)
            hid_hi[s, r : r + chunk, :] = high
            hid_lo[s, r : r + chunk, :] = low
            slope_one[s, r : r + chunk, :] = slope
            curve_one[s, r : r + chunk, :] = curve
        yield

        act_two[s] = mm(lhs_two[...], stacked(hid_hi[s], hid_lo[s], hid_hi[s]))
        yield
        total = jnp.zeros((8, BLOCK), F32)
        for r in high_chunks:
            value, slope, curve = silu_parts_twice(act_two[s, r : r + chunk, :] + picked(256 + r))
            head = across(head_w[r : r + chunk, :LANES])
            weighed = head * value
            for k in range(0, chunk, 8):
                total = total + weighed[k : k + 8, :]
            high, low = halves(head * slope)
            gate_hi[s, r : r + chunk, :] = high
            gate_lo[s, r : r + chunk, :] = low
            act_two[s, r : r + chunk, :] = value
            slope_two[s, r : r + chunk, :] = slope
            curve_two[s, r : r + chunk, :] = curve
        summed = jnp.sum(total, axis=0, keepdims=True)
        yield

        back_one[s] = mm(lhs_back[...], stacked(gate_hi[s], gate_lo[s], gate_hi[s]))
        yield
        totals = [jnp.zeros((8, BLOCK), F32) for _ in range(3)]
        for r in low_chunks:
            grad = back_one[s, r : r + chunk, :] * slope_one[s, r : r + chunk, :]
            for i in range(3):
                weighed = across(coord_w[r : r + chunk, i * LANES : (i + 1) * LANES]) * grad
                for k in range(0, chunk, 8):
                    totals[i] = totals[i] + weighed[k : k + 8, :]
        lead = [
            2.0 * jnp.sum(totals[i], axis=0, keepdims=True)
            + back_one[s, MIDDLE + i : MIDDLE + i + 1, :]
            for i in range(3)
        ]

        predicted = jnp.tanh(2.0 * summed + head_bias)
        flank = 1.0 - predicted * predicted
        slope = [flank * q for q in lead]
        excess = slope[0] * slope[0] + slope[1] * slope[1] + slope[2] * slope[2] - 1.0
        capped = jnp.tanh(predicted / DELTA)
        misfit = DELTA * capped - DELTA * jnp.tanh(target / DELTA)
        fitting = jnp.sqrt(misfit * misfit + SMOOTH * SMOOTH)
        sum_loss[0:1, :] += valid * (fitting + EIK_WEIGHT * excess * excess)
        share = valid * (1.0 / ALL_POINTS)
        pull = [(4.0 * EIK_WEIGHT) * excess * v for v in slope]
        by_flank = sum(p * q for p, q in zip(pull, lead))
        by_predicted = misfit / fitting * (1.0 - capped * capped) - 2.0 * predicted * by_flank
        bar_out = share * by_predicted * flank
        sum_loss[1:2, :] += bar_out
        half_bar = 0.5 * bar_out
        pull = [share * flank * p for p in pull]

        last = stacked(blank5, *pull)
        twice = [2.0 * p for p in pull]
        for r in low_chunks:
            grad = 0.0
            for i in range(3):
                grad = grad + across(coord_w[r : r + chunk, i * LANES : (i + 1) * LANES]) * twice[i]
            slope = slope_one[s, r : r + chunk, :]
            back = back_one[s, r : r + chunk, :]
            near = back * slope
            for i in range(3):
                sum_coord[r : r + chunk, i * LANES : (i + 1) * LANES] += folded(near * pull[i])
            through = grad * slope
            if r + chunk == 256:
                inside = rows_of_lanes(0, (8, BLOCK)) < MIDDLE - 248
                end = jnp.where(inside, through[chunk - 8 :], last)
                through = stacked(through[: chunk - 8], end)
            high, low = halves(through)
            tang_hi[s, r : r + chunk, :] = high
            tang_lo[s, r : r + chunk, :] = low
            curve_one[s, r : r + chunk, :] = (
                grad * back * curve_one[s, r : r + chunk, :]
            )
        yield
        act_tang[s] = mm(lhs_two[...], stacked(tang_hi[s], tang_lo[s], tang_hi[s]))

        for c in range(0, CODE_ROWS, LANES):
            code = (rows_of_lanes(1, (LANES, LANES)) + c).astype(F32)
            seen = jnp.zeros((8, LANES), F32)
            for i in range(TILES):
                wanted = code_row[:, i * LANES : (i + 1) * LANES] - 1.0
                mark = jnp.where(code == jnp.broadcast_to(wanted, (LANES, LANES)).T, 1.0, 0.0)
                hot[s, i * LANES : (i + 1) * LANES, c : c + LANES] = mark.astype(BF16)
                for k in range(0, LANES, 8):
                    seen = seen + mark[k : k + 8, :]
            sum_count[:, c : c + LANES] += seen
        yield
        for r in high_chunks:
            tangent = act_tang[s, r : r + chunk, :]
            slope = slope_two[s, r : r + chunk, :]
            head = across(head_w[r : r + chunk, LANES:])
            bar = head * (half_bar * slope + tangent * curve_two[s, r : r + chunk, :])
            by_head = act_two[s, r : r + chunk, :] * bar_out + slope * tangent
            sum_head[r : r + chunk, :] += folded(by_head)
            high, low = halves(bar)
            bar_hi[s, r : r + chunk, :] = high
            bar_lo[s, r : r + chunk, :] = low
        yield

        back_one[s] = mm(lhs_back[...], stacked(bar_hi[s], bar_lo[s], bar_hi[s]))
        yield
        for r in low_chunks:
            bar = (
                back_one[s, r : r + chunk, :] * slope_one[s, r : r + chunk, :]
                + curve_one[s, r : r + chunk, :]
            )
            for i in range(3):
                sum_coord[r : r + chunk, i * LANES : (i + 1) * LANES] += folded(bar * place[i])
            high, low = halves(bar)
            low_hi[s, r : r + chunk, :] = high
            low_lo[s, r : r + chunk, :] = low
        yield

        sum_two[...] += mm_nt(
            beside(bar_hi[s], bar_hi[s], bar_lo[s], gate_hi[s], gate_hi[s], gate_lo[s]),
            beside(hid_hi[s], hid_lo[s], hid_hi[s], tang_hi[s], tang_lo[s], tang_hi[s]),
        )
        marks = stacked(hot[s], hot[s])
        sum_codes[256:768, :] += mm(beside(bar_hi[s], bar_lo[s]), marks)
        sum_codes[0:256, :] += mm(beside(low_hi[s], low_lo[s]), marks)

    def step_body(step, carry):
        waiting = [block_stages(step, s) for s in range(SUBS)]
        active = []
        while waiting or active:
            if waiting:
                active.append(waiting.pop(0))
            active = [work for work in active if next(work, work) is not work]
        return carry

    steps = SLOTS * DEVICES // (SUBS * BLOCK)
    if steps == 1:
        step_body(0, 0)
    else:
        lax.fori_loop(0, steps, step_body, 0)


def code_kernel(codes_ref, latent_w, sum_codes, sum_count, sum_loss, code_grad_ref, facts_ref):
    codes = codes_ref[...]
    count = jnp.sum(sum_count[...], axis=0, keepdims=True)
    count = twice(jnp.broadcast_to(count, (LANES, CODE_ROWS)).T)
    turned_hi, turned_lo = halves(sum_codes[...].T)
    weight_hi, weight_lo = halves(latent_w[...])
    code_grad = mm(
        beside(turned_hi, turned_hi, turned_lo), stacked(weight_hi, weight_lo, weight_hi)
    )
    code_grad = code_grad + (2.0 * CODE_WEIGHT / ALL_POINTS) * count * codes
    code_grad_ref[...] = code_grad
    loss = jnp.sum(sum_loss[0:1, :], axis=1, keepdims=True)
    loss = (loss + CODE_WEIGHT * total_of(count * codes * codes)) / ALL_POINTS
    left = rows_of_lanes(1, facts_ref.shape) < LANES // 2
    facts_ref[...] = jnp.where(left, total_of(code_grad * code_grad), loss)


def weight_kernel(
    core_ref,
    codes_ref,
    first_w,
    second_w,
    roots,
    scales,
    sum_two,
    sum_codes,
    sum_coord,
    sum_head,
    _,
    sum_loss,
    keep_ref,
    give_ref,
    flat,
    tails,
    first_grad,
    second_grad,
):
    core = core_ref[0]
    codes = codes_ref[...]
    by_code = sum_codes[...]
    code_hi, code_lo = halves(codes)
    by_hi, by_lo = halves(by_code)
    latent_grad = mm(beside(by_hi, by_hi, by_lo), stacked(code_hi, code_lo, code_hi))

    bias_grad = row_sums(by_code[:, :LANES] + by_code[:, LANES:])
    lane = rows_of_lanes(1, (256, LANES))
    real = rows_of_lanes(0, (256, LANES)) < MIDDLE
    near_grad = 0.0
    for i in range(3):
        column = row_sums(sum_coord[:, i * LANES : (i + 1) * LANES])
        near_grad = jnp.where(lane == i, column, near_grad)
    low_grad = latent_grad[0:256, :]
    first_low = first_w[:, : 2 * LANES]
    first_near = jnp.where(lane < 3, first_w[:, 2 * LANES :], 0.0)
    root, scale = roots[0:256, :], scales[0:256, :]
    product = first_low * low_grad
    product = product[:, :LANES] + product[:, LANES:] + first_near * near_grad
    along = row_sums(product)
    inward = scale * root * root * along
    end = scale * near_grad - first_near * inward
    end = jnp.where(lane == 3, root * along, end)
    end = jnp.where(lane == 4, bias_grad[0:256, :], end)
    low_grad = twice(scale) * low_grad - first_low * twice(inward)
    first_grad[:, : 2 * LANES] = jnp.where(beside(real, real), low_grad, 0.0)
    first_grad[:, 2 * LANES :] = jnp.where(real, end, 0.0)

    is_hidden = rows_of_lanes(1, (HID, 256)) < MIDDLE
    hidden_grad = sum_two[...]
    moved = pltpu.roll(latent_grad[256:768, :], 256 - 3, 1)
    grad_a = jnp.where(is_hidden, hidden_grad, moved)
    grad_b = jnp.where(is_hidden, moved, hidden_grad)
    second_a = second_w[:, 0:256]
    second_b = second_w[:, 256:512]
    root, scale = roots[256:768, :], scales[256:768, :]
    product = second_a * grad_a + second_b * grad_b
    along = row_sums(product[:, :LANES] + product[:, LANES:])
    inward = scale * root * root * along
    second_grad[:, 0:256] = twice(scale) * grad_a - second_a * twice(inward)
    second_grad[:, 256:512] = twice(scale) * grad_b - second_b * twice(inward)
    head_grad = row_sums(sum_head[...])
    lane = rows_of_lanes(1, (HID, LANES))
    end = jnp.where(lane == 0, root * along, 0.0)
    end = jnp.where(lane == 1, bias_grad[256:768, :], end)
    second_grad[:, 512:640] = jnp.where(lane == 2, head_grad, end)

    for ref in (flat, tails):
        clear(ref, 128)
    pack_units(first_grad, flat, tails, *FIRST_UNITS)
    pack_units(second_grad, flat, tails, *SECOND_UNITS)
    row = HEAD_ENTRY // LANES
    lane = rows_of_lanes(1, (1, LANES))
    bias_total = jnp.sum(sum_loss[1:2, :], axis=1, keepdims=True)
    flat[row : row + 1, :] += jnp.where(lane == HEAD_ENTRY % LANES, bias_total, 0.0)
    size = 16 * SHARD_ROWS
    for which in range(2):

        @pl.when(core == which)
        def _(which=which):
            for z in range(4):
                for c in range(2):
                    target = keep_ref if c == which else give_ref
                    first = (z * 2 + c) * size
                    target[z * size : (z + 1) * size, :] = (
                        flat[first : first + size, :] + tails[first : first + size, :]
                    )


def vmem(count):
    return [pl.BlockSpec(memory_space=pltpu.VMEM)] * count


PARAMS = pltpu.CompilerParams(vmem_limit_bytes=48 * 1024 * 1024)


HBM = pl.BlockSpec(memory_space=pltpu.HBM)
SMEM = pl.BlockSpec(memory_space=pltpu.SMEM)


def f32(*shape):
    return jax.ShapeDtypeStruct(shape, F32)


def pack_boxes(weights, coords, distances, index):
    return pl.pallas_call(
        pack_kernel,
        out_shape=f32(PEERS * BOX_ROWS, LANES),
        in_specs=[HBM] * 4,
        out_specs=HBM,
        scratch_shapes=[
            pltpu.VMEM(weights.shape, F32),
            pltpu.VMEM(coords.shape, F32),
            pltpu.VMEM(distances.shape, F32),
            pltpu.VMEM(index.shape, jnp.int32),
            pltpu.VMEM((PEERS * BOX_ROWS, LANES), F32),
            pltpu.SemaphoreType.DMA((5,)),
        ],
        compiler_params=pltpu.CompilerParams(vmem_limit_bytes=60 * 1024 * 1024),
    )(weights, coords, distances, index)


def main_kernel(
    core_ref, mine_ref, other_ref, codes_ref, keep_ref, give_ref, code_grad_ref, facts_ref, *scratch
):
    first_w, second_w, latent_w, roots, scales, *sums = scratch[:11]
    flat = scratch[11]
    loop_kernel(core_ref, mine_ref, other_ref, codes_ref, *scratch[:-3])
    code_kernel(codes_ref, latent_w, sums[1], sums[4], sums[5], code_grad_ref, facts_ref)
    weight_kernel(core_ref, codes_ref, first_w, second_w, roots, scales, *sums, keep_ref, give_ref, flat, *scratch[-3:])


def main_call(core, mine, other, codes):
    pair = (SUBS, 256, BLOCK)
    pair_two = (SUBS, HID, BLOCK)
    scratch = [
        ((256, 3 * LANES), F32),
        ((HID, 5 * LANES), F32),
        ((768, 256), F32),
        ((768, LANES), F32),
        ((768, LANES), F32),
        ((HID, 256), F32),
        ((768, 256), F32),
        ((256, 3 * LANES), F32),
        ((HID, LANES), F32),
        ((8, CODE_ROWS), F32),
        ((2, BLOCK), F32),
        ((FLAT_ROWS + 8, LANES), F32),
        ((768, CODE_ROWS), F32),
        ((HID, 768), BF16),
        ((256, 1536), BF16),
        ((256, 3 * LANES), F32),
        ((HID, 2 * LANES), F32),
        ((LANES, LANES), F32),
        (pair, F32),
        (pair, F32),
        (pair, F32),
        (pair, BF16),
        (pair, BF16),
        ((SUBS, BLOCK, CODE_ROWS), BF16),
        (pair_two, F32),
        (pair_two, F32),
        (pair_two, F32),
        (pair_two, F32),
        (pair_two, BF16),
        (pair_two, BF16),
        (pair, BF16),
        (pair, BF16),
        (pair_two, BF16),
        (pair_two, BF16),
        (pair, BF16),
        (pair, BF16),
        ((FLAT_ROWS + 8, LANES), F32),
        ((256, 3 * LANES), F32),
        ((HID, 5 * LANES), F32),
    ]
    boxes = f32(PEERS * SHARD_ROWS, LANES)
    return pl.pallas_call(
        main_kernel,
        out_shape=(boxes, boxes, f32(CODE_ROWS, LATENT), f32(8, LANES)),
        in_specs=[SMEM] + vmem(3),
        out_specs=tuple(vmem(4)),
        scratch_shapes=[pltpu.VMEM(shape, dtype) for shape, dtype in scratch],
        compiler_params=PARAMS,
    )(core, mine, other, codes)


def adam_update(value, first, second, grad, rate):
    first_new = BETA_ONE * first + (1.0 - BETA_ONE) * grad
    second_new = BETA_TWO * second + (1.0 - BETA_TWO) * grad * grad
    first_hat = first_new / (1.0 - BETA_ONE**STEP)
    second_hat = second_new / (1.0 - BETA_TWO**STEP)
    value_new = value - rate * (first_hat / (jnp.sqrt(second_hat) + ADAM_EPS) + DECAY * value)
    return (value_new, first_new, second_new)


def shard_kernel(parts_ref, facts_ref, shard_ref, all_facts_ref):
    total = parts_ref[0:SHARD_ROWS, :]
    for peer in range(1, PEERS):
        total = total + parts_ref[peer * SHARD_ROWS : (peer + 1) * SHARD_ROWS, :]
    shard_ref[...] = total
    facts = facts_ref[...]
    left = rows_of_lanes(1, facts.shape) < LANES // 2
    all_facts_ref[...] = facts + jnp.where(left, total_of(total * total), 0.0)


def sum_shards(parts, facts):
    return pl.pallas_call(
        shard_kernel,
        out_shape=(f32(SHARD_ROWS, LANES), f32(8, LANES)),
        in_specs=vmem(2),
        out_specs=tuple(vmem(2)),
        compiler_params=PARAMS,
    )(parts, facts)


def update_kernel(
    seen_ref,
    shard_ref,
    weights_ref,
    moment_one_ref,
    moment_two_ref,
    codes_ref,
    code_first_ref,
    code_second_ref,
    code_grad_ref,
    loss_out,
    norm_out,
    weights_out,
    moment_one_out,
    moment_two_out,
    weights_copy_out,
    codes_out,
    code_first_out,
    code_second_out,
    codes_copy_out,
):
    total = jnp.sum(seen_ref[...], axis=0, keepdims=True)
    loss_out[...] = total[:, LANES // 2 : LANES // 2 + 1]
    norm = jnp.sqrt(total[:, 0:1])
    norm_out[...] = norm
    factor = jnp.minimum(1.0, CLIP / (norm + 1e-06))
    value, first, second = adam_update(
        weights_ref[...],
        moment_one_ref[...],
        moment_two_ref[...],
        factor * shard_ref[...],
        WEIGHT_RATE,
    )
    weights_out[...] = value
    moment_one_out[...] = first
    moment_two_out[...] = second
    weights_copy_out[...] = value.astype(BF16)

    def step(i, carry):
        rows = pl.ds(pl.multiple_of(i * 64, 8), 64)
        value, first, second = adam_update(
            codes_ref[rows, :],
            code_first_ref[rows, :],
            code_second_ref[rows, :],
            factor * code_grad_ref[rows, :],
            CODE_RATE,
        )
        codes_out[rows, :] = value
        code_first_out[rows, :] = first
        code_second_out[rows, :] = second
        codes_copy_out[rows, :] = value.astype(BF16)
        return carry

    lax.fori_loop(0, CODE_ROWS // 64, step, 0)


def update_all(*args):
    scalar = jax.ShapeDtypeStruct((1, 1), F32)
    shard = [jax.ShapeDtypeStruct((SHARD_ROWS, LANES), t) for t in (F32, F32, F32, BF16)]
    table = [jax.ShapeDtypeStruct((CODE_ROWS, LATENT), t) for t in (F32, F32, F32, BF16)]
    return pl.pallas_call(
        update_kernel,
        out_shape=(scalar, scalar, *shard, *table),
        in_specs=vmem(9),
        out_specs=tuple(vmem(10)),
        compiler_params=PARAMS,
    )(*args)


def swap_cores(v):
    return lax.ppermute(v, "core", [(0, 1), (1, 0)])


def exchange(v):
    return lax.all_to_all(v, ("z", "wide"), split_axis=0, concat_axis=0)


def body(
    weights_flat,
    moment_one,
    moment_two,
    codes,
    code_first,
    code_second,
    coords,
    distances,
    shape_index,
):
    boxes = pack_boxes(
        weights_flat.reshape(SHARD_ROWS, LANES),
        coords,
        distances.reshape(1, POINTS_DEV),
        shape_index.reshape(1, POINTS_DEV),
    )
    mine = exchange(boxes.reshape(PEERS, BOX_ROWS, LANES))
    other = swap_cores(mine)
    core = lax.axis_index("core").astype(jnp.int32).reshape(1)
    keep, give, code_grad, facts = main_call(
        core,
        mine.reshape(PEERS * BOX_ROWS, LANES),
        other.reshape(PEERS * BOX_ROWS, LANES),
        codes,
    )
    pair_sum = (keep + swap_cores(give)).reshape(PEERS, 1, SHARD_ROWS * LANES)
    parts = exchange(pair_sum).reshape(PEERS * SHARD_ROWS, LANES)
    shard, facts = sum_shards(parts, facts)
    facts = facts + swap_cores(facts)
    facts = jnp.broadcast_to(facts[0:1], (PEERS, LANES)).reshape(PEERS, 1, LANES)
    flat = lambda v: v.reshape(SHARD_ROWS, LANES)
    out = update_all(
        exchange(facts).reshape(PEERS, LANES),
        shard,
        flat(weights_flat),
        flat(moment_one),
        flat(moment_two),
        codes,
        code_first,
        code_second,
        code_grad,
    )
    return (
        out[0].reshape(()),
        out[1].reshape(()),
        *[v.reshape(weights_flat.shape) for v in out[2:6]],
        *out[6:],
    )


def solution(mesh):
    parts = Mesh(mesh.devices.reshape(4, 2, 16), ALL)
    return jax.shard_map(
        body,
        mesh=parts,
        in_specs=(
            P(ALL),
            P(ALL),
            P(ALL),
            P(ALL, None),
            P(ALL, None),
            P(ALL, None),
            P(None, ALL),
            P(ALL),
            P(ALL),
        ),
        out_specs=(
            P(),
            P(),
            P(ALL),
            P(ALL),
            P(ALL),
            P(ALL),
            P(ALL, None),
            P(ALL, None),
            P(ALL, None),
            P(ALL, None),
        ),
        check_vma=False,
    )
```

```python
import jax
import jax.numpy as jnp
from jax import lax
from jax.experimental import pallas as pl
from jax.experimental.pallas import tpu as pltpu
from jax.sharding import Mesh
from jax.sharding import PartitionSpec as P

LATENT = 256
HID = 512
MIDDLE = HID - LATENT - 3
STEP = 10

DELTA = 0.1
SMOOTH = 0.01
CODE_WEIGHT = 0.001
EIK_WEIGHT = 0.1
CLIP = 0.001
WEIGHT_RATE = 0.02
CODE_RATE = 0.15
BETA_ONE = 0.9
BETA_TWO = 0.999
ADAM_EPS = 1e-08
DECAY = 0.01

LANES = 128
DEVICES = 128
PEERS = 64
SHARD_ROWS = 21
BOX_ROWS = 24
SLOTS = 16
POINTS_DEV = 1024
CODE_ROWS = 256
FLAT_ROWS = DEVICES * SHARD_ROWS
BLOCK = 256
SUBS = 4
TILES = BLOCK // LANES
ALL_POINTS = POINTS_DEV * DEVICES

F32 = jnp.float32
BF16 = jnp.bfloat16
ALL = ("z", "core", "wide")


def rows_of_lanes(lead, shape):
    return lax.broadcasted_iota(jnp.int32, shape, lead)


def halves(v):
    high = v.astype(BF16)
    return high, (v - high.astype(F32)).astype(BF16)


def thirds(v):
    high = v.astype(BF16).astype(F32)
    rest = v - high
    mid = rest.astype(BF16).astype(F32)
    return high, mid, rest - mid


def mm(a, b):
    return lax.dot_general(a, b, (((1,), (0,)), ((), ())), preferred_element_type=F32)


def mm_nt(a, b):
    return lax.dot_general(a, b, (((1,), (1,)), ((), ())), preferred_element_type=F32)


def beside(*parts):
    return jnp.concatenate(parts, axis=1)


def row_sums(v):
    high, low = halves(v)
    return mm(beside(high, low), jnp.ones((2 * v.shape[1], LANES), BF16))


def picked_lanes(v, count):
    shape = (LANES, count * LANES)
    row, column = rows_of_lanes(0, shape), rows_of_lanes(1, shape)
    chosen = jnp.where(column >> 7 == row, 1.0, 0.0).astype(BF16)
    parts = beside(*[part.astype(BF16) for part in thirds(v)])
    wide = mm(parts, stacked(chosen, chosen, chosen))
    return [wide[:, i * LANES : (i + 1) * LANES] for i in range(count)]


def twice(v):
    return beside(v, v)


def total_of(v):
    return jnp.sum(jnp.sum(v, axis=0, keepdims=True), axis=1, keepdims=True)


def stacked(*parts):
    return jnp.concatenate(parts, axis=0)


def pack_kernel(weights_ref, points_ref, index_ref, out_ref):
    shard = stacked(weights_ref[...], jnp.zeros((BOX_ROWS - SHARD_ROWS, LANES), F32))

    def fill(i, carry):
        for k in range(8):
            place = pl.ds(pl.multiple_of((i * 8 + k) * BOX_ROWS, 8), BOX_ROWS)
            out_ref[place, :] = shard
        return carry

    lax.fori_loop(0, PEERS // 8, fill, 0)
    index = index_ref[...]
    owner = lax.shift_right_logical(index, 8)
    row = lax.bitwise_and(index, CODE_ROWS - 1)
    sent = (rows_of_lanes(0, (DEVICES, POINTS_DEV)) == owner).astype(F32)
    sent_low = sent.astype(BF16)
    width = 256
    earlier = rows_of_lanes(0, (width, width)) < rows_of_lanes(1, (width, width))
    earlier = earlier.astype(F32).astype(BF16)
    ones = jnp.ones((width, width), BF16)
    ranks = [
        mm(sent_low[:, : (part + 1) * width], stacked(*([ones] * part + [earlier])))
        for part in range(POINTS_DEV // width)
    ]
    placed = jnp.sum(sent * beside(*ranks), axis=0, keepdims=True).astype(jnp.int32)
    at_slot = rows_of_lanes(0, (SLOTS, POINTS_DEV)) == placed
    values = [points_ref[i : i + 1, :] for i in range(4)]
    values.append((row + 1).astype(F32))
    pieces = [[], [], []]
    for value in values:
        for k, third in enumerate(thirds(value)):
            pieces[k].append(jnp.where(at_slot, third, 0.0))
    spare = jnp.zeros((LANES - SLOTS * len(values), POINTS_DEV), F32)
    boxes = mm_nt(
        beside(sent_low, sent_low, sent_low),
        beside(*[stacked(*piece, spare).astype(BF16) for piece in pieces]),
    )
    for z in range(4):
        for core in range(2):
            place = pl.ds(z * 16 * BOX_ROWS + SHARD_ROWS + core, 16, stride=BOX_ROWS)
            first = z * 32 + core * 16
            out_ref[place, :] = boxes[first : first + 16, :]


def unit_groups(count, stride_rows, extra, first_entry):
    for group in range(count):
        entry = first_entry + group * 8 * (stride_rows * LANES + extra)
        yield group, entry // LANES, entry % LANES


def unpack_units(flat_ref, out_ref, count, stride_rows, extra, first_entry):
    lane = rows_of_lanes(1, (8, LANES))
    slope = rows_of_lanes(0, (8, LANES)) * extra
    for group, first, shift in unit_groups(count, stride_rows, extra, first_entry):
        start = slope + shift
        wraps = shift + 7 * extra >= LANES
        turn = lax.bitwise_and(lane + start, LANES - 1)
        tiles = []
        for a in range(stride_rows + 2 + wraps):
            tile = flat_ref[pl.ds(first + a, 8, stride=stride_rows), :]
            tiles.append(jnp.take_along_axis(tile, turn, axis=1, mode="promise_in_bounds"))
        for c in range(stride_rows + 1):
            value = jnp.where(lane + start < LANES, tiles[c], tiles[c + 1])
            if wraps:
                value = jnp.where(lane + start < 2 * LANES, value, tiles[c + 2])
            out_ref[group * 8 : group * 8 + 8, c * LANES : (c + 1) * LANES] = value


def pack_units(value_ref, heads_ref, tails_ref, count, stride_rows, extra, first_entry):
    lane = rows_of_lanes(1, (8, LANES))
    slope = rows_of_lanes(0, (8, LANES)) * extra
    zero = jnp.zeros((8, LANES), F32)
    for group, first, shift in unit_groups(count, stride_rows, extra, first_entry):
        start = slope + shift
        wraps = shift + 7 * extra >= LANES
        turn = lax.bitwise_and(lane - start, LANES - 1)
        tiles = [zero, zero]
        for c in range(stride_rows + 1):
            value = value_ref[group * 8 : group * 8 + 8, c * LANES : (c + 1) * LANES]
            tiles.append(jnp.take_along_axis(value, turn, axis=1, mode="promise_in_bounds"))
        tiles.append(zero)
        for a in range(stride_rows + 2):
            value = jnp.where(lane >= start, tiles[a + 2], tiles[a + 1])
            if wraps:
                value = jnp.where(lane >= start - LANES, value, tiles[a])
            target = heads_ref if a < stride_rows else tails_ref
            target[pl.ds(first + a, 8, stride=stride_rows), :] = value


def clear(ref, rows):
    def step(i, carry):
        place = pl.ds(pl.multiple_of(i * rows, 8), rows)
        ref[place, :] = jnp.zeros((rows, ref.shape[1]), F32)
        return carry

    lax.fori_loop(0, ref.shape[0] // rows, step, 0)


FIRST_UNITS = (32, 2, 5, 0)
SECOND_UNITS = (64, 4, 3, MIDDLE * (LATENT + 5))
HEAD_ENTRY = MIDDLE * (LATENT + 5) + HID * (HID + 3)


def across(column):
    return beside(*[column] * TILES)


def folded(v):
    return sum(v[:, i * LANES : (i + 1) * LANES] for i in range(TILES))


def silu_parts(half):
    gate = jnp.tanh(half)
    low = 0.5 * gate
    bend = 0.5 - gate * low
    bent = half * gate
    return half + bent, (0.5 + low) + half * bend, bend * (1.0 - bent)


def silu_parts_twice(half):
    gate = jnp.tanh(half)
    bend = 1.0 - gate * gate
    bent = half * gate
    return half + bent, (1.0 + gate) + half * bend, bend * (1.0 - bent)


def loop_kernel(
    core_ref,
    mine_ref,
    other_ref,
    codes_ref,
    first_w,
    second_w,
    latent_w,
    roots,
    scales,
    sum_two,
    sum_codes,
    sum_coord,
    sum_head,
    sum_count,
    sum_loss,
    flat,
    table,
    lhs_two,
    lhs_back,
    coord_w,
    head_w,
    spots,
    slope_one,
    curve_one,
    back_one,
    hid_hi,
    hid_lo,
    hot,
    act_two,
    slope_two,
    curve_two,
    act_tang,
    gate_hi,
    gate_lo,
    tang_hi,
    tang_lo,
    bar_hi,
    bar_lo,
    low_hi,
    low_lo,
):
    core = core_ref[0]

    for which in range(2):

        @pl.when(core == which)
        def _(which=which):
            for d in range(DEVICES):
                z, c, w = d // 32, d // 16 % 2, d % 16
                box = (z * 16 + w) * BOX_ROWS
                source = mine_ref if c == which else other_ref
                flat[d * SHARD_ROWS : d * SHARD_ROWS + BOX_ROWS, :] = source[box : box + BOX_ROWS, :]
            rows = pl.ds(SHARD_ROWS + which, PEERS, stride=BOX_ROWS)
            spots[...] = stacked(mine_ref[rows, :], other_ref[rows, :]).T

    unpack_units(flat, first_w, *FIRST_UNITS)
    unpack_units(flat, second_w, *SECOND_UNITS)
    head_bias = flat[HEAD_ENTRY // LANES : HEAD_ENTRY // LANES + 1, :][
        :, HEAD_ENTRY % LANES : HEAD_ENTRY % LANES + 1
    ]

    lane = rows_of_lanes(1, (256, LANES))
    unit = rows_of_lanes(0, (256, LANES))
    real = unit < MIDDLE

    first_low = jnp.where(beside(real, real), first_w[:, : 2 * LANES], 0.0)
    first_end = jnp.where(real, first_w[:, 2 * LANES :], 0.0)
    first_near = jnp.where(lane < 3, first_end, 0.0)
    first_w[:, : 2 * LANES] = first_low
    first_w[:, 2 * LANES :] = first_end
    *near_columns, gain, first_bias = picked_lanes(first_end, 5)
    square = first_low * first_low
    square = square[:, :LANES] + square[:, LANES:] + first_near * first_near
    root = lax.rsqrt(row_sums(square) + 1e-12)
    scale = gain * root
    roots[0:256, :] = root
    scales[0:256, :] = scale
    latent_w[0:256, :] = first_low * twice(scale)
    for i in range(3):
        coord_w[:, i * LANES : (i + 1) * LANES] = 0.5 * near_columns[i] * scale

    second_a = second_w[:, 0:256]
    second_b = second_w[:, 256:512]
    gain, second_bias, head = picked_lanes(second_w[:, 512:640], 3)
    head_w[:, :LANES] = 0.5 * head
    head_w[:, LANES:] = head
    square = second_a * second_a + second_b * second_b
    root = lax.rsqrt(row_sums(square[:, :LANES] + square[:, LANES:]) + 1e-12)
    scale = gain * root
    roots[256:768, :] = root
    scales[256:768, :] = scale
    second_a = second_a * twice(scale)
    second_b = second_b * twice(scale)
    is_hidden = rows_of_lanes(1, (HID, 256)) < MIDDLE
    hidden_cols = jnp.where(is_hidden, second_a, second_b)
    latent_cols = pltpu.roll(jnp.where(is_hidden, second_b, second_a), 3, 1)
    latent_w[256:768, :] = latent_cols

    hidden_hi, hidden_lo = halves(0.5 * hidden_cols)
    lhs_two[:, 0:256] = hidden_hi
    lhs_two[:, 256:512] = hidden_hi
    lhs_two[:, 512:768] = hidden_lo
    back_hi, back_lo = halves(hidden_cols.T)
    lhs_back[:, 0:512] = back_hi
    lhs_back[:, 512:1024] = back_hi
    lhs_back[:, 1024:1536] = back_lo

    code_hi, code_lo = halves(codes_ref[...])
    weight_hi, weight_lo = halves(latent_w[...])
    by_code = mm_nt(
        beside(weight_hi, weight_hi, weight_lo), beside(code_hi, code_lo, code_hi)
    )
    table[0:256, :] = 0.5 * (by_code[0:256, :] + twice(first_bias))
    table[256:768, :] = 0.5 * (by_code[256:768, :] + twice(second_bias))

    for ref in (sum_two, sum_codes, sum_coord, sum_head):
        clear(ref, 64)
    sum_count[...] = jnp.zeros(sum_count.shape, F32)
    sum_loss[...] = jnp.zeros(sum_loss.shape, F32)

    def feature(which, step, sub):
        first = which * SLOTS + (step * SUBS + sub) * TILES
        return beside(*[spots[pl.ds(first + i, 1), :] for i in range(TILES)])

    blank5 = jnp.zeros((5, BLOCK), F32)
    chunk = 8192 // BLOCK
    low_chunks = range(0, 256, chunk)
    high_chunks = range(0, HID, chunk)

    def block_stages(step, s):
        place = [feature(i, step, s) for i in range(3)]
        target = feature(3, step, s)
        code_row = feature(4, step, s)
        valid = (code_row > 0.5).astype(F32)

        code = jnp.broadcast_to(jnp.maximum(code_row - 1.0, 0.0).astype(jnp.int32), (chunk, BLOCK))
        upper = code >= LANES
        code = lax.bitwise_and(code, LANES - 1)

        def picked(first):
            rows = slice(first, first + chunk)
            tiles = []
            for i in range(TILES):
                part = slice(i * LANES, (i + 1) * LANES)
                both = [
                    jnp.take_along_axis(
                        table[rows, c : c + LANES], code[:, part], axis=1, mode="promise_in_bounds"
                    )
                    for c in (0, LANES)
                ]
                tiles.append(jnp.where(upper[:, part], both[1], both[0]))
            return beside(*tiles)

        last = stacked(blank5, *place)
        for r in low_chunks:
            pre = picked(r)
            for i in range(3):
                pre = pre + across(coord_w[r : r + chunk, i * LANES : (i + 1) * LANES]) * place[i]
            value, slope, curve = silu_parts(pre)
            if r + chunk == 256:
                inside = rows_of_lanes(0, (chunk, BLOCK)) + r < MIDDLE
                end = jnp.where(inside[chunk - 8 :], value[chunk - 8 :], last)
                value = stacked(value[: chunk - 8], end)
                slope = jnp.where(inside, slope, 0.0)
                curve = jnp.where(inside, curve, 0.0)
            high, low = halves(value)
            hid_hi[s, r : r + chunk, :] = high
            hid_lo[s, r : r + chunk, :] = low
            slope_one[s, r : r + chunk, :] = slope
            curve_one[s, r : r + chunk, :] = curve
        yield

        act_two[s] = mm(lhs_two[...], stacked(hid_hi[s], hid_lo[s], hid_hi[s]))
        yield
        total = jnp.zeros((8, BLOCK), F32)
        for r in high_chunks:
            value, slope, curve = silu_parts_twice(act_two[s, r : r + chunk, :] + picked(256 + r))
            head = across(head_w[r : r + chunk, :LANES])
            weighed = head * value
            for k in range(0, chunk, 8):
                total = total + weighed[k : k + 8, :]
            high, low = halves(head * slope)
            gate_hi[s, r : r + chunk, :] = high
            gate_lo[s, r : r + chunk, :] = low
            act_two[s, r : r + chunk, :] = value
            slope_two[s, r : r + chunk, :] = slope
            curve_two[s, r : r + chunk, :] = curve
        summed = jnp.sum(total, axis=0, keepdims=True)
        yield

        back_one[s] = mm(lhs_back[...], stacked(gate_hi[s], gate_lo[s], gate_hi[s]))
        yield
        totals = [jnp.zeros((8, BLOCK), F32) for _ in range(3)]
        for r in low_chunks:
            grad = back_one[s, r : r + chunk, :] * slope_one[s, r : r + chunk, :]
            for i in range(3):
                weighed = across(coord_w[r : r + chunk, i * LANES : (i + 1) * LANES]) * grad
                for k in range(0, chunk, 8):
                    totals[i] = totals[i] + weighed[k : k + 8, :]
        lead = [
            2.0 * jnp.sum(totals[i], axis=0, keepdims=True)
            + back_one[s, MIDDLE + i : MIDDLE + i + 1, :]
            for i in range(3)
        ]

        predicted = jnp.tanh(2.0 * summed + head_bias)
        flank = 1.0 - predicted * predicted
        slope = [flank * q for q in lead]
        excess = slope[0] * slope[0] + slope[1] * slope[1] + slope[2] * slope[2] - 1.0
        capped = jnp.tanh(predicted / DELTA)
        misfit = DELTA * capped - DELTA * jnp.tanh(target / DELTA)
        fitting = jnp.sqrt(misfit * misfit + SMOOTH * SMOOTH)
        sum_loss[0:1, :] += valid * (fitting + EIK_WEIGHT * excess * excess)
        share = valid * (1.0 / ALL_POINTS)
        pull = [(4.0 * EIK_WEIGHT) * excess * v for v in slope]
        by_flank = sum(p * q for p, q in zip(pull, lead))
        by_predicted = misfit / fitting * (1.0 - capped * capped) - 2.0 * predicted * by_flank
        bar_out = share * by_predicted * flank
        sum_loss[1:2, :] += bar_out
        half_bar = 0.5 * bar_out
        pull = [share * flank * p for p in pull]

        last = stacked(blank5, *pull)
        twice = [2.0 * p for p in pull]
        for r in low_chunks:
            grad = 0.0
            for i in range(3):
                grad = grad + across(coord_w[r : r + chunk, i * LANES : (i + 1) * LANES]) * twice[i]
            slope = slope_one[s, r : r + chunk, :]
            back = back_one[s, r : r + chunk, :]
            near = back * slope
            for i in range(3):
                sum_coord[r : r + chunk, i * LANES : (i + 1) * LANES] += folded(near * pull[i])
            through = grad * slope
            if r + chunk == 256:
                inside = rows_of_lanes(0, (8, BLOCK)) < MIDDLE - 248
                end = jnp.where(inside, through[chunk - 8 :], last)
                through = stacked(through[: chunk - 8], end)
            high, low = halves(through)
            tang_hi[s, r : r + chunk, :] = high
            tang_lo[s, r : r + chunk, :] = low
            curve_one[s, r : r + chunk, :] = (
                grad * back * curve_one[s, r : r + chunk, :]
            )
        yield
        act_tang[s] = mm(lhs_two[...], stacked(tang_hi[s], tang_lo[s], tang_hi[s]))

        for c in range(0, CODE_ROWS, LANES):
            code = (rows_of_lanes(1, (LANES, LANES)) + c).astype(F32)
            seen = jnp.zeros((8, LANES), F32)
            for i in range(TILES):
                wanted = code_row[:, i * LANES : (i + 1) * LANES] - 1.0
                mark = jnp.where(code == jnp.broadcast_to(wanted, (LANES, LANES)).T, 1.0, 0.0)
                hot[s, i * LANES : (i + 1) * LANES, c : c + LANES] = mark.astype(BF16)
                for k in range(0, LANES, 8):
                    seen = seen + mark[k : k + 8, :]
            sum_count[:, c : c + LANES] += seen
        yield
        for r in high_chunks:
            tangent = act_tang[s, r : r + chunk, :]
            slope = slope_two[s, r : r + chunk, :]
            head = across(head_w[r : r + chunk, LANES:])
            bar = head * (half_bar * slope + tangent * curve_two[s, r : r + chunk, :])
            by_head = act_two[s, r : r + chunk, :] * bar_out + slope * tangent
            sum_head[r : r + chunk, :] += folded(by_head)
            high, low = halves(bar)
            bar_hi[s, r : r + chunk, :] = high
            bar_lo[s, r : r + chunk, :] = low
        yield

        back_one[s] = mm(lhs_back[...], stacked(bar_hi[s], bar_lo[s], bar_hi[s]))
        yield
        for r in low_chunks:
            bar = (
                back_one[s, r : r + chunk, :] * slope_one[s, r : r + chunk, :]
                + curve_one[s, r : r + chunk, :]
            )
            for i in range(3):
                sum_coord[r : r + chunk, i * LANES : (i + 1) * LANES] += folded(bar * place[i])
            high, low = halves(bar)
            low_hi[s, r : r + chunk, :] = high
            low_lo[s, r : r + chunk, :] = low
        yield

        if s % 2 == 0:
            return
        both = (s - 1, s)
        left, right = [], []
        for k in both:
            left += [bar_hi[k], bar_hi[k], bar_lo[k], gate_hi[k], gate_hi[k], gate_lo[k]]
            right += [hid_hi[k], hid_lo[k], hid_hi[k], tang_hi[k], tang_lo[k], tang_hi[k]]
        sum_two[...] += mm_nt(beside(*left), beside(*right))
        marks = stacked(*[hot[k] for k in both for _ in range(2)])
        bars = beside(*[ref[k] for k in both for ref in (bar_hi, bar_lo)])
        sum_codes[256:768, :] += mm(bars, marks)
        bars = beside(*[ref[k] for k in both for ref in (low_hi, low_lo)])
        sum_codes[0:256, :] += mm(bars, marks)

    def step_body(step, carry):
        waiting = [block_stages(step, s) for s in range(SUBS)]
        active = []
        while waiting or active:
            if waiting:
                active.append(waiting.pop(0))
            active = [work for work in active if next(work, work) is not work]
        return carry

    steps = SLOTS * DEVICES // (SUBS * BLOCK)
    if steps == 1:
        step_body(0, 0)
    else:
        lax.fori_loop(0, steps, step_body, 0)


def code_kernel(codes_ref, latent_w, sum_codes, sum_count, sum_loss, code_grad_ref, facts_ref):
    codes = codes_ref[...]
    count = jnp.sum(sum_count[...], axis=0, keepdims=True)
    count = twice(jnp.broadcast_to(count, (LANES, CODE_ROWS)).T)
    turned_hi, turned_lo = halves(sum_codes[...].T)
    weight_hi, weight_lo = halves(latent_w[...])
    code_grad = mm(
        beside(turned_hi, turned_hi, turned_lo), stacked(weight_hi, weight_lo, weight_hi)
    )
    code_grad = code_grad + (2.0 * CODE_WEIGHT / ALL_POINTS) * count * codes
    code_grad_ref[...] = code_grad
    loss = jnp.sum(sum_loss[0:1, :], axis=1, keepdims=True)
    loss = (loss + CODE_WEIGHT * total_of(count * codes * codes)) / ALL_POINTS
    left = rows_of_lanes(1, facts_ref.shape) < LANES // 2
    facts_ref[...] = jnp.where(left, total_of(code_grad * code_grad), loss)


def weight_kernel(
    core_ref,
    codes_ref,
    first_w,
    second_w,
    roots,
    scales,
    sum_two,
    sum_codes,
    sum_coord,
    sum_head,
    _,
    sum_loss,
    keep_ref,
    give_ref,
    flat,
    tails,
    first_grad,
    second_grad,
):
    core = core_ref[0]
    codes = codes_ref[...]
    by_code = sum_codes[...]
    code_hi, code_lo = halves(codes)
    by_hi, by_lo = halves(by_code)
    latent_grad = mm(beside(by_hi, by_hi, by_lo), stacked(code_hi, code_lo, code_hi))

    bias_grad = row_sums(by_code[:, :LANES] + by_code[:, LANES:])
    lane = rows_of_lanes(1, (256, LANES))
    real = rows_of_lanes(0, (256, LANES)) < MIDDLE
    near_grad = 0.0
    for i in range(3):
        column = row_sums(sum_coord[:, i * LANES : (i + 1) * LANES])
        near_grad = jnp.where(lane == i, column, near_grad)
    low_grad = latent_grad[0:256, :]
    first_low = first_w[:, : 2 * LANES]
    first_near = jnp.where(lane < 3, first_w[:, 2 * LANES :], 0.0)
    root, scale = roots[0:256, :], scales[0:256, :]
    product = first_low * low_grad
    product = product[:, :LANES] + product[:, LANES:] + first_near * near_grad
    along = row_sums(product)
    inward = scale * root * root * along
    end = scale * near_grad - first_near * inward
    end = jnp.where(lane == 3, root * along, end)
    end = jnp.where(lane == 4, bias_grad[0:256, :], end)
    low_grad = twice(scale) * low_grad - first_low * twice(inward)
    first_grad[:, : 2 * LANES] = jnp.where(beside(real, real), low_grad, 0.0)
    first_grad[:, 2 * LANES :] = jnp.where(real, end, 0.0)

    is_hidden = rows_of_lanes(1, (HID, 256)) < MIDDLE
    hidden_grad = sum_two[...]
    moved = pltpu.roll(latent_grad[256:768, :], 256 - 3, 1)
    grad_a = jnp.where(is_hidden, hidden_grad, moved)
    grad_b = jnp.where(is_hidden, moved, hidden_grad)
    second_a = second_w[:, 0:256]
    second_b = second_w[:, 256:512]
    root, scale = roots[256:768, :], scales[256:768, :]
    product = second_a * grad_a + second_b * grad_b
    along = row_sums(product[:, :LANES] + product[:, LANES:])
    inward = scale * root * root * along
    second_grad[:, 0:256] = twice(scale) * grad_a - second_a * twice(inward)
    second_grad[:, 256:512] = twice(scale) * grad_b - second_b * twice(inward)
    head_grad = row_sums(sum_head[...])
    lane = rows_of_lanes(1, (HID, LANES))
    end = jnp.where(lane == 0, root * along, 0.0)
    end = jnp.where(lane == 1, bias_grad[256:768, :], end)
    second_grad[:, 512:640] = jnp.where(lane == 2, head_grad, end)

    for ref in (flat, tails):
        clear(ref, 128)
    pack_units(first_grad, flat, tails, *FIRST_UNITS)
    pack_units(second_grad, flat, tails, *SECOND_UNITS)
    row = HEAD_ENTRY // LANES
    lane = rows_of_lanes(1, (1, LANES))
    bias_total = jnp.sum(sum_loss[1:2, :], axis=1, keepdims=True)
    flat[row : row + 1, :] += jnp.where(lane == HEAD_ENTRY % LANES, bias_total, 0.0)
    size = 16 * SHARD_ROWS
    for which in range(2):

        @pl.when(core == which)
        def _(which=which):
            for z in range(4):
                for c in range(2):
                    target = keep_ref if c == which else give_ref
                    first = (z * 2 + c) * size
                    target[z * size : (z + 1) * size, :] = (
                        flat[first : first + size, :] + tails[first : first + size, :]
                    )


def vmem(count):
    return [pl.BlockSpec(memory_space=pltpu.VMEM)] * count


PARAMS = pltpu.CompilerParams(vmem_limit_bytes=48 * 1024 * 1024)


SMEM = pl.BlockSpec(memory_space=pltpu.SMEM)


def f32(*shape):
    return jax.ShapeDtypeStruct(shape, F32)


def pack_boxes(weights, points, index):
    return pl.pallas_call(
        pack_kernel,
        out_shape=f32(PEERS * BOX_ROWS, LANES),
        in_specs=vmem(3),
        out_specs=vmem(1)[0],
        compiler_params=PARAMS,
    )(weights, points, index)


def main_kernel(
    core_ref, mine_ref, other_ref, codes_ref, keep_ref, give_ref, code_grad_ref, facts_ref, *scratch
):
    first_w, second_w, latent_w, roots, scales, *sums = scratch[:11]
    flat = scratch[11]
    loop_kernel(core_ref, mine_ref, other_ref, codes_ref, *scratch[:-3])
    code_kernel(codes_ref, latent_w, sums[1], sums[4], sums[5], code_grad_ref, facts_ref)
    weight_kernel(core_ref, codes_ref, first_w, second_w, roots, scales, *sums, keep_ref, give_ref, flat, *scratch[-3:])


def main_call(core, mine, other, codes):
    pair = (SUBS, 256, BLOCK)
    pair_two = (SUBS, HID, BLOCK)
    scratch = [
        ((256, 3 * LANES), F32),
        ((HID, 5 * LANES), F32),
        ((768, 256), F32),
        ((768, LANES), F32),
        ((768, LANES), F32),
        ((HID, 256), F32),
        ((768, 256), F32),
        ((256, 3 * LANES), F32),
        ((HID, LANES), F32),
        ((8, CODE_ROWS), F32),
        ((2, BLOCK), F32),
        ((FLAT_ROWS + 8, LANES), F32),
        ((768, CODE_ROWS), F32),
        ((HID, 768), BF16),
        ((256, 1536), BF16),
        ((256, 3 * LANES), F32),
        ((HID, 2 * LANES), F32),
        ((LANES, LANES), F32),
        (pair, F32),
        (pair, F32),
        (pair, F32),
        (pair, BF16),
        (pair, BF16),
        ((SUBS, BLOCK, CODE_ROWS), BF16),
        (pair_two, F32),
        (pair_two, F32),
        (pair_two, F32),
        (pair_two, F32),
        (pair_two, BF16),
        (pair_two, BF16),
        (pair, BF16),
        (pair, BF16),
        (pair_two, BF16),
        (pair_two, BF16),
        (pair, BF16),
        (pair, BF16),
        ((FLAT_ROWS + 8, LANES), F32),
        ((256, 3 * LANES), F32),
        ((HID, 5 * LANES), F32),
    ]
    boxes = f32(PEERS * SHARD_ROWS, LANES)
    return pl.pallas_call(
        main_kernel,
        out_shape=(boxes, boxes, f32(CODE_ROWS, LATENT), f32(8, LANES)),
        in_specs=[SMEM] + vmem(3),
        out_specs=tuple(vmem(4)),
        scratch_shapes=[pltpu.VMEM(shape, dtype) for shape, dtype in scratch],
        compiler_params=PARAMS,
    )(core, mine, other, codes)


def adam_update(value, first, second, grad, rate):
    first_new = BETA_ONE * first + (1.0 - BETA_ONE) * grad
    second_new = BETA_TWO * second + (1.0 - BETA_TWO) * grad * grad
    first_hat = first_new / (1.0 - BETA_ONE**STEP)
    second_hat = second_new / (1.0 - BETA_TWO**STEP)
    value_new = value - rate * (first_hat / (jnp.sqrt(second_hat) + ADAM_EPS) + DECAY * value)
    return (value_new, first_new, second_new)


def shard_kernel(parts_ref, facts_ref, shard_ref, all_facts_ref):
    total = parts_ref[0:SHARD_ROWS, :]
    for peer in range(1, PEERS):
        total = total + parts_ref[peer * SHARD_ROWS : (peer + 1) * SHARD_ROWS, :]
    shard_ref[...] = total
    facts = facts_ref[...]
    left = rows_of_lanes(1, facts.shape) < LANES // 2
    all_facts_ref[...] = facts + jnp.where(left, total_of(total * total), 0.0)


def sum_shards(parts, facts):
    return pl.pallas_call(
        shard_kernel,
        out_shape=(f32(SHARD_ROWS, LANES), f32(8, LANES)),
        in_specs=vmem(2),
        out_specs=tuple(vmem(2)),
        compiler_params=PARAMS,
    )(parts, facts)


def update_kernel(
    seen_ref,
    shard_ref,
    weights_ref,
    moment_one_ref,
    moment_two_ref,
    codes_ref,
    code_first_ref,
    code_second_ref,
    code_grad_ref,
    loss_out,
    norm_out,
    weights_out,
    moment_one_out,
    moment_two_out,
    weights_copy_out,
    codes_out,
    code_first_out,
    code_second_out,
    codes_copy_out,
):
    total = jnp.sum(seen_ref[...], axis=0, keepdims=True)
    loss_out[...] = total[:, LANES // 2 : LANES // 2 + 1]
    norm = jnp.sqrt(total[:, 0:1])
    norm_out[...] = norm
    factor = jnp.minimum(1.0, CLIP / (norm + 1e-06))
    value, first, second = adam_update(
        weights_ref[...],
        moment_one_ref[...],
        moment_two_ref[...],
        factor * shard_ref[...],
        WEIGHT_RATE,
    )
    weights_out[...] = value
    moment_one_out[...] = first
    moment_two_out[...] = second
    weights_copy_out[...] = value.astype(BF16)
    for r in range(0, CODE_ROWS, 32):
        rows = slice(r, r + 32)
        value, first, second = adam_update(
            codes_ref[rows, :],
            code_first_ref[rows, :],
            code_second_ref[rows, :],
            factor * code_grad_ref[rows, :],
            CODE_RATE,
        )
        codes_out[rows, :] = value
        code_first_out[rows, :] = first
        code_second_out[rows, :] = second
        codes_copy_out[rows, :] = value.astype(BF16)


def update_all(*args):
    scalar = jax.ShapeDtypeStruct((1, 1), F32)
    shard = [jax.ShapeDtypeStruct((SHARD_ROWS, LANES), t) for t in (F32, F32, F32, BF16)]
    table = [jax.ShapeDtypeStruct((CODE_ROWS, LATENT), t) for t in (F32, F32, F32, BF16)]
    return pl.pallas_call(
        update_kernel,
        out_shape=(scalar, scalar, *shard, *table),
        in_specs=vmem(9),
        out_specs=tuple(vmem(10)),
        compiler_params=PARAMS,
    )(*args)


def swap_cores(v):
    return lax.ppermute(v, "core", [(0, 1), (1, 0)])


def exchange(v):
    return lax.all_to_all(v, ("z", "wide"), split_axis=0, concat_axis=0)


def body(
    weights_flat,
    moment_one,
    moment_two,
    codes,
    code_first,
    code_second,
    coords,
    distances,
    shape_index,
):
    boxes = pack_boxes(
        weights_flat.reshape(SHARD_ROWS, LANES),
        jnp.concatenate([coords, distances[None]]),
        shape_index.reshape(1, POINTS_DEV),
    )
    mine = exchange(boxes.reshape(PEERS, BOX_ROWS, LANES))
    other = swap_cores(mine)
    core = lax.axis_index("core").astype(jnp.int32).reshape(1)
    keep, give, code_grad, facts = main_call(
        core,
        mine.reshape(PEERS * BOX_ROWS, LANES),
        other.reshape(PEERS * BOX_ROWS, LANES),
        codes,
    )
    pair_sum = (keep + swap_cores(give)).reshape(PEERS, 1, SHARD_ROWS * LANES)
    parts = exchange(pair_sum).reshape(PEERS * SHARD_ROWS, LANES)
    shard, facts = sum_shards(parts, facts)
    facts = facts + swap_cores(facts)
    facts = jnp.broadcast_to(facts[0:1], (PEERS, LANES)).reshape(PEERS, 1, LANES)
    flat = lambda v: v.reshape(SHARD_ROWS, LANES)
    out = update_all(
        exchange(facts).reshape(PEERS, LANES),
        shard,
        flat(weights_flat),
        flat(moment_one),
        flat(moment_two),
        codes,
        code_first,
        code_second,
        code_grad,
    )
    return (
        out[0].reshape(()),
        out[1].reshape(()),
        *[v.reshape(weights_flat.shape) for v in out[2:6]],
        *out[6:],
    )


def solution(mesh):
    parts = Mesh(mesh.devices.reshape(4, 2, 16), ALL)
    return jax.shard_map(
        body,
        mesh=parts,
        in_specs=(
            P(ALL),
            P(ALL),
            P(ALL),
            P(ALL, None),
            P(ALL, None),
            P(ALL, None),
            P(None, ALL),
            P(ALL),
            P(ALL),
        ),
        out_specs=(
            P(),
            P(),
            P(ALL),
            P(ALL),
            P(ALL),
            P(ALL),
            P(ALL, None),
            P(ALL, None),
            P(ALL, None),
            P(ALL, None),
        ),
        check_vma=False,
    )
```

```python
import jax
import jax.numpy as jnp
from jax import lax
from jax.experimental import pallas as pl
from jax.experimental.pallas import tpu as pltpu
from jax.sharding import Mesh
from jax.sharding import PartitionSpec as P

LATENT = 256
HID = 512
MIDDLE = HID - LATENT - 3
STEP = 10

DELTA = 0.1
SMOOTH = 0.01
CODE_WEIGHT = 0.001
EIK_WEIGHT = 0.1
CLIP = 0.001
WEIGHT_RATE = 0.02
CODE_RATE = 0.15
BETA_ONE = 0.9
BETA_TWO = 0.999
ADAM_EPS = 1e-08
DECAY = 0.01

LANES = 128
DEVICES = 128
PEERS = 64
SHARD_ROWS = 21
BOX_ROWS = 24
SLOTS = 16
POINTS_DEV = 1024
CODE_ROWS = 256
FLAT_ROWS = DEVICES * SHARD_ROWS
BLOCK = 256
SUBS = 4
TILES = BLOCK // LANES
ALL_POINTS = POINTS_DEV * DEVICES

F32 = jnp.float32
BF16 = jnp.bfloat16
ALL = ("z", "core", "wide")


def rows_of_lanes(lead, shape):
    return lax.broadcasted_iota(jnp.int32, shape, lead)


def halves(v):
    high = v.astype(BF16)
    return high, (v - high.astype(F32)).astype(BF16)


def thirds(v):
    high = v.astype(BF16).astype(F32)
    rest = v - high
    mid = rest.astype(BF16).astype(F32)
    return high, mid, rest - mid


def mm(a, b):
    return lax.dot_general(a, b, (((1,), (0,)), ((), ())), preferred_element_type=F32)


def mm_nt(a, b):
    return lax.dot_general(a, b, (((1,), (1,)), ((), ())), preferred_element_type=F32)


def beside(*parts):
    return jnp.concatenate(parts, axis=1)


def row_sums(v):
    high, low = halves(v)
    return mm(beside(high, low), jnp.ones((2 * v.shape[1], LANES), BF16))


def picked_lanes(v, count):
    shape = (LANES, count * LANES)
    row, column = rows_of_lanes(0, shape), rows_of_lanes(1, shape)
    chosen = jnp.where(column >> 7 == row, 1.0, 0.0).astype(BF16)
    parts = beside(*[part.astype(BF16) for part in thirds(v)])
    wide = mm(parts, stacked(chosen, chosen, chosen))
    return [wide[:, i * LANES : (i + 1) * LANES] for i in range(count)]


def twice(v):
    return beside(v, v)


def total_of(v):
    return jnp.sum(jnp.sum(v, axis=0, keepdims=True), axis=1, keepdims=True)


def stacked(*parts):
    return jnp.concatenate(parts, axis=0)


def pack_kernel(weights_ref, points_ref, index_ref, out_ref):
    shard = stacked(weights_ref[...], jnp.zeros((BOX_ROWS - SHARD_ROWS, LANES), F32))

    def fill(i, carry):
        for k in range(8):
            place = pl.ds(pl.multiple_of((i * 8 + k) * BOX_ROWS, 8), BOX_ROWS)
            out_ref[place, :] = shard
        return carry

    lax.fori_loop(0, PEERS // 8, fill, 0)
    index = index_ref[...]
    owner = lax.shift_right_logical(index, 8)
    row = lax.bitwise_and(index, CODE_ROWS - 1)
    sent = (rows_of_lanes(0, (DEVICES, POINTS_DEV)) == owner).astype(F32)
    sent_low = sent.astype(BF16)
    width = 256
    earlier = rows_of_lanes(0, (width, width)) < rows_of_lanes(1, (width, width))
    earlier = earlier.astype(F32).astype(BF16)
    ones = jnp.ones((width, width), BF16)
    ranks = [
        mm(sent_low[:, : (part + 1) * width], stacked(*([ones] * part + [earlier])))
        for part in range(POINTS_DEV // width)
    ]
    placed = jnp.sum(sent * beside(*ranks), axis=0, keepdims=True).astype(jnp.int32)
    at_slot = rows_of_lanes(0, (SLOTS, POINTS_DEV)) == placed
    values = [points_ref[i : i + 1, :] for i in range(4)]
    values.append((row + 1).astype(F32))
    pieces = [[], [], []]
    for value in values:
        for k, third in enumerate(thirds(value)):
            pieces[k].append(jnp.where(at_slot, third, 0.0))
    spare = jnp.zeros((LANES - SLOTS * len(values), POINTS_DEV), F32)
    boxes = mm_nt(
        beside(sent_low, sent_low, sent_low),
        beside(*[stacked(*piece, spare).astype(BF16) for piece in pieces]),
    )
    for z in range(4):
        for core in range(2):
            place = pl.ds(z * 16 * BOX_ROWS + SHARD_ROWS + core, 16, stride=BOX_ROWS)
            first = z * 32 + core * 16
            out_ref[place, :] = boxes[first : first + 16, :]


def unit_groups(count, stride_rows, extra, first_entry):
    for group in range(count):
        entry = first_entry + group * 8 * (stride_rows * LANES + extra)
        yield group, entry // LANES, entry % LANES


def unpack_units(flat_ref, out_ref, count, stride_rows, extra, first_entry):
    lane = rows_of_lanes(1, (8, LANES))
    slope = rows_of_lanes(0, (8, LANES)) * extra
    for group, first, shift in unit_groups(count, stride_rows, extra, first_entry):
        start = slope + shift
        wraps = shift + 7 * extra >= LANES
        turn = lax.bitwise_and(lane + start, LANES - 1)
        tiles = []
        for a in range(stride_rows + 2 + wraps):
            tile = flat_ref[pl.ds(first + a, 8, stride=stride_rows), :]
            tiles.append(jnp.take_along_axis(tile, turn, axis=1, mode="promise_in_bounds"))
        for c in range(stride_rows + 1):
            value = jnp.where(lane + start < LANES, tiles[c], tiles[c + 1])
            if wraps:
                value = jnp.where(lane + start < 2 * LANES, value, tiles[c + 2])
            out_ref[group * 8 : group * 8 + 8, c * LANES : (c + 1) * LANES] = value


def pack_units(value_ref, heads_ref, tails_ref, count, stride_rows, extra, first_entry):
    lane = rows_of_lanes(1, (8, LANES))
    slope = rows_of_lanes(0, (8, LANES)) * extra
    zero = jnp.zeros((8, LANES), F32)
    for group, first, shift in unit_groups(count, stride_rows, extra, first_entry):
        start = slope + shift
        wraps = shift + 7 * extra >= LANES
        turn = lax.bitwise_and(lane - start, LANES - 1)
        tiles = [zero, zero]
        for c in range(stride_rows + 1):
            value = value_ref[group * 8 : group * 8 + 8, c * LANES : (c + 1) * LANES]
            tiles.append(jnp.take_along_axis(value, turn, axis=1, mode="promise_in_bounds"))
        tiles.append(zero)
        for a in range(stride_rows + 2):
            value = jnp.where(lane >= start, tiles[a + 2], tiles[a + 1])
            if wraps:
                value = jnp.where(lane >= start - LANES, value, tiles[a])
            target = heads_ref if a < stride_rows else tails_ref
            target[pl.ds(first + a, 8, stride=stride_rows), :] = value


def clear(ref, rows):
    def step(i, carry):
        place = pl.ds(pl.multiple_of(i * rows, 8), rows)
        ref[place, :] = jnp.zeros((rows, ref.shape[1]), F32)
        return carry

    lax.fori_loop(0, ref.shape[0] // rows, step, 0)


FIRST_UNITS = (32, 2, 5, 0)
SECOND_UNITS = (64, 4, 3, MIDDLE * (LATENT + 5))
HEAD_ENTRY = MIDDLE * (LATENT + 5) + HID * (HID + 3)


def across(column):
    return beside(*[column] * TILES)


def folded(v):
    return sum(v[:, i * LANES : (i + 1) * LANES] for i in range(TILES))


def silu_parts(half):
    gate = jnp.tanh(half)
    low = 0.5 * gate
    bend = 0.5 - gate * low
    bent = half * gate
    return half + bent, (0.5 + low) + half * bend, bend * (1.0 - bent)


def silu_parts_twice(half):
    gate = jnp.tanh(half)
    bend = 1.0 - gate * gate
    bent = half * gate
    return half + bent, (1.0 + gate) + half * bend, bend * (1.0 - bent)


def loop_kernel(
    core_ref,
    mine_ref,
    other_ref,
    codes_ref,
    first_w,
    second_w,
    latent_w,
    roots,
    scales,
    sum_two,
    sum_codes,
    sum_coord,
    sum_head,
    sum_count,
    sum_loss,
    flat,
    table,
    lhs_two,
    lhs_back,
    coord_w,
    head_w,
    spots,
    slope_one,
    curve_one,
    back_one,
    hid_hi,
    hid_lo,
    hot,
    act_two,
    slope_two,
    curve_two,
    act_tang,
    gate_hi,
    gate_lo,
    tang_hi,
    tang_lo,
    bar_hi,
    bar_lo,
    low_hi,
    low_lo,
):
    core = core_ref[0]

    for which in range(2):

        @pl.when(core == which)
        def _(which=which):
            for d in range(DEVICES):
                z, c, w = d // 32, d // 16 % 2, d % 16
                box = (z * 16 + w) * BOX_ROWS
                source = mine_ref if c == which else other_ref
                flat[d * SHARD_ROWS : d * SHARD_ROWS + BOX_ROWS, :] = source[box : box + BOX_ROWS, :]
            rows = pl.ds(SHARD_ROWS + which, PEERS, stride=BOX_ROWS)
            spots[...] = stacked(mine_ref[rows, :], other_ref[rows, :]).T

    unpack_units(flat, first_w, *FIRST_UNITS)
    unpack_units(flat, second_w, *SECOND_UNITS)
    head_bias = flat[HEAD_ENTRY // LANES : HEAD_ENTRY // LANES + 1, :][
        :, HEAD_ENTRY % LANES : HEAD_ENTRY % LANES + 1
    ]

    lane = rows_of_lanes(1, (256, LANES))
    unit = rows_of_lanes(0, (256, LANES))
    real = unit < MIDDLE

    first_low = jnp.where(beside(real, real), first_w[:, : 2 * LANES], 0.0)
    first_end = jnp.where(real, first_w[:, 2 * LANES :], 0.0)
    first_near = jnp.where(lane < 3, first_end, 0.0)
    first_w[:, : 2 * LANES] = first_low
    first_w[:, 2 * LANES :] = first_end
    *near_columns, gain, first_bias = picked_lanes(first_end, 5)
    square = first_low * first_low
    square = square[:, :LANES] + square[:, LANES:] + first_near * first_near
    root = lax.rsqrt(row_sums(square) + 1e-12)
    scale = gain * root
    roots[0:256, :] = root
    scales[0:256, :] = scale
    latent_w[0:256, :] = first_low * twice(scale)
    for i in range(3):
        coord_w[:, i * LANES : (i + 1) * LANES] = 0.5 * near_columns[i] * scale

    second_a = second_w[:, 0:256]
    second_b = second_w[:, 256:512]
    gain, second_bias, head = picked_lanes(second_w[:, 512:640], 3)
    head_w[:, :LANES] = 0.5 * head
    head_w[:, LANES:] = head
    square = second_a * second_a + second_b * second_b
    root = lax.rsqrt(row_sums(square[:, :LANES] + square[:, LANES:]) + 1e-12)
    scale = gain * root
    roots[256:768, :] = root
    scales[256:768, :] = scale
    second_a = second_a * twice(scale)
    second_b = second_b * twice(scale)
    is_hidden = rows_of_lanes(1, (HID, 256)) < MIDDLE
    hidden_cols = jnp.where(is_hidden, second_a, second_b)
    latent_cols = pltpu.roll(jnp.where(is_hidden, second_b, second_a), 3, 1)
    latent_w[256:768, :] = latent_cols

    hidden_hi, hidden_lo = halves(0.5 * hidden_cols)
    lhs_two[:, 0:256] = hidden_hi
    lhs_two[:, 256:512] = hidden_hi
    lhs_two[:, 512:768] = hidden_lo
    back_hi, back_lo = halves(hidden_cols.T)
    lhs_back[:, 0:512] = back_hi
    lhs_back[:, 512:1024] = back_hi
    lhs_back[:, 1024:1536] = back_lo

    code_hi, code_lo = halves(codes_ref[...])
    weight_hi, weight_lo = halves(latent_w[...])
    by_code = mm_nt(
        beside(weight_hi, weight_hi, weight_lo), beside(code_hi, code_lo, code_hi)
    )
    table[0:256, :] = 0.5 * (by_code[0:256, :] + twice(first_bias))
    table[256:768, :] = 0.5 * (by_code[256:768, :] + twice(second_bias))

    for ref in (sum_two, sum_codes, sum_coord, sum_head):
        clear(ref, 64)
    sum_count[...] = jnp.zeros(sum_count.shape, F32)
    sum_loss[...] = jnp.zeros(sum_loss.shape, F32)

    def feature(which, step, sub):
        first = which * SLOTS + (step * SUBS + sub) * TILES
        return beside(*[spots[pl.ds(first + i, 1), :] for i in range(TILES)])

    blank5 = jnp.zeros((5, BLOCK), F32)
    chunk = 8192 // BLOCK
    low_chunks = range(0, 256, chunk)
    high_chunks = range(0, HID, chunk)

    def block_stages(step, s):
        place = [feature(i, step, s) for i in range(3)]
        target = feature(3, step, s)
        code_row = feature(4, step, s)
        valid = (code_row > 0.5).astype(F32)

        code = jnp.broadcast_to(jnp.maximum(code_row - 1.0, 0.0).astype(jnp.int32), (chunk, BLOCK))
        upper = code >= LANES
        code = lax.bitwise_and(code, LANES - 1)

        def picked(first):
            rows = slice(first, first + chunk)
            tiles = []
            for i in range(TILES):
                part = slice(i * LANES, (i + 1) * LANES)
                both = [
                    jnp.take_along_axis(
                        table[rows, c : c + LANES], code[:, part], axis=1, mode="promise_in_bounds"
                    )
                    for c in (0, LANES)
                ]
                tiles.append(jnp.where(upper[:, part], both[1], both[0]))
            return beside(*tiles)

        last = stacked(blank5, *place)
        for r in low_chunks:
            pre = picked(r)
            for i in range(3):
                pre = pre + across(coord_w[r : r + chunk, i * LANES : (i + 1) * LANES]) * place[i]
            value, slope, curve = silu_parts(pre)
            if r + chunk == 256:
                inside = rows_of_lanes(0, (chunk, BLOCK)) + r < MIDDLE
                end = jnp.where(inside[chunk - 8 :], value[chunk - 8 :], last)
                value = stacked(value[: chunk - 8], end)
                slope = jnp.where(inside, slope, 0.0)
                curve = jnp.where(inside, curve, 0.0)
            high, low = halves(value)
            hid_hi[s, r : r + chunk, :] = high
            hid_lo[s, r : r + chunk, :] = low
            slope_one[s, r : r + chunk, :] = slope
            curve_one[s, r : r + chunk, :] = curve
        yield

        act_two[s] = mm(lhs_two[...], stacked(hid_hi[s], hid_lo[s], hid_hi[s]))
        yield
        total = jnp.zeros((8, BLOCK), F32)
        for r in high_chunks:
            value, slope, curve = silu_parts_twice(act_two[s, r : r + chunk, :] + picked(256 + r))
            head = across(head_w[r : r + chunk, :LANES])
            weighed = head * value
            for k in range(0, chunk, 8):
                total = total + weighed[k : k + 8, :]
            high, low = halves(head * slope)
            gate_hi[s, r : r + chunk, :] = high
            gate_lo[s, r : r + chunk, :] = low
            act_two[s, r : r + chunk, :] = value
            slope_two[s, r : r + chunk, :] = slope
            curve_two[s, r : r + chunk, :] = curve
        summed = jnp.sum(total, axis=0, keepdims=True)
        yield

        back_one[s] = mm(lhs_back[...], stacked(gate_hi[s], gate_lo[s], gate_hi[s]))
        yield
        totals = [jnp.zeros((8, BLOCK), F32) for _ in range(3)]
        for r in low_chunks:
            grad = back_one[s, r : r + chunk, :] * slope_one[s, r : r + chunk, :]
            for i in range(3):
                weighed = across(coord_w[r : r + chunk, i * LANES : (i + 1) * LANES]) * grad
                for k in range(0, chunk, 8):
                    totals[i] = totals[i] + weighed[k : k + 8, :]
        lead = [
            2.0 * jnp.sum(totals[i], axis=0, keepdims=True)
            + back_one[s, MIDDLE + i : MIDDLE + i + 1, :]
            for i in range(3)
        ]

        predicted = jnp.tanh(2.0 * summed + head_bias)
        flank = 1.0 - predicted * predicted
        slope = [flank * q for q in lead]
        excess = slope[0] * slope[0] + slope[1] * slope[1] + slope[2] * slope[2] - 1.0
        capped = jnp.tanh(predicted / DELTA)
        misfit = DELTA * capped - DELTA * jnp.tanh(target / DELTA)
        fitting = jnp.sqrt(misfit * misfit + SMOOTH * SMOOTH)
        sum_loss[0:1, :] += valid * (fitting + EIK_WEIGHT * excess * excess)
        share = valid * (1.0 / ALL_POINTS)
        pull = [(4.0 * EIK_WEIGHT) * excess * v for v in slope]
        by_flank = sum(p * q for p, q in zip(pull, lead))
        by_predicted = misfit / fitting * (1.0 - capped * capped) - 2.0 * predicted * by_flank
        bar_out = share * by_predicted * flank
        sum_loss[1:2, :] += bar_out
        half_bar = 0.5 * bar_out
        pull = [share * flank * p for p in pull]

        last = stacked(blank5, *pull)
        twice = [2.0 * p for p in pull]
        for r in low_chunks:
            grad = 0.0
            for i in range(3):
                grad = grad + across(coord_w[r : r + chunk, i * LANES : (i + 1) * LANES]) * twice[i]
            slope = slope_one[s, r : r + chunk, :]
            back = back_one[s, r : r + chunk, :]
            near = back * slope
            for i in range(3):
                sum_coord[r : r + chunk, i * LANES : (i + 1) * LANES] += folded(near * pull[i])
            through = grad * slope
            if r + chunk == 256:
                inside = rows_of_lanes(0, (8, BLOCK)) < MIDDLE - 248
                end = jnp.where(inside, through[chunk - 8 :], last)
                through = stacked(through[: chunk - 8], end)
            high, low = halves(through)
            tang_hi[s, r : r + chunk, :] = high
            tang_lo[s, r : r + chunk, :] = low
            curve_one[s, r : r + chunk, :] = (
                grad * back * curve_one[s, r : r + chunk, :]
            )
        yield
        act_tang[s] = mm(lhs_two[...], stacked(tang_hi[s], tang_lo[s], tang_hi[s]))
        sum_two[...] += mm_nt(
            beside(gate_hi[s], gate_hi[s], gate_lo[s]), beside(tang_hi[s], tang_lo[s], tang_hi[s])
        )

        for c in range(0, CODE_ROWS, LANES):
            code = (rows_of_lanes(1, (LANES, LANES)) + c).astype(F32)
            seen = jnp.zeros((8, LANES), F32)
            for i in range(TILES):
                wanted = code_row[:, i * LANES : (i + 1) * LANES] - 1.0
                mark = jnp.where(code == jnp.broadcast_to(wanted, (LANES, LANES)).T, 1.0, 0.0)
                hot[s, i * LANES : (i + 1) * LANES, c : c + LANES] = mark.astype(BF16)
                for k in range(0, LANES, 8):
                    seen = seen + mark[k : k + 8, :]
            sum_count[:, c : c + LANES] += seen
        yield
        for r in high_chunks:
            tangent = act_tang[s, r : r + chunk, :]
            slope = slope_two[s, r : r + chunk, :]
            head = across(head_w[r : r + chunk, LANES:])
            bar = head * (half_bar * slope + tangent * curve_two[s, r : r + chunk, :])
            by_head = act_two[s, r : r + chunk, :] * bar_out + slope * tangent
            sum_head[r : r + chunk, :] += folded(by_head)
            high, low = halves(bar)
            bar_hi[s, r : r + chunk, :] = high
            bar_lo[s, r : r + chunk, :] = low
        yield

        back_one[s] = mm(lhs_back[...], stacked(bar_hi[s], bar_lo[s], bar_hi[s]))
        sum_two[...] += mm_nt(
            beside(bar_hi[s], bar_hi[s], bar_lo[s]), beside(hid_hi[s], hid_lo[s], hid_hi[s])
        )
        marks = stacked(hot[s], hot[s])
        sum_codes[256:768, :] += mm(beside(bar_hi[s], bar_lo[s]), marks)
        yield
        for r in low_chunks:
            bar = (
                back_one[s, r : r + chunk, :] * slope_one[s, r : r + chunk, :]
                + curve_one[s, r : r + chunk, :]
            )
            for i in range(3):
                sum_coord[r : r + chunk, i * LANES : (i + 1) * LANES] += folded(bar * place[i])
            high, low = halves(bar)
            low_hi[s, r : r + chunk, :] = high
            low_lo[s, r : r + chunk, :] = low
        yield

        sum_codes[0:256, :] += mm(beside(low_hi[s], low_lo[s]), marks)

    def step_body(step, carry):
        waiting = [block_stages(step, s) for s in range(SUBS)]
        active = []
        while waiting or active:
            if waiting:
                active.append(waiting.pop(0))
            active = [work for work in active if next(work, work) is not work]
        return carry

    steps = SLOTS * DEVICES // (SUBS * BLOCK)
    if steps == 1:
        step_body(0, 0)
    else:
        lax.fori_loop(0, steps, step_body, 0)


def code_kernel(codes_ref, latent_w, sum_codes, sum_count, sum_loss, code_grad_ref, facts_ref):
    codes = codes_ref[...]
    count = jnp.sum(sum_count[...], axis=0, keepdims=True)
    count = twice(jnp.broadcast_to(count, (LANES, CODE_ROWS)).T)
    turned_hi, turned_lo = halves(sum_codes[...].T)
    weight_hi, weight_lo = halves(latent_w[...])
    code_grad = mm(
        beside(turned_hi, turned_hi, turned_lo), stacked(weight_hi, weight_lo, weight_hi)
    )
    code_grad = code_grad + (2.0 * CODE_WEIGHT / ALL_POINTS) * count * codes
    code_grad_ref[...] = code_grad
    loss = jnp.sum(sum_loss[0:1, :], axis=1, keepdims=True)
    loss = (loss + CODE_WEIGHT * total_of(count * codes * codes)) / ALL_POINTS
    left = rows_of_lanes(1, facts_ref.shape) < LANES // 2
    facts_ref[...] = jnp.where(left, total_of(code_grad * code_grad), loss)


def weight_kernel(
    core_ref,
    codes_ref,
    first_w,
    second_w,
    roots,
    scales,
    sum_two,
    sum_codes,
    sum_coord,
    sum_head,
    _,
    sum_loss,
    keep_ref,
    give_ref,
    flat,
    tails,
    first_grad,
    second_grad,
):
    core = core_ref[0]
    codes = codes_ref[...]
    by_code = sum_codes[...]
    code_hi, code_lo = halves(codes)
    by_hi, by_lo = halves(by_code)
    latent_grad = mm(beside(by_hi, by_hi, by_lo), stacked(code_hi, code_lo, code_hi))

    bias_grad = row_sums(by_code[:, :LANES] + by_code[:, LANES:])
    lane = rows_of_lanes(1, (256, LANES))
    real = rows_of_lanes(0, (256, LANES)) < MIDDLE
    near_grad = 0.0
    for i in range(3):
        column = row_sums(sum_coord[:, i * LANES : (i + 1) * LANES])
        near_grad = jnp.where(lane == i, column, near_grad)
    low_grad = latent_grad[0:256, :]
    first_low = first_w[:, : 2 * LANES]
    first_near = jnp.where(lane < 3, first_w[:, 2 * LANES :], 0.0)
    root, scale = roots[0:256, :], scales[0:256, :]
    product = first_low * low_grad
    product = product[:, :LANES] + product[:, LANES:] + first_near * near_grad
    along = row_sums(product)
    inward = scale * root * root * along
    end = scale * near_grad - first_near * inward
    end = jnp.where(lane == 3, root * along, end)
    end = jnp.where(lane == 4, bias_grad[0:256, :], end)
    low_grad = twice(scale) * low_grad - first_low * twice(inward)
    first_grad[:, : 2 * LANES] = jnp.where(beside(real, real), low_grad, 0.0)
    first_grad[:, 2 * LANES :] = jnp.where(real, end, 0.0)

    is_hidden = rows_of_lanes(1, (HID, 256)) < MIDDLE
    hidden_grad = sum_two[...]
    moved = pltpu.roll(latent_grad[256:768, :], 256 - 3, 1)
    grad_a = jnp.where(is_hidden, hidden_grad, moved)
    grad_b = jnp.where(is_hidden, moved, hidden_grad)
    second_a = second_w[:, 0:256]
    second_b = second_w[:, 256:512]
    root, scale = roots[256:768, :], scales[256:768, :]
    product = second_a * grad_a + second_b * grad_b
    along = row_sums(product[:, :LANES] + product[:, LANES:])
    inward = scale * root * root * along
    second_grad[:, 0:256] = twice(scale) * grad_a - second_a * twice(inward)
    second_grad[:, 256:512] = twice(scale) * grad_b - second_b * twice(inward)
    head_grad = row_sums(sum_head[...])
    lane = rows_of_lanes(1, (HID, LANES))
    end = jnp.where(lane == 0, root * along, 0.0)
    end = jnp.where(lane == 1, bias_grad[256:768, :], end)
    second_grad[:, 512:640] = jnp.where(lane == 2, head_grad, end)

    for ref in (flat, tails):
        clear(ref, 128)
    pack_units(first_grad, flat, tails, *FIRST_UNITS)
    pack_units(second_grad, flat, tails, *SECOND_UNITS)
    row = HEAD_ENTRY // LANES
    lane = rows_of_lanes(1, (1, LANES))
    bias_total = jnp.sum(sum_loss[1:2, :], axis=1, keepdims=True)
    flat[row : row + 1, :] += jnp.where(lane == HEAD_ENTRY % LANES, bias_total, 0.0)
    size = 16 * SHARD_ROWS
    for which in range(2):

        @pl.when(core == which)
        def _(which=which):
            for z in range(4):
                for c in range(2):
                    target = keep_ref if c == which else give_ref
                    first = (z * 2 + c) * size
                    target[z * size : (z + 1) * size, :] = (
                        flat[first : first + size, :] + tails[first : first + size, :]
                    )


def vmem(count):
    return [pl.BlockSpec(memory_space=pltpu.VMEM)] * count


PARAMS = pltpu.CompilerParams(vmem_limit_bytes=48 * 1024 * 1024)


SMEM = pl.BlockSpec(memory_space=pltpu.SMEM)


def f32(*shape):
    return jax.ShapeDtypeStruct(shape, F32)


def pack_boxes(weights, points, index):
    return pl.pallas_call(
        pack_kernel,
        out_shape=f32(PEERS * BOX_ROWS, LANES),
        in_specs=vmem(3),
        out_specs=vmem(1)[0],
        compiler_params=PARAMS,
    )(weights, points, index)


def main_kernel(
    core_ref, mine_ref, other_ref, codes_ref, keep_ref, give_ref, code_grad_ref, facts_ref, *scratch
):
    first_w, second_w, latent_w, roots, scales, *sums = scratch[:11]
    flat = scratch[11]
    loop_kernel(core_ref, mine_ref, other_ref, codes_ref, *scratch[:-3])
    code_kernel(codes_ref, latent_w, sums[1], sums[4], sums[5], code_grad_ref, facts_ref)
    weight_kernel(core_ref, codes_ref, first_w, second_w, roots, scales, *sums, keep_ref, give_ref, flat, *scratch[-3:])


def main_call(core, mine, other, codes):
    pair = (SUBS, 256, BLOCK)
    pair_two = (SUBS, HID, BLOCK)
    scratch = [
        ((256, 3 * LANES), F32),
        ((HID, 5 * LANES), F32),
        ((768, 256), F32),
        ((768, LANES), F32),
        ((768, LANES), F32),
        ((HID, 256), F32),
        ((768, 256), F32),
        ((256, 3 * LANES), F32),
        ((HID, LANES), F32),
        ((8, CODE_ROWS), F32),
        ((2, BLOCK), F32),
        ((FLAT_ROWS + 8, LANES), F32),
        ((768, CODE_ROWS), F32),
        ((HID, 768), BF16),
        ((256, 1536), BF16),
        ((256, 3 * LANES), F32),
        ((HID, 2 * LANES), F32),
        ((LANES, LANES), F32),
        (pair, F32),
        (pair, F32),
        (pair, F32),
        (pair, BF16),
        (pair, BF16),
        ((SUBS, BLOCK, CODE_ROWS), BF16),
        (pair_two, F32),
        (pair_two, F32),
        (pair_two, F32),
        (pair_two, F32),
        (pair_two, BF16),
        (pair_two, BF16),
        (pair, BF16),
        (pair, BF16),
        (pair_two, BF16),
        (pair_two, BF16),
        (pair, BF16),
        (pair, BF16),
        ((FLAT_ROWS + 8, LANES), F32),
        ((256, 3 * LANES), F32),
        ((HID, 5 * LANES), F32),
    ]
    boxes = f32(PEERS * SHARD_ROWS, LANES)
    return pl.pallas_call(
        main_kernel,
        out_shape=(boxes, boxes, f32(CODE_ROWS, LATENT), f32(8, LANES)),
        in_specs=[SMEM] + vmem(3),
        out_specs=tuple(vmem(4)),
        scratch_shapes=[pltpu.VMEM(shape, dtype) for shape, dtype in scratch],
        compiler_params=PARAMS,
    )(core, mine, other, codes)


def adam_update(value, first, second, grad, rate):
    first_new = BETA_ONE * first + (1.0 - BETA_ONE) * grad
    second_new = BETA_TWO * second + (1.0 - BETA_TWO) * grad * grad
    first_hat = first_new / (1.0 - BETA_ONE**STEP)
    second_hat = second_new / (1.0 - BETA_TWO**STEP)
    value_new = value - rate * (first_hat / (jnp.sqrt(second_hat) + ADAM_EPS) + DECAY * value)
    return (value_new, first_new, second_new)


def shard_kernel(parts_ref, facts_ref, shard_ref, all_facts_ref):
    total = parts_ref[0:SHARD_ROWS, :]
    for peer in range(1, PEERS):
        total = total + parts_ref[peer * SHARD_ROWS : (peer + 1) * SHARD_ROWS, :]
    shard_ref[...] = total
    facts = facts_ref[...]
    left = rows_of_lanes(1, facts.shape) < LANES // 2
    all_facts_ref[...] = facts + jnp.where(left, total_of(total * total), 0.0)


def sum_shards(parts, facts):
    return pl.pallas_call(
        shard_kernel,
        out_shape=(f32(SHARD_ROWS, LANES), f32(8, LANES)),
        in_specs=vmem(2),
        out_specs=tuple(vmem(2)),
        compiler_params=PARAMS,
    )(parts, facts)


def update_kernel(
    seen_ref,
    shard_ref,
    weights_ref,
    moment_one_ref,
    moment_two_ref,
    codes_ref,
    code_first_ref,
    code_second_ref,
    code_grad_ref,
    loss_out,
    norm_out,
    weights_out,
    moment_one_out,
    moment_two_out,
    weights_copy_out,
    codes_out,
    code_first_out,
    code_second_out,
    codes_copy_out,
):
    total = jnp.sum(seen_ref[...], axis=0, keepdims=True)
    loss_out[...] = total[:, LANES // 2 : LANES // 2 + 1]
    norm = jnp.sqrt(total[:, 0:1])
    norm_out[...] = norm
    factor = jnp.minimum(1.0, CLIP / (norm + 1e-06))
    value, first, second = adam_update(
        weights_ref[...],
        moment_one_ref[...],
        moment_two_ref[...],
        factor * shard_ref[...],
        WEIGHT_RATE,
    )
    weights_out[...] = value
    moment_one_out[...] = first
    moment_two_out[...] = second
    weights_copy_out[...] = value.astype(BF16)
    for r in range(0, CODE_ROWS, 32):
        rows = slice(r, r + 32)
        value, first, second = adam_update(
            codes_ref[rows, :],
            code_first_ref[rows, :],
            code_second_ref[rows, :],
            factor * code_grad_ref[rows, :],
            CODE_RATE,
        )
        codes_out[rows, :] = value
        code_first_out[rows, :] = first
        code_second_out[rows, :] = second
        codes_copy_out[rows, :] = value.astype(BF16)


def update_all(*args):
    scalar = jax.ShapeDtypeStruct((1, 1), F32)
    shard = [jax.ShapeDtypeStruct((SHARD_ROWS, LANES), t) for t in (F32, F32, F32, BF16)]
    table = [jax.ShapeDtypeStruct((CODE_ROWS, LATENT), t) for t in (F32, F32, F32, BF16)]
    return pl.pallas_call(
        update_kernel,
        out_shape=(scalar, scalar, *shard, *table),
        in_specs=vmem(9),
        out_specs=tuple(vmem(10)),
        compiler_params=PARAMS,
    )(*args)


def swap_cores(v):
    return lax.ppermute(v, "core", [(0, 1), (1, 0)])


def exchange(v):
    return lax.all_to_all(v, ("z", "wide"), split_axis=0, concat_axis=0)


def body(
    weights_flat,
    moment_one,
    moment_two,
    codes,
    code_first,
    code_second,
    coords,
    distances,
    shape_index,
):
    boxes = pack_boxes(
        weights_flat.reshape(SHARD_ROWS, LANES),
        jnp.concatenate([coords, distances[None]]),
        shape_index.reshape(1, POINTS_DEV),
    )
    mine = exchange(boxes.reshape(PEERS, BOX_ROWS, LANES))
    other = swap_cores(mine)
    core = lax.axis_index("core").astype(jnp.int32).reshape(1)
    keep, give, code_grad, facts = main_call(
        core,
        mine.reshape(PEERS * BOX_ROWS, LANES),
        other.reshape(PEERS * BOX_ROWS, LANES),
        codes,
    )
    pair_sum = (keep + swap_cores(give)).reshape(PEERS, 1, SHARD_ROWS * LANES)
    parts = exchange(pair_sum).reshape(PEERS * SHARD_ROWS, LANES)
    shard, facts = sum_shards(parts, facts)
    facts = facts + swap_cores(facts)
    facts = jnp.broadcast_to(facts[0:1], (PEERS, LANES)).reshape(PEERS, 1, LANES)
    flat = lambda v: v.reshape(SHARD_ROWS, LANES)
    out = update_all(
        exchange(facts).reshape(PEERS, LANES),
        shard,
        flat(weights_flat),
        flat(moment_one),
        flat(moment_two),
        codes,
        code_first,
        code_second,
        code_grad,
    )
    return (
        out[0].reshape(()),
        out[1].reshape(()),
        *[v.reshape(weights_flat.shape) for v in out[2:6]],
        *out[6:],
    )


def solution(mesh):
    parts = Mesh(mesh.devices.reshape(4, 2, 16), ALL)
    return jax.shard_map(
        body,
        mesh=parts,
        in_specs=(
            P(ALL),
            P(ALL),
            P(ALL),
            P(ALL, None),
            P(ALL, None),
            P(ALL, None),
            P(None, ALL),
            P(ALL),
            P(ALL),
        ),
        out_specs=(
            P(),
            P(),
            P(ALL),
            P(ALL),
            P(ALL),
            P(ALL),
            P(ALL, None),
            P(ALL, None),
            P(ALL, None),
            P(ALL, None),
        ),
        check_vma=False,
    )
```

```python
import jax
import jax.numpy as jnp
from jax import lax
from jax.experimental import pallas as pl
from jax.experimental.pallas import tpu as pltpu
from jax.sharding import Mesh
from jax.sharding import PartitionSpec as P

LATENT = 256
HID = 512
MIDDLE = HID - LATENT - 3
STEP = 10

DELTA = 0.1
SMOOTH = 0.01
CODE_WEIGHT = 0.001
EIK_WEIGHT = 0.1
CLIP = 0.001
WEIGHT_RATE = 0.02
CODE_RATE = 0.15
BETA_ONE = 0.9
BETA_TWO = 0.999
ADAM_EPS = 1e-08
DECAY = 0.01

LANES = 128
DEVICES = 128
PEERS = 64
SHARD_ROWS = 21
BOX_ROWS = 24
SLOTS = 16
POINTS_DEV = 1024
CODE_ROWS = 256
FLAT_ROWS = DEVICES * SHARD_ROWS
BLOCK = 256
SUBS = 4
TILES = BLOCK // LANES
ALL_POINTS = POINTS_DEV * DEVICES

F32 = jnp.float32
BF16 = jnp.bfloat16
ALL = ("z", "core", "wide")


def rows_of_lanes(lead, shape):
    return lax.broadcasted_iota(jnp.int32, shape, lead)


def halves(v):
    high = v.astype(BF16)
    return high, (v - high.astype(F32)).astype(BF16)


def thirds(v):
    high = v.astype(BF16).astype(F32)
    rest = v - high
    mid = rest.astype(BF16).astype(F32)
    return high, mid, rest - mid


def mm(a, b):
    return lax.dot_general(a, b, (((1,), (0,)), ((), ())), preferred_element_type=F32)


def mm_nt(a, b):
    return lax.dot_general(a, b, (((1,), (1,)), ((), ())), preferred_element_type=F32)


def beside(*parts):
    return jnp.concatenate(parts, axis=1)


def row_sums(v):
    high, low = halves(v)
    return mm(beside(high, low), jnp.ones((2 * v.shape[1], LANES), BF16))


def picked_lanes(v, count):
    shape = (LANES, count * LANES)
    row, column = rows_of_lanes(0, shape), rows_of_lanes(1, shape)
    chosen = jnp.where(column >> 7 == row, 1.0, 0.0).astype(BF16)
    parts = beside(*[part.astype(BF16) for part in thirds(v)])
    wide = mm(parts, stacked(chosen, chosen, chosen))
    return [wide[:, i * LANES : (i + 1) * LANES] for i in range(count)]


def twice(v):
    return beside(v, v)


def total_of(v):
    return jnp.sum(jnp.sum(v, axis=0, keepdims=True), axis=1, keepdims=True)


def stacked(*parts):
    return jnp.concatenate(parts, axis=0)


def pack_kernel(weights_ref, points_ref, index_ref, out_ref):
    shard = stacked(weights_ref[...], jnp.zeros((BOX_ROWS - SHARD_ROWS, LANES), F32))

    def fill(i, carry):
        for k in range(8):
            place = pl.ds(pl.multiple_of((i * 8 + k) * BOX_ROWS, 8), BOX_ROWS)
            out_ref[place, :] = shard
        return carry

    lax.fori_loop(0, PEERS // 8, fill, 0)
    index = index_ref[...]
    owner = lax.shift_right_logical(index, 8)
    row = lax.bitwise_and(index, CODE_ROWS - 1)
    sent = (rows_of_lanes(0, (DEVICES, POINTS_DEV)) == owner).astype(F32)
    sent_low = sent.astype(BF16)
    width = 256
    earlier = rows_of_lanes(0, (width, width)) < rows_of_lanes(1, (width, width))
    earlier = earlier.astype(F32).astype(BF16)
    ones = jnp.ones((width, width), BF16)
    ranks = [
        mm(sent_low[:, : (part + 1) * width], stacked(*([ones] * part + [earlier])))
        for part in range(POINTS_DEV // width)
    ]
    placed = jnp.sum(sent * beside(*ranks), axis=0, keepdims=True).astype(jnp.int32)
    at_slot = rows_of_lanes(0, (SLOTS, POINTS_DEV)) == placed
    values = [points_ref[i : i + 1, :] for i in range(4)]
    values.append((row + 1).astype(F32))
    pieces = [[], [], []]
    for value in values:
        for k, third in enumerate(thirds(value)):
            pieces[k].append(jnp.where(at_slot, third, 0.0))
    spare = jnp.zeros((LANES - SLOTS * len(values), POINTS_DEV), F32)
    boxes = mm_nt(
        beside(sent_low, sent_low, sent_low),
        beside(*[stacked(*piece, spare).astype(BF16) for piece in pieces]),
    )
    for z in range(4):
        for core in range(2):
            place = pl.ds(z * 16 * BOX_ROWS + SHARD_ROWS + core, 16, stride=BOX_ROWS)
            first = z * 32 + core * 16
            out_ref[place, :] = boxes[first : first + 16, :]


def unit_groups(count, stride_rows, extra, first_entry):
    for group in range(count):
        entry = first_entry + group * 8 * (stride_rows * LANES + extra)
        yield group, entry // LANES, entry % LANES


def unpack_units(flat_ref, out_ref, count, stride_rows, extra, first_entry):
    lane = rows_of_lanes(1, (8, LANES))
    slope = rows_of_lanes(0, (8, LANES)) * extra
    for group, first, shift in unit_groups(count, stride_rows, extra, first_entry):
        start = slope + shift
        wraps = shift + 7 * extra >= LANES
        turn = lax.bitwise_and(lane + start, LANES - 1)
        tiles = []
        for a in range(stride_rows + 2 + wraps):
            tile = flat_ref[pl.ds(first + a, 8, stride=stride_rows), :]
            tiles.append(jnp.take_along_axis(tile, turn, axis=1, mode="promise_in_bounds"))
        for c in range(stride_rows + 1):
            value = jnp.where(lane + start < LANES, tiles[c], tiles[c + 1])
            if wraps:
                value = jnp.where(lane + start < 2 * LANES, value, tiles[c + 2])
            out_ref[group * 8 : group * 8 + 8, c * LANES : (c + 1) * LANES] = value


def pack_units(value_ref, heads_ref, tails_ref, count, stride_rows, extra, first_entry):
    lane = rows_of_lanes(1, (8, LANES))
    slope = rows_of_lanes(0, (8, LANES)) * extra
    zero = jnp.zeros((8, LANES), F32)
    for group, first, shift in unit_groups(count, stride_rows, extra, first_entry):
        start = slope + shift
        wraps = shift + 7 * extra >= LANES
        turn = lax.bitwise_and(lane - start, LANES - 1)
        tiles = [zero, zero]
        for c in range(stride_rows + 1):
            value = value_ref[group * 8 : group * 8 + 8, c * LANES : (c + 1) * LANES]
            tiles.append(jnp.take_along_axis(value, turn, axis=1, mode="promise_in_bounds"))
        tiles.append(zero)
        for a in range(stride_rows + 2):
            value = jnp.where(lane >= start, tiles[a + 2], tiles[a + 1])
            if wraps:
                value = jnp.where(lane >= start - LANES, value, tiles[a])
            target = heads_ref if a < stride_rows else tails_ref
            target[pl.ds(first + a, 8, stride=stride_rows), :] = value


def clear(ref, rows):
    def step(i, carry):
        place = pl.ds(pl.multiple_of(i * rows, 8), rows)
        ref[place, :] = jnp.zeros((rows, ref.shape[1]), F32)
        return carry

    lax.fori_loop(0, ref.shape[0] // rows, step, 0)


FIRST_UNITS = (32, 2, 5, 0)
SECOND_UNITS = (64, 4, 3, MIDDLE * (LATENT + 5))
HEAD_ENTRY = MIDDLE * (LATENT + 5) + HID * (HID + 3)


def across(column):
    return beside(*[column] * TILES)


def folded(v):
    return sum(v[:, i * LANES : (i + 1) * LANES] for i in range(TILES))


def silu_parts(half):
    gate = jnp.tanh(half)
    low = 0.5 * gate
    bend = 0.5 - gate * low
    bent = half * gate
    return half + bent, (0.5 + low) + half * bend, bend * (1.0 - bent)


def silu_parts_twice(half):
    gate = jnp.tanh(half)
    bend = 1.0 - gate * gate
    bent = half * gate
    return half + bent, (1.0 + gate) + half * bend, bend * (1.0 - bent)


def loop_kernel(
    core_ref,
    mine_ref,
    other_ref,
    codes_ref,
    first_w,
    second_w,
    latent_w,
    roots,
    scales,
    sum_two,
    sum_codes,
    sum_coord,
    sum_head,
    sum_count,
    sum_loss,
    flat,
    table,
    lhs_two,
    lhs_back,
    coord_w,
    head_w,
    spots,
    slope_one,
    curve_one,
    back_one,
    back_two,
    hid_hi,
    hid_lo,
    hot,
    act_two,
    slope_two,
    curve_two,
    act_tang,
    gate_hi,
    gate_lo,
    tang_hi,
    tang_lo,
    bar_hi,
    bar_lo,
    low_hi,
    low_lo,
):
    core = core_ref[0]

    for which in range(2):

        @pl.when(core == which)
        def _(which=which):
            for d in range(DEVICES):
                z, c, w = d // 32, d // 16 % 2, d % 16
                box = (z * 16 + w) * BOX_ROWS
                source = mine_ref if c == which else other_ref
                flat[d * SHARD_ROWS : d * SHARD_ROWS + BOX_ROWS, :] = source[box : box + BOX_ROWS, :]
            rows = pl.ds(SHARD_ROWS + which, PEERS, stride=BOX_ROWS)
            spots[...] = stacked(mine_ref[rows, :], other_ref[rows, :]).T

    unpack_units(flat, first_w, *FIRST_UNITS)
    unpack_units(flat, second_w, *SECOND_UNITS)
    head_bias = flat[HEAD_ENTRY // LANES : HEAD_ENTRY // LANES + 1, :][
        :, HEAD_ENTRY % LANES : HEAD_ENTRY % LANES + 1
    ]

    lane = rows_of_lanes(1, (256, LANES))
    unit = rows_of_lanes(0, (256, LANES))
    real = unit < MIDDLE

    first_low = jnp.where(beside(real, real), first_w[:, : 2 * LANES], 0.0)
    first_end = jnp.where(real, first_w[:, 2 * LANES :], 0.0)
    first_near = jnp.where(lane < 3, first_end, 0.0)
    first_w[:, : 2 * LANES] = first_low
    first_w[:, 2 * LANES :] = first_end
    *near_columns, gain, first_bias = picked_lanes(first_end, 5)
    square = first_low * first_low
    square = square[:, :LANES] + square[:, LANES:] + first_near * first_near
    root = lax.rsqrt(row_sums(square) + 1e-12)
    scale = gain * root
    roots[0:256, :] = root
    scales[0:256, :] = scale
    latent_w[0:256, :] = first_low * twice(scale)
    for i in range(3):
        coord_w[:, i * LANES : (i + 1) * LANES] = 0.5 * near_columns[i] * scale

    second_a = second_w[:, 0:256]
    second_b = second_w[:, 256:512]
    gain, second_bias, head = picked_lanes(second_w[:, 512:640], 3)
    head_w[:, :LANES] = 0.5 * head
    head_w[:, LANES:] = head
    square = second_a * second_a + second_b * second_b
    root = lax.rsqrt(row_sums(square[:, :LANES] + square[:, LANES:]) + 1e-12)
    scale = gain * root
    roots[256:768, :] = root
    scales[256:768, :] = scale
    second_a = second_a * twice(scale)
    second_b = second_b * twice(scale)
    is_hidden = rows_of_lanes(1, (HID, 256)) < MIDDLE
    hidden_cols = jnp.where(is_hidden, second_a, second_b)
    latent_cols = pltpu.roll(jnp.where(is_hidden, second_b, second_a), 3, 1)
    latent_w[256:768, :] = latent_cols

    hidden_hi, hidden_lo = halves(0.5 * hidden_cols)
    lhs_two[:, 0:256] = hidden_hi
    lhs_two[:, 256:512] = hidden_hi
    lhs_two[:, 512:768] = hidden_lo
    back_hi, back_lo = halves(hidden_cols.T)
    lhs_back[:, 0:512] = back_hi
    lhs_back[:, 512:1024] = back_hi
    lhs_back[:, 1024:1536] = back_lo

    code_hi, code_lo = halves(codes_ref[...])
    weight_hi, weight_lo = halves(latent_w[...])
    by_code = mm_nt(
        beside(weight_hi, weight_hi, weight_lo), beside(code_hi, code_lo, code_hi)
    )
    table[0:256, :] = 0.5 * (by_code[0:256, :] + twice(first_bias))
    table[256:768, :] = 0.5 * (by_code[256:768, :] + twice(second_bias))

    for ref in (sum_two, sum_codes, sum_coord, sum_head):
        clear(ref, 64)
    sum_count[...] = jnp.zeros(sum_count.shape, F32)
    sum_loss[...] = jnp.zeros(sum_loss.shape, F32)

    def feature(which, step, sub):
        first = which * SLOTS + (step * SUBS + sub) * TILES
        return beside(*[spots[pl.ds(first + i, 1), :] for i in range(TILES)])

    blank5 = jnp.zeros((5, BLOCK), F32)
    chunk = 8192 // BLOCK
    low_chunks = range(0, 256, chunk)
    high_chunks = range(0, HID, chunk)

    def block_stages(step, s):
        place = [feature(i, step, s) for i in range(3)]
        target = feature(3, step, s)
        code_row = feature(4, step, s)
        valid = (code_row > 0.5).astype(F32)

        code = jnp.broadcast_to(jnp.maximum(code_row - 1.0, 0.0).astype(jnp.int32), (chunk, BLOCK))
        upper = code >= LANES
        code = lax.bitwise_and(code, LANES - 1)

        def picked(first):
            rows = slice(first, first + chunk)
            tiles = []
            for i in range(TILES):
                part = slice(i * LANES, (i + 1) * LANES)
                both = [
                    jnp.take_along_axis(
                        table[rows, c : c + LANES], code[:, part], axis=1, mode="promise_in_bounds"
                    )
                    for c in (0, LANES)
                ]
                tiles.append(jnp.where(upper[:, part], both[1], both[0]))
            return beside(*tiles)

        last = stacked(blank5, *place)
        for r in low_chunks:
            pre = picked(r)
            for i in range(3):
                pre = pre + across(coord_w[r : r + chunk, i * LANES : (i + 1) * LANES]) * place[i]
            value, slope, curve = silu_parts(pre)
            if r + chunk == 256:
                inside = rows_of_lanes(0, (chunk, BLOCK)) + r < MIDDLE
                end = jnp.where(inside[chunk - 8 :], value[chunk - 8 :], last)
                value = stacked(value[: chunk - 8], end)
                slope = jnp.where(inside, slope, 0.0)
                curve = jnp.where(inside, curve, 0.0)
            high, low = halves(value)
            hid_hi[s, r : r + chunk, :] = high
            hid_lo[s, r : r + chunk, :] = low
            slope_one[s, r : r + chunk, :] = slope
            curve_one[s, r : r + chunk, :] = curve
        yield

        act_two[s] = mm(lhs_two[...], stacked(hid_hi[s], hid_lo[s], hid_hi[s]))
        yield
        total = jnp.zeros((8, BLOCK), F32)
        for r in high_chunks:
            value, slope, curve = silu_parts_twice(act_two[s, r : r + chunk, :] + picked(256 + r))
            head = across(head_w[r : r + chunk, :LANES])
            weighed = head * value
            for k in range(0, chunk, 8):
                total = total + weighed[k : k + 8, :]
            high, low = halves(head * slope)
            gate_hi[s, r : r + chunk, :] = high
            gate_lo[s, r : r + chunk, :] = low
            act_two[s, r : r + chunk, :] = value
            slope_two[s, r : r + chunk, :] = slope
            curve_two[s, r : r + chunk, :] = curve
        summed = jnp.sum(total, axis=0, keepdims=True)
        yield

        predicted = jnp.tanh(2.0 * summed + head_bias)
        flank = 1.0 - predicted * predicted
        capped = jnp.tanh(predicted / DELTA)
        misfit = DELTA * capped - DELTA * jnp.tanh(target / DELTA)
        square = misfit * misfit + SMOOTH * SMOOTH
        inverse = lax.rsqrt(square)
        fitting = square * inverse
        by_fit = misfit * inverse * (1.0 - capped * capped)
        share_flank = valid * (1.0 / ALL_POINTS) * flank

        back_one[s] = mm(lhs_back[...], stacked(gate_hi[s], gate_lo[s], gate_hi[s]))
        yield
        totals = [jnp.zeros((8, BLOCK), F32) for _ in range(3)]
        for r in low_chunks:
            grad = back_one[s, r : r + chunk, :] * slope_one[s, r : r + chunk, :]
            for i in range(3):
                weighed = across(coord_w[r : r + chunk, i * LANES : (i + 1) * LANES]) * grad
                for k in range(0, chunk, 8):
                    totals[i] = totals[i] + weighed[k : k + 8, :]
        lead = [
            2.0 * jnp.sum(totals[i], axis=0, keepdims=True)
            + back_one[s, MIDDLE + i : MIDDLE + i + 1, :]
            for i in range(3)
        ]

        slope = [flank * q for q in lead]
        excess = slope[0] * slope[0] + slope[1] * slope[1] + slope[2] * slope[2] - 1.0
        sum_loss[0:1, :] += valid * (fitting + EIK_WEIGHT * excess * excess)
        pull = [(4.0 * EIK_WEIGHT) * excess * v for v in slope]
        by_flank = sum(p * q for p, q in zip(pull, lead))
        bar_out = share_flank * (by_fit - 2.0 * predicted * by_flank)
        sum_loss[1:2, :] += bar_out
        half_bar = 0.5 * bar_out
        pull = [share_flank * p for p in pull]

        last = stacked(blank5, *pull)
        twice = [2.0 * p for p in pull]
        for r in low_chunks:
            grad = 0.0
            for i in range(3):
                grad = grad + across(coord_w[r : r + chunk, i * LANES : (i + 1) * LANES]) * twice[i]
            slope = slope_one[s, r : r + chunk, :]
            back = back_one[s, r : r + chunk, :]
            through = grad * slope
            if r + chunk == 256:
                inside = rows_of_lanes(0, (8, BLOCK)) < MIDDLE - 248
                end = jnp.where(inside, through[chunk - 8 :], last)
                through = stacked(through[: chunk - 8], end)
            high, low = halves(through)
            tang_hi[s, r : r + chunk, :] = high
            tang_lo[s, r : r + chunk, :] = low
            curve_one[s, r : r + chunk, :] = (
                grad * back * curve_one[s, r : r + chunk, :]
            )
        yield
        act_tang[s] = mm(lhs_two[...], stacked(tang_hi[s], tang_lo[s], tang_hi[s]))
        sum_two[...] += mm_nt(
            beside(gate_hi[s], gate_hi[s], gate_lo[s]), beside(tang_hi[s], tang_lo[s], tang_hi[s])
        )

        for c in range(0, CODE_ROWS, LANES):
            code = (rows_of_lanes(1, (LANES, LANES)) + c).astype(F32)
            seen = jnp.zeros((8, LANES), F32)
            for i in range(TILES):
                wanted = code_row[:, i * LANES : (i + 1) * LANES] - 1.0
                mark = jnp.where(code == jnp.broadcast_to(wanted, (LANES, LANES)).T, 1.0, 0.0)
                hot[s, i * LANES : (i + 1) * LANES, c : c + LANES] = mark.astype(BF16)
                for k in range(0, LANES, 8):
                    seen = seen + mark[k : k + 8, :]
            sum_count[:, c : c + LANES] += seen
        yield
        for r in high_chunks:
            tangent = act_tang[s, r : r + chunk, :]
            slope = slope_two[s, r : r + chunk, :]
            head = across(head_w[r : r + chunk, LANES:])
            bar = head * (half_bar * slope + tangent * curve_two[s, r : r + chunk, :])
            by_head = act_two[s, r : r + chunk, :] * bar_out + slope * tangent
            sum_head[r : r + chunk, :] += folded(by_head)
            high, low = halves(bar)
            bar_hi[s, r : r + chunk, :] = high
            bar_lo[s, r : r + chunk, :] = low
        yield

        back_two[s] = mm(lhs_back[...], stacked(bar_hi[s], bar_lo[s], bar_hi[s]))
        sum_two[...] += mm_nt(
            beside(bar_hi[s], bar_hi[s], bar_lo[s]), beside(hid_hi[s], hid_lo[s], hid_hi[s])
        )
        marks = stacked(hot[s], hot[s])
        sum_codes[256:768, :] += mm(beside(bar_hi[s], bar_lo[s]), marks)
        yield
        for r in low_chunks:
            slope = slope_one[s, r : r + chunk, :]
            bar = back_two[s, r : r + chunk, :] * slope + curve_one[s, r : r + chunk, :]
            near = back_one[s, r : r + chunk, :] * slope
            for i in range(3):
                sum_coord[r : r + chunk, i * LANES : (i + 1) * LANES] += folded(
                    bar * place[i] + near * pull[i]
                )
            high, low = halves(bar)
            low_hi[s, r : r + chunk, :] = high
            low_lo[s, r : r + chunk, :] = low
        yield

        sum_codes[0:256, :] += mm(beside(low_hi[s], low_lo[s]), marks)

    def step_body(step, carry):
        waiting = [block_stages(step, s) for s in range(SUBS)]
        active = []
        while waiting or active:
            if waiting:
                active.append(waiting.pop(0))
            active = [work for work in active if next(work, work) is not work]
        return carry

    steps = SLOTS * DEVICES // (SUBS * BLOCK)
    if steps == 1:
        step_body(0, 0)
    else:
        lax.fori_loop(0, steps, step_body, 0)


def code_kernel(codes_ref, latent_w, sum_codes, sum_count, sum_loss, code_grad_ref, facts_ref):
    codes = codes_ref[...]
    count = jnp.sum(sum_count[...], axis=0, keepdims=True)
    count = twice(jnp.broadcast_to(count, (LANES, CODE_ROWS)).T)
    turned_hi, turned_lo = halves(sum_codes[...].T)
    weight_hi, weight_lo = halves(latent_w[...])
    code_grad = mm(
        beside(turned_hi, turned_hi, turned_lo), stacked(weight_hi, weight_lo, weight_hi)
    )
    code_grad = code_grad + (2.0 * CODE_WEIGHT / ALL_POINTS) * count * codes
    code_grad_ref[...] = code_grad
    loss = jnp.sum(sum_loss[0:1, :], axis=1, keepdims=True)
    loss = (loss + CODE_WEIGHT * total_of(count * codes * codes)) / ALL_POINTS
    left = rows_of_lanes(1, facts_ref.shape) < LANES // 2
    facts_ref[...] = jnp.where(left, total_of(code_grad * code_grad), loss)


def weight_kernel(
    core_ref,
    codes_ref,
    first_w,
    second_w,
    roots,
    scales,
    sum_two,
    sum_codes,
    sum_coord,
    sum_head,
    _,
    sum_loss,
    keep_ref,
    give_ref,
    flat,
    tails,
    first_grad,
    second_grad,
):
    core = core_ref[0]
    codes = codes_ref[...]
    by_code = sum_codes[...]
    code_hi, code_lo = halves(codes)
    by_hi, by_lo = halves(by_code)
    latent_grad = mm(beside(by_hi, by_hi, by_lo), stacked(code_hi, code_lo, code_hi))

    bias_grad = row_sums(by_code[:, :LANES] + by_code[:, LANES:])
    lane = rows_of_lanes(1, (256, LANES))
    real = rows_of_lanes(0, (256, LANES)) < MIDDLE
    near_grad = 0.0
    for i in range(3):
        column = row_sums(sum_coord[:, i * LANES : (i + 1) * LANES])
        near_grad = jnp.where(lane == i, column, near_grad)
    low_grad = latent_grad[0:256, :]
    first_low = first_w[:, : 2 * LANES]
    first_near = jnp.where(lane < 3, first_w[:, 2 * LANES :], 0.0)
    root, scale = roots[0:256, :], scales[0:256, :]
    product = first_low * low_grad
    product = product[:, :LANES] + product[:, LANES:] + first_near * near_grad
    along = row_sums(product)
    inward = scale * root * root * along
    end = scale * near_grad - first_near * inward
    end = jnp.where(lane == 3, root * along, end)
    end = jnp.where(lane == 4, bias_grad[0:256, :], end)
    low_grad = twice(scale) * low_grad - first_low * twice(inward)
    first_grad[:, : 2 * LANES] = jnp.where(beside(real, real), low_grad, 0.0)
    first_grad[:, 2 * LANES :] = jnp.where(real, end, 0.0)

    is_hidden = rows_of_lanes(1, (HID, 256)) < MIDDLE
    hidden_grad = sum_two[...]
    moved = pltpu.roll(latent_grad[256:768, :], 256 - 3, 1)
    grad_a = jnp.where(is_hidden, hidden_grad, moved)
    grad_b = jnp.where(is_hidden, moved, hidden_grad)
    second_a = second_w[:, 0:256]
    second_b = second_w[:, 256:512]
    root, scale = roots[256:768, :], scales[256:768, :]
    product = second_a * grad_a + second_b * grad_b
    along = row_sums(product[:, :LANES] + product[:, LANES:])
    inward = scale * root * root * along
    second_grad[:, 0:256] = twice(scale) * grad_a - second_a * twice(inward)
    second_grad[:, 256:512] = twice(scale) * grad_b - second_b * twice(inward)
    head_grad = row_sums(sum_head[...])
    lane = rows_of_lanes(1, (HID, LANES))
    end = jnp.where(lane == 0, root * along, 0.0)
    end = jnp.where(lane == 1, bias_grad[256:768, :], end)
    second_grad[:, 512:640] = jnp.where(lane == 2, head_grad, end)

    for ref in (flat, tails):
        clear(ref, 128)
    pack_units(first_grad, flat, tails, *FIRST_UNITS)
    pack_units(second_grad, flat, tails, *SECOND_UNITS)
    row = HEAD_ENTRY // LANES
    lane = rows_of_lanes(1, (1, LANES))
    bias_total = jnp.sum(sum_loss[1:2, :], axis=1, keepdims=True)
    flat[row : row + 1, :] += jnp.where(lane == HEAD_ENTRY % LANES, bias_total, 0.0)
    size = 16 * SHARD_ROWS
    for which in range(2):

        @pl.when(core == which)
        def _(which=which):
            for z in range(4):
                for c in range(2):
                    target = keep_ref if c == which else give_ref
                    first = (z * 2 + c) * size
                    target[z * size : (z + 1) * size, :] = (
                        flat[first : first + size, :] + tails[first : first + size, :]
                    )


def vmem(count):
    return [pl.BlockSpec(memory_space=pltpu.VMEM)] * count


PARAMS = pltpu.CompilerParams(vmem_limit_bytes=48 * 1024 * 1024)


SMEM = pl.BlockSpec(memory_space=pltpu.SMEM)


def f32(*shape):
    return jax.ShapeDtypeStruct(shape, F32)


def pack_boxes(weights, points, index):
    return pl.pallas_call(
        pack_kernel,
        out_shape=f32(PEERS * BOX_ROWS, LANES),
        in_specs=vmem(3),
        out_specs=vmem(1)[0],
        compiler_params=PARAMS,
    )(weights, points, index)


def main_kernel(
    core_ref, mine_ref, other_ref, codes_ref, keep_ref, give_ref, code_grad_ref, facts_ref, *scratch
):
    first_w, second_w, latent_w, roots, scales, *sums = scratch[:11]
    flat = scratch[11]
    loop_kernel(core_ref, mine_ref, other_ref, codes_ref, *scratch[:-3])
    code_kernel(codes_ref, latent_w, sums[1], sums[4], sums[5], code_grad_ref, facts_ref)
    weight_kernel(core_ref, codes_ref, first_w, second_w, roots, scales, *sums, keep_ref, give_ref, flat, *scratch[-3:])


def main_call(core, mine, other, codes):
    pair = (SUBS, 256, BLOCK)
    pair_two = (SUBS, HID, BLOCK)
    scratch = [
        ((256, 3 * LANES), F32),
        ((HID, 5 * LANES), F32),
        ((768, 256), F32),
        ((768, LANES), F32),
        ((768, LANES), F32),
        ((HID, 256), F32),
        ((768, 256), F32),
        ((256, 3 * LANES), F32),
        ((HID, LANES), F32),
        ((8, CODE_ROWS), F32),
        ((2, BLOCK), F32),
        ((FLAT_ROWS + 8, LANES), F32),
        ((768, CODE_ROWS), F32),
        ((HID, 768), BF16),
        ((256, 1536), BF16),
        ((256, 3 * LANES), F32),
        ((HID, 2 * LANES), F32),
        ((LANES, LANES), F32),
        (pair, F32),
        (pair, F32),
        (pair, F32),
        (pair, F32),
        (pair, BF16),
        (pair, BF16),
        ((SUBS, BLOCK, CODE_ROWS), BF16),
        (pair_two, F32),
        (pair_two, F32),
        (pair_two, F32),
        (pair_two, F32),
        (pair_two, BF16),
        (pair_two, BF16),
        (pair, BF16),
        (pair, BF16),
        (pair_two, BF16),
        (pair_two, BF16),
        (pair, BF16),
        (pair, BF16),
        ((FLAT_ROWS + 8, LANES), F32),
        ((256, 3 * LANES), F32),
        ((HID, 5 * LANES), F32),
    ]
    boxes = f32(PEERS * SHARD_ROWS, LANES)
    return pl.pallas_call(
        main_kernel,
        out_shape=(boxes, boxes, f32(CODE_ROWS, LATENT), f32(8, LANES)),
        in_specs=[SMEM] + vmem(3),
        out_specs=tuple(vmem(4)),
        scratch_shapes=[pltpu.VMEM(shape, dtype) for shape, dtype in scratch],
        compiler_params=PARAMS,
    )(core, mine, other, codes)


def adam_update(value, first, second, grad, rate):
    first_new = BETA_ONE * first + (1.0 - BETA_ONE) * grad
    second_new = BETA_TWO * second + (1.0 - BETA_TWO) * grad * grad
    first_hat = first_new / (1.0 - BETA_ONE**STEP)
    second_hat = second_new / (1.0 - BETA_TWO**STEP)
    value_new = value - rate * (first_hat / (jnp.sqrt(second_hat) + ADAM_EPS) + DECAY * value)
    return (value_new, first_new, second_new)


def shard_kernel(parts_ref, facts_ref, shard_ref, all_facts_ref):
    total = parts_ref[0:SHARD_ROWS, :]
    for peer in range(1, PEERS):
        total = total + parts_ref[peer * SHARD_ROWS : (peer + 1) * SHARD_ROWS, :]
    shard_ref[...] = total
    facts = facts_ref[...]
    left = rows_of_lanes(1, facts.shape) < LANES // 2
    all_facts_ref[...] = facts + jnp.where(left, total_of(total * total), 0.0)


def sum_shards(parts, facts):
    return pl.pallas_call(
        shard_kernel,
        out_shape=(f32(SHARD_ROWS, LANES), f32(8, LANES)),
        in_specs=vmem(2),
        out_specs=tuple(vmem(2)),
        compiler_params=PARAMS,
    )(parts, facts)


def update_kernel(
    seen_ref,
    shard_ref,
    weights_ref,
    moment_one_ref,
    moment_two_ref,
    codes_ref,
    code_first_ref,
    code_second_ref,
    code_grad_ref,
    loss_out,
    norm_out,
    weights_out,
    moment_one_out,
    moment_two_out,
    weights_copy_out,
    codes_out,
    code_first_out,
    code_second_out,
    codes_copy_out,
):
    total = jnp.sum(seen_ref[...], axis=0, keepdims=True)
    loss_out[...] = total[:, LANES // 2 : LANES // 2 + 1]
    norm = jnp.sqrt(total[:, 0:1])
    norm_out[...] = norm
    factor = jnp.minimum(1.0, CLIP / (norm + 1e-06))
    value, first, second = adam_update(
        weights_ref[...],
        moment_one_ref[...],
        moment_two_ref[...],
        factor * shard_ref[...],
        WEIGHT_RATE,
    )
    weights_out[...] = value
    moment_one_out[...] = first
    moment_two_out[...] = second
    weights_copy_out[...] = value.astype(BF16)
    for r in range(0, CODE_ROWS, 32):
        rows = slice(r, r + 32)
        value, first, second = adam_update(
            codes_ref[rows, :],
            code_first_ref[rows, :],
            code_second_ref[rows, :],
            factor * code_grad_ref[rows, :],
            CODE_RATE,
        )
        codes_out[rows, :] = value
        code_first_out[rows, :] = first
        code_second_out[rows, :] = second
        codes_copy_out[rows, :] = value.astype(BF16)


def update_all(*args):
    scalar = jax.ShapeDtypeStruct((1, 1), F32)
    shard = [jax.ShapeDtypeStruct((SHARD_ROWS, LANES), t) for t in (F32, F32, F32, BF16)]
    table = [jax.ShapeDtypeStruct((CODE_ROWS, LATENT), t) for t in (F32, F32, F32, BF16)]
    return pl.pallas_call(
        update_kernel,
        out_shape=(scalar, scalar, *shard, *table),
        in_specs=vmem(9),
        out_specs=tuple(vmem(10)),
        compiler_params=PARAMS,
    )(*args)


def swap_cores(v):
    return lax.ppermute(v, "core", [(0, 1), (1, 0)])


def exchange(v):
    return lax.all_to_all(v, ("z", "wide"), split_axis=0, concat_axis=0)


def body(
    weights_flat,
    moment_one,
    moment_two,
    codes,
    code_first,
    code_second,
    coords,
    distances,
    shape_index,
):
    boxes = pack_boxes(
        weights_flat.reshape(SHARD_ROWS, LANES),
        jnp.concatenate([coords, distances[None]]),
        shape_index.reshape(1, POINTS_DEV),
    )
    mine = exchange(boxes.reshape(PEERS, BOX_ROWS, LANES))
    other = swap_cores(mine)
    core = lax.axis_index("core").astype(jnp.int32).reshape(1)
    keep, give, code_grad, facts = main_call(
        core,
        mine.reshape(PEERS * BOX_ROWS, LANES),
        other.reshape(PEERS * BOX_ROWS, LANES),
        codes,
    )
    pair_sum = (keep + swap_cores(give)).reshape(PEERS, 1, SHARD_ROWS * LANES)
    parts = exchange(pair_sum).reshape(PEERS * SHARD_ROWS, LANES)
    shard, facts = sum_shards(parts, facts)
    facts = facts + swap_cores(facts)
    facts = jnp.broadcast_to(facts[0:1], (PEERS, LANES)).reshape(PEERS, 1, LANES)
    flat = lambda v: v.reshape(SHARD_ROWS, LANES)
    out = update_all(
        exchange(facts).reshape(PEERS, LANES),
        shard,
        flat(weights_flat),
        flat(moment_one),
        flat(moment_two),
        codes,
        code_first,
        code_second,
        code_grad,
    )
    return (
        out[0].reshape(()),
        out[1].reshape(()),
        *[v.reshape(weights_flat.shape) for v in out[2:6]],
        *out[6:],
    )


def solution(mesh):
    parts = Mesh(mesh.devices.reshape(4, 2, 16), ALL)
    return jax.shard_map(
        body,
        mesh=parts,
        in_specs=(
            P(ALL),
            P(ALL),
            P(ALL),
            P(ALL, None),
            P(ALL, None),
            P(ALL, None),
            P(None, ALL),
            P(ALL),
            P(ALL),
        ),
        out_specs=(
            P(),
            P(),
            P(ALL),
            P(ALL),
            P(ALL),
            P(ALL),
            P(ALL, None),
            P(ALL, None),
            P(ALL, None),
            P(ALL, None),
        ),
        check_vma=False,
    )
```

```python
import jax
import jax.numpy as jnp
from jax import lax
from jax.experimental import pallas as pl
from jax.experimental.pallas import tpu as pltpu
from jax.sharding import Mesh
from jax.sharding import PartitionSpec as P

LATENT = 256
HID = 512
MIDDLE = HID - LATENT - 3
STEP = 10

DELTA = 0.1
SMOOTH = 0.01
CODE_WEIGHT = 0.001
EIK_WEIGHT = 0.1
CLIP = 0.001
WEIGHT_RATE = 0.02
CODE_RATE = 0.15
BETA_ONE = 0.9
BETA_TWO = 0.999
ADAM_EPS = 1e-08
DECAY = 0.01

LANES = 128
DEVICES = 128
PEERS = 64
SHARD_ROWS = 21
BOX_ROWS = 24
SLOTS = 16
POINTS_DEV = 1024
CODE_ROWS = 256
FLAT_ROWS = DEVICES * SHARD_ROWS
BLOCK = 256
SUBS = 4
TILES = BLOCK // LANES
ALL_POINTS = POINTS_DEV * DEVICES

F32 = jnp.float32
BF16 = jnp.bfloat16
ALL = ("z", "core", "wide")


def rows_of_lanes(lead, shape):
    return lax.broadcasted_iota(jnp.int32, shape, lead)


def halves(v):
    high = v.astype(BF16)
    return high, (v - high.astype(F32)).astype(BF16)


def thirds(v):
    high = v.astype(BF16).astype(F32)
    rest = v - high
    mid = rest.astype(BF16).astype(F32)
    return high, mid, rest - mid


def mm(a, b):
    return lax.dot_general(a, b, (((1,), (0,)), ((), ())), preferred_element_type=F32)


def mm_nt(a, b):
    return lax.dot_general(a, b, (((1,), (1,)), ((), ())), preferred_element_type=F32)


def beside(*parts):
    return jnp.concatenate(parts, axis=1)


def row_sums(v):
    high, low = halves(v)
    return mm(beside(high, low), jnp.ones((2 * v.shape[1], LANES), BF16))


def picked_lanes(v, count):
    shape = (LANES, count * LANES)
    row, column = rows_of_lanes(0, shape), rows_of_lanes(1, shape)
    chosen = jnp.where(column >> 7 == row, 1.0, 0.0).astype(BF16)
    parts = beside(*[part.astype(BF16) for part in thirds(v)])
    wide = mm(parts, stacked(chosen, chosen, chosen))
    return [wide[:, i * LANES : (i + 1) * LANES] for i in range(count)]


def twice(v):
    return beside(v, v)


def total_of(v):
    return jnp.sum(jnp.sum(v, axis=0, keepdims=True), axis=1, keepdims=True)


def stacked(*parts):
    return jnp.concatenate(parts, axis=0)


def pack_kernel(weights_ref, points_ref, index_ref, out_ref):
    shard = stacked(weights_ref[...], jnp.zeros((BOX_ROWS - SHARD_ROWS, LANES), F32))

    def fill(i, carry):
        for k in range(8):
            place = pl.ds(pl.multiple_of((i * 8 + k) * BOX_ROWS, 8), BOX_ROWS)
            out_ref[place, :] = shard
        return carry

    lax.fori_loop(0, PEERS // 8, fill, 0)
    index = index_ref[...]
    owner = lax.shift_right_logical(index, 8)
    row = lax.bitwise_and(index, CODE_ROWS - 1)
    sent = (rows_of_lanes(0, (DEVICES, POINTS_DEV)) == owner).astype(F32)
    sent_low = sent.astype(BF16)
    width = 256
    earlier = rows_of_lanes(0, (width, width)) < rows_of_lanes(1, (width, width))
    earlier = earlier.astype(F32).astype(BF16)
    ones = jnp.ones((width, width), BF16)
    ranks = [
        mm(sent_low[:, : (part + 1) * width], stacked(*([ones] * part + [earlier])))
        for part in range(POINTS_DEV // width)
    ]
    placed = jnp.sum(sent * beside(*ranks), axis=0, keepdims=True).astype(jnp.int32)
    at_slot = rows_of_lanes(0, (SLOTS, POINTS_DEV)) == placed
    values = [points_ref[i : i + 1, :] for i in range(4)]
    values.append((row + 1).astype(F32))
    pieces = [[], [], []]
    for value in values:
        for k, third in enumerate(thirds(value)):
            pieces[k].append(jnp.where(at_slot, third, 0.0))
    spare = jnp.zeros((LANES - SLOTS * len(values), POINTS_DEV), F32)
    boxes = mm_nt(
        beside(sent_low, sent_low, sent_low),
        beside(*[stacked(*piece, spare).astype(BF16) for piece in pieces]),
    )
    for z in range(4):
        for core in range(2):
            place = pl.ds(z * 16 * BOX_ROWS + SHARD_ROWS + core, 16, stride=BOX_ROWS)
            first = z * 32 + core * 16
            out_ref[place, :] = boxes[first : first + 16, :]


def unit_groups(count, stride_rows, extra, first_entry):
    for group in range(count):
        entry = first_entry + group * 8 * (stride_rows * LANES + extra)
        yield group, entry // LANES, entry % LANES


def unpack_units(flat_ref, out_ref, count, stride_rows, extra, first_entry):
    lane = rows_of_lanes(1, (8, LANES))
    slope = rows_of_lanes(0, (8, LANES)) * extra
    for group, first, shift in unit_groups(count, stride_rows, extra, first_entry):
        start = slope + shift
        wraps = shift + 7 * extra >= LANES
        turn = lax.bitwise_and(lane + start, LANES - 1)
        tiles = []
        for a in range(stride_rows + 2 + wraps):
            tile = flat_ref[pl.ds(first + a, 8, stride=stride_rows), :]
            tiles.append(jnp.take_along_axis(tile, turn, axis=1, mode="promise_in_bounds"))
        for c in range(stride_rows + 1):
            value = jnp.where(lane + start < LANES, tiles[c], tiles[c + 1])
            if wraps:
                value = jnp.where(lane + start < 2 * LANES, value, tiles[c + 2])
            out_ref[group * 8 : group * 8 + 8, c * LANES : (c + 1) * LANES] = value


def pack_units(value_ref, heads_ref, tails_ref, count, stride_rows, extra, first_entry):
    lane = rows_of_lanes(1, (8, LANES))
    slope = rows_of_lanes(0, (8, LANES)) * extra
    zero = jnp.zeros((8, LANES), F32)
    for group, first, shift in unit_groups(count, stride_rows, extra, first_entry):
        start = slope + shift
        wraps = shift + 7 * extra >= LANES
        turn = lax.bitwise_and(lane - start, LANES - 1)
        tiles = [zero, zero]
        for c in range(stride_rows + 1):
            value = value_ref[group * 8 : group * 8 + 8, c * LANES : (c + 1) * LANES]
            tiles.append(jnp.take_along_axis(value, turn, axis=1, mode="promise_in_bounds"))
        tiles.append(zero)
        for a in range(stride_rows + 2):
            value = jnp.where(lane >= start, tiles[a + 2], tiles[a + 1])
            if wraps:
                value = jnp.where(lane >= start - LANES, value, tiles[a])
            target = heads_ref if a < stride_rows else tails_ref
            target[pl.ds(first + a, 8, stride=stride_rows), :] = value


def clear(ref, rows):
    def step(i, carry):
        place = pl.ds(pl.multiple_of(i * rows, 8), rows)
        ref[place, :] = jnp.zeros((rows, ref.shape[1]), F32)
        return carry

    lax.fori_loop(0, ref.shape[0] // rows, step, 0)


FIRST_UNITS = (32, 2, 5, 0)
SECOND_UNITS = (64, 4, 3, MIDDLE * (LATENT + 5))
HEAD_ENTRY = MIDDLE * (LATENT + 5) + HID * (HID + 3)


def across(column):
    return beside(*[column] * TILES)


def folded(v):
    return sum(v[:, i * LANES : (i + 1) * LANES] for i in range(TILES))


def silu_parts(half):
    gate = jnp.tanh(half)
    low = 0.5 * gate
    bend = 0.5 - gate * low
    bent = half * gate
    return half + bent, (0.5 + low) + half * bend, bend * (1.0 - bent)


def silu_parts_twice(half):
    gate = jnp.tanh(half)
    bend = 1.0 - gate * gate
    bent = half * gate
    return half + bent, (1.0 + gate) + half * bend, bend * (1.0 - bent)


def loop_kernel(
    core_ref,
    mine_ref,
    other_ref,
    codes_ref,
    first_w,
    second_w,
    latent_w,
    roots,
    scales,
    sum_two,
    sum_codes,
    sum_coord,
    sum_head,
    sum_count,
    sum_loss,
    flat,
    table,
    lhs_two,
    lhs_back,
    coord_w,
    head_w,
    spots,
    slope_one,
    curve_one,
    back_one,
    back_two,
    hid_hi,
    hid_lo,
    hot,
    act_two,
    slope_two,
    curve_two,
    act_tang,
    gate_hi,
    gate_lo,
    tang_hi,
    tang_lo,
    bar_hi,
    bar_lo,
    low_hi,
    low_lo,
):
    core = core_ref[0]

    for which in range(2):

        @pl.when(core == which)
        def _(which=which):
            for d in range(DEVICES):
                z, c, w = d // 32, d // 16 % 2, d % 16
                box = (z * 16 + w) * BOX_ROWS
                source = mine_ref if c == which else other_ref
                flat[d * SHARD_ROWS : d * SHARD_ROWS + BOX_ROWS, :] = source[box : box + BOX_ROWS, :]
            rows = pl.ds(SHARD_ROWS + which, PEERS, stride=BOX_ROWS)
            spots[...] = stacked(mine_ref[rows, :], other_ref[rows, :]).T

    unpack_units(flat, first_w, *FIRST_UNITS)
    unpack_units(flat, second_w, *SECOND_UNITS)
    head_bias = flat[HEAD_ENTRY // LANES : HEAD_ENTRY // LANES + 1, :][
        :, HEAD_ENTRY % LANES : HEAD_ENTRY % LANES + 1
    ]

    lane = rows_of_lanes(1, (256, LANES))
    unit = rows_of_lanes(0, (256, LANES))
    real = unit < MIDDLE

    first_low = jnp.where(beside(real, real), first_w[:, : 2 * LANES], 0.0)
    first_end = jnp.where(real, first_w[:, 2 * LANES :], 0.0)
    first_near = jnp.where(lane < 3, first_end, 0.0)
    first_w[:, : 2 * LANES] = first_low
    first_w[:, 2 * LANES :] = first_end
    *near_columns, gain, first_bias = picked_lanes(first_end, 5)
    square = first_low * first_low
    square = square[:, :LANES] + square[:, LANES:] + first_near * first_near
    root = lax.rsqrt(row_sums(square) + 1e-12)
    scale = gain * root
    roots[0:256, :] = root
    scales[0:256, :] = scale
    latent_w[0:256, :] = first_low * twice(scale)
    for i in range(3):
        coord_w[:, i * LANES : (i + 1) * LANES] = 0.5 * near_columns[i] * scale

    second_a = second_w[:, 0:256]
    second_b = second_w[:, 256:512]
    gain, second_bias, head = picked_lanes(second_w[:, 512:640], 3)
    head_w[:, :LANES] = 0.5 * head
    head_w[:, LANES:] = head
    square = second_a * second_a + second_b * second_b
    root = lax.rsqrt(row_sums(square[:, :LANES] + square[:, LANES:]) + 1e-12)
    scale = gain * root
    roots[256:768, :] = root
    scales[256:768, :] = scale
    second_a = second_a * twice(scale)
    second_b = second_b * twice(scale)
    is_hidden = rows_of_lanes(1, (HID, 256)) < MIDDLE
    hidden_cols = jnp.where(is_hidden, second_a, second_b)
    latent_cols = pltpu.roll(jnp.where(is_hidden, second_b, second_a), 3, 1)
    latent_w[256:768, :] = latent_cols

    hidden_hi, hidden_lo = halves(0.5 * hidden_cols)
    lhs_two[:, 0:256] = hidden_hi
    lhs_two[:, 256:512] = hidden_hi
    lhs_two[:, 512:768] = hidden_lo
    back_hi, back_lo = halves(hidden_cols.T)
    lhs_back[:, 0:512] = back_hi
    lhs_back[:, 512:1024] = back_hi
    lhs_back[:, 1024:1536] = back_lo

    code_hi, code_lo = halves(codes_ref[...])
    weight_hi, weight_lo = halves(latent_w[...])
    by_code = mm_nt(
        beside(weight_hi, weight_hi, weight_lo), beside(code_hi, code_lo, code_hi)
    )
    table[0:256, :] = 0.5 * (by_code[0:256, :] + twice(first_bias))
    table[256:768, :] = 0.5 * (by_code[256:768, :] + twice(second_bias))

    for ref in (sum_two, sum_codes, sum_coord, sum_head):
        clear(ref, 64)
    sum_count[...] = jnp.zeros(sum_count.shape, F32)
    sum_loss[...] = jnp.zeros(sum_loss.shape, F32)

    def feature(which, step, sub):
        first = which * SLOTS + (step * SUBS + sub) * TILES
        return beside(*[spots[pl.ds(first + i, 1), :] for i in range(TILES)])

    blank5 = jnp.zeros((5, BLOCK), F32)
    chunk = 4096 // BLOCK
    low_chunks = range(0, 256, chunk)
    high_chunks = range(0, HID, chunk)

    def block_stages(step, s):
        place = [feature(i, step, s) for i in range(3)]
        target = feature(3, step, s)
        code_row = feature(4, step, s)
        valid = (code_row > 0.5).astype(F32)

        code = jnp.broadcast_to(jnp.maximum(code_row - 1.0, 0.0).astype(jnp.int32), (chunk, BLOCK))
        upper = code >= LANES
        code = lax.bitwise_and(code, LANES - 1)

        def picked(first):
            rows = slice(first, first + chunk)
            tiles = []
            for i in range(TILES):
                part = slice(i * LANES, (i + 1) * LANES)
                both = [
                    jnp.take_along_axis(
                        table[rows, c : c + LANES], code[:, part], axis=1, mode="promise_in_bounds"
                    )
                    for c in (0, LANES)
                ]
                tiles.append(jnp.where(upper[:, part], both[1], both[0]))
            return beside(*tiles)

        last = stacked(blank5, *place)
        for r in low_chunks:
            pre = picked(r)
            for i in range(3):
                pre = pre + across(coord_w[r : r + chunk, i * LANES : (i + 1) * LANES]) * place[i]
            value, slope, curve = silu_parts(pre)
            if r + chunk == 256:
                inside = rows_of_lanes(0, (chunk, BLOCK)) + r < MIDDLE
                end = jnp.where(inside[chunk - 8 :], value[chunk - 8 :], last)
                value = stacked(value[: chunk - 8], end)
                slope = jnp.where(inside, slope, 0.0)
                curve = jnp.where(inside, curve, 0.0)
            high, low = halves(value)
            hid_hi[s, r : r + chunk, :] = high
            hid_lo[s, r : r + chunk, :] = low
            slope_one[s, r : r + chunk, :] = slope
            curve_one[s, r : r + chunk, :] = curve
        yield

        act_two[s] = mm(lhs_two[...], stacked(hid_hi[s], hid_lo[s], hid_hi[s]))
        yield
        total = jnp.zeros((8, BLOCK), F32)
        for r in high_chunks:
            value, slope, curve = silu_parts_twice(act_two[s, r : r + chunk, :] + picked(256 + r))
            head = across(head_w[r : r + chunk, :LANES])
            weighed = head * value
            for k in range(0, chunk, 8):
                total = total + weighed[k : k + 8, :]
            high, low = halves(head * slope)
            gate_hi[s, r : r + chunk, :] = high
            gate_lo[s, r : r + chunk, :] = low
            act_two[s, r : r + chunk, :] = value
            slope_two[s, r : r + chunk, :] = slope
            curve_two[s, r : r + chunk, :] = curve
        summed = jnp.sum(total, axis=0, keepdims=True)
        yield

        predicted = jnp.tanh(2.0 * summed + head_bias)
        flank = 1.0 - predicted * predicted
        capped = jnp.tanh(predicted / DELTA)
        misfit = DELTA * capped - DELTA * jnp.tanh(target / DELTA)
        square = misfit * misfit + SMOOTH * SMOOTH
        inverse = lax.rsqrt(square)
        fitting = square * inverse
        by_fit = misfit * inverse * (1.0 - capped * capped)
        share_flank = valid * (1.0 / ALL_POINTS) * flank

        back_one[s] = mm(lhs_back[...], stacked(gate_hi[s], gate_lo[s], gate_hi[s]))
        yield
        totals = [jnp.zeros((8, BLOCK), F32) for _ in range(3)]
        for r in low_chunks:
            grad = back_one[s, r : r + chunk, :] * slope_one[s, r : r + chunk, :]
            for i in range(3):
                weighed = across(coord_w[r : r + chunk, i * LANES : (i + 1) * LANES]) * grad
                for k in range(0, chunk, 8):
                    totals[i] = totals[i] + weighed[k : k + 8, :]
        lead = [
            2.0 * jnp.sum(totals[i], axis=0, keepdims=True)
            + back_one[s, MIDDLE + i : MIDDLE + i + 1, :]
            for i in range(3)
        ]

        slope = [flank * q for q in lead]
        excess = slope[0] * slope[0] + slope[1] * slope[1] + slope[2] * slope[2] - 1.0
        sum_loss[0:1, :] += valid * (fitting + EIK_WEIGHT * excess * excess)
        pull = [(4.0 * EIK_WEIGHT) * excess * v for v in slope]
        by_flank = sum(p * q for p, q in zip(pull, lead))
        bar_out = share_flank * (by_fit - 2.0 * predicted * by_flank)
        sum_loss[1:2, :] += bar_out
        half_bar = 0.5 * bar_out
        pull = [share_flank * p for p in pull]

        last = stacked(blank5, *pull)
        twice = [2.0 * p for p in pull]
        for r in low_chunks:
            grad = 0.0
            for i in range(3):
                grad = grad + across(coord_w[r : r + chunk, i * LANES : (i + 1) * LANES]) * twice[i]
            slope = slope_one[s, r : r + chunk, :]
            back = back_one[s, r : r + chunk, :]
            through = grad * slope
            if r + chunk == 256:
                inside = rows_of_lanes(0, (8, BLOCK)) < MIDDLE - 248
                end = jnp.where(inside, through[chunk - 8 :], last)
                through = stacked(through[: chunk - 8], end)
            high, low = halves(through)
            tang_hi[s, r : r + chunk, :] = high
            tang_lo[s, r : r + chunk, :] = low
            curve_one[s, r : r + chunk, :] = (
                grad * back * curve_one[s, r : r + chunk, :]
            )
        yield
        act_tang[s] = mm(lhs_two[...], stacked(tang_hi[s], tang_lo[s], tang_hi[s]))
        sum_two[...] += mm_nt(
            beside(gate_hi[s], gate_hi[s], gate_lo[s]), beside(tang_hi[s], tang_lo[s], tang_hi[s])
        )

        for c in range(0, CODE_ROWS, LANES):
            code = (rows_of_lanes(1, (LANES, LANES)) + c).astype(F32)
            seen = jnp.zeros((8, LANES), F32)
            for i in range(TILES):
                wanted = code_row[:, i * LANES : (i + 1) * LANES] - 1.0
                mark = jnp.where(code == jnp.broadcast_to(wanted, (LANES, LANES)).T, 1.0, 0.0)
                hot[s, i * LANES : (i + 1) * LANES, c : c + LANES] = mark.astype(BF16)
                for k in range(0, LANES, 8):
                    seen = seen + mark[k : k + 8, :]
            sum_count[:, c : c + LANES] += seen
        yield
        for r in high_chunks:
            tangent = act_tang[s, r : r + chunk, :]
            slope = slope_two[s, r : r + chunk, :]
            head = across(head_w[r : r + chunk, LANES:])
            bar = head * (half_bar * slope + tangent * curve_two[s, r : r + chunk, :])
            by_head = act_two[s, r : r + chunk, :] * bar_out + slope * tangent
            sum_head[r : r + chunk, :] += folded(by_head)
            high, low = halves(bar)
            bar_hi[s, r : r + chunk, :] = high
            bar_lo[s, r : r + chunk, :] = low
        yield

        back_two[s] = mm(lhs_back[...], stacked(bar_hi[s], bar_lo[s], bar_hi[s]))
        sum_two[...] += mm_nt(
            beside(bar_hi[s], bar_hi[s], bar_lo[s]), beside(hid_hi[s], hid_lo[s], hid_hi[s])
        )
        marks = stacked(hot[s], hot[s])
        sum_codes[256:768, :] += mm(beside(bar_hi[s], bar_lo[s]), marks)
        yield
        for r in low_chunks:
            slope = slope_one[s, r : r + chunk, :]
            bar = back_two[s, r : r + chunk, :] * slope + curve_one[s, r : r + chunk, :]
            near = back_one[s, r : r + chunk, :] * slope
            for i in range(3):
                sum_coord[r : r + chunk, i * LANES : (i + 1) * LANES] += folded(
                    bar * place[i] + near * pull[i]
                )
            high, low = halves(bar)
            low_hi[s, r : r + chunk, :] = high
            low_lo[s, r : r + chunk, :] = low
        yield

        sum_codes[0:256, :] += mm(beside(low_hi[s], low_lo[s]), marks)

    def step_body(step, carry):
        waiting = [block_stages(step, s) for s in range(SUBS)]
        active = []
        while waiting or active:
            if waiting:
                active.append(waiting.pop(0))
            active = [work for work in active if next(work, work) is not work]
        return carry

    steps = SLOTS * DEVICES // (SUBS * BLOCK)
    if steps == 1:
        step_body(0, 0)
    else:
        lax.fori_loop(0, steps, step_body, 0)


def code_kernel(codes_ref, latent_w, sum_codes, sum_count, sum_loss, code_grad_ref, facts_ref):
    codes = codes_ref[...]
    count = jnp.sum(sum_count[...], axis=0, keepdims=True)
    count = twice(jnp.broadcast_to(count, (LANES, CODE_ROWS)).T)
    turned_hi, turned_lo = halves(sum_codes[...].T)
    weight_hi, weight_lo = halves(latent_w[...])
    code_grad = mm(
        beside(turned_hi, turned_hi, turned_lo), stacked(weight_hi, weight_lo, weight_hi)
    )
    code_grad = code_grad + (2.0 * CODE_WEIGHT / ALL_POINTS) * count * codes
    code_grad_ref[...] = code_grad
    loss = jnp.sum(sum_loss[0:1, :], axis=1, keepdims=True)
    loss = (loss + CODE_WEIGHT * total_of(count * codes * codes)) / ALL_POINTS
    left = rows_of_lanes(1, facts_ref.shape) < LANES // 2
    facts_ref[...] = jnp.where(left, total_of(code_grad * code_grad), loss)


def weight_kernel(
    core_ref,
    codes_ref,
    first_w,
    second_w,
    roots,
    scales,
    sum_two,
    sum_codes,
    sum_coord,
    sum_head,
    _,
    sum_loss,
    keep_ref,
    give_ref,
    flat,
    tails,
    first_grad,
    second_grad,
):
    core = core_ref[0]
    codes = codes_ref[...]
    by_code = sum_codes[...]
    code_hi, code_lo = halves(codes)
    by_hi, by_lo = halves(by_code)
    latent_grad = mm(beside(by_hi, by_hi, by_lo), stacked(code_hi, code_lo, code_hi))

    bias_grad = row_sums(by_code[:, :LANES] + by_code[:, LANES:])
    lane = rows_of_lanes(1, (256, LANES))
    real = rows_of_lanes(0, (256, LANES)) < MIDDLE
    near_grad = 0.0
    for i in range(3):
        column = row_sums(sum_coord[:, i * LANES : (i + 1) * LANES])
        near_grad = jnp.where(lane == i, column, near_grad)
    low_grad = latent_grad[0:256, :]
    first_low = first_w[:, : 2 * LANES]
    first_near = jnp.where(lane < 3, first_w[:, 2 * LANES :], 0.0)
    root, scale = roots[0:256, :], scales[0:256, :]
    product = first_low * low_grad
    product = product[:, :LANES] + product[:, LANES:] + first_near * near_grad
    along = row_sums(product)
    inward = scale * root * root * along
    end = scale * near_grad - first_near * inward
    end = jnp.where(lane == 3, root * along, end)
    end = jnp.where(lane == 4, bias_grad[0:256, :], end)
    low_grad = twice(scale) * low_grad - first_low * twice(inward)
    first_grad[:, : 2 * LANES] = jnp.where(beside(real, real), low_grad, 0.0)
    first_grad[:, 2 * LANES :] = jnp.where(real, end, 0.0)

    is_hidden = rows_of_lanes(1, (HID, 256)) < MIDDLE
    hidden_grad = sum_two[...]
    moved = pltpu.roll(latent_grad[256:768, :], 256 - 3, 1)
    grad_a = jnp.where(is_hidden, hidden_grad, moved)
    grad_b = jnp.where(is_hidden, moved, hidden_grad)
    second_a = second_w[:, 0:256]
    second_b = second_w[:, 256:512]
    root, scale = roots[256:768, :], scales[256:768, :]
    product = second_a * grad_a + second_b * grad_b
    along = row_sums(product[:, :LANES] + product[:, LANES:])
    inward = scale * root * root * along
    second_grad[:, 0:256] = twice(scale) * grad_a - second_a * twice(inward)
    second_grad[:, 256:512] = twice(scale) * grad_b - second_b * twice(inward)
    head_grad = row_sums(sum_head[...])
    lane = rows_of_lanes(1, (HID, LANES))
    end = jnp.where(lane == 0, root * along, 0.0)
    end = jnp.where(lane == 1, bias_grad[256:768, :], end)
    second_grad[:, 512:640] = jnp.where(lane == 2, head_grad, end)

    for ref in (flat, tails):
        clear(ref, 128)
    pack_units(first_grad, flat, tails, *FIRST_UNITS)
    pack_units(second_grad, flat, tails, *SECOND_UNITS)
    row = HEAD_ENTRY // LANES
    lane = rows_of_lanes(1, (1, LANES))
    bias_total = jnp.sum(sum_loss[1:2, :], axis=1, keepdims=True)
    flat[row : row + 1, :] += jnp.where(lane == HEAD_ENTRY % LANES, bias_total, 0.0)
    size = 16 * SHARD_ROWS
    for which in range(2):

        @pl.when(core == which)
        def _(which=which):
            for z in range(4):
                for c in range(2):
                    target = keep_ref if c == which else give_ref
                    first = (z * 2 + c) * size
                    target[z * size : (z + 1) * size, :] = (
                        flat[first : first + size, :] + tails[first : first + size, :]
                    )


def vmem(count):
    return [pl.BlockSpec(memory_space=pltpu.VMEM)] * count


PARAMS = pltpu.CompilerParams(vmem_limit_bytes=48 * 1024 * 1024)


SMEM = pl.BlockSpec(memory_space=pltpu.SMEM)


def f32(*shape):
    return jax.ShapeDtypeStruct(shape, F32)


def pack_boxes(weights, points, index):
    return pl.pallas_call(
        pack_kernel,
        out_shape=f32(PEERS * BOX_ROWS, LANES),
        in_specs=vmem(3),
        out_specs=vmem(1)[0],
        compiler_params=PARAMS,
    )(weights, points, index)


def main_kernel(
    core_ref, mine_ref, other_ref, codes_ref, keep_ref, give_ref, code_grad_ref, facts_ref, *scratch
):
    first_w, second_w, latent_w, roots, scales, *sums = scratch[:11]
    flat = scratch[11]
    loop_kernel(core_ref, mine_ref, other_ref, codes_ref, *scratch[:-3])
    code_kernel(codes_ref, latent_w, sums[1], sums[4], sums[5], code_grad_ref, facts_ref)
    weight_kernel(core_ref, codes_ref, first_w, second_w, roots, scales, *sums, keep_ref, give_ref, flat, *scratch[-3:])


def main_call(core, mine, other, codes):
    pair = (SUBS, 256, BLOCK)
    pair_two = (SUBS, HID, BLOCK)
    scratch = [
        ((256, 3 * LANES), F32),
        ((HID, 5 * LANES), F32),
        ((768, 256), F32),
        ((768, LANES), F32),
        ((768, LANES), F32),
        ((HID, 256), F32),
        ((768, 256), F32),
        ((256, 3 * LANES), F32),
        ((HID, LANES), F32),
        ((8, CODE_ROWS), F32),
        ((2, BLOCK), F32),
        ((FLAT_ROWS + 8, LANES), F32),
        ((768, CODE_ROWS), F32),
        ((HID, 768), BF16),
        ((256, 1536), BF16),
        ((256, 3 * LANES), F32),
        ((HID, 2 * LANES), F32),
        ((LANES, LANES), F32),
        (pair, F32),
        (pair, F32),
        (pair, F32),
        (pair, F32),
        (pair, BF16),
        (pair, BF16),
        ((SUBS, BLOCK, CODE_ROWS), BF16),
        (pair_two, F32),
        (pair_two, F32),
        (pair_two, F32),
        (pair_two, F32),
        (pair_two, BF16),
        (pair_two, BF16),
        (pair, BF16),
        (pair, BF16),
        (pair_two, BF16),
        (pair_two, BF16),
        (pair, BF16),
        (pair, BF16),
        ((FLAT_ROWS + 8, LANES), F32),
        ((256, 3 * LANES), F32),
        ((HID, 5 * LANES), F32),
    ]
    boxes = f32(PEERS * SHARD_ROWS, LANES)
    return pl.pallas_call(
        main_kernel,
        out_shape=(boxes, boxes, f32(CODE_ROWS, LATENT), f32(8, LANES)),
        in_specs=[SMEM] + vmem(3),
        out_specs=tuple(vmem(4)),
        scratch_shapes=[pltpu.VMEM(shape, dtype) for shape, dtype in scratch],
        compiler_params=PARAMS,
    )(core, mine, other, codes)


def adam_update(value, first, second, grad, rate):
    first_new = BETA_ONE * first + (1.0 - BETA_ONE) * grad
    second_new = BETA_TWO * second + (1.0 - BETA_TWO) * grad * grad
    first_hat = first_new / (1.0 - BETA_ONE**STEP)
    second_hat = second_new / (1.0 - BETA_TWO**STEP)
    value_new = value - rate * (first_hat / (jnp.sqrt(second_hat) + ADAM_EPS) + DECAY * value)
    return (value_new, first_new, second_new)


def shard_kernel(parts_ref, facts_ref, shard_ref, all_facts_ref):
    total = parts_ref[0:SHARD_ROWS, :]
    for peer in range(1, PEERS):
        total = total + parts_ref[peer * SHARD_ROWS : (peer + 1) * SHARD_ROWS, :]
    shard_ref[...] = total
    facts = facts_ref[...]
    left = rows_of_lanes(1, facts.shape) < LANES // 2
    all_facts_ref[...] = facts + jnp.where(left, total_of(total * total), 0.0)


def sum_shards(parts, facts):
    return pl.pallas_call(
        shard_kernel,
        out_shape=(f32(SHARD_ROWS, LANES), f32(8, LANES)),
        in_specs=vmem(2),
        out_specs=tuple(vmem(2)),
        compiler_params=PARAMS,
    )(parts, facts)


def update_kernel(
    seen_ref,
    shard_ref,
    weights_ref,
    moment_one_ref,
    moment_two_ref,
    codes_ref,
    code_first_ref,
    code_second_ref,
    code_grad_ref,
    loss_out,
    norm_out,
    weights_out,
    moment_one_out,
    moment_two_out,
    weights_copy_out,
    codes_out,
    code_first_out,
    code_second_out,
    codes_copy_out,
):
    total = jnp.sum(seen_ref[...], axis=0, keepdims=True)
    loss_out[...] = total[:, LANES // 2 : LANES // 2 + 1]
    norm = jnp.sqrt(total[:, 0:1])
    norm_out[...] = norm
    factor = jnp.minimum(1.0, CLIP / (norm + 1e-06))
    value, first, second = adam_update(
        weights_ref[...],
        moment_one_ref[...],
        moment_two_ref[...],
        factor * shard_ref[...],
        WEIGHT_RATE,
    )
    weights_out[...] = value
    moment_one_out[...] = first
    moment_two_out[...] = second
    weights_copy_out[...] = value.astype(BF16)
    for r in range(0, CODE_ROWS, 32):
        rows = slice(r, r + 32)
        value, first, second = adam_update(
            codes_ref[rows, :],
            code_first_ref[rows, :],
            code_second_ref[rows, :],
            factor * code_grad_ref[rows, :],
            CODE_RATE,
        )
        codes_out[rows, :] = value
        code_first_out[rows, :] = first
        code_second_out[rows, :] = second
        codes_copy_out[rows, :] = value.astype(BF16)


def update_all(*args):
    scalar = jax.ShapeDtypeStruct((1, 1), F32)
    shard = [jax.ShapeDtypeStruct((SHARD_ROWS, LANES), t) for t in (F32, F32, F32, BF16)]
    table = [jax.ShapeDtypeStruct((CODE_ROWS, LATENT), t) for t in (F32, F32, F32, BF16)]
    return pl.pallas_call(
        update_kernel,
        out_shape=(scalar, scalar, *shard, *table),
        in_specs=vmem(9),
        out_specs=tuple(vmem(10)),
        compiler_params=PARAMS,
    )(*args)


def swap_cores(v):
    return lax.ppermute(v, "core", [(0, 1), (1, 0)])


def exchange(v):
    return lax.all_to_all(v, ("z", "wide"), split_axis=0, concat_axis=0)


def body(
    weights_flat,
    moment_one,
    moment_two,
    codes,
    code_first,
    code_second,
    coords,
    distances,
    shape_index,
):
    boxes = pack_boxes(
        weights_flat.reshape(SHARD_ROWS, LANES),
        jnp.concatenate([coords, distances[None]]),
        shape_index.reshape(1, POINTS_DEV),
    )
    mine = exchange(boxes.reshape(PEERS, BOX_ROWS, LANES))
    other = swap_cores(mine)
    core = lax.axis_index("core").astype(jnp.int32).reshape(1)
    keep, give, code_grad, facts = main_call(
        core,
        mine.reshape(PEERS * BOX_ROWS, LANES),
        other.reshape(PEERS * BOX_ROWS, LANES),
        codes,
    )
    pair_sum = (keep + swap_cores(give)).reshape(PEERS, 1, SHARD_ROWS * LANES)
    parts = exchange(pair_sum).reshape(PEERS * SHARD_ROWS, LANES)
    shard, facts = sum_shards(parts, facts)
    facts = facts + swap_cores(facts)
    facts = jnp.broadcast_to(facts[0:1], (PEERS, LANES)).reshape(PEERS, 1, LANES)
    flat = lambda v: v.reshape(SHARD_ROWS, LANES)
    out = update_all(
        exchange(facts).reshape(PEERS, LANES),
        shard,
        flat(weights_flat),
        flat(moment_one),
        flat(moment_two),
        codes,
        code_first,
        code_second,
        code_grad,
    )
    return (
        out[0].reshape(()),
        out[1].reshape(()),
        *[v.reshape(weights_flat.shape) for v in out[2:6]],
        *out[6:],
    )


def solution(mesh):
    parts = Mesh(mesh.devices.reshape(4, 2, 16), ALL)
    return jax.shard_map(
        body,
        mesh=parts,
        in_specs=(
            P(ALL),
            P(ALL),
            P(ALL),
            P(ALL, None),
            P(ALL, None),
            P(ALL, None),
            P(None, ALL),
            P(ALL),
            P(ALL),
        ),
        out_specs=(
            P(),
            P(),
            P(ALL),
            P(ALL),
            P(ALL),
            P(ALL),
            P(ALL, None),
            P(ALL, None),
            P(ALL, None),
            P(ALL, None),
        ),
        check_vma=False,
    )
```

```python
import jax
import jax.numpy as jnp
from jax import lax
from jax.experimental import pallas as pl
from jax.experimental.pallas import tpu as pltpu
from jax.sharding import Mesh
from jax.sharding import PartitionSpec as P

LATENT = 256
HID = 512
MIDDLE = HID - LATENT - 3
STEP = 10

DELTA = 0.1
SMOOTH = 0.01
CODE_WEIGHT = 0.001
EIK_WEIGHT = 0.1
CLIP = 0.001
WEIGHT_RATE = 0.02
CODE_RATE = 0.15
BETA_ONE = 0.9
BETA_TWO = 0.999
ADAM_EPS = 1e-08
DECAY = 0.01

LANES = 128
DEVICES = 128
PEERS = 64
SHARD_ROWS = 21
BOX_ROWS = 23
SLOTS = 16
POINTS_DEV = 1024
CODE_ROWS = 256
FLAT_ROWS = DEVICES * SHARD_ROWS
BLOCK = 256
SUBS = 4
TILES = BLOCK // LANES
ALL_POINTS = POINTS_DEV * DEVICES

F32 = jnp.float32
BF16 = jnp.bfloat16
ALL = ("z", "core", "wide")


def rows_of_lanes(lead, shape):
    return lax.broadcasted_iota(jnp.int32, shape, lead)


def halves(v):
    high = v.astype(BF16)
    return high, (v - high.astype(F32)).astype(BF16)


def thirds(v):
    high = v.astype(BF16).astype(F32)
    rest = v - high
    mid = rest.astype(BF16).astype(F32)
    return high, mid, rest - mid


def mm(a, b):
    return lax.dot_general(a, b, (((1,), (0,)), ((), ())), preferred_element_type=F32)


def mm_nt(a, b):
    return lax.dot_general(a, b, (((1,), (1,)), ((), ())), preferred_element_type=F32)


def beside(*parts):
    return jnp.concatenate(parts, axis=1)


def row_sums(v):
    high, low = halves(v)
    return mm(beside(high, low), jnp.ones((2 * v.shape[1], LANES), BF16))


def picked_lanes(v, count):
    shape = (LANES, count * LANES)
    row, column = rows_of_lanes(0, shape), rows_of_lanes(1, shape)
    chosen = jnp.where(column >> 7 == row, 1.0, 0.0).astype(BF16)
    parts = beside(*[part.astype(BF16) for part in thirds(v)])
    wide = mm(parts, stacked(chosen, chosen, chosen))
    return [wide[:, i * LANES : (i + 1) * LANES] for i in range(count)]


def twice(v):
    return beside(v, v)


def total_of(v):
    return jnp.sum(jnp.sum(v, axis=0, keepdims=True), axis=1, keepdims=True)


def stacked(*parts):
    return jnp.concatenate(parts, axis=0)


def pack_kernel(weights_ref, points_ref, index_ref, out_ref):
    shard = stacked(weights_ref[...], jnp.zeros((BOX_ROWS - SHARD_ROWS, LANES), F32))

    def fill(i, carry):
        for k in range(8):
            place = pl.ds(pl.multiple_of(i * 8 * BOX_ROWS, 8) + k * BOX_ROWS, BOX_ROWS)
            out_ref[place, :] = shard
        return carry

    lax.fori_loop(0, PEERS // 8, fill, 0)
    index = index_ref[...]
    owner = lax.shift_right_logical(index, 8)
    row = lax.bitwise_and(index, CODE_ROWS - 1)
    sent = (rows_of_lanes(0, (DEVICES, POINTS_DEV)) == owner).astype(F32)
    sent_low = sent.astype(BF16)
    width = 256
    earlier = rows_of_lanes(0, (width, width)) < rows_of_lanes(1, (width, width))
    earlier = earlier.astype(F32).astype(BF16)
    ones = jnp.ones((width, width), BF16)
    ranks = [
        mm(sent_low[:, : (part + 1) * width], stacked(*([ones] * part + [earlier])))
        for part in range(POINTS_DEV // width)
    ]
    placed = jnp.sum(sent * beside(*ranks), axis=0, keepdims=True).astype(jnp.int32)
    at_slot = rows_of_lanes(0, (SLOTS, POINTS_DEV)) == placed
    values = [points_ref[i : i + 1, :] for i in range(4)]
    values.append((row + 1).astype(F32))
    pieces = [[], [], []]
    for value in values:
        for k, third in enumerate(thirds(value)):
            pieces[k].append(jnp.where(at_slot, third, 0.0))
    spare = jnp.zeros((LANES - SLOTS * len(values), POINTS_DEV), F32)
    boxes = mm_nt(
        beside(sent_low, sent_low, sent_low),
        beside(*[stacked(*piece, spare).astype(BF16) for piece in pieces]),
    )
    for z in range(4):
        for core in range(2):
            place = pl.ds(z * 16 * BOX_ROWS + SHARD_ROWS + core, 16, stride=BOX_ROWS)
            first = z * 32 + core * 16
            out_ref[place, :] = boxes[first : first + 16, :]


def unit_groups(count, stride_rows, extra, first_entry):
    for group in range(count):
        entry = first_entry + group * 8 * (stride_rows * LANES + extra)
        yield group, entry // LANES, entry % LANES


def unpack_units(flat_ref, out_ref, count, stride_rows, extra, first_entry):
    lane = rows_of_lanes(1, (8, LANES))
    slope = rows_of_lanes(0, (8, LANES)) * extra
    for group, first, shift in unit_groups(count, stride_rows, extra, first_entry):
        start = slope + shift
        wraps = shift + 7 * extra >= LANES
        turn = lax.bitwise_and(lane + start, LANES - 1)
        tiles = []
        for a in range(stride_rows + 2 + wraps):
            tile = flat_ref[pl.ds(first + a, 8, stride=stride_rows), :]
            tiles.append(jnp.take_along_axis(tile, turn, axis=1, mode="promise_in_bounds"))
        for c in range(stride_rows + 1):
            value = jnp.where(lane + start < LANES, tiles[c], tiles[c + 1])
            if wraps:
                value = jnp.where(lane + start < 2 * LANES, value, tiles[c + 2])
            out_ref[group * 8 : group * 8 + 8, c * LANES : (c + 1) * LANES] = value


def pack_units(value_ref, heads_ref, tails_ref, count, stride_rows, extra, first_entry):
    lane = rows_of_lanes(1, (8, LANES))
    slope = rows_of_lanes(0, (8, LANES)) * extra
    zero = jnp.zeros((8, LANES), F32)
    for group, first, shift in unit_groups(count, stride_rows, extra, first_entry):
        start = slope + shift
        wraps = shift + 7 * extra >= LANES
        turn = lax.bitwise_and(lane - start, LANES - 1)
        tiles = [zero, zero]
        for c in range(stride_rows + 1):
            value = value_ref[group * 8 : group * 8 + 8, c * LANES : (c + 1) * LANES]
            tiles.append(jnp.take_along_axis(value, turn, axis=1, mode="promise_in_bounds"))
        tiles.append(zero)
        for a in range(stride_rows + 2):
            value = jnp.where(lane >= start, tiles[a + 2], tiles[a + 1])
            if wraps:
                value = jnp.where(lane >= start - LANES, value, tiles[a])
            target = heads_ref if a < stride_rows else tails_ref
            target[pl.ds(first + a, 8, stride=stride_rows), :] = value


def clear(ref, rows):
    def step(i, carry):
        place = pl.ds(pl.multiple_of(i * rows, 8), rows)
        ref[place, :] = jnp.zeros((rows, ref.shape[1]), F32)
        return carry

    lax.fori_loop(0, ref.shape[0] // rows, step, 0)


FIRST_UNITS = (32, 2, 5, 0)
SECOND_UNITS = (64, 4, 3, MIDDLE * (LATENT + 5))
HEAD_ENTRY = MIDDLE * (LATENT + 5) + HID * (HID + 3)


def across(column):
    return beside(*[column] * TILES)


def folded(v):
    return sum(v[:, i * LANES : (i + 1) * LANES] for i in range(TILES))


def silu_parts(half):
    gate = jnp.tanh(half)
    low = 0.5 * gate
    bend = 0.5 - gate * low
    bent = half * gate
    return half + bent, (0.5 + low) + half * bend, bend * (1.0 - bent)


def silu_parts_twice(half):
    gate = jnp.tanh(half)
    bend = 1.0 - gate * gate
    bent = half * gate
    return half + bent, (1.0 + gate) + half * bend, bend * (1.0 - bent)


def loop_kernel(
    core_ref,
    mine_ref,
    other_ref,
    codes_ref,
    first_w,
    second_w,
    latent_w,
    roots,
    scales,
    sum_two,
    sum_codes,
    sum_coord,
    sum_head,
    sum_count,
    sum_loss,
    flat,
    table,
    lhs_two,
    lhs_back,
    coord_w,
    head_w,
    spots,
    slope_one,
    curve_one,
    back_one,
    hid_hi,
    hid_lo,
    hot,
    act_two,
    slope_two,
    curve_two,
    act_tang,
    gate_hi,
    gate_lo,
    tang_hi,
    tang_lo,
    bar_hi,
    bar_lo,
    low_hi,
    low_lo,
):
    core = core_ref[0]

    for which in range(2):

        @pl.when(core == which)
        def _(which=which):
            for d in range(DEVICES):
                z, c, w = d // 32, d // 16 % 2, d % 16
                box = (z * 16 + w) * BOX_ROWS
                source = mine_ref if c == which else other_ref
                flat[d * SHARD_ROWS : d * SHARD_ROWS + BOX_ROWS, :] = source[box : box + BOX_ROWS, :]
            rows = pl.ds(SHARD_ROWS + which, PEERS, stride=BOX_ROWS)
            spots[...] = stacked(mine_ref[rows, :], other_ref[rows, :]).T

    unpack_units(flat, first_w, *FIRST_UNITS)
    unpack_units(flat, second_w, *SECOND_UNITS)
    head_bias = flat[HEAD_ENTRY // LANES : HEAD_ENTRY // LANES + 1, :][
        :, HEAD_ENTRY % LANES : HEAD_ENTRY % LANES + 1
    ]

    lane = rows_of_lanes(1, (256, LANES))
    unit = rows_of_lanes(0, (256, LANES))
    real = unit < MIDDLE

    first_low = jnp.where(beside(real, real), first_w[:, : 2 * LANES], 0.0)
    first_end = jnp.where(real, first_w[:, 2 * LANES :], 0.0)
    first_near = jnp.where(lane < 3, first_end, 0.0)
    first_w[:, : 2 * LANES] = first_low
    first_w[:, 2 * LANES :] = first_end
    *near_columns, gain, first_bias = picked_lanes(first_end, 5)
    square = first_low * first_low
    square = square[:, :LANES] + square[:, LANES:] + first_near * first_near
    root = lax.rsqrt(row_sums(square) + 1e-12)
    scale = gain * root
    roots[0:256, :] = root
    scales[0:256, :] = scale
    latent_w[0:256, :] = first_low * twice(scale)
    for i in range(3):
        coord_w[:, i * LANES : (i + 1) * LANES] = 0.5 * near_columns[i] * scale

    second_a = second_w[:, 0:256]
    second_b = second_w[:, 256:512]
    gain, second_bias, head = picked_lanes(second_w[:, 512:640], 3)
    head_w[:, :LANES] = 0.5 * head
    head_w[:, LANES:] = head
    square = second_a * second_a + second_b * second_b
    root = lax.rsqrt(row_sums(square[:, :LANES] + square[:, LANES:]) + 1e-12)
    scale = gain * root
    roots[256:768, :] = root
    scales[256:768, :] = scale
    second_a = second_a * twice(scale)
    second_b = second_b * twice(scale)
    is_hidden = rows_of_lanes(1, (HID, 256)) < MIDDLE
    hidden_cols = jnp.where(is_hidden, second_a, second_b)
    latent_cols = pltpu.roll(jnp.where(is_hidden, second_b, second_a), 3, 1)
    latent_w[256:768, :] = latent_cols

    hidden_hi, hidden_lo = halves(0.5 * hidden_cols)
    lhs_two[:, 0:256] = hidden_hi
    lhs_two[:, 256:512] = hidden_hi
    lhs_two[:, 512:768] = hidden_lo
    back_hi, back_lo = halves(hidden_cols.T)
    lhs_back[:, 0:512] = back_hi
    lhs_back[:, 512:1024] = back_hi
    lhs_back[:, 1024:1536] = back_lo

    code_hi, code_lo = halves(codes_ref[...])
    weight_hi, weight_lo = halves(latent_w[...])
    by_code = mm_nt(
        beside(weight_hi, weight_hi, weight_lo), beside(code_hi, code_lo, code_hi)
    )
    table[0:256, :] = 0.5 * (by_code[0:256, :] + twice(first_bias))
    table[256:768, :] = 0.5 * (by_code[256:768, :] + twice(second_bias))

    for ref in (sum_two, sum_codes, sum_coord, sum_head):
        clear(ref, 64)
    sum_count[...] = jnp.zeros(sum_count.shape, F32)
    sum_loss[...] = jnp.zeros(sum_loss.shape, F32)

    def feature(which, step, sub):
        first = which * SLOTS + (step * SUBS + sub) * TILES
        return beside(*[spots[pl.ds(first + i, 1), :] for i in range(TILES)])

    blank5 = jnp.zeros((5, BLOCK), F32)
    chunk = 8192 // BLOCK
    low_chunks = range(0, 256, chunk)
    high_chunks = range(0, HID, chunk)

    def block_stages(step, s):
        place = [feature(i, step, s) for i in range(3)]
        target = feature(3, step, s)
        code_row = feature(4, step, s)
        valid = (code_row > 0.5).astype(F32)

        code = jnp.broadcast_to(jnp.maximum(code_row - 1.0, 0.0).astype(jnp.int32), (chunk, BLOCK))
        upper = code >= LANES
        code = lax.bitwise_and(code, LANES - 1)

        def picked(first):
            rows = slice(first, first + chunk)
            tiles = []
            for i in range(TILES):
                part = slice(i * LANES, (i + 1) * LANES)
                both = [
                    jnp.take_along_axis(
                        table[rows, c : c + LANES], code[:, part], axis=1, mode="promise_in_bounds"
                    )
                    for c in (0, LANES)
                ]
                tiles.append(jnp.where(upper[:, part], both[1], both[0]))
            return beside(*tiles)

        last = stacked(blank5, *place)
        for r in low_chunks:
            pre = picked(r)
            for i in range(3):
                pre = pre + across(coord_w[r : r + chunk, i * LANES : (i + 1) * LANES]) * place[i]
            value, slope, curve = silu_parts(pre)
            if r + chunk == 256:
                inside = rows_of_lanes(0, (chunk, BLOCK)) + r < MIDDLE
                end = jnp.where(inside[chunk - 8 :], value[chunk - 8 :], last)
                value = stacked(value[: chunk - 8], end)
                slope = jnp.where(inside, slope, 0.0)
                curve = jnp.where(inside, curve, 0.0)
            high, low = halves(value)
            hid_hi[s, r : r + chunk, :] = high
            hid_lo[s, r : r + chunk, :] = low
            slope_one[s, r : r + chunk, :] = slope
            curve_one[s, r : r + chunk, :] = curve
        yield

        act_two[s] = mm(lhs_two[...], stacked(hid_hi[s], hid_lo[s], hid_hi[s]))
        yield
        total = jnp.zeros((8, BLOCK), F32)
        for r in high_chunks:
            value, slope, curve = silu_parts_twice(act_two[s, r : r + chunk, :] + picked(256 + r))
            head = across(head_w[r : r + chunk, :LANES])
            weighed = head * value
            for k in range(0, chunk, 8):
                total = total + weighed[k : k + 8, :]
            high, low = halves(head * slope)
            gate_hi[s, r : r + chunk, :] = high
            gate_lo[s, r : r + chunk, :] = low
            act_two[s, r : r + chunk, :] = value
            slope_two[s, r : r + chunk, :] = slope
            curve_two[s, r : r + chunk, :] = curve
        summed = jnp.sum(total, axis=0, keepdims=True)
        yield

        back_one[s] = mm(lhs_back[...], stacked(gate_hi[s], gate_lo[s], gate_hi[s]))
        yield
        totals = [jnp.zeros((8, BLOCK), F32) for _ in range(3)]
        for r in low_chunks:
            grad = back_one[s, r : r + chunk, :] * slope_one[s, r : r + chunk, :]
            for i in range(3):
                weighed = across(coord_w[r : r + chunk, i * LANES : (i + 1) * LANES]) * grad
                for k in range(0, chunk, 8):
                    totals[i] = totals[i] + weighed[k : k + 8, :]
        lead = [
            2.0 * jnp.sum(totals[i], axis=0, keepdims=True)
            + back_one[s, MIDDLE + i : MIDDLE + i + 1, :]
            for i in range(3)
        ]

        predicted = jnp.tanh(2.0 * summed + head_bias)
        flank = 1.0 - predicted * predicted
        slope = [flank * q for q in lead]
        excess = slope[0] * slope[0] + slope[1] * slope[1] + slope[2] * slope[2] - 1.0
        capped = jnp.tanh(predicted / DELTA)
        misfit = DELTA * capped - DELTA * jnp.tanh(target / DELTA)
        fitting = jnp.sqrt(misfit * misfit + SMOOTH * SMOOTH)
        sum_loss[0:1, :] += valid * (fitting + EIK_WEIGHT * excess * excess)
        share = valid * (1.0 / ALL_POINTS)
        pull = [(4.0 * EIK_WEIGHT) * excess * v for v in slope]
        by_flank = sum(p * q for p, q in zip(pull, lead))
        by_predicted = misfit / fitting * (1.0 - capped * capped) - 2.0 * predicted * by_flank
        bar_out = share * by_predicted * flank
        sum_loss[1:2, :] += bar_out
        half_bar = 0.5 * bar_out
        pull = [share * flank * p for p in pull]

        last = stacked(blank5, *pull)
        twice = [2.0 * p for p in pull]
        for r in low_chunks:
            grad = 0.0
            for i in range(3):
                grad = grad + across(coord_w[r : r + chunk, i * LANES : (i + 1) * LANES]) * twice[i]
            slope = slope_one[s, r : r + chunk, :]
            back = back_one[s, r : r + chunk, :]
            near = back * slope
            for i in range(3):
                sum_coord[r : r + chunk, i * LANES : (i + 1) * LANES] += folded(near * pull[i])
            through = grad * slope
            if r + chunk == 256:
                inside = rows_of_lanes(0, (8, BLOCK)) < MIDDLE - 248
                end = jnp.where(inside, through[chunk - 8 :], last)
                through = stacked(through[: chunk - 8], end)
            high, low = halves(through)
            tang_hi[s, r : r + chunk, :] = high
            tang_lo[s, r : r + chunk, :] = low
            curve_one[s, r : r + chunk, :] = (
                grad * back * curve_one[s, r : r + chunk, :]
            )
        yield
        act_tang[s] = mm(lhs_two[...], stacked(tang_hi[s], tang_lo[s], tang_hi[s]))
        sum_two[...] += mm_nt(
            beside(gate_hi[s], gate_hi[s], gate_lo[s]), beside(tang_hi[s], tang_lo[s], tang_hi[s])
        )

        for c in range(0, CODE_ROWS, LANES):
            code = (rows_of_lanes(1, (LANES, LANES)) + c).astype(F32)
            seen = jnp.zeros((8, LANES), F32)
            for i in range(TILES):
                wanted = code_row[:, i * LANES : (i + 1) * LANES] - 1.0
                mark = jnp.where(code == jnp.broadcast_to(wanted, (LANES, LANES)).T, 1.0, 0.0)
                hot[s, i * LANES : (i + 1) * LANES, c : c + LANES] = mark.astype(BF16)
                for k in range(0, LANES, 8):
                    seen = seen + mark[k : k + 8, :]
            sum_count[:, c : c + LANES] += seen
        yield
        for r in high_chunks:
            tangent = act_tang[s, r : r + chunk, :]
            slope = slope_two[s, r : r + chunk, :]
            head = across(head_w[r : r + chunk, LANES:])
            bar = head * (half_bar * slope + tangent * curve_two[s, r : r + chunk, :])
            by_head = act_two[s, r : r + chunk, :] * bar_out + slope * tangent
            sum_head[r : r + chunk, :] += folded(by_head)
            high, low = halves(bar)
            bar_hi[s, r : r + chunk, :] = high
            bar_lo[s, r : r + chunk, :] = low
        yield

        back_one[s] = mm(lhs_back[...], stacked(bar_hi[s], bar_lo[s], bar_hi[s]))
        sum_two[...] += mm_nt(
            beside(bar_hi[s], bar_hi[s], bar_lo[s]), beside(hid_hi[s], hid_lo[s], hid_hi[s])
        )
        marks = stacked(hot[s], hot[s])
        sum_codes[256:768, :] += mm(beside(bar_hi[s], bar_lo[s]), marks)
        yield
        for r in low_chunks:
            bar = (
                back_one[s, r : r + chunk, :] * slope_one[s, r : r + chunk, :]
                + curve_one[s, r : r + chunk, :]
            )
            for i in range(3):
                sum_coord[r : r + chunk, i * LANES : (i + 1) * LANES] += folded(bar * place[i])
            high, low = halves(bar)
            low_hi[s, r : r + chunk, :] = high
            low_lo[s, r : r + chunk, :] = low
        yield

        sum_codes[0:256, :] += mm(beside(low_hi[s], low_lo[s]), marks)

    def step_body(step, carry):
        waiting = [block_stages(step, s) for s in range(SUBS)]
        active = []
        while waiting or active:
            if waiting:
                active.append(waiting.pop(0))
            active = [work for work in active if next(work, work) is not work]
        return carry

    steps = SLOTS * DEVICES // (SUBS * BLOCK)
    if steps == 1:
        step_body(0, 0)
    else:
        lax.fori_loop(0, steps, step_body, 0)


def code_kernel(codes_ref, latent_w, sum_codes, sum_count, sum_loss, code_grad_ref, facts_ref):
    codes = codes_ref[...]
    count = jnp.sum(sum_count[...], axis=0, keepdims=True)
    count = twice(jnp.broadcast_to(count, (LANES, CODE_ROWS)).T)
    turned_hi, turned_lo = halves(sum_codes[...].T)
    weight_hi, weight_lo = halves(latent_w[...])
    code_grad = mm(
        beside(turned_hi, turned_hi, turned_lo), stacked(weight_hi, weight_lo, weight_hi)
    )
    code_grad = code_grad + (2.0 * CODE_WEIGHT / ALL_POINTS) * count * codes
    code_grad_ref[...] = code_grad
    loss = jnp.sum(sum_loss[0:1, :], axis=1, keepdims=True)
    loss = (loss + CODE_WEIGHT * total_of(count * codes * codes)) / ALL_POINTS
    left = rows_of_lanes(1, facts_ref.shape) < LANES // 2
    facts_ref[...] = jnp.where(left, total_of(code_grad * code_grad), loss)


def weight_kernel(
    core_ref,
    codes_ref,
    first_w,
    second_w,
    roots,
    scales,
    sum_two,
    sum_codes,
    sum_coord,
    sum_head,
    _,
    sum_loss,
    keep_ref,
    give_ref,
    flat,
    tails,
    first_grad,
    second_grad,
):
    core = core_ref[0]
    codes = codes_ref[...]
    by_code = sum_codes[...]
    code_hi, code_lo = halves(codes)
    by_hi, by_lo = halves(by_code)
    latent_grad = mm(beside(by_hi, by_hi, by_lo), stacked(code_hi, code_lo, code_hi))

    bias_grad = row_sums(by_code[:, :LANES] + by_code[:, LANES:])
    lane = rows_of_lanes(1, (256, LANES))
    real = rows_of_lanes(0, (256, LANES)) < MIDDLE
    near_grad = 0.0
    for i in range(3):
        column = row_sums(sum_coord[:, i * LANES : (i + 1) * LANES])
        near_grad = jnp.where(lane == i, column, near_grad)
    low_grad = latent_grad[0:256, :]
    first_low = first_w[:, : 2 * LANES]
    first_near = jnp.where(lane < 3, first_w[:, 2 * LANES :], 0.0)
    root, scale = roots[0:256, :], scales[0:256, :]
    product = first_low * low_grad
    product = product[:, :LANES] + product[:, LANES:] + first_near * near_grad
    along = row_sums(product)
    inward = scale * root * root * along
    end = scale * near_grad - first_near * inward
    end = jnp.where(lane == 3, root * along, end)
    end = jnp.where(lane == 4, bias_grad[0:256, :], end)
    low_grad = twice(scale) * low_grad - first_low * twice(inward)
    first_grad[:, : 2 * LANES] = jnp.where(beside(real, real), low_grad, 0.0)
    first_grad[:, 2 * LANES :] = jnp.where(real, end, 0.0)

    is_hidden = rows_of_lanes(1, (HID, 256)) < MIDDLE
    hidden_grad = sum_two[...]
    moved = pltpu.roll(latent_grad[256:768, :], 256 - 3, 1)
    grad_a = jnp.where(is_hidden, hidden_grad, moved)
    grad_b = jnp.where(is_hidden, moved, hidden_grad)
    second_a = second_w[:, 0:256]
    second_b = second_w[:, 256:512]
    root, scale = roots[256:768, :], scales[256:768, :]
    product = second_a * grad_a + second_b * grad_b
    along = row_sums(product[:, :LANES] + product[:, LANES:])
    inward = scale * root * root * along
    second_grad[:, 0:256] = twice(scale) * grad_a - second_a * twice(inward)
    second_grad[:, 256:512] = twice(scale) * grad_b - second_b * twice(inward)
    head_grad = row_sums(sum_head[...])
    lane = rows_of_lanes(1, (HID, LANES))
    end = jnp.where(lane == 0, root * along, 0.0)
    end = jnp.where(lane == 1, bias_grad[256:768, :], end)
    second_grad[:, 512:640] = jnp.where(lane == 2, head_grad, end)

    for ref in (flat, tails):
        clear(ref, 128)
    pack_units(first_grad, flat, tails, *FIRST_UNITS)
    pack_units(second_grad, flat, tails, *SECOND_UNITS)
    row = HEAD_ENTRY // LANES
    lane = rows_of_lanes(1, (1, LANES))
    bias_total = jnp.sum(sum_loss[1:2, :], axis=1, keepdims=True)
    flat[row : row + 1, :] += jnp.where(lane == HEAD_ENTRY % LANES, bias_total, 0.0)
    size = 16 * SHARD_ROWS
    for which in range(2):

        @pl.when(core == which)
        def _(which=which):
            for z in range(4):
                for c in range(2):
                    target = keep_ref if c == which else give_ref
                    first = (z * 2 + c) * size
                    target[z * size : (z + 1) * size, :] = (
                        flat[first : first + size, :] + tails[first : first + size, :]
                    )


def vmem(count):
    return [pl.BlockSpec(memory_space=pltpu.VMEM)] * count


PARAMS = pltpu.CompilerParams(vmem_limit_bytes=48 * 1024 * 1024)


SMEM = pl.BlockSpec(memory_space=pltpu.SMEM)


def f32(*shape):
    return jax.ShapeDtypeStruct(shape, F32)


def pack_boxes(weights, points, index):
    return pl.pallas_call(
        pack_kernel,
        out_shape=f32(PEERS * BOX_ROWS, LANES),
        in_specs=vmem(3),
        out_specs=vmem(1)[0],
        compiler_params=PARAMS,
    )(weights, points, index)


def main_kernel(
    core_ref, mine_ref, other_ref, codes_ref, keep_ref, give_ref, code_grad_ref, facts_ref, *scratch
):
    first_w, second_w, latent_w, roots, scales, *sums = scratch[:11]
    flat = scratch[11]
    loop_kernel(core_ref, mine_ref, other_ref, codes_ref, *scratch[:-3])
    code_kernel(codes_ref, latent_w, sums[1], sums[4], sums[5], code_grad_ref, facts_ref)
    weight_kernel(core_ref, codes_ref, first_w, second_w, roots, scales, *sums, keep_ref, give_ref, flat, *scratch[-3:])


def main_call(core, mine, other, codes):
    pair = (SUBS, 256, BLOCK)
    pair_two = (SUBS, HID, BLOCK)
    scratch = [
        ((256, 3 * LANES), F32),
        ((HID, 5 * LANES), F32),
        ((768, 256), F32),
        ((768, LANES), F32),
        ((768, LANES), F32),
        ((HID, 256), F32),
        ((768, 256), F32),
        ((256, 3 * LANES), F32),
        ((HID, LANES), F32),
        ((8, CODE_ROWS), F32),
        ((2, BLOCK), F32),
        ((FLAT_ROWS + 8, LANES), F32),
        ((768, CODE_ROWS), F32),
        ((HID, 768), BF16),
        ((256, 1536), BF16),
        ((256, 3 * LANES), F32),
        ((HID, 2 * LANES), F32),
        ((LANES, LANES), F32),
        (pair, F32),
        (pair, F32),
        (pair, F32),
        (pair, BF16),
        (pair, BF16),
        ((SUBS, BLOCK, CODE_ROWS), BF16),
        (pair_two, F32),
        (pair_two, F32),
        (pair_two, F32),
        (pair_two, F32),
        (pair_two, BF16),
        (pair_two, BF16),
        (pair, BF16),
        (pair, BF16),
        (pair_two, BF16),
        (pair_two, BF16),
        (pair, BF16),
        (pair, BF16),
        ((FLAT_ROWS + 8, LANES), F32),
        ((256, 3 * LANES), F32),
        ((HID, 5 * LANES), F32),
    ]
    boxes = f32(PEERS * SHARD_ROWS, LANES)
    return pl.pallas_call(
        main_kernel,
        out_shape=(boxes, boxes, f32(CODE_ROWS, LATENT), f32(8, LANES)),
        in_specs=[SMEM] + vmem(3),
        out_specs=tuple(vmem(4)),
        scratch_shapes=[pltpu.VMEM(shape, dtype) for shape, dtype in scratch],
        compiler_params=PARAMS,
    )(core, mine, other, codes)


def adam_update(value, first, second, grad, rate):
    first_new = BETA_ONE * first + (1.0 - BETA_ONE) * grad
    second_new = BETA_TWO * second + (1.0 - BETA_TWO) * grad * grad
    first_hat = first_new / (1.0 - BETA_ONE**STEP)
    second_hat = second_new / (1.0 - BETA_TWO**STEP)
    value_new = value - rate * (first_hat / (jnp.sqrt(second_hat) + ADAM_EPS) + DECAY * value)
    return (value_new, first_new, second_new)


def shard_kernel(parts_ref, facts_ref, shard_ref, all_facts_ref):
    total = parts_ref[0:SHARD_ROWS, :]
    for peer in range(1, PEERS):
        total = total + parts_ref[peer * SHARD_ROWS : (peer + 1) * SHARD_ROWS, :]
    shard_ref[...] = total
    facts = facts_ref[...]
    left = rows_of_lanes(1, facts.shape) < LANES // 2
    all_facts_ref[...] = facts + jnp.where(left, total_of(total * total), 0.0)


def sum_shards(parts, facts):
    return pl.pallas_call(
        shard_kernel,
        out_shape=(f32(SHARD_ROWS, LANES), f32(8, LANES)),
        in_specs=vmem(2),
        out_specs=tuple(vmem(2)),
        compiler_params=PARAMS,
    )(parts, facts)


def update_kernel(
    seen_ref,
    shard_ref,
    weights_ref,
    moment_one_ref,
    moment_two_ref,
    codes_ref,
    code_first_ref,
    code_second_ref,
    code_grad_ref,
    loss_out,
    norm_out,
    weights_out,
    moment_one_out,
    moment_two_out,
    weights_copy_out,
    codes_out,
    code_first_out,
    code_second_out,
    codes_copy_out,
):
    total = jnp.sum(seen_ref[...], axis=0, keepdims=True)
    loss_out[...] = total[:, LANES // 2 : LANES // 2 + 1]
    norm = jnp.sqrt(total[:, 0:1])
    norm_out[...] = norm
    factor = jnp.minimum(1.0, CLIP / (norm + 1e-06))
    value, first, second = adam_update(
        weights_ref[...],
        moment_one_ref[...],
        moment_two_ref[...],
        factor * shard_ref[...],
        WEIGHT_RATE,
    )
    weights_out[...] = value
    moment_one_out[...] = first
    moment_two_out[...] = second
    weights_copy_out[...] = value.astype(BF16)
    for r in range(0, CODE_ROWS, 32):
        rows = slice(r, r + 32)
        value, first, second = adam_update(
            codes_ref[rows, :],
            code_first_ref[rows, :],
            code_second_ref[rows, :],
            factor * code_grad_ref[rows, :],
            CODE_RATE,
        )
        codes_out[rows, :] = value
        code_first_out[rows, :] = first
        code_second_out[rows, :] = second
        codes_copy_out[rows, :] = value.astype(BF16)


def update_all(*args):
    scalar = jax.ShapeDtypeStruct((1, 1), F32)
    shard = [jax.ShapeDtypeStruct((SHARD_ROWS, LANES), t) for t in (F32, F32, F32, BF16)]
    table = [jax.ShapeDtypeStruct((CODE_ROWS, LATENT), t) for t in (F32, F32, F32, BF16)]
    return pl.pallas_call(
        update_kernel,
        out_shape=(scalar, scalar, *shard, *table),
        in_specs=vmem(9),
        out_specs=tuple(vmem(10)),
        compiler_params=PARAMS,
    )(*args)


def swap_cores(v):
    return lax.ppermute(v, "core", [(0, 1), (1, 0)])


def exchange(v):
    return lax.all_to_all(v, ("z", "wide"), split_axis=0, concat_axis=0)


def body(
    weights_flat,
    moment_one,
    moment_two,
    codes,
    code_first,
    code_second,
    coords,
    distances,
    shape_index,
):
    boxes = pack_boxes(
        weights_flat.reshape(SHARD_ROWS, LANES),
        jnp.concatenate([coords, distances[None]]),
        shape_index.reshape(1, POINTS_DEV),
    )
    mine = exchange(boxes.reshape(PEERS, 1, BOX_ROWS * LANES))
    other = swap_cores(mine)
    core = lax.axis_index("core").astype(jnp.int32).reshape(1)
    keep, give, code_grad, facts = main_call(
        core,
        mine.reshape(PEERS * BOX_ROWS, LANES),
        other.reshape(PEERS * BOX_ROWS, LANES),
        codes,
    )
    pair_sum = (keep + swap_cores(give)).reshape(PEERS, 1, SHARD_ROWS * LANES)
    parts = exchange(pair_sum).reshape(PEERS * SHARD_ROWS, LANES)
    shard, facts = sum_shards(parts, facts)
    facts = facts + swap_cores(facts)
    facts = jnp.broadcast_to(facts[0:1], (PEERS, LANES)).reshape(PEERS, 1, LANES)
    flat = lambda v: v.reshape(SHARD_ROWS, LANES)
    out = update_all(
        exchange(facts).reshape(PEERS, LANES),
        shard,
        flat(weights_flat),
        flat(moment_one),
        flat(moment_two),
        codes,
        code_first,
        code_second,
        code_grad,
    )
    return (
        out[0].reshape(()),
        out[1].reshape(()),
        *[v.reshape(weights_flat.shape) for v in out[2:6]],
        *out[6:],
    )


def solution(mesh):
    parts = Mesh(mesh.devices.reshape(4, 2, 16), ALL)
    return jax.shard_map(
        body,
        mesh=parts,
        in_specs=(
            P(ALL),
            P(ALL),
            P(ALL),
            P(ALL, None),
            P(ALL, None),
            P(ALL, None),
            P(None, ALL),
            P(ALL),
            P(ALL),
        ),
        out_specs=(
            P(),
            P(),
            P(ALL),
            P(ALL),
            P(ALL),
            P(ALL),
            P(ALL, None),
            P(ALL, None),
            P(ALL, None),
            P(ALL, None),
        ),
        check_vma=False,
    )
```
